32 devices in a mesh: group: 2 (over y), ctx: 4 (over z), req: 4 (over x, core).
Axes of the slice: x: 2, y: 2, z: 4, core: 2. Of those that a mesh axis runs over, the one named last changes fastest.
Arguments:
- hidden_states: bfloat16 [8, 512, 3584], P(('group', 'req'), 'ctx'), parts along dimension 0, may hold values from -6 to 6
- queries_base: bfloat16 [8, 512, 2688], P(('group', 'req'), 'ctx'), parts along dimension 0, may hold values from -6 to 6
- kv_base: bfloat16 [8, 512, 768], P(('group', 'req'), 'ctx'), parts along dimension 0, may hold values from -6 to 6
- adapter_down: bfloat16 [128, 3584, 128], P(('group', 'req'), 'ctx'), parts along dimension 0, may hold values from -0.09375 to 0.09375
- adapter_up: bfloat16 [128, 128, 2688], P(('group', 'req'), 'ctx'), parts along dimension 0, may hold values from -0.75 to 0.75
- adapter_ids: int32 [8], P('group'), parts along dimension 0, may hold values from 0 to 63
- adapter_slots: int32 [128], P('group'), parts along dimension 0, may hold values from 0 to 63, each once
- rank_buckets: int32 [128], P('group'), parts along dimension 0, may hold values from 16 to 128, as said below
- lengths: int32 [8], P(('group', 'req')), parts along dimension 0, may hold values from 128 to 512, as said below
Outputs:
- attended: bfloat16 [8, 512, 2688], P(('group', 'req'), 'ctx'), parts along dimension 0
The draws below stay inside these ranges and needn't reach their ends.
There are 2 independent parts, one for each index of `group`. The reference program is written for one: setup_inputs(seed, part) draws one part's arguments, and reference() takes and returns one part's arrays. A program takes and returns all parts, laid end to end along the dimension named above; each array names one. Nothing has to cross between parts.
Inputs may be any that keep to these rules, and one draw needn't show every extreme that they name: `adapter_slots`: each slot once; slot k lies on store shard k // 16. `rank_buckets`: each is 16, 64 or 128. `lengths`: multiples of 128.
All inputs are finite; a program needn't handle non-finite values.
Results may differ from the reference program's by a relative error of at most 0.0076.
Values may be sent and summed in bfloat16 or wider, within the bound.
No kernel may reach another device: no remote copies, remote signals or barrier semaphores. Data moves between devices by JAX's collectives and lax.ppermute only.
A program may use at most 128 MiB of HBM per device.

```python
import math
import jax
import jax.numpy as jnp
import numpy as np
from jax import lax

TOK_DEV = 128
D = 3584
HD = 128
KVH = 3
GROUP = 7
R = 128
QW = 2688
KVW = 384
RANK_SMALL = 16
RANK_MID = 64
ADAPTERS = 64
REQS = 4
CTX_LEN = 512


def draw_queries_base(key, part):
    key = jax.random.fold_in(key, 5)
    base = 1.5 * jax.random.truncated_normal(key, -4.0, 4.0, (REQS, CTX_LEN, QW), jnp.float32)
    return base.astype(jnp.bfloat16)


def draw_kv_base(key, part):
    key = jax.random.fold_in(key, 7)
    first, second = jax.random.split(key)
    keys = 2.0 * jax.random.truncated_normal(first, -3.0, 3.0, (REQS, CTX_LEN, KVW), jnp.float32)
    values = jax.random.truncated_normal(second, -6.0, 6.0, (REQS, CTX_LEN, KVW), jnp.float32)
    return jnp.concatenate([keys, values], axis=2).astype(jnp.bfloat16)


def draw_rank_buckets(key, part):
    key = jax.random.fold_in(key, 3)
    first, second, third = jax.random.split(key, 3)
    picked = jax.random.randint(first, (ADAPTERS,), 0, 3)
    values = jnp.where(picked == 0, RANK_SMALL, jnp.where(picked == 1, RANK_MID, R))
    highest = jax.random.randint(second, (), 0, ADAPTERS)
    lowest = (highest + 1 + jax.random.randint(third, (), 0, ADAPTERS - 1)) % ADAPTERS
    index = jnp.arange(ADAPTERS)
    values = jnp.where(index == highest, R, jnp.where(index == lowest, RANK_SMALL, values))
    return values.astype(jnp.int32)


def draw_lengths(key, part):
    key = jax.random.fold_in(key, 11)
    first, second = jax.random.split(key)
    blocks_all = CTX_LEN // TOK_DEV
    fewest = max(blocks_all // 4, 1)
    blocks = jax.random.randint(first, (REQS,), fewest, blocks_all + 1)
    longest = jax.random.randint(second, (), 0, REQS)
    blocks = jnp.where(jnp.arange(REQS) == longest, blocks_all, blocks)
    return (blocks * TOK_DEV).astype(jnp.int32)


def touch_ends(entries, own_key, smallest, top_value):
    extent = entries.shape
    index_at = [jax.random.randint(jax.random.fold_in(own_key, axis), (), 0, extent[axis]) for axis in range(len(extent))]
    entries = entries.at[tuple(index_at)].set(smallest)
    longest = extent.index(max(extent))
    index_at[longest] = (index_at[longest] + 1) % extent[longest]
    return entries.at[tuple(index_at)].set(top_value)


def block_scale(own_key, extent, cuts, least, high):
    loudness, own = 1.0, jax.random.fold_in(own_key, 6)
    for position, parts in cuts:
        draws = jnp.exp(jax.random.uniform(jax.random.fold_in(own, position), (parts,), jnp.float32, least / len(cuts), high / len(cuts)))
        loudness = loudness * jnp.repeat(draws, extent[position] // parts).reshape([-1 if axis == position else 1 for axis in range(len(extent))])
    return loudness


def rank_table(count, skew):
    portions = [(1 << 20) // math.isqrt(rank ** skew) + 1 for rank in range(1, count + 1)]
    scale = 1 + sum(portions) // (1 << 30)
    return np.cumsum(np.array([max(1, weight // scale) for weight in portions]))


def ranked_ids(own_key, shape, number_of, lean):
    listing = rank_table(number_of, lean)
    pick = jax.random.randint(jax.random.fold_in(own_key, 1), shape, 0, int(listing[number_of - 1]))
    standing = jnp.searchsorted(jnp.asarray(listing, jnp.int32), pick, side="right")
    return jax.random.permutation(jax.random.fold_in(own_key, 2), number_of)[standing].astype(jnp.int32)


def gaussian(own_key, extent, scale, bound, pieces=(), kind=jnp.bfloat16):
    values = jax.random.normal(own_key, extent, jnp.float32) * scale
    if len(pieces) > 0:
        values = block_scale(own_key, extent, pieces, -0.22, 0.18) * values
    return jnp.clip(values, min=-bound, max=bound).astype(kind)


def setup_inputs(seed: int = 0, part: int = 0) -> dict:
    seeds = jax.random.split(jax.random.key(seed), 10)
    part_splits = jax.random.split(jax.random.fold_in(seeds[9], part), 10)
    hidden_states = gaussian(part_splits[0], (REQS, CTX_LEN, D), 1.0, 6.0, ((0, 4), (1, 4)))
    queries_base = draw_queries_base(jax.random.fold_in(jax.random.fold_in(seeds[9], part), 71), part)
    kv_base = draw_kv_base(jax.random.fold_in(jax.random.fold_in(seeds[9], part), 71), part)
    adapter_down = gaussian(part_splits[3], (ADAPTERS, D, R), D ** -0.5, 0.09375, ((0, 4), (1, 4)))
    adapter_up = gaussian(part_splits[4], (ADAPTERS, R, QW), (R // 2) ** -0.5, 0.75, ((0, 4), (1, 4)))
    adapter_ids = touch_ends(ranked_ids(part_splits[5], (REQS,), ADAPTERS, 2), jax.random.fold_in(part_splits[5], 3), 0, ADAPTERS - 1).astype(jnp.int32)
    adapter_slots = jax.random.permutation(part_splits[6], ADAPTERS).astype(jnp.int32)
    rank_buckets = draw_rank_buckets(jax.random.fold_in(jax.random.fold_in(seeds[9], part), 71), part)
    lengths = draw_lengths(jax.random.fold_in(jax.random.fold_in(seeds[9], part), 71), part)
    return {"hidden_states": hidden_states, "queries_base": queries_base, "kv_base": kv_base, "adapter_down": adapter_down, "adapter_up": adapter_up, "adapter_ids": adapter_ids, "adapter_slots": adapter_slots, "rank_buckets": rank_buckets, "lengths": lengths}


def attend_request(features, base, packed, down, upper, rank, length):
    low_rank = jnp.dot(features, down, preferred_element_type=jnp.float32)
    low_rank = jnp.where(jnp.arange(R)[None, :] < rank, low_rank, 0.0).astype(jnp.bfloat16)
    queries = (base.astype(jnp.float32) + jnp.dot(low_rank, upper, preferred_element_type=jnp.float32)).astype(jnp.bfloat16)
    keys = packed[:, :KVW].astype(jnp.float32).reshape(CTX_LEN, KVH, HD)
    values = packed[:, KVW:].astype(jnp.float32).reshape(CTX_LEN, KVH, HD)
    key_pos = jnp.arange(CTX_LEN, dtype=jnp.int32)
    rows = math.gcd(CTX_LEN, 512)
    scale = 1.0 / math.sqrt(HD)

    def block(index):
        start = (index * rows).astype(jnp.int32)
        block_q = lax.dynamic_slice_in_dim(queries, start, rows, 0).astype(jnp.float32).reshape(rows, KVH, GROUP, HD)
        query_pos = start + jnp.arange(rows, dtype=jnp.int32)
        score = jnp.einsum('tkgd,skd->kgts', block_q, keys) * scale
        allowed = (key_pos[None, :] <= query_pos[:, None]) & (key_pos[None, :] < length)
        masked = jnp.where(allowed, score, -1e+30)
        largest = lax.optimization_barrier(jnp.max(masked, axis=-1, keepdims=True))
        weight = jnp.where(allowed, jnp.exp(score - largest), 0.0)
        total = lax.optimization_barrier(jnp.sum(weight, axis=-1))
        rounded = lax.optimization_barrier(weight.astype(jnp.bfloat16)).astype(jnp.float32)
        output = jnp.einsum('kgts,skd->kgtd', rounded, values) / total[..., None]
        output = jnp.transpose(output, (2, 0, 1, 3)).reshape(rows, KVH * GROUP * HD)
        return jnp.where(query_pos[:, None] < length, output, 0.0).astype(jnp.bfloat16)
    result = lax.map(block, jnp.arange(CTX_LEN // rows, dtype=jnp.int32))
    return result.reshape(CTX_LEN, KVH * GROUP * HD)

def reference(hidden_states, queries_base, kv_base, adapter_down, adapter_up, adapter_ids, adapter_slots, rank_buckets, lengths):
    slots = adapter_slots[adapter_ids]
    ranks = rank_buckets[adapter_ids]

    def request(index):
        slot = slots[index]
        return attend_request(hidden_states[index], queries_base[index], kv_base[index], adapter_down[slot], adapter_up[slot], ranks[index], lengths[index])
    return lax.map(request, jnp.arange(REQS, dtype=jnp.int32))
```

```python
import math

import jax
import jax.numpy as jnp
from jax import lax
from jax.experimental import pallas as pl
from jax.experimental.pallas import tpu as pltpu
from jax.sharding import PartitionSpec as P

HD = 128
KVH = 3
GROUP = 7
HEADS = KVH * GROUP
SMEM = pltpu.SMEM
VMEM = pltpu.VMEM
ANY = pl.ANY
LOG2E = 1.0 / math.log(2.0)


def spec(space):
    return pl.BlockSpec(memory_space=space)


def select_kernel(ids, slots, down, up, out, sems):
    per_shard, down_rows, _ = down.shape
    up_rows = up.shape[1]
    requests = ids.shape[0]
    first = lax.axis_index("req") * per_shard
    for q in range(requests):
        local = slots[ids[q]] - first

        @pl.when((local >= 0) & (local < per_shard))
        def _():
            pltpu.make_async_copy(
                down.at[local], out.at[q, pl.ds(0, down_rows)], sems.at[q]
            ).start()
            for j in range(HEADS):
                pltpu.make_async_copy(
                    up.at[local, :, pl.ds(j * HD, HD)],
                    out.at[q, pl.ds(down_rows + j * up_rows, up_rows)],
                    sems.at[q],
                ).start()

    for q in range(requests):
        local = slots[ids[q]] - first

        @pl.when((local >= 0) & (local < per_shard))
        def _():
            pltpu.make_async_copy(out.at[q], out.at[q], sems.at[q]).wait()


def select(ids, slots, down, up):
    rows = down.shape[1] + HEADS * up.shape[1]
    requests = ids.shape[0]
    return pl.pallas_call(
        select_kernel,
        out_shape=jax.ShapeDtypeStruct((requests, rows, HD), jnp.bfloat16),
        in_specs=[spec(SMEM), spec(SMEM), spec(ANY), spec(ANY)],
        out_specs=spec(ANY),
        scratch_shapes=[pltpu.SemaphoreType.DMA((requests,))],
    )(ids, slots, down, up)


def pack_kernel(ids, slots, got, kv, out, sem, *, per_shard):
    rows = got.shape[1]
    tokens = kv.shape[0]
    owner = slots[ids[lax.axis_index("req")]] // per_shard
    pltpu.make_async_copy(got.at[owner], out.at[pl.ds(0, rows)], sem.at[0]).start()
    for j in range(2 * KVH):
        pltpu.make_async_copy(
            kv.at[:, pl.ds(j * HD, HD)], out.at[pl.ds(rows + j * tokens, tokens)], sem.at[0]
        ).start()
    pltpu.make_async_copy(out, out, sem.at[0]).wait()


def pack(ids, slots, got, kv, per_shard):
    rows = got.shape[1] + 2 * KVH * kv.shape[0]

    def kernel(*refs):
        pack_kernel(*refs, per_shard=per_shard)

    return pl.pallas_call(
        kernel,
        out_shape=jax.ShapeDtypeStruct((rows, HD), jnp.bfloat16),
        in_specs=[spec(SMEM), spec(SMEM), spec(ANY), spec(ANY)],
        out_specs=spec(ANY),
        scratch_shapes=[pltpu.SemaphoreType.DMA((1,))],
    )(ids, slots, got, kv)


def attend_kernel(ids, ranks, lengths, hidden, base, pieces, out, *, down_rows, up_rows):
    shards = pieces.shape[0]
    tokens = hidden.shape[0]
    kv_at = down_rows + HEADS * up_rows
    rank = ranks[ids[lax.axis_index("req")]]
    length = lengths[0]
    first_query = lax.axis_index("ctx") * tokens

    low = jnp.zeros((tokens, HD), jnp.float32)
    for z in range(shards):
        low += jnp.dot(
            hidden[:, z * down_rows : (z + 1) * down_rows],
            pieces[z, :down_rows, :],
            preferred_element_type=jnp.float32,
        )
    column = lax.broadcasted_iota(jnp.int32, (tokens, HD), 1)
    low = jnp.where(column < rank, low, 0.0).astype(jnp.bfloat16)

    count = shards * tokens
    query_pos = first_query + lax.broadcasted_iota(jnp.int32, (tokens, count), 0)
    key_pos = lax.broadcasted_iota(jnp.int32, (tokens, count), 1)
    allowed = (key_pos <= query_pos) & (key_pos < length)
    live = first_query + lax.broadcasted_iota(jnp.int32, (tokens, HD), 0) < length
    factor = LOG2E / math.sqrt(HD)
    for h in range(KVH):
        key_from = kv_at + h * tokens
        value_from = kv_at + (KVH + h) * tokens
        keys = jnp.concatenate(
            [pieces[z, key_from : key_from + tokens, :] for z in range(shards)], axis=0
        )
        values = jnp.concatenate(
            [pieces[z, value_from : value_from + tokens, :] for z in range(shards)], axis=0
        )
        for g in range(GROUP):
            j = h * GROUP + g
            up_from = down_rows + j * up_rows
            up = jnp.concatenate(
                [pieces[z, up_from : up_from + up_rows, :] for z in range(shards)], axis=0
            )
            delta = jnp.dot(low, up, preferred_element_type=jnp.float32)
            columns = slice(j * HD, (j + 1) * HD)
            query = (base[:, columns].astype(jnp.float32) + delta).astype(jnp.bfloat16)
            score = lax.dot_general(
                query, keys, (((1,), (1,)), ((), ())), preferred_element_type=jnp.float32
            )
            masked = jnp.where(allowed, score, -1e30)
            largest = jnp.max(masked, axis=1, keepdims=True)
            weight = jnp.exp2((masked - largest) * factor)
            total = jnp.sum(weight, axis=1, keepdims=True)
            product = jnp.dot(
                weight.astype(jnp.bfloat16), values, preferred_element_type=jnp.float32
            )
            out[:, columns] = jnp.where(live, product / total, 0.0).astype(jnp.bfloat16)


def attend(ids, ranks, lengths, hidden, base, pieces, down_rows, up_rows):
    def kernel(*refs):
        attend_kernel(*refs, down_rows=down_rows, up_rows=up_rows)

    return pl.pallas_call(
        kernel,
        out_shape=jax.ShapeDtypeStruct(base.shape, jnp.bfloat16),
        in_specs=[spec(SMEM)] * 3 + [spec(VMEM)] * 3,
        out_specs=spec(VMEM),
        compiler_params=pltpu.CompilerParams(vmem_limit_bytes=48 * 1024 * 1024),
    )(ids, ranks, lengths, hidden, base, pieces)


def body(
    hidden_states,
    queries_base,
    kv_base,
    adapter_down,
    adapter_up,
    adapter_ids,
    adapter_slots,
    rank_buckets,
    lengths,
):
    per_shard, down_rows, _ = adapter_down.shape
    up_rows = adapter_up.shape[1]
    send = select(adapter_ids, adapter_slots, adapter_down, adapter_up)
    got = lax.all_to_all(send, "req", split_axis=0, concat_axis=0, tiled=True)
    piece = pack(adapter_ids, adapter_slots, got, kv_base[0], per_shard)
    pieces = lax.all_gather(piece, "ctx", axis=0, tiled=False)
    output = attend(
        adapter_ids,
        rank_buckets,
        lengths,
        hidden_states[0],
        queries_base[0],
        pieces,
        down_rows,
        up_rows,
    )
    return output[None]


def plain_body(
    hidden_states,
    queries_base,
    kv_base,
    adapter_down,
    adapter_up,
    adapter_ids,
    adapter_slots,
    rank_buckets,
    lengths,
):
    req_index = lax.axis_index("req")
    ctx_index = lax.axis_index("ctx")
    per_shard = adapter_down.shape[0]
    requests = adapter_ids.shape[0]
    store = adapter_slots.shape[0]
    rank_width = adapter_down.shape[2]
    tokens = hidden_states.shape[1]
    query_width = queries_base.shape[2]
    store_range = jnp.arange(store, dtype=jnp.int32)
    chosen = adapter_ids[:, None] == store_range[None, :]
    slot_of = jnp.sum(jnp.where(chosen, adapter_slots[None, :], 0), axis=1)
    rank_of = jnp.sum(jnp.where(chosen, rank_buckets[None, :], 0), axis=1)
    mine = jnp.arange(requests, dtype=jnp.int32) == req_index
    my_slot = jnp.sum(jnp.where(mine, slot_of, 0))
    my_rank = jnp.sum(jnp.where(mine, rank_of, 0))
    held = (
        slot_of[:, None] == req_index * per_shard + jnp.arange(per_shard, dtype=jnp.int32)[None, :]
    )
    select = held.astype(jnp.bfloat16)
    send_down = jnp.einsum(
        "qa,ard->qrd", select, adapter_down, preferred_element_type=jnp.float32
    ).astype(jnp.bfloat16)
    send_up = jnp.einsum(
        "qa,ard->qrd", select, adapter_up, preferred_element_type=jnp.float32
    ).astype(jnp.bfloat16)
    got_down, got_up = (
        lax.all_to_all(send_down, "req", split_axis=0, concat_axis=0, tiled=True),
        lax.all_to_all(send_up, "req", split_axis=0, concat_axis=0, tiled=True),
    )
    owner = my_slot // per_shard
    down_mine = lax.dynamic_index_in_dim(got_down, owner, 0, keepdims=False)
    up_mine = lax.dynamic_index_in_dim(got_up, owner, 0, keepdims=False)
    features = hidden_states[0]
    columns = features
    low_rank = jnp.dot(
        columns,
        lax.all_gather(down_mine, "ctx", axis=0, tiled=True),
        preferred_element_type=jnp.float32,
    )
    low_rank = jnp.where(
        jnp.arange(rank_width, dtype=jnp.int32)[None, :] < my_rank, low_rank, 0.0
    ).astype(jnp.bfloat16)
    columns = low_rank
    delta = jnp.dot(
        columns,
        lax.all_gather(up_mine, "ctx", axis=0, tiled=True),
        preferred_element_type=jnp.float32,
    )
    queries = (
        (queries_base[0].astype(jnp.float32) + delta)
        .astype(jnp.bfloat16)
        .reshape(tokens, KVH, GROUP, HD)
    )
    length = lengths[0]
    first_query = ctx_index * tokens
    query_pos = first_query + jnp.arange(tokens, dtype=jnp.int32)
    last_needed = jnp.minimum(first_query + tokens - 1, length - 1)
    scale = 1.0 / math.sqrt(HD)
    key_width = KVH * HD
    initial = (
        jnp.full((KVH, GROUP, tokens), -1e30, jnp.float32),
        jnp.zeros((KVH, GROUP, tokens), jnp.float32),
        jnp.zeros((KVH, GROUP, tokens, HD), jnp.float32),
    )
    piece = lax.all_gather(kv_base[0], "ctx", axis=0, tiled=True)
    count = piece.shape[0]
    width = math.gcd(count, 512)

    def key_block(index, state):
        largest, total, accum = state
        offset = index * width
        rows = lax.dynamic_slice_in_dim(piece, offset, width, 0)
        keys = rows[:, :key_width].reshape(width, KVH, HD)
        values = rows[:, key_width:].reshape(width, KVH, HD)
        key_pos = offset + jnp.arange(width, dtype=jnp.int32)
        score = (
            jnp.einsum("tkgd,skd->kgts", queries, keys, preferred_element_type=jnp.float32) * scale
        )
        allowed = (key_pos[None, :] <= query_pos[:, None]) & (key_pos[None, :] < length)
        masked = jnp.where(allowed, score, -1e30)
        newest = jnp.maximum(largest, jnp.max(masked, axis=-1))
        weight = jnp.where(allowed, jnp.exp(score - newest[..., None]), 0.0)
        factor = jnp.exp(largest - newest)
        total = total * factor + jnp.sum(weight, axis=-1)
        product = jnp.einsum(
            "kgts,skd->kgtd",
            weight.astype(jnp.bfloat16),
            values,
            preferred_element_type=jnp.float32,
        )
        accum = accum * factor[..., None] + product
        return (newest, total, accum)

    def compute(state):
        return lax.fori_loop(0, count // width, key_block, state)

    needed = (jnp.int32(0) <= last_needed) & (first_query < length)
    largest, total, accum = lax.cond(needed, compute, lambda state: state, initial)
    safe_total = jnp.where(total > 0.0, total, 1.0)
    output = accum / safe_total[..., None]
    output = jnp.transpose(output, (2, 0, 1, 3)).reshape(tokens, query_width)
    output = jnp.where(query_pos[:, None] < length, output, 0.0).astype(jnp.bfloat16)
    return output[None]


def solution(mesh):
    wide = mesh.shape["ctx"] * mesh.shape["req"] > 16
    return jax.shard_map(
        plain_body if wide else body,
        mesh=mesh,
        in_specs=(
            P(("group", "req"), "ctx", None),
            P(("group", "req"), "ctx", None),
            P(("group", "req"), "ctx", None),
            P(("group", "req"), "ctx", None),
            P(("group", "req"), "ctx", None),
            P("group"),
            P("group"),
            P("group"),
            P(("group", "req")),
        ),
        out_specs=P(("group", "req"), "ctx", None),
        check_vma=False,
    )
```

```python
import functools
import math

import jax
import jax.numpy as jnp
from jax import lax
from jax.experimental import pallas as pl
from jax.experimental.pallas import tpu as pltpu
from jax.sharding import PartitionSpec as P

HD = 128
KVH = 3
GROUP = 7
HEADS = KVH * GROUP
SMEM = pltpu.SMEM
VMEM = pltpu.VMEM
ANY = pl.ANY
LOG2E = 1.0 / math.log(2.0)
PARAMS = pltpu.CompilerParams(vmem_limit_bytes=48 * 1024 * 1024)


def spec(space):
    return pl.BlockSpec(memory_space=space)


def select_kernel(ids, slots, store, keep, give, sems):
    per_shard = store.shape[0]
    me = lax.axis_index("req")
    first = me * per_shard
    targets = [(keep, 0, 0), (keep, 1, 2), (give, 0, 1), (give, 1, 3)]
    for i, (out, k, flip) in enumerate(targets):
        local = slots[ids[me ^ flip]] - first
        held = (local >= 0) & (local < per_shard)

        @pl.when(held)
        def _():
            pltpu.make_async_copy(store.at[local], out.at[k], sems.at[i]).start()

        @pl.when(jnp.logical_not(held))
        def _():
            out[k] = jnp.zeros(out.shape[1:], out.dtype)

    for i, (out, k, flip) in enumerate(targets):
        local = slots[ids[me ^ flip]] - first
        held = (local >= 0) & (local < per_shard)

        @pl.when(held)
        def _():
            pltpu.make_async_copy(store.at[local], out.at[k], sems.at[i]).wait()


def select(ids, slots, store):
    shape = jax.ShapeDtypeStruct((2, *store.shape[1:]), store.dtype)
    return pl.pallas_call(
        select_kernel,
        out_shape=(shape, shape),
        in_specs=[spec(SMEM), spec(SMEM), spec(ANY)],
        out_specs=(spec(VMEM), spec(VMEM)),
        scratch_shapes=[pltpu.SemaphoreType.DMA((4,))],
        compiler_params=PARAMS,
    )(ids, slots, store)


def fetch(ids, slots, store):
    keep, give = select(ids, slots, store)
    near = lax.ppermute(give, "req", [(i, i ^ 1) for i in range(4)])
    far = lax.ppermute(keep[1] + near[1], "req", [(i, i ^ 2) for i in range(4)])
    return keep[0] + near[0] + far


def chain(array, step, count):
    pairs = [(i, i + step) for i in range(count) if 0 <= i + step < count]
    found = []
    for _ in range(count - 1):
        array = lax.ppermute(array, "ctx", pairs)
        found.append(array)
    return found


def order(count):
    return [0] + [-s for s in range(1, count)] + [s for s in range(1, count)]


def low_rank_kernel(ids, ranks, hidden, *rest, count):
    pieces, out, accum = rest[:-2], rest[-2], rest[-1]
    rows = pieces[0].shape[0]
    z = lax.axis_index("ctx")
    rank = ranks[ids[lax.axis_index("req")]]
    accum[...] = jnp.zeros_like(accum)
    for offset, piece in zip(order(count), pieces):
        place = z + offset

        @pl.when((place >= 0) & (place < count))
        def _():
            columns = pl.ds(pl.multiple_of(place * rows, HD), rows)
            accum[...] += jnp.dot(
                hidden[:, columns], piece[...], preferred_element_type=jnp.float32
            )

    column = lax.broadcasted_iota(jnp.int32, accum.shape, 1)
    out[...] = jnp.where(column < rank, accum[...], 0.0).astype(jnp.bfloat16)


def low_rank(ids, ranks, hidden, pieces, count):
    shape = (hidden.shape[0], pieces[0].shape[1])
    return pl.pallas_call(
        functools.partial(low_rank_kernel, count=count),
        out_shape=jax.ShapeDtypeStruct(shape, jnp.bfloat16),
        in_specs=[spec(SMEM)] * 2 + [spec(VMEM)] * (1 + len(pieces)),
        out_specs=spec(VMEM),
        scratch_shapes=[VMEM(shape, jnp.float32)],
        compiler_params=PARAMS,
        cost_estimate=pl.CostEstimate(flops=1 << 27, bytes_accessed=1 << 22, transcendentals=0),
    )(ids, ranks, hidden, *pieces)


def attend_kernel(lengths, base, low, *rest, count):
    kvs, ups = rest[:count], rest[count:-2]
    out, upper = rest[-2:]
    tokens = base.shape[0]
    rows = ups[0].shape[0]
    z = lax.axis_index("ctx")
    for offset, piece in zip(order(count), ups):
        place = z + offset

        @pl.when((place >= 0) & (place < count))
        def _():
            upper[pl.ds(pl.multiple_of(place * rows, rows), rows), :] = piece[...]

    live = z * tokens < lengths[0]
    factor = LOG2E / math.sqrt(HD)
    query_pos = lax.broadcasted_iota(jnp.int32, (tokens, tokens), 0)
    key_pos = lax.broadcasted_iota(jnp.int32, (tokens, tokens), 1)
    causal = key_pos <= query_pos

    @pl.when(jnp.logical_not(live))
    def _():
        out[...] = jnp.zeros_like(out)

    for behind in range(count):

        @pl.when(live & (z == behind))
        def _():
            for h in range(KVH):
                keys = [kv[:, h * HD : (h + 1) * HD] for kv in kvs[: behind + 1]]
                values = [
                    kv[:, (KVH + h) * HD : (KVH + h + 1) * HD] for kv in kvs[: behind + 1]
                ]
                keys = jnp.concatenate(keys, axis=0)
                values = jnp.concatenate(values, axis=0)
                for g in range(GROUP):
                    columns = slice((h * GROUP + g) * HD, (h * GROUP + g + 1) * HD)
                    delta = jnp.dot(low[...], upper[:, columns], preferred_element_type=jnp.float32)
                    query = (base[:, columns].astype(jnp.float32) + delta).astype(jnp.bfloat16)
                    score = lax.dot_general(
                        query, keys, (((1,), (1,)), ((), ())), preferred_element_type=jnp.float32
                    )
                    own = jnp.where(causal, score[:, :tokens], -1e30)
                    if behind:
                        own = jnp.concatenate([own, score[:, tokens:]], axis=1)
                    score = own
                    largest = jnp.max(score, axis=1, keepdims=True)
                    weight = jnp.exp2((score - largest) * factor)
                    total = jnp.sum(weight, axis=1, keepdims=True)
                    product = jnp.dot(
                        weight.astype(jnp.bfloat16), values, preferred_element_type=jnp.float32
                    )
                    out[:, columns] = (product / total).astype(jnp.bfloat16)


def attend(lengths, base, low, kvs, ups, count):
    return pl.pallas_call(
        functools.partial(attend_kernel, count=count),
        out_shape=jax.ShapeDtypeStruct(base.shape, jnp.bfloat16),
        in_specs=[spec(SMEM)] + [spec(VMEM)] * (2 + len(kvs) + len(ups)),
        out_specs=spec(VMEM),
        scratch_shapes=[VMEM((low.shape[1], base.shape[1]), jnp.bfloat16)],
        compiler_params=PARAMS,
        cost_estimate=pl.CostEstimate(
            flops=1 << 30, bytes_accessed=1 << 22, transcendentals=1 << 21
        ),
    )(lengths, base, low, *kvs, *ups)


def body(
    hidden_states,
    queries_base,
    kv_base,
    adapter_down,
    adapter_up,
    adapter_ids,
    adapter_slots,
    rank_buckets,
    lengths,
    *,
    count,
):
    kv = kv_base[0]
    kvs = [kv] + chain(kv, 1, count)
    down = fetch(adapter_ids, adapter_slots, adapter_down)
    downs = [down] + chain(down, 1, count) + chain(down, -1, count)
    up = fetch(adapter_ids, adapter_slots, adapter_up)
    ups = [up] + chain(up, 1, count) + chain(up, -1, count)
    low = low_rank(adapter_ids, rank_buckets, hidden_states[0], downs, count)
    return attend(lengths, queries_base[0], low, kvs, ups, count)[None]


def plain_body(
    hidden_states,
    queries_base,
    kv_base,
    adapter_down,
    adapter_up,
    adapter_ids,
    adapter_slots,
    rank_buckets,
    lengths,
):
    req_index = lax.axis_index("req")
    ctx_index = lax.axis_index("ctx")
    per_shard = adapter_down.shape[0]
    requests = adapter_ids.shape[0]
    store = adapter_slots.shape[0]
    rank_width = adapter_down.shape[2]
    tokens = hidden_states.shape[1]
    query_width = queries_base.shape[2]
    store_range = jnp.arange(store, dtype=jnp.int32)
    chosen = adapter_ids[:, None] == store_range[None, :]
    slot_of = jnp.sum(jnp.where(chosen, adapter_slots[None, :], 0), axis=1)
    rank_of = jnp.sum(jnp.where(chosen, rank_buckets[None, :], 0), axis=1)
    mine = jnp.arange(requests, dtype=jnp.int32) == req_index
    my_slot = jnp.sum(jnp.where(mine, slot_of, 0))
    my_rank = jnp.sum(jnp.where(mine, rank_of, 0))
    held = (
        slot_of[:, None] == req_index * per_shard + jnp.arange(per_shard, dtype=jnp.int32)[None, :]
    )
    select = held.astype(jnp.bfloat16)
    send_down = jnp.einsum(
        "qa,ard->qrd", select, adapter_down, preferred_element_type=jnp.float32
    ).astype(jnp.bfloat16)
    send_up = jnp.einsum(
        "qa,ard->qrd", select, adapter_up, preferred_element_type=jnp.float32
    ).astype(jnp.bfloat16)
    got_down, got_up = (
        lax.all_to_all(send_down, "req", split_axis=0, concat_axis=0, tiled=True),
        lax.all_to_all(send_up, "req", split_axis=0, concat_axis=0, tiled=True),
    )
    owner = my_slot // per_shard
    down_mine = lax.dynamic_index_in_dim(got_down, owner, 0, keepdims=False)
    up_mine = lax.dynamic_index_in_dim(got_up, owner, 0, keepdims=False)
    features = hidden_states[0]
    columns = features
    low_rank = jnp.dot(
        columns,
        lax.all_gather(down_mine, "ctx", axis=0, tiled=True),
        preferred_element_type=jnp.float32,
    )
    low_rank = jnp.where(
        jnp.arange(rank_width, dtype=jnp.int32)[None, :] < my_rank, low_rank, 0.0
    ).astype(jnp.bfloat16)
    columns = low_rank
    delta = jnp.dot(
        columns,
        lax.all_gather(up_mine, "ctx", axis=0, tiled=True),
        preferred_element_type=jnp.float32,
    )
    queries = (
        (queries_base[0].astype(jnp.float32) + delta)
        .astype(jnp.bfloat16)
        .reshape(tokens, KVH, GROUP, HD)
    )
    length = lengths[0]
    first_query = ctx_index * tokens
    query_pos = first_query + jnp.arange(tokens, dtype=jnp.int32)
    last_needed = jnp.minimum(first_query + tokens - 1, length - 1)
    scale = 1.0 / math.sqrt(HD)
    key_width = KVH * HD
    initial = (
        jnp.full((KVH, GROUP, tokens), -1e30, jnp.float32),
        jnp.zeros((KVH, GROUP, tokens), jnp.float32),
        jnp.zeros((KVH, GROUP, tokens, HD), jnp.float32),
    )
    piece = lax.all_gather(kv_base[0], "ctx", axis=0, tiled=True)
    count = piece.shape[0]
    width = math.gcd(count, 512)

    def key_block(index, state):
        largest, total, accum = state
        offset = index * width
        rows = lax.dynamic_slice_in_dim(piece, offset, width, 0)
        keys = rows[:, :key_width].reshape(width, KVH, HD)
        values = rows[:, key_width:].reshape(width, KVH, HD)
        key_pos = offset + jnp.arange(width, dtype=jnp.int32)
        score = (
            jnp.einsum("tkgd,skd->kgts", queries, keys, preferred_element_type=jnp.float32) * scale
        )
        allowed = (key_pos[None, :] <= query_pos[:, None]) & (key_pos[None, :] < length)
        masked = jnp.where(allowed, score, -1e30)
        newest = jnp.maximum(largest, jnp.max(masked, axis=-1))
        weight = jnp.where(allowed, jnp.exp(score - newest[..., None]), 0.0)
        factor = jnp.exp(largest - newest)
        total = total * factor + jnp.sum(weight, axis=-1)
        product = jnp.einsum(
            "kgts,skd->kgtd",
            weight.astype(jnp.bfloat16),
            values,
            preferred_element_type=jnp.float32,
        )
        accum = accum * factor[..., None] + product
        return (newest, total, accum)

    def compute(state):
        return lax.fori_loop(0, count // width, key_block, state)

    needed = (jnp.int32(0) <= last_needed) & (first_query < length)
    largest, total, accum = lax.cond(needed, compute, lambda state: state, initial)
    safe_total = jnp.where(total > 0.0, total, 1.0)
    output = accum / safe_total[..., None]
    output = jnp.transpose(output, (2, 0, 1, 3)).reshape(tokens, query_width)
    output = jnp.where(query_pos[:, None] < length, output, 0.0).astype(jnp.bfloat16)
    return output[None]


def solution(mesh):
    count = mesh.shape["ctx"]
    if count == 4 and mesh.shape["req"] == 4:
        local = functools.partial(body, count=count)
    else:
        local = plain_body
    return jax.shard_map(
        local,
        mesh=mesh,
        in_specs=(
            P(("group", "req"), "ctx", None),
            P(("group", "req"), "ctx", None),
            P(("group", "req"), "ctx", None),
            P(("group", "req"), "ctx", None),
            P(("group", "req"), "ctx", None),
            P("group"),
            P("group"),
            P("group"),
            P(("group", "req")),
        ),
        out_specs=P(("group", "req"), "ctx", None),
        check_vma=False,
    )
```

```python
import math

import jax
import jax.numpy as jnp
from jax import lax
from jax.experimental import pallas as pl
from jax.experimental.pallas import tpu as pltpu
from jax.sharding import PartitionSpec as P

HD = 128
KVH = 3
GROUP = 7
HEADS = KVH * GROUP
SMEM = pltpu.SMEM
VMEM = pltpu.VMEM
HBM = pltpu.HBM
LOG2E = 1.0 / math.log(2.0)
PARAMS = pltpu.CompilerParams(vmem_limit_bytes=48 * 1024 * 1024)
WHOLE = pltpu.CompilerParams(vmem_limit_bytes=62 * 1024 * 1024)


def spec(space):
    return pl.BlockSpec(memory_space=space)


def select_kernel(ids, slots, store, keep, give, sems):
    per_shard = store.shape[0]
    me = lax.axis_index("req")
    first = me * per_shard
    targets = [(keep, 0, 0), (keep, 1, 2), (give, 0, 1), (give, 1, 3)]
    for i, (out, k, flip) in enumerate(targets):
        local = slots[ids[me ^ flip]] - first
        held = (local >= 0) & (local < per_shard)

        @pl.when(held)
        def _():
            pltpu.make_async_copy(store.at[local], out.at[k], sems.at[i]).start()

        @pl.when(jnp.logical_not(held))
        def _():
            out[k] = jnp.zeros(out.shape[1:], out.dtype)

    for i, (out, k, flip) in enumerate(targets):
        local = slots[ids[me ^ flip]] - first
        held = (local >= 0) & (local < per_shard)

        @pl.when(held)
        def _():
            pltpu.make_async_copy(store.at[local], out.at[k], sems.at[i]).wait()


def select(ids, slots, store):
    shape = jax.ShapeDtypeStruct((2, *store.shape[1:]), store.dtype)
    return pl.pallas_call(
        select_kernel,
        out_shape=(shape, shape),
        in_specs=[spec(SMEM), spec(SMEM), spec(HBM)],
        out_specs=(spec(VMEM), spec(VMEM)),
        scratch_shapes=[pltpu.SemaphoreType.DMA((4,))],
        compiler_params=WHOLE,
    )(ids, slots, store)


def fetch(ids, slots, store):
    keep, give = select(ids, slots, store)
    near = lax.ppermute(give, "req", [(i, i ^ 1) for i in range(4)])
    far = lax.ppermute(keep[1] + near[1], "req", [(i, i ^ 2) for i in range(4)])
    return keep[0] + near[0] + far


def spread(shard):
    near = lax.ppermute(shard, "ctx", [(0, 1), (1, 0), (2, 3), (3, 2)])
    cross = lax.ppermute(shard, "ctx", [(0, 3), (3, 0), (1, 2), (2, 1)])
    inner = lax.ppermute(near, "ctx", [(1, 2), (2, 1)])
    outer = lax.ppermute(cross, "ctx", [(1, 0), (2, 3)])
    return [shard, near, cross, inner, outer]


def places(z):
    inner = (z == 1) | (z == 2)
    return [(z, None), (z ^ 1, None), (z ^ 3, None), (z ^ 2, inner), (z ^ 2, jnp.logical_not(inner))]


def when(condition):
    return (lambda f: f()) if condition is None else pl.when(condition)


def spread_up(shard):
    return [
        shard,
        lax.ppermute(shard, "ctx", [(0, 1), (2, 3)]),
        lax.ppermute(shard, "ctx", [(0, 2), (1, 3)]),
        lax.ppermute(shard, "ctx", [(0, 3), (1, 2)]),
    ]


def low_rank_kernel(ids, ranks, hidden, *rest):
    pieces, out, accum = rest[:-2], rest[-2], rest[-1]
    rows = pieces[0].shape[0]
    rank = ranks[ids[lax.axis_index("req")]]
    accum[...] = jnp.zeros_like(accum)
    for (place, there), piece in zip(places(lax.axis_index("ctx")), pieces):

        @when(there)
        def _():
            columns = pl.ds(pl.multiple_of(place * rows, HD), rows)
            accum[...] += jnp.dot(
                hidden[:, columns], piece[...], preferred_element_type=jnp.float32
            )

    column = lax.broadcasted_iota(jnp.int32, accum.shape, 1)
    out[...] = jnp.where(column < rank, accum[...], 0.0).astype(jnp.bfloat16)


def low_rank(ids, ranks, hidden, pieces):
    shape = (hidden.shape[0], pieces[0].shape[1])
    return pl.pallas_call(
        low_rank_kernel,
        out_shape=jax.ShapeDtypeStruct(shape, jnp.bfloat16),
        in_specs=[spec(SMEM)] * 2 + [spec(VMEM)] * (1 + len(pieces)),
        out_specs=spec(VMEM),
        scratch_shapes=[VMEM(shape, jnp.float32)],
        compiler_params=PARAMS,
        cost_estimate=pl.CostEstimate(flops=1 << 27, bytes_accessed=1 << 22, transcendentals=0),
    )(ids, ranks, hidden, *pieces)


def attend_kernel(lengths, base, low, *rest):
    kvs, ups = rest[:4], rest[4:9]
    out, upper, queries = rest[9:]
    tokens = base.shape[0]
    rows = ups[0].shape[0]
    z = lax.axis_index("ctx")
    live = z * tokens < lengths[0]
    factor = LOG2E / math.sqrt(HD)
    block = GROUP * tokens

    @pl.when(live)
    def _():
        for (place, there), piece in zip(places(z), ups):

            @when(there)
            def _():
                upper[pl.ds(pl.multiple_of(place * rows, rows), rows), :] = piece[...]

        for j in range(HEADS):
            columns = slice(j * HD, (j + 1) * HD)
            delta = jnp.dot(low[...], upper[:, columns], preferred_element_type=jnp.float32)
            queries[j * tokens : (j + 1) * tokens, :] = (
                base[:, columns].astype(jnp.float32) + delta
            ).astype(jnp.bfloat16)

    @pl.when(jnp.logical_not(live))
    def _():
        out[...] = jnp.zeros_like(out)

    query_pos = lax.broadcasted_iota(jnp.int32, (tokens, tokens), 0)
    key_pos = lax.broadcasted_iota(jnp.int32, (tokens, tokens), 1)
    causal = key_pos <= query_pos
    for mine, needed in enumerate(((0,), (0, 1), (0, 3, 2), (0, 1, 2, 3))):

        @pl.when(live & (z == mine))
        def _():
            for h in range(KVH):
                keys = [kvs[i][:, h * HD : (h + 1) * HD] for i in needed]
                values = [kvs[i][:, (KVH + h) * HD : (KVH + h + 1) * HD] for i in needed]
                keys = jnp.concatenate(keys, axis=0)
                values = jnp.concatenate(values, axis=0)
                scores = lax.dot_general(
                    queries[h * block : (h + 1) * block, :],
                    keys,
                    (((1,), (1,)), ((), ())),
                    preferred_element_type=jnp.float32,
                )
                weights, totals = [], []
                for g in range(GROUP):
                    score = scores[g * tokens : (g + 1) * tokens, :]
                    own = jnp.where(causal, score[:, :tokens], -1e30)
                    if mine:
                        own = jnp.concatenate([own, score[:, tokens:]], axis=1)
                    largest = jnp.max(own, axis=1, keepdims=True)
                    weight = jnp.exp2((own - largest) * factor)
                    totals.append(jnp.sum(weight, axis=1, keepdims=True))
                    weights.append(weight.astype(jnp.bfloat16))
                product = jnp.dot(
                    jnp.concatenate(weights, axis=0), values, preferred_element_type=jnp.float32
                )
                for g in range(GROUP):
                    j = h * GROUP + g
                    out[:, j * HD : (j + 1) * HD] = (
                        product[g * tokens : (g + 1) * tokens, :] / totals[g]
                    ).astype(jnp.bfloat16)


def attend(lengths, base, low, kvs, ups):
    tokens, width = base.shape
    return pl.pallas_call(
        attend_kernel,
        out_shape=jax.ShapeDtypeStruct(base.shape, jnp.bfloat16),
        in_specs=[spec(SMEM)] + [spec(VMEM)] * (2 + len(kvs) + len(ups)),
        out_specs=spec(VMEM),
        scratch_shapes=[
            VMEM((low.shape[1], width), jnp.bfloat16),
            VMEM((HEADS * tokens, HD), jnp.bfloat16),
        ],
        compiler_params=PARAMS,
        cost_estimate=pl.CostEstimate(
            flops=1 << 30, bytes_accessed=1 << 22, transcendentals=1 << 21
        ),
    )(lengths, base, low, *kvs, *ups)


def body(
    hidden_states,
    queries_base,
    kv_base,
    adapter_down,
    adapter_up,
    adapter_ids,
    adapter_slots,
    rank_buckets,
    lengths,
):
    kvs = spread_up(kv_base[0])
    down = fetch(adapter_ids, adapter_slots, adapter_down)
    down, kvs[1] = lax.optimization_barrier((down, kvs[1]))
    downs = spread(down)
    up = fetch(adapter_ids, adapter_slots, adapter_up)
    up, kvs[2], kvs[3] = lax.optimization_barrier((up, kvs[2], kvs[3]))
    ups = spread(up)
    low = low_rank(adapter_ids, rank_buckets, hidden_states[0], downs)
    return attend(lengths, queries_base[0], low, kvs, ups)[None]


def plain_body(
    hidden_states,
    queries_base,
    kv_base,
    adapter_down,
    adapter_up,
    adapter_ids,
    adapter_slots,
    rank_buckets,
    lengths,
):
    req_index = lax.axis_index("req")
    ctx_index = lax.axis_index("ctx")
    per_shard = adapter_down.shape[0]
    requests = adapter_ids.shape[0]
    store = adapter_slots.shape[0]
    rank_width = adapter_down.shape[2]
    tokens = hidden_states.shape[1]
    query_width = queries_base.shape[2]
    store_range = jnp.arange(store, dtype=jnp.int32)
    chosen = adapter_ids[:, None] == store_range[None, :]
    slot_of = jnp.sum(jnp.where(chosen, adapter_slots[None, :], 0), axis=1)
    rank_of = jnp.sum(jnp.where(chosen, rank_buckets[None, :], 0), axis=1)
    mine = jnp.arange(requests, dtype=jnp.int32) == req_index
    my_slot = jnp.sum(jnp.where(mine, slot_of, 0))
    my_rank = jnp.sum(jnp.where(mine, rank_of, 0))
    held = (
        slot_of[:, None] == req_index * per_shard + jnp.arange(per_shard, dtype=jnp.int32)[None, :]
    )
    select = held.astype(jnp.bfloat16)
    send_down = jnp.einsum(
        "qa,ard->qrd", select, adapter_down, preferred_element_type=jnp.float32
    ).astype(jnp.bfloat16)
    send_up = jnp.einsum(
        "qa,ard->qrd", select, adapter_up, preferred_element_type=jnp.float32
    ).astype(jnp.bfloat16)
    got_down, got_up = (
        lax.all_to_all(send_down, "req", split_axis=0, concat_axis=0, tiled=True),
        lax.all_to_all(send_up, "req", split_axis=0, concat_axis=0, tiled=True),
    )
    owner = my_slot // per_shard
    down_mine = lax.dynamic_index_in_dim(got_down, owner, 0, keepdims=False)
    up_mine = lax.dynamic_index_in_dim(got_up, owner, 0, keepdims=False)
    features = hidden_states[0]
    columns = features
    low_rank = jnp.dot(
        columns,
        lax.all_gather(down_mine, "ctx", axis=0, tiled=True),
        preferred_element_type=jnp.float32,
    )
    low_rank = jnp.where(
        jnp.arange(rank_width, dtype=jnp.int32)[None, :] < my_rank, low_rank, 0.0
    ).astype(jnp.bfloat16)
    columns = low_rank
    delta = jnp.dot(
        columns,
        lax.all_gather(up_mine, "ctx", axis=0, tiled=True),
        preferred_element_type=jnp.float32,
    )
    queries = (
        (queries_base[0].astype(jnp.float32) + delta)
        .astype(jnp.bfloat16)
        .reshape(tokens, KVH, GROUP, HD)
    )
    length = lengths[0]
    first_query = ctx_index * tokens
    query_pos = first_query + jnp.arange(tokens, dtype=jnp.int32)
    last_needed = jnp.minimum(first_query + tokens - 1, length - 1)
    scale = 1.0 / math.sqrt(HD)
    key_width = KVH * HD
    initial = (
        jnp.full((KVH, GROUP, tokens), -1e30, jnp.float32),
        jnp.zeros((KVH, GROUP, tokens), jnp.float32),
        jnp.zeros((KVH, GROUP, tokens, HD), jnp.float32),
    )
    piece = lax.all_gather(kv_base[0], "ctx", axis=0, tiled=True)
    count = piece.shape[0]
    width = math.gcd(count, 512)

    def key_block(index, state):
        largest, total, accum = state
        offset = index * width
        rows = lax.dynamic_slice_in_dim(piece, offset, width, 0)
        keys = rows[:, :key_width].reshape(width, KVH, HD)
        values = rows[:, key_width:].reshape(width, KVH, HD)
        key_pos = offset + jnp.arange(width, dtype=jnp.int32)
        score = (
            jnp.einsum("tkgd,skd->kgts", queries, keys, preferred_element_type=jnp.float32) * scale
        )
        allowed = (key_pos[None, :] <= query_pos[:, None]) & (key_pos[None, :] < length)
        masked = jnp.where(allowed, score, -1e30)
        newest = jnp.maximum(largest, jnp.max(masked, axis=-1))
        weight = jnp.where(allowed, jnp.exp(score - newest[..., None]), 0.0)
        factor = jnp.exp(largest - newest)
        total = total * factor + jnp.sum(weight, axis=-1)
        product = jnp.einsum(
            "kgts,skd->kgtd",
            weight.astype(jnp.bfloat16),
            values,
            preferred_element_type=jnp.float32,
        )
        accum = accum * factor[..., None] + product
        return (newest, total, accum)

    def compute(state):
        return lax.fori_loop(0, count // width, key_block, state)

    needed = (jnp.int32(0) <= last_needed) & (first_query < length)
    largest, total, accum = lax.cond(needed, compute, lambda state: state, initial)
    safe_total = jnp.where(total > 0.0, total, 1.0)
    output = accum / safe_total[..., None]
    output = jnp.transpose(output, (2, 0, 1, 3)).reshape(tokens, query_width)
    output = jnp.where(query_pos[:, None] < length, output, 0.0).astype(jnp.bfloat16)
    return output[None]


def solution(mesh):
    paired = mesh.shape["ctx"] == 4 and mesh.shape["req"] == 4
    return jax.shard_map(
        body if paired else plain_body,
        mesh=mesh,
        in_specs=(
            P(("group", "req"), "ctx", None),
            P(("group", "req"), "ctx", None),
            P(("group", "req"), "ctx", None),
            P(("group", "req"), "ctx", None),
            P(("group", "req"), "ctx", None),
            P("group"),
            P("group"),
            P("group"),
            P(("group", "req")),
        ),
        out_specs=P(("group", "req"), "ctx", None),
        check_vma=False,
    )
```

```python
import math

import jax
import jax.numpy as jnp
from jax import lax
from jax.experimental import pallas as pl
from jax.experimental.pallas import tpu as pltpu
from jax.sharding import PartitionSpec as P

HD = 128
KVH = 3
GROUP = 7
HEADS = KVH * GROUP
SMEM = pltpu.SMEM
VMEM = pltpu.VMEM
HBM = pltpu.HBM
LOG2E = 1.0 / math.log(2.0)
PARAMS = pltpu.CompilerParams(vmem_limit_bytes=48 * 1024 * 1024)
WHOLE = pltpu.CompilerParams(vmem_limit_bytes=52 * 1024 * 1024)


def spec(space):
    return pl.BlockSpec(memory_space=space)


def select_kernel(ids, slots, *rest):
    stores, outs, sems = rest[:2], rest[2:6], rest[6]
    per_shard = stores[0].shape[0]
    me = lax.axis_index("req")
    first = me * per_shard
    copies = []
    for i, flip in enumerate((0, 2, 1, 3)):
        local = slots[ids[me ^ flip]] - first
        held = (local >= 0) & (local < per_shard)
        for f, store in enumerate(stores):
            out = outs[2 * f + i // 2]
            copies.append((held, local, store, out, i % 2, sems.at[4 * f + i]))
    for held, local, store, out, k, sem in copies:

        @pl.when(held)
        def _():
            pltpu.make_async_copy(store.at[local], out.at[k], sem).start()

        @pl.when(jnp.logical_not(held))
        def _():
            out[k] = jnp.zeros(out.shape[1:], out.dtype)

    for held, local, store, out, k, sem in copies:

        @pl.when(held)
        def _():
            pltpu.make_async_copy(store.at[local], out.at[k], sem).wait()


def select(ids, slots, down, up):
    shapes = [jax.ShapeDtypeStruct((2, *x.shape[1:]), x.dtype) for x in (down, down, up, up)]
    return pl.pallas_call(
        select_kernel,
        out_shape=shapes,
        in_specs=[spec(SMEM), spec(SMEM), spec(HBM), spec(HBM)],
        out_specs=[spec(VMEM)] * 4,
        scratch_shapes=[pltpu.SemaphoreType.DMA((8,))],
        compiler_params=WHOLE,
    )(ids, slots, down, up)


SIBLING = [(0, 1), (1, 0), (2, 3), (3, 2)]
ACROSS = [(0, 2), (1, 3), (2, 0), (3, 1)]
def spread(shard):
    near = lax.ppermute(shard, "ctx", [(i, i ^ 1) for i in range(4)])
    two = lax.ppermute(shard, "ctx", [(i, i ^ 2) for i in range(4)])
    cross = lax.ppermute(two, "ctx", [(i, i ^ 1) for i in range(4)])
    return [shard, near, two, cross]


def low_rank_kernel(ids, ranks, hidden, *rest):
    pieces, out, accum = rest[:-2], rest[-2], rest[-1]
    rows = pieces[0].shape[0]
    rank = ranks[ids[lax.axis_index("req")]]
    accum[...] = jnp.zeros_like(accum)
    for flip, piece in enumerate(pieces):
        place = lax.axis_index("ctx") ^ flip
        columns = pl.ds(pl.multiple_of(place * rows, HD), rows)
        accum[...] += jnp.dot(hidden[:, columns], piece[...], preferred_element_type=jnp.float32)

    column = lax.broadcasted_iota(jnp.int32, accum.shape, 1)
    out[...] = jnp.where(column < rank, accum[...], 0.0).astype(jnp.bfloat16)


def low_rank(ids, ranks, hidden, pieces):
    shape = (hidden.shape[0], pieces[0].shape[1])
    return pl.pallas_call(
        low_rank_kernel,
        out_shape=jax.ShapeDtypeStruct(shape, jnp.bfloat16),
        in_specs=[spec(SMEM)] * 2 + [spec(VMEM)] * (1 + len(pieces)),
        out_specs=spec(VMEM),
        scratch_shapes=[VMEM(shape, jnp.float32)],
        compiler_params=PARAMS,
        cost_estimate=pl.CostEstimate(flops=1 << 27, bytes_accessed=1 << 22, transcendentals=0),
    )(ids, ranks, hidden, *pieces)


def attend_kernel(lengths, base, low, *rest):
    kvs, ups = rest[:4], rest[4:8]
    out, upper, queries = rest[8:]
    tokens = base.shape[0]
    rows = ups[0].shape[0]
    z = lax.axis_index("ctx")
    live = z * tokens < lengths[0]
    factor = LOG2E / math.sqrt(HD)
    block = GROUP * tokens

    @pl.when(live)
    def _():
        for flip, piece in enumerate(ups):
            upper[pl.ds(pl.multiple_of((z ^ flip) * rows, rows), rows), :] = piece[...]

        for j in range(HEADS):
            columns = slice(j * HD, (j + 1) * HD)
            delta = jnp.dot(low[...], upper[:, columns], preferred_element_type=jnp.float32)
            queries[j * tokens : (j + 1) * tokens, :] = (
                base[:, columns].astype(jnp.float32) + delta
            ).astype(jnp.bfloat16)

    @pl.when(jnp.logical_not(live))
    def _():
        out[...] = jnp.zeros_like(out)

    query_pos = lax.broadcasted_iota(jnp.int32, (tokens, tokens), 0)
    key_pos = lax.broadcasted_iota(jnp.int32, (tokens, tokens), 1)
    causal = key_pos <= query_pos
    for mine, needed in enumerate(((0,), (0, 1), (0, 2, 3), (0, 1, 2, 3))):

        @pl.when(live & (z == mine))
        def _():
            for h in range(KVH):
                keys = [kvs[i][:, h * HD : (h + 1) * HD] for i in needed]
                values = [kvs[i][:, (KVH + h) * HD : (KVH + h + 1) * HD] for i in needed]
                keys = jnp.concatenate(keys, axis=0)
                values = jnp.concatenate(values, axis=0)
                scores = lax.dot_general(
                    queries[h * block : (h + 1) * block, :],
                    keys,
                    (((1,), (1,)), ((), ())),
                    preferred_element_type=jnp.float32,
                )
                weights, totals = [], []
                for g in range(GROUP):
                    score = scores[g * tokens : (g + 1) * tokens, :]
                    own = jnp.where(causal, score[:, :tokens], -1e30)
                    if mine:
                        own = jnp.concatenate([own, score[:, tokens:]], axis=1)
                    largest = jnp.max(own, axis=1, keepdims=True)
                    weight = jnp.exp2((own - largest) * factor)
                    totals.append(jnp.sum(weight, axis=1, keepdims=True))
                    weights.append(weight.astype(jnp.bfloat16))
                product = jnp.dot(
                    jnp.concatenate(weights, axis=0), values, preferred_element_type=jnp.float32
                )
                for g in range(GROUP):
                    j = h * GROUP + g
                    out[:, j * HD : (j + 1) * HD] = (
                        product[g * tokens : (g + 1) * tokens, :] / totals[g]
                    ).astype(jnp.bfloat16)


def attend(lengths, base, low, kvs, ups):
    tokens, width = base.shape
    return pl.pallas_call(
        attend_kernel,
        out_shape=jax.ShapeDtypeStruct(base.shape, jnp.bfloat16),
        in_specs=[spec(SMEM)] + [spec(VMEM)] * (2 + len(kvs) + len(ups)),
        out_specs=spec(VMEM),
        scratch_shapes=[
            VMEM((low.shape[1], width), jnp.bfloat16),
            VMEM((HEADS * tokens, HD), jnp.bfloat16),
        ],
        compiler_params=PARAMS,
        cost_estimate=pl.CostEstimate(
            flops=1 << 30, bytes_accessed=1 << 22, transcendentals=1 << 21
        ),
    )(lengths, base, low, *kvs, *ups)


def body(
    hidden_states,
    queries_base,
    kv_base,
    adapter_down,
    adapter_up,
    adapter_ids,
    adapter_slots,
    rank_buckets,
    lengths,
):
    keep_down, give_down, keep_up, give_up = select(
        adapter_ids, adapter_slots, adapter_down, adapter_up
    )
    near_down = lax.ppermute(give_down, "req", SIBLING)
    near_up = lax.ppermute(give_up, "req", SIBLING)
    far_down = lax.ppermute(keep_down[1] + near_down[1], "req", ACROSS)
    pass_up, kv = lax.optimization_barrier((keep_up[1] + near_up[1], kv_base[0]))
    far_up = lax.ppermute(pass_up, "req", ACROSS)
    kvs = spread(kv)
    down = keep_down[0] + near_down[0] + far_down
    down, kvs[1] = lax.optimization_barrier((down, kvs[1]))
    downs = spread(down)
    up = keep_up[0] + near_up[0] + far_up
    up, kvs[2] = lax.optimization_barrier((up, kvs[2]))
    ups = spread(up)
    low = low_rank(adapter_ids, rank_buckets, hidden_states[0], downs)
    return attend(lengths, queries_base[0], low, kvs, ups)[None]


def plain_body(
    hidden_states,
    queries_base,
    kv_base,
    adapter_down,
    adapter_up,
    adapter_ids,
    adapter_slots,
    rank_buckets,
    lengths,
):
    req_index = lax.axis_index("req")
    ctx_index = lax.axis_index("ctx")
    per_shard = adapter_down.shape[0]
    requests = adapter_ids.shape[0]
    store = adapter_slots.shape[0]
    rank_width = adapter_down.shape[2]
    tokens = hidden_states.shape[1]
    query_width = queries_base.shape[2]
    store_range = jnp.arange(store, dtype=jnp.int32)
    chosen = adapter_ids[:, None] == store_range[None, :]
    slot_of = jnp.sum(jnp.where(chosen, adapter_slots[None, :], 0), axis=1)
    rank_of = jnp.sum(jnp.where(chosen, rank_buckets[None, :], 0), axis=1)
    mine = jnp.arange(requests, dtype=jnp.int32) == req_index
    my_slot = jnp.sum(jnp.where(mine, slot_of, 0))
    my_rank = jnp.sum(jnp.where(mine, rank_of, 0))
    held = (
        slot_of[:, None] == req_index * per_shard + jnp.arange(per_shard, dtype=jnp.int32)[None, :]
    )
    select = held.astype(jnp.bfloat16)
    send_down = jnp.einsum(
        "qa,ard->qrd", select, adapter_down, preferred_element_type=jnp.float32
    ).astype(jnp.bfloat16)
    send_up = jnp.einsum(
        "qa,ard->qrd", select, adapter_up, preferred_element_type=jnp.float32
    ).astype(jnp.bfloat16)
    got_down, got_up = (
        lax.all_to_all(send_down, "req", split_axis=0, concat_axis=0, tiled=True),
        lax.all_to_all(send_up, "req", split_axis=0, concat_axis=0, tiled=True),
    )
    owner = my_slot // per_shard
    down_mine = lax.dynamic_index_in_dim(got_down, owner, 0, keepdims=False)
    up_mine = lax.dynamic_index_in_dim(got_up, owner, 0, keepdims=False)
    features = hidden_states[0]
    columns = features
    low_rank = jnp.dot(
        columns,
        lax.all_gather(down_mine, "ctx", axis=0, tiled=True),
        preferred_element_type=jnp.float32,
    )
    low_rank = jnp.where(
        jnp.arange(rank_width, dtype=jnp.int32)[None, :] < my_rank, low_rank, 0.0
    ).astype(jnp.bfloat16)
    columns = low_rank
    delta = jnp.dot(
        columns,
        lax.all_gather(up_mine, "ctx", axis=0, tiled=True),
        preferred_element_type=jnp.float32,
    )
    queries = (
        (queries_base[0].astype(jnp.float32) + delta)
        .astype(jnp.bfloat16)
        .reshape(tokens, KVH, GROUP, HD)
    )
    length = lengths[0]
    first_query = ctx_index * tokens
    query_pos = first_query + jnp.arange(tokens, dtype=jnp.int32)
    last_needed = jnp.minimum(first_query + tokens - 1, length - 1)
    scale = 1.0 / math.sqrt(HD)
    key_width = KVH * HD
    initial = (
        jnp.full((KVH, GROUP, tokens), -1e30, jnp.float32),
        jnp.zeros((KVH, GROUP, tokens), jnp.float32),
        jnp.zeros((KVH, GROUP, tokens, HD), jnp.float32),
    )
    piece = lax.all_gather(kv_base[0], "ctx", axis=0, tiled=True)
    count = piece.shape[0]
    width = math.gcd(count, 512)

    def key_block(index, state):
        largest, total, accum = state
        offset = index * width
        rows = lax.dynamic_slice_in_dim(piece, offset, width, 0)
        keys = rows[:, :key_width].reshape(width, KVH, HD)
        values = rows[:, key_width:].reshape(width, KVH, HD)
        key_pos = offset + jnp.arange(width, dtype=jnp.int32)
        score = (
            jnp.einsum("tkgd,skd->kgts", queries, keys, preferred_element_type=jnp.float32) * scale
        )
        allowed = (key_pos[None, :] <= query_pos[:, None]) & (key_pos[None, :] < length)
        masked = jnp.where(allowed, score, -1e30)
        newest = jnp.maximum(largest, jnp.max(masked, axis=-1))
        weight = jnp.where(allowed, jnp.exp(score - newest[..., None]), 0.0)
        factor = jnp.exp(largest - newest)
        total = total * factor + jnp.sum(weight, axis=-1)
        product = jnp.einsum(
            "kgts,skd->kgtd",
            weight.astype(jnp.bfloat16),
            values,
            preferred_element_type=jnp.float32,
        )
        accum = accum * factor[..., None] + product
        return (newest, total, accum)

    def compute(state):
        return lax.fori_loop(0, count // width, key_block, state)

    needed = (jnp.int32(0) <= last_needed) & (first_query < length)
    largest, total, accum = lax.cond(needed, compute, lambda state: state, initial)
    safe_total = jnp.where(total > 0.0, total, 1.0)
    output = accum / safe_total[..., None]
    output = jnp.transpose(output, (2, 0, 1, 3)).reshape(tokens, query_width)
    output = jnp.where(query_pos[:, None] < length, output, 0.0).astype(jnp.bfloat16)
    return output[None]


def solution(mesh):
    paired = mesh.shape["ctx"] == 4 and mesh.shape["req"] == 4
    return jax.shard_map(
        body if paired else plain_body,
        mesh=mesh,
        in_specs=(
            P(("group", "req"), "ctx", None),
            P(("group", "req"), "ctx", None),
            P(("group", "req"), "ctx", None),
            P(("group", "req"), "ctx", None),
            P(("group", "req"), "ctx", None),
            P("group"),
            P("group"),
            P("group"),
            P(("group", "req")),
        ),
        out_specs=P(("group", "req"), "ctx", None),
        check_vma=False,
    )
```

```python
import math

import jax
import jax.numpy as jnp
from jax import lax
from jax.experimental import pallas as pl
from jax.experimental.pallas import tpu as pltpu
from jax.sharding import PartitionSpec as P

HD = 128
KVH = 3
GROUP = 7
HEADS = KVH * GROUP
SMEM = pltpu.SMEM
VMEM = pltpu.VMEM
HBM = pltpu.HBM
LOG2E = 1.0 / math.log(2.0)
PARAMS = pltpu.CompilerParams(vmem_limit_bytes=48 * 1024 * 1024)
WHOLE = pltpu.CompilerParams(vmem_limit_bytes=52 * 1024 * 1024)


def spec(space):
    return pl.BlockSpec(memory_space=space)


def select_kernel(ids, slots, *rest):
    stores, outs, sems = rest[:2], rest[2:6], rest[6]
    per_shard = stores[0].shape[0]
    me = lax.axis_index("req")
    first = me * per_shard
    copies = []
    for i, flip in enumerate((0, 2, 1, 3)):
        local = slots[ids[me ^ flip]] - first
        held = (local >= 0) & (local < per_shard)
        for f, store in enumerate(stores):
            out = outs[2 * f + i // 2]
            copies.append((held, local, store, out, i % 2, sems.at[4 * f + i]))
    for held, local, store, out, k, sem in copies:

        @pl.when(held)
        def _():
            pltpu.make_async_copy(store.at[local], out.at[k], sem).start()

        @pl.when(jnp.logical_not(held))
        def _():
            out[k] = jnp.zeros(out.shape[1:], out.dtype)

    for held, local, store, out, k, sem in copies:

        @pl.when(held)
        def _():
            pltpu.make_async_copy(store.at[local], out.at[k], sem).wait()


def select(ids, slots, down, up):
    shapes = [jax.ShapeDtypeStruct((2, *x.shape[1:]), x.dtype) for x in (down, down, up, up)]
    return pl.pallas_call(
        select_kernel,
        out_shape=shapes,
        in_specs=[spec(SMEM), spec(SMEM), spec(HBM), spec(HBM)],
        out_specs=[spec(VMEM)] * 4,
        scratch_shapes=[pltpu.SemaphoreType.DMA((8,))],
        compiler_params=WHOLE,
    )(ids, slots, down, up)


SIBLING = [(0, 1), (1, 0), (2, 3), (3, 2)]
ACROSS = [(0, 2), (1, 3), (2, 0), (3, 1)]
def spread(shard):
    near = lax.ppermute(shard, "ctx", [(i, i ^ 1) for i in range(4)])
    two = lax.ppermute(shard, "ctx", [(i, i ^ 2) for i in range(4)])
    cross = lax.ppermute(two, "ctx", [(i, i ^ 1) for i in range(4)])
    return [shard, near, two, cross]


def low_rank_kernel(ids, ranks, hidden, *rest):
    pieces, out, accum = rest[:-2], rest[-2], rest[-1]
    rows = pieces[0].shape[0]
    rank = ranks[ids[lax.axis_index("req")]]
    accum[...] = jnp.zeros_like(accum)
    for flip, piece in enumerate(pieces):
        place = lax.axis_index("ctx") ^ flip
        columns = pl.ds(pl.multiple_of(place * rows, HD), rows)
        accum[...] += jnp.dot(hidden[:, columns], piece[...], preferred_element_type=jnp.float32)

    column = lax.broadcasted_iota(jnp.int32, accum.shape, 1)
    out[...] = jnp.where(column < rank, accum[...], 0.0).astype(jnp.bfloat16)


def low_rank(ids, ranks, hidden, pieces):
    shape = (hidden.shape[0], pieces[0].shape[1])
    return pl.pallas_call(
        low_rank_kernel,
        out_shape=jax.ShapeDtypeStruct(shape, jnp.bfloat16),
        in_specs=[spec(SMEM)] * 2 + [spec(VMEM)] * (1 + len(pieces)),
        out_specs=spec(VMEM),
        scratch_shapes=[VMEM(shape, jnp.float32)],
        compiler_params=PARAMS,
        cost_estimate=pl.CostEstimate(flops=1 << 27, bytes_accessed=1 << 22, transcendentals=0),
    )(ids, ranks, hidden, *pieces)


def attend_kernel(lengths, base, low, *rest):
    kvs, ups = rest[:4], rest[4:8]
    out, upper, queries = rest[8:]
    tokens = base.shape[0]
    rows = ups[0].shape[0]
    z = lax.axis_index("ctx")
    live = z * tokens < lengths[0]
    factor = LOG2E / math.sqrt(HD)
    block = GROUP * tokens

    @pl.when(live)
    def _():
        for flip, piece in enumerate(ups):
            upper[pl.ds(pl.multiple_of((z ^ flip) * rows, rows), rows), :] = piece[...]

        for j in range(HEADS):
            columns = slice(j * HD, (j + 1) * HD)
            delta = jnp.dot(low[...], upper[:, columns], preferred_element_type=jnp.float32)
            queries[j * tokens : (j + 1) * tokens, :] = (
                base[:, columns].astype(jnp.float32) + delta
            ).astype(jnp.bfloat16)

    @pl.when(jnp.logical_not(live))
    def _():
        out[...] = jnp.zeros_like(out)

    query_pos = lax.broadcasted_iota(jnp.int32, (tokens, tokens), 0)
    key_pos = lax.broadcasted_iota(jnp.int32, (tokens, tokens), 1)
    causal = key_pos <= query_pos
    for mine, needed in enumerate(((0,), (0, 1), (0, 2, 3), (0, 1, 2, 3))):

        @pl.when(live & (z == mine))
        def _():
            for h in range(KVH):
                keys = [kvs[i][:, h * HD : (h + 1) * HD] for i in needed]
                values = [kvs[i][:, (KVH + h) * HD : (KVH + h + 1) * HD] for i in needed]
                keys = jnp.concatenate(keys, axis=0)
                values = jnp.concatenate(values, axis=0)
                scores = lax.dot_general(
                    queries[h * block : (h + 1) * block, :],
                    keys,
                    (((1,), (1,)), ((), ())),
                    preferred_element_type=jnp.float32,
                )
                weights, totals = [], []
                for g in range(GROUP):
                    score = scores[g * tokens : (g + 1) * tokens, :]
                    own = jnp.where(causal, score[:, :tokens], -1e30)
                    if mine:
                        own = jnp.concatenate([own, score[:, tokens:]], axis=1)
                    largest = jnp.max(own, axis=1, keepdims=True)
                    weight = jnp.exp2((own - largest) * factor)
                    totals.append(jnp.sum(weight, axis=1, keepdims=True))
                    weights.append(weight.astype(jnp.bfloat16))
                product = jnp.dot(
                    jnp.concatenate(weights, axis=0), values, preferred_element_type=jnp.float32
                )
                for g in range(GROUP):
                    j = h * GROUP + g
                    out[:, j * HD : (j + 1) * HD] = (
                        product[g * tokens : (g + 1) * tokens, :] / totals[g]
                    ).astype(jnp.bfloat16)


def attend(lengths, base, low, kvs, ups):
    tokens, width = base.shape
    return pl.pallas_call(
        attend_kernel,
        out_shape=jax.ShapeDtypeStruct(base.shape, jnp.bfloat16),
        in_specs=[spec(SMEM)] + [spec(VMEM)] * (2 + len(kvs) + len(ups)),
        out_specs=spec(VMEM),
        scratch_shapes=[
            VMEM((low.shape[1], width), jnp.bfloat16),
            VMEM((HEADS * tokens, HD), jnp.bfloat16),
        ],
        compiler_params=PARAMS,
        cost_estimate=pl.CostEstimate(
            flops=1 << 30, bytes_accessed=1 << 22, transcendentals=1 << 21
        ),
    )(lengths, base, low, *kvs, *ups)


def body(
    hidden_states,
    queries_base,
    kv_base,
    adapter_down,
    adapter_up,
    adapter_ids,
    adapter_slots,
    rank_buckets,
    lengths,
):
    keep_down, give_down, keep_up, give_up = select(
        adapter_ids, adapter_slots, adapter_down, adapter_up
    )
    near_down = lax.ppermute(give_down, "req", SIBLING)
    near_up = lax.ppermute(give_up, "req", SIBLING)
    far_down = lax.ppermute(keep_down[1] + near_down[1], "req", ACROSS)
    pass_up = keep_up[1] + near_up[1]
    far_up = lax.ppermute(pass_up, "req", ACROSS)
    kvs = spread(kv_base[0])
    down = keep_down[0] + near_down[0] + far_down
    down, kvs[1] = lax.optimization_barrier((down, kvs[1]))
    downs = spread(down)
    up = keep_up[0] + near_up[0] + far_up
    up, downs[1] = lax.optimization_barrier((up, downs[1]))
    ups = spread(up)
    low = low_rank(adapter_ids, rank_buckets, hidden_states[0], downs)
    return attend(lengths, queries_base[0], low, kvs, ups)[None]


def plain_body(
    hidden_states,
    queries_base,
    kv_base,
    adapter_down,
    adapter_up,
    adapter_ids,
    adapter_slots,
    rank_buckets,
    lengths,
):
    req_index = lax.axis_index("req")
    ctx_index = lax.axis_index("ctx")
    per_shard = adapter_down.shape[0]
    requests = adapter_ids.shape[0]
    store = adapter_slots.shape[0]
    rank_width = adapter_down.shape[2]
    tokens = hidden_states.shape[1]
    query_width = queries_base.shape[2]
    store_range = jnp.arange(store, dtype=jnp.int32)
    chosen = adapter_ids[:, None] == store_range[None, :]
    slot_of = jnp.sum(jnp.where(chosen, adapter_slots[None, :], 0), axis=1)
    rank_of = jnp.sum(jnp.where(chosen, rank_buckets[None, :], 0), axis=1)
    mine = jnp.arange(requests, dtype=jnp.int32) == req_index
    my_slot = jnp.sum(jnp.where(mine, slot_of, 0))
    my_rank = jnp.sum(jnp.where(mine, rank_of, 0))
    held = (
        slot_of[:, None] == req_index * per_shard + jnp.arange(per_shard, dtype=jnp.int32)[None, :]
    )
    select = held.astype(jnp.bfloat16)
    send_down = jnp.einsum(
        "qa,ard->qrd", select, adapter_down, preferred_element_type=jnp.float32
    ).astype(jnp.bfloat16)
    send_up = jnp.einsum(
        "qa,ard->qrd", select, adapter_up, preferred_element_type=jnp.float32
    ).astype(jnp.bfloat16)
    got_down, got_up = (
        lax.all_to_all(send_down, "req", split_axis=0, concat_axis=0, tiled=True),
        lax.all_to_all(send_up, "req", split_axis=0, concat_axis=0, tiled=True),
    )
    owner = my_slot // per_shard
    down_mine = lax.dynamic_index_in_dim(got_down, owner, 0, keepdims=False)
    up_mine = lax.dynamic_index_in_dim(got_up, owner, 0, keepdims=False)
    features = hidden_states[0]
    columns = features
    low_rank = jnp.dot(
        columns,
        lax.all_gather(down_mine, "ctx", axis=0, tiled=True),
        preferred_element_type=jnp.float32,
    )
    low_rank = jnp.where(
        jnp.arange(rank_width, dtype=jnp.int32)[None, :] < my_rank, low_rank, 0.0
    ).astype(jnp.bfloat16)
    columns = low_rank
    delta = jnp.dot(
        columns,
        lax.all_gather(up_mine, "ctx", axis=0, tiled=True),
        preferred_element_type=jnp.float32,
    )
    queries = (
        (queries_base[0].astype(jnp.float32) + delta)
        .astype(jnp.bfloat16)
        .reshape(tokens, KVH, GROUP, HD)
    )
    length = lengths[0]
    first_query = ctx_index * tokens
    query_pos = first_query + jnp.arange(tokens, dtype=jnp.int32)
    last_needed = jnp.minimum(first_query + tokens - 1, length - 1)
    scale = 1.0 / math.sqrt(HD)
    key_width = KVH * HD
    initial = (
        jnp.full((KVH, GROUP, tokens), -1e30, jnp.float32),
        jnp.zeros((KVH, GROUP, tokens), jnp.float32),
        jnp.zeros((KVH, GROUP, tokens, HD), jnp.float32),
    )
    piece = lax.all_gather(kv_base[0], "ctx", axis=0, tiled=True)
    count = piece.shape[0]
    width = math.gcd(count, 512)

    def key_block(index, state):
        largest, total, accum = state
        offset = index * width
        rows = lax.dynamic_slice_in_dim(piece, offset, width, 0)
        keys = rows[:, :key_width].reshape(width, KVH, HD)
        values = rows[:, key_width:].reshape(width, KVH, HD)
        key_pos = offset + jnp.arange(width, dtype=jnp.int32)
        score = (
            jnp.einsum("tkgd,skd->kgts", queries, keys, preferred_element_type=jnp.float32) * scale
        )
        allowed = (key_pos[None, :] <= query_pos[:, None]) & (key_pos[None, :] < length)
        masked = jnp.where(allowed, score, -1e30)
        newest = jnp.maximum(largest, jnp.max(masked, axis=-1))
        weight = jnp.where(allowed, jnp.exp(score - newest[..., None]), 0.0)
        factor = jnp.exp(largest - newest)
        total = total * factor + jnp.sum(weight, axis=-1)
        product = jnp.einsum(
            "kgts,skd->kgtd",
            weight.astype(jnp.bfloat16),
            values,
            preferred_element_type=jnp.float32,
        )
        accum = accum * factor[..., None] + product
        return (newest, total, accum)

    def compute(state):
        return lax.fori_loop(0, count // width, key_block, state)

    needed = (jnp.int32(0) <= last_needed) & (first_query < length)
    largest, total, accum = lax.cond(needed, compute, lambda state: state, initial)
    safe_total = jnp.where(total > 0.0, total, 1.0)
    output = accum / safe_total[..., None]
    output = jnp.transpose(output, (2, 0, 1, 3)).reshape(tokens, query_width)
    output = jnp.where(query_pos[:, None] < length, output, 0.0).astype(jnp.bfloat16)
    return output[None]


def solution(mesh):
    paired = mesh.shape["ctx"] == 4 and mesh.shape["req"] == 4
    return jax.shard_map(
        body if paired else plain_body,
        mesh=mesh,
        in_specs=(
            P(("group", "req"), "ctx", None),
            P(("group", "req"), "ctx", None),
            P(("group", "req"), "ctx", None),
            P(("group", "req"), "ctx", None),
            P(("group", "req"), "ctx", None),
            P("group"),
            P("group"),
            P("group"),
            P(("group", "req")),
        ),
        out_specs=P(("group", "req"), "ctx", None),
        check_vma=False,
    )
```

```python
import functools
import math

import jax
import jax.numpy as jnp
from jax import lax
from jax.experimental import pallas as pl
from jax.experimental.pallas import tpu as pltpu
from jax.sharding import PartitionSpec as P

HD = 128
KVH = 3
GROUP = 7
HEADS = KVH * GROUP
SMEM = pltpu.SMEM
VMEM = pltpu.VMEM
HBM = pltpu.HBM
LOG2E = 1.0 / math.log(2.0)
PARAMS = pltpu.CompilerParams(vmem_limit_bytes=48 * 1024 * 1024)
WHOLE = pltpu.CompilerParams(vmem_limit_bytes=52 * 1024 * 1024)


def spec(space):
    return pl.BlockSpec(memory_space=space)


def select_kernel(ids, slots, down, up, keep, give, sems):
    per_shard, down_rows, _ = down.shape
    up_rows = up.shape[1]
    me = lax.axis_index("req")
    first = me * per_shard
    pieces = []
    for i, flip in enumerate((0, 2, 1, 3)):
        local = slots[ids[me ^ flip]] - first
        held = (local >= 0) & (local < per_shard)
        pieces.append((held, local, (keep, give)[i // 2].at[i % 2], sems.at[i]))
    for held, local, out, sem in pieces:

        @pl.when(held)
        def _():
            pltpu.make_async_copy(down.at[local], out.at[pl.ds(0, down_rows)], sem).start()
            for j in range(HEADS):
                pltpu.make_async_copy(
                    up.at[local, :, pl.ds(j * HD, HD)],
                    out.at[pl.ds(down_rows + j * up_rows, up_rows)],
                    sem,
                ).start()

        @pl.when(jnp.logical_not(held))
        def _():
            out[...] = jnp.zeros(out.shape, out.dtype)

    for held, local, out, sem in pieces:

        @pl.when(held)
        def _():
            pltpu.make_async_copy(out, out, sem).wait()


def select(ids, slots, down, up):
    rows = down.shape[1] + HEADS * up.shape[1]
    shape = jax.ShapeDtypeStruct((2, rows, HD), down.dtype)
    return pl.pallas_call(
        select_kernel,
        out_shape=(shape, shape),
        in_specs=[spec(SMEM), spec(SMEM), spec(HBM), spec(HBM)],
        out_specs=(spec(VMEM), spec(VMEM)),
        scratch_shapes=[pltpu.SemaphoreType.DMA((4,))],
        compiler_params=WHOLE,
    )(ids, slots, down, up)


SIBLING = [(0, 1), (1, 0), (2, 3), (3, 2)]
ACROSS = [(0, 2), (1, 3), (2, 0), (3, 1)]
ONE = [(i, i ^ 1) for i in range(4)]
TWO = [(i, i ^ 2) for i in range(4)]
LAST = [(0, 0), (1, 1), (2, 3), (3, 2)]


def spread(shard, forward, *before):
    near = lax.ppermute(shard, "ctx", ONE)
    two = lax.ppermute(shard, "ctx", TWO)
    two, *before = lax.optimization_barrier((two, *before))
    return [shard, near, two, lax.ppermute(two, "ctx", forward), *before]


def chunk_product(hidden, piece, rows, flip):
    place = lax.axis_index("ctx") ^ flip
    columns = pl.ds(pl.multiple_of(place * rows, HD), rows)
    return jnp.dot(hidden[:, columns], piece[:rows, :], preferred_element_type=jnp.float32)


def low_rank_kernel(hidden, *rest, rows):
    pieces, out = rest[:-1], rest[-1]
    out[...] = sum(chunk_product(hidden, piece, rows, i) for i, piece in enumerate(pieces))


def low_rank(hidden, pieces, rows):
    return pl.pallas_call(
        functools.partial(low_rank_kernel, rows=rows),
        out_shape=jax.ShapeDtypeStruct((hidden.shape[0], HD), jnp.float32),
        in_specs=[spec(VMEM)] * (1 + len(pieces)),
        out_specs=spec(VMEM),
        compiler_params=PARAMS,
        cost_estimate=pl.CostEstimate(flops=1 << 27, bytes_accessed=1 << 21, transcendentals=0),
    )(hidden, *pieces)


def attend_kernel(ids, ranks, lengths, hidden, base, low, *rest, down_rows):
    kvs, pieces = rest[:4], rest[4:8]
    out, upper, queries = rest[8:]
    tokens = base.shape[0]
    rows = (pieces[0].shape[0] - down_rows) // HEADS
    z = lax.axis_index("ctx")
    rank = ranks[ids[lax.axis_index("req")]]
    live = z * tokens < lengths[0]
    factor = LOG2E / math.sqrt(HD)
    block = GROUP * tokens

    @pl.when(live)
    def _():
        whole = low[...] + chunk_product(hidden, pieces[3], down_rows, 3)
        column = lax.broadcasted_iota(jnp.int32, whole.shape, 1)
        whole = jnp.where(column < rank, whole, 0.0).astype(jnp.bfloat16)
        for flip, piece in enumerate(pieces):
            place = pl.ds(pl.multiple_of((z ^ flip) * rows, rows), rows)
            for j in range(HEADS):
                start = down_rows + j * rows
                upper[place, j * HD : (j + 1) * HD] = piece[start : start + rows, :]
        for j in range(HEADS):
            columns = slice(j * HD, (j + 1) * HD)
            delta = jnp.dot(whole, upper[:, columns], preferred_element_type=jnp.float32)
            queries[j * tokens : (j + 1) * tokens, :] = (
                base[:, columns].astype(jnp.float32) + delta
            ).astype(jnp.bfloat16)

    @pl.when(jnp.logical_not(live))
    def _():
        out[...] = jnp.zeros_like(out)

    query_pos = lax.broadcasted_iota(jnp.int32, (tokens, tokens), 0)
    key_pos = lax.broadcasted_iota(jnp.int32, (tokens, tokens), 1)
    causal = key_pos <= query_pos
    for mine, needed in enumerate(((0,), (0, 1), (0, 2, 3), (0, 1, 2, 3))):

        @pl.when(live & (z == mine))
        def _():
            for h in range(KVH):
                keys = [kvs[i][:, h * HD : (h + 1) * HD] for i in needed]
                values = [kvs[i][:, (KVH + h) * HD : (KVH + h + 1) * HD] for i in needed]
                keys = jnp.concatenate(keys, axis=0)
                values = jnp.concatenate(values, axis=0)
                scores = lax.dot_general(
                    queries[h * block : (h + 1) * block, :],
                    keys,
                    (((1,), (1,)), ((), ())),
                    preferred_element_type=jnp.float32,
                )
                weights, totals = [], []
                for g in range(GROUP):
                    score = scores[g * tokens : (g + 1) * tokens, :]
                    own = jnp.where(causal, score[:, :tokens], -1e30)
                    if mine:
                        own = jnp.concatenate([own, score[:, tokens:]], axis=1)
                    largest = jnp.max(own, axis=1, keepdims=True)
                    weight = jnp.exp2((own - largest) * factor)
                    totals.append(jnp.sum(weight, axis=1, keepdims=True))
                    weights.append(weight.astype(jnp.bfloat16))
                product = jnp.dot(
                    jnp.concatenate(weights, axis=0), values, preferred_element_type=jnp.float32
                )
                for g in range(GROUP):
                    j = h * GROUP + g
                    out[:, j * HD : (j + 1) * HD] = (
                        product[g * tokens : (g + 1) * tokens, :] / totals[g]
                    ).astype(jnp.bfloat16)


def attend(ids, ranks, lengths, hidden, base, low, kvs, pieces, down_rows):
    tokens, width = base.shape
    return pl.pallas_call(
        functools.partial(attend_kernel, down_rows=down_rows),
        out_shape=jax.ShapeDtypeStruct(base.shape, jnp.bfloat16),
        in_specs=[spec(SMEM)] * 3 + [spec(VMEM)] * (3 + len(kvs) + len(pieces)),
        out_specs=spec(VMEM),
        scratch_shapes=[
            VMEM((low.shape[1], width), jnp.bfloat16),
            VMEM((HEADS * tokens, HD), jnp.bfloat16),
        ],
        compiler_params=PARAMS,
        cost_estimate=pl.CostEstimate(
            flops=1 << 30, bytes_accessed=1 << 22, transcendentals=1 << 21
        ),
    )(ids, ranks, lengths, hidden, base, low, *kvs, *pieces)


def body(
    hidden_states,
    queries_base,
    kv_base,
    adapter_down,
    adapter_up,
    adapter_ids,
    adapter_slots,
    rank_buckets,
    lengths,
):
    down_rows = adapter_down.shape[1]
    keep, give = select(adapter_ids, adapter_slots, adapter_down, adapter_up)
    kvs = spread(kv_base[0], LAST)
    near = lax.ppermute(give, "req", SIBLING)
    far = lax.ppermute(keep[1] + near[1], "req", ACROSS)
    piece = keep[0] + near[0] + far
    piece, kvs[1], kvs[2] = lax.optimization_barrier((piece, kvs[1], kvs[2]))
    *pieces, kvs[3] = spread(piece, ONE, kvs[3])
    low = low_rank(hidden_states[0], pieces[:3], down_rows)
    output = attend(
        adapter_ids,
        rank_buckets,
        lengths,
        hidden_states[0],
        queries_base[0],
        low,
        kvs,
        pieces,
        down_rows,
    )
    return output[None]


def plain_body(
    hidden_states,
    queries_base,
    kv_base,
    adapter_down,
    adapter_up,
    adapter_ids,
    adapter_slots,
    rank_buckets,
    lengths,
):
    req_index = lax.axis_index("req")
    ctx_index = lax.axis_index("ctx")
    per_shard = adapter_down.shape[0]
    requests = adapter_ids.shape[0]
    store = adapter_slots.shape[0]
    rank_width = adapter_down.shape[2]
    tokens = hidden_states.shape[1]
    query_width = queries_base.shape[2]
    store_range = jnp.arange(store, dtype=jnp.int32)
    chosen = adapter_ids[:, None] == store_range[None, :]
    slot_of = jnp.sum(jnp.where(chosen, adapter_slots[None, :], 0), axis=1)
    rank_of = jnp.sum(jnp.where(chosen, rank_buckets[None, :], 0), axis=1)
    mine = jnp.arange(requests, dtype=jnp.int32) == req_index
    my_slot = jnp.sum(jnp.where(mine, slot_of, 0))
    my_rank = jnp.sum(jnp.where(mine, rank_of, 0))
    held = (
        slot_of[:, None] == req_index * per_shard + jnp.arange(per_shard, dtype=jnp.int32)[None, :]
    )
    select = held.astype(jnp.bfloat16)
    send_down = jnp.einsum(
        "qa,ard->qrd", select, adapter_down, preferred_element_type=jnp.float32
    ).astype(jnp.bfloat16)
    send_up = jnp.einsum(
        "qa,ard->qrd", select, adapter_up, preferred_element_type=jnp.float32
    ).astype(jnp.bfloat16)
    got_down, got_up = (
        lax.all_to_all(send_down, "req", split_axis=0, concat_axis=0, tiled=True),
        lax.all_to_all(send_up, "req", split_axis=0, concat_axis=0, tiled=True),
    )
    owner = my_slot // per_shard
    down_mine = lax.dynamic_index_in_dim(got_down, owner, 0, keepdims=False)
    up_mine = lax.dynamic_index_in_dim(got_up, owner, 0, keepdims=False)
    features = hidden_states[0]
    columns = features
    low_rank = jnp.dot(
        columns,
        lax.all_gather(down_mine, "ctx", axis=0, tiled=True),
        preferred_element_type=jnp.float32,
    )
    low_rank = jnp.where(
        jnp.arange(rank_width, dtype=jnp.int32)[None, :] < my_rank, low_rank, 0.0
    ).astype(jnp.bfloat16)
    columns = low_rank
    delta = jnp.dot(
        columns,
        lax.all_gather(up_mine, "ctx", axis=0, tiled=True),
        preferred_element_type=jnp.float32,
    )
    queries = (
        (queries_base[0].astype(jnp.float32) + delta)
        .astype(jnp.bfloat16)
        .reshape(tokens, KVH, GROUP, HD)
    )
    length = lengths[0]
    first_query = ctx_index * tokens
    query_pos = first_query + jnp.arange(tokens, dtype=jnp.int32)
    last_needed = jnp.minimum(first_query + tokens - 1, length - 1)
    scale = 1.0 / math.sqrt(HD)
    key_width = KVH * HD
    initial = (
        jnp.full((KVH, GROUP, tokens), -1e30, jnp.float32),
        jnp.zeros((KVH, GROUP, tokens), jnp.float32),
        jnp.zeros((KVH, GROUP, tokens, HD), jnp.float32),
    )
    piece = lax.all_gather(kv_base[0], "ctx", axis=0, tiled=True)
    count = piece.shape[0]
    width = math.gcd(count, 512)

    def key_block(index, state):
        largest, total, accum = state
        offset = index * width
        rows = lax.dynamic_slice_in_dim(piece, offset, width, 0)
        keys = rows[:, :key_width].reshape(width, KVH, HD)
        values = rows[:, key_width:].reshape(width, KVH, HD)
        key_pos = offset + jnp.arange(width, dtype=jnp.int32)
        score = (
            jnp.einsum("tkgd,skd->kgts", queries, keys, preferred_element_type=jnp.float32) * scale
        )
        allowed = (key_pos[None, :] <= query_pos[:, None]) & (key_pos[None, :] < length)
        masked = jnp.where(allowed, score, -1e30)
        newest = jnp.maximum(largest, jnp.max(masked, axis=-1))
        weight = jnp.where(allowed, jnp.exp(score - newest[..., None]), 0.0)
        factor = jnp.exp(largest - newest)
        total = total * factor + jnp.sum(weight, axis=-1)
        product = jnp.einsum(
            "kgts,skd->kgtd",
            weight.astype(jnp.bfloat16),
            values,
            preferred_element_type=jnp.float32,
        )
        accum = accum * factor[..., None] + product
        return (newest, total, accum)

    def compute(state):
        return lax.fori_loop(0, count // width, key_block, state)

    needed = (jnp.int32(0) <= last_needed) & (first_query < length)
    largest, total, accum = lax.cond(needed, compute, lambda state: state, initial)
    safe_total = jnp.where(total > 0.0, total, 1.0)
    output = accum / safe_total[..., None]
    output = jnp.transpose(output, (2, 0, 1, 3)).reshape(tokens, query_width)
    output = jnp.where(query_pos[:, None] < length, output, 0.0).astype(jnp.bfloat16)
    return output[None]


def solution(mesh):
    paired = mesh.shape["ctx"] == 4 and mesh.shape["req"] == 4
    return jax.shard_map(
        body if paired else plain_body,
        mesh=mesh,
        in_specs=(
            P(("group", "req"), "ctx", None),
            P(("group", "req"), "ctx", None),
            P(("group", "req"), "ctx", None),
            P(("group", "req"), "ctx", None),
            P(("group", "req"), "ctx", None),
            P("group"),
            P("group"),
            P("group"),
            P(("group", "req")),
        ),
        out_specs=P(("group", "req"), "ctx", None),
        check_vma=False,
    )
```

```python
import functools
import math

import jax
import jax.numpy as jnp
from jax import lax
from jax.experimental import pallas as pl
from jax.experimental.pallas import tpu as pltpu
from jax.sharding import PartitionSpec as P

HD = 128
KVH = 3
GROUP = 7
HEADS = KVH * GROUP
SMEM = pltpu.SMEM
VMEM = pltpu.VMEM
HBM = pltpu.HBM
LOG2E = 1.0 / math.log(2.0)
PARAMS = pltpu.CompilerParams(vmem_limit_bytes=48 * 1024 * 1024)
WHOLE = pltpu.CompilerParams(vmem_limit_bytes=52 * 1024 * 1024)


def spec(space):
    return pl.BlockSpec(memory_space=space)


def select_kernel(table, *rest, requests):
    stores, outs, sems = rest[:2], rest[2:6], rest[6]
    per_shard = stores[0].shape[0]
    me = lax.axis_index("req")
    first = me * per_shard
    copies = []
    for i, flip in enumerate((0, 2, 1, 3)):
        local = table[requests + table[me ^ flip]] - first
        held = (local >= 0) & (local < per_shard)
        for f, store in enumerate(stores):
            out = outs[2 * f + i // 2]
            copies.append((held, local, store, out, i % 2, sems.at[4 * f + i]))
    for held, local, store, out, k, sem in copies:

        @pl.when(held)
        def _():
            pltpu.make_async_copy(store.at[local], out.at[k], sem).start()

        @pl.when(jnp.logical_not(held))
        def _():
            out[k] = jnp.zeros(out.shape[1:], out.dtype)

    for held, local, store, out, k, sem in copies:

        @pl.when(held)
        def _():
            pltpu.make_async_copy(store.at[local], out.at[k], sem).wait()


def select(ids, slots, down, up):
    shapes = [jax.ShapeDtypeStruct((2, *x.shape[1:]), x.dtype) for x in (down, down, up, up)]
    return pl.pallas_call(
        functools.partial(select_kernel, requests=ids.shape[0]),
        out_shape=shapes,
        in_specs=[spec(SMEM), spec(HBM), spec(HBM)],
        out_specs=[spec(VMEM)] * 4,
        scratch_shapes=[pltpu.SemaphoreType.DMA((8,))],
        compiler_params=WHOLE,
    )(jnp.concatenate([ids, slots]), down, up)


SIBLING = [(0, 1), (1, 0), (2, 3), (3, 2)]
ACROSS = [(0, 2), (1, 3), (2, 0), (3, 1)]
ONE = [(i, i ^ 1) for i in range(4)]
TWO = [(i, i ^ 2) for i in range(4)]
LAST = [(0, 0), (1, 1), (2, 3), (3, 2)]


def spread(shard):
    return lax.ppermute(shard, "ctx", ONE), lax.ppermute(shard, "ctx", TWO)


def low_rank_kernel(ids, ranks, hidden, *rest):
    pieces, out, accum = rest[:-2], rest[-2], rest[-1]
    rows = pieces[0].shape[0]
    rank = ranks[ids[lax.axis_index("req")]]
    accum[...] = jnp.zeros_like(accum)
    for flip, piece in enumerate(pieces):
        place = lax.axis_index("ctx") ^ flip
        columns = pl.ds(pl.multiple_of(place * rows, HD), rows)
        accum[...] += jnp.dot(hidden[:, columns], piece[...], preferred_element_type=jnp.float32)

    column = lax.broadcasted_iota(jnp.int32, accum.shape, 1)
    out[...] = jnp.where(column < rank, accum[...], 0.0).astype(jnp.bfloat16)


def low_rank(ids, ranks, hidden, pieces):
    shape = (hidden.shape[0], pieces[0].shape[1])
    return pl.pallas_call(
        low_rank_kernel,
        out_shape=jax.ShapeDtypeStruct(shape, jnp.bfloat16),
        in_specs=[spec(SMEM)] * 2 + [spec(VMEM)] * (1 + len(pieces)),
        out_specs=spec(VMEM),
        scratch_shapes=[VMEM(shape, jnp.float32)],
        compiler_params=PARAMS,
        cost_estimate=pl.CostEstimate(flops=1 << 27, bytes_accessed=1 << 22, transcendentals=0),
    )(ids, ranks, hidden, *pieces)


def attend_kernel(lengths, base, low, *rest):
    kvs, ups = rest[:4], rest[4:8]
    out, upper, queries = rest[8:]
    tokens = base.shape[0]
    rows = ups[0].shape[0]
    z = lax.axis_index("ctx")
    live = z * tokens < lengths[0]
    factor = LOG2E / math.sqrt(HD)
    block = GROUP * tokens

    @pl.when(live)
    def _():
        for flip, piece in enumerate(ups):
            upper[pl.ds(pl.multiple_of((z ^ flip) * rows, rows), rows), :] = piece[...]

        for j in range(HEADS):
            columns = slice(j * HD, (j + 1) * HD)
            delta = jnp.dot(low[...], upper[:, columns], preferred_element_type=jnp.float32)
            queries[j * tokens : (j + 1) * tokens, :] = (
                base[:, columns].astype(jnp.float32) + delta
            ).astype(jnp.bfloat16)

    @pl.when(jnp.logical_not(live))
    def _():
        out[...] = jnp.zeros_like(out)

    query_pos = lax.broadcasted_iota(jnp.int32, (tokens, tokens), 0)
    key_pos = lax.broadcasted_iota(jnp.int32, (tokens, tokens), 1)
    causal = key_pos <= query_pos
    for mine, needed in enumerate(((0,), (0, 1), (0, 2, 3), (0, 1, 2, 3))):

        @pl.when(live & (z == mine))
        def _():
            for h in range(KVH):
                keys = [kvs[i][:, h * HD : (h + 1) * HD] for i in needed]
                values = [kvs[i][:, (KVH + h) * HD : (KVH + h + 1) * HD] for i in needed]
                keys = jnp.concatenate(keys, axis=0)
                values = jnp.concatenate(values, axis=0)
                scores = lax.dot_general(
                    queries[h * block : (h + 1) * block, :],
                    keys,
                    (((1,), (1,)), ((), ())),
                    preferred_element_type=jnp.float32,
                )
                weights, totals = [], []
                for g in range(GROUP):
                    score = scores[g * tokens : (g + 1) * tokens, :]
                    own = jnp.where(causal, score[:, :tokens], -1e30)
                    if mine:
                        own = jnp.concatenate([own, score[:, tokens:]], axis=1)
                    largest = jnp.max(own, axis=1, keepdims=True)
                    weight = jnp.exp2((own - largest) * factor)
                    totals.append(jnp.sum(weight, axis=1, keepdims=True))
                    weights.append(weight.astype(jnp.bfloat16))
                product = jnp.dot(
                    jnp.concatenate(weights, axis=0), values, preferred_element_type=jnp.float32
                )
                for g in range(GROUP):
                    j = h * GROUP + g
                    out[:, j * HD : (j + 1) * HD] = (
                        product[g * tokens : (g + 1) * tokens, :] / totals[g]
                    ).astype(jnp.bfloat16)


def attend(lengths, base, low, kvs, ups):
    tokens, width = base.shape
    return pl.pallas_call(
        attend_kernel,
        out_shape=jax.ShapeDtypeStruct(base.shape, jnp.bfloat16),
        in_specs=[spec(SMEM)] + [spec(VMEM)] * (2 + len(kvs) + len(ups)),
        out_specs=spec(VMEM),
        scratch_shapes=[
            VMEM((low.shape[1], width), jnp.bfloat16),
            VMEM((HEADS * tokens, HD), jnp.bfloat16),
        ],
        compiler_params=PARAMS,
        cost_estimate=pl.CostEstimate(
            flops=1 << 30, bytes_accessed=1 << 22, transcendentals=1 << 21
        ),
    )(lengths, base, low, *kvs, *ups)


def body(
    hidden_states,
    queries_base,
    kv_base,
    adapter_down,
    adapter_up,
    adapter_ids,
    adapter_slots,
    rank_buckets,
    lengths,
):
    keep_down, give_down, keep_up, give_up = select(
        adapter_ids, adapter_slots, adapter_down, adapter_up
    )
    near_down = lax.ppermute(give_down, "req", SIBLING)
    near_up = lax.ppermute(give_up, "req", SIBLING)
    pass_down, kv = lax.optimization_barrier((keep_down[1] + near_down[1], kv_base[0]))
    far_down = lax.ppermute(pass_down, "req", ACROSS)
    kv_one, kv_two = spread(kv)
    pass_up, far_down = lax.optimization_barrier((keep_up[1] + near_up[1], far_down))
    far_up = lax.ppermute(pass_up, "req", ACROSS)
    down = keep_down[0] + near_down[0] + far_down
    down, kv_one, kv_two = lax.optimization_barrier((down, kv_one, kv_two))
    down_one, down_two = spread(down)
    kv_three = lax.ppermute(kv_two, "ctx", LAST)
    up = keep_up[0] + near_up[0] + far_up
    up, down_one = lax.optimization_barrier((up, down_one))
    up_one, up_two = spread(up)
    down_two, up_one, kv_three = lax.optimization_barrier((down_two, up_one, kv_three))
    down_three = lax.ppermute(down_two, "ctx", ONE)
    up_three = lax.ppermute(up_two, "ctx", ONE)
    kvs = [kv, kv_one, kv_two, kv_three]
    downs = [down, down_one, down_two, down_three]
    ups = [up, up_one, up_two, up_three]
    low = low_rank(adapter_ids, rank_buckets, hidden_states[0], downs)
    return attend(lengths, queries_base[0], low, kvs, ups)[None]


def plain_body(
    hidden_states,
    queries_base,
    kv_base,
    adapter_down,
    adapter_up,
    adapter_ids,
    adapter_slots,
    rank_buckets,
    lengths,
):
    req_index = lax.axis_index("req")
    ctx_index = lax.axis_index("ctx")
    per_shard = adapter_down.shape[0]
    requests = adapter_ids.shape[0]
    store = adapter_slots.shape[0]
    rank_width = adapter_down.shape[2]
    tokens = hidden_states.shape[1]
    query_width = queries_base.shape[2]
    store_range = jnp.arange(store, dtype=jnp.int32)
    chosen = adapter_ids[:, None] == store_range[None, :]
    slot_of = jnp.sum(jnp.where(chosen, adapter_slots[None, :], 0), axis=1)
    rank_of = jnp.sum(jnp.where(chosen, rank_buckets[None, :], 0), axis=1)
    mine = jnp.arange(requests, dtype=jnp.int32) == req_index
    my_slot = jnp.sum(jnp.where(mine, slot_of, 0))
    my_rank = jnp.sum(jnp.where(mine, rank_of, 0))
    held = (
        slot_of[:, None] == req_index * per_shard + jnp.arange(per_shard, dtype=jnp.int32)[None, :]
    )
    select = held.astype(jnp.bfloat16)
    send_down = jnp.einsum(
        "qa,ard->qrd", select, adapter_down, preferred_element_type=jnp.float32
    ).astype(jnp.bfloat16)
    send_up = jnp.einsum(
        "qa,ard->qrd", select, adapter_up, preferred_element_type=jnp.float32
    ).astype(jnp.bfloat16)
    got_down, got_up = (
        lax.all_to_all(send_down, "req", split_axis=0, concat_axis=0, tiled=True),
        lax.all_to_all(send_up, "req", split_axis=0, concat_axis=0, tiled=True),
    )
    owner = my_slot // per_shard
    down_mine = lax.dynamic_index_in_dim(got_down, owner, 0, keepdims=False)
    up_mine = lax.dynamic_index_in_dim(got_up, owner, 0, keepdims=False)
    features = hidden_states[0]
    columns = features
    low_rank = jnp.dot(
        columns,
        lax.all_gather(down_mine, "ctx", axis=0, tiled=True),
        preferred_element_type=jnp.float32,
    )
    low_rank = jnp.where(
        jnp.arange(rank_width, dtype=jnp.int32)[None, :] < my_rank, low_rank, 0.0
    ).astype(jnp.bfloat16)
    columns = low_rank
    delta = jnp.dot(
        columns,
        lax.all_gather(up_mine, "ctx", axis=0, tiled=True),
        preferred_element_type=jnp.float32,
    )
    queries = (
        (queries_base[0].astype(jnp.float32) + delta)
        .astype(jnp.bfloat16)
        .reshape(tokens, KVH, GROUP, HD)
    )
    length = lengths[0]
    first_query = ctx_index * tokens
    query_pos = first_query + jnp.arange(tokens, dtype=jnp.int32)
    last_needed = jnp.minimum(first_query + tokens - 1, length - 1)
    scale = 1.0 / math.sqrt(HD)
    key_width = KVH * HD
    initial = (
        jnp.full((KVH, GROUP, tokens), -1e30, jnp.float32),
        jnp.zeros((KVH, GROUP, tokens), jnp.float32),
        jnp.zeros((KVH, GROUP, tokens, HD), jnp.float32),
    )
    piece = lax.all_gather(kv_base[0], "ctx", axis=0, tiled=True)
    count = piece.shape[0]
    width = math.gcd(count, 512)

    def key_block(index, state):
        largest, total, accum = state
        offset = index * width
        rows = lax.dynamic_slice_in_dim(piece, offset, width, 0)
        keys = rows[:, :key_width].reshape(width, KVH, HD)
        values = rows[:, key_width:].reshape(width, KVH, HD)
        key_pos = offset + jnp.arange(width, dtype=jnp.int32)
        score = (
            jnp.einsum("tkgd,skd->kgts", queries, keys, preferred_element_type=jnp.float32) * scale
        )
        allowed = (key_pos[None, :] <= query_pos[:, None]) & (key_pos[None, :] < length)
        masked = jnp.where(allowed, score, -1e30)
        newest = jnp.maximum(largest, jnp.max(masked, axis=-1))
        weight = jnp.where(allowed, jnp.exp(score - newest[..., None]), 0.0)
        factor = jnp.exp(largest - newest)
        total = total * factor + jnp.sum(weight, axis=-1)
        product = jnp.einsum(
            "kgts,skd->kgtd",
            weight.astype(jnp.bfloat16),
            values,
            preferred_element_type=jnp.float32,
        )
        accum = accum * factor[..., None] + product
        return (newest, total, accum)

    def compute(state):
        return lax.fori_loop(0, count // width, key_block, state)

    needed = (jnp.int32(0) <= last_needed) & (first_query < length)
    largest, total, accum = lax.cond(needed, compute, lambda state: state, initial)
    safe_total = jnp.where(total > 0.0, total, 1.0)
    output = accum / safe_total[..., None]
    output = jnp.transpose(output, (2, 0, 1, 3)).reshape(tokens, query_width)
    output = jnp.where(query_pos[:, None] < length, output, 0.0).astype(jnp.bfloat16)
    return output[None]


def solution(mesh):
    paired = mesh.shape["ctx"] == 4 and mesh.shape["req"] == 4
    return jax.shard_map(
        body if paired else plain_body,
        mesh=mesh,
        in_specs=(
            P(("group", "req"), "ctx", None),
            P(("group", "req"), "ctx", None),
            P(("group", "req"), "ctx", None),
            P(("group", "req"), "ctx", None),
            P(("group", "req"), "ctx", None),
            P("group"),
            P("group"),
            P("group"),
            P(("group", "req")),
        ),
        out_specs=P(("group", "req"), "ctx", None),
        check_vma=False,
    )
```

```python
import functools
import math

import jax
import jax.numpy as jnp
from jax import lax
from jax.experimental import pallas as pl
from jax.experimental.pallas import tpu as pltpu
from jax.sharding import PartitionSpec as P

HD = 128
KVH = 3
GROUP = 7
HEADS = KVH * GROUP
SMEM = pltpu.SMEM
VMEM = pltpu.VMEM
HBM = pltpu.HBM
LOG2E = 1.0 / math.log(2.0)
PARAMS = pltpu.CompilerParams(vmem_limit_bytes=48 * 1024 * 1024)
WHOLE = pltpu.CompilerParams(vmem_limit_bytes=52 * 1024 * 1024)


def spec(space):
    return pl.BlockSpec(memory_space=space)


def select_kernel(table, *rest, requests):
    stores, outs, sems = rest[:2], rest[2:6], rest[6]
    per_shard = stores[0].shape[0]
    me = lax.axis_index("req")
    first = me * per_shard
    copies = []
    for i, flip in enumerate((0, 2, 1, 3)):
        local = table[requests + table[me ^ flip]] - first
        held = (local >= 0) & (local < per_shard)
        for f, store in enumerate(stores):
            out = outs[2 * f + i // 2]
            copies.append((held, local, store, out, i % 2, sems.at[4 * f + i]))
    for held, local, store, out, k, sem in copies:

        @pl.when(held)
        def _():
            pltpu.make_async_copy(store.at[local], out.at[k], sem).start()

        @pl.when(jnp.logical_not(held))
        def _():
            out[k] = jnp.zeros(out.shape[1:], out.dtype)

    for held, local, store, out, k, sem in copies:

        @pl.when(held)
        def _():
            pltpu.make_async_copy(store.at[local], out.at[k], sem).wait()


def select(ids, slots, down, up):
    shapes = [jax.ShapeDtypeStruct((2, *x.shape[1:]), x.dtype) for x in (down, down, up, up)]
    return pl.pallas_call(
        functools.partial(select_kernel, requests=ids.shape[0]),
        out_shape=shapes,
        in_specs=[spec(SMEM), spec(HBM), spec(HBM)],
        out_specs=[spec(VMEM)] * 4,
        scratch_shapes=[pltpu.SemaphoreType.DMA((8,))],
        compiler_params=WHOLE,
    )(jnp.concatenate([ids, slots]), down, up)


SIBLING = [(0, 1), (1, 0), (2, 3), (3, 2)]
ACROSS = [(0, 2), (1, 3), (2, 0), (3, 1)]
ONE = [(i, i ^ 1) for i in range(4)]
TWO = [(i, i ^ 2) for i in range(4)]
THREE = [(i, i ^ 3) for i in range(4)]


def spread(shard):
    return lax.ppermute(shard, "ctx", ONE), lax.ppermute(shard, "ctx", TWO)


def low_rank_kernel(ids, ranks, hidden, *rest):
    pieces, out, accum = rest[:-2], rest[-2], rest[-1]
    rows = pieces[0].shape[0]
    rank = ranks[ids[lax.axis_index("req")]]
    accum[...] = jnp.zeros_like(accum)
    for flip, piece in enumerate(pieces):
        place = lax.axis_index("ctx") ^ flip
        columns = pl.ds(pl.multiple_of(place * rows, HD), rows)
        accum[...] += jnp.dot(hidden[:, columns], piece[...], preferred_element_type=jnp.float32)

    column = lax.broadcasted_iota(jnp.int32, accum.shape, 1)
    out[...] = jnp.where(column < rank, accum[...], 0.0).astype(jnp.bfloat16)


def low_rank(ids, ranks, hidden, pieces):
    shape = (hidden.shape[0], pieces[0].shape[1])
    return pl.pallas_call(
        low_rank_kernel,
        out_shape=jax.ShapeDtypeStruct(shape, jnp.bfloat16),
        in_specs=[spec(SMEM)] * 2 + [spec(VMEM)] * (1 + len(pieces)),
        out_specs=spec(VMEM),
        scratch_shapes=[VMEM(shape, jnp.float32)],
        compiler_params=PARAMS,
        cost_estimate=pl.CostEstimate(flops=1 << 27, bytes_accessed=1 << 22, transcendentals=0),
    )(ids, ranks, hidden, *pieces)


def attend_kernel(lengths, base, low, *rest):
    kvs, ups = rest[:4], rest[4:8]
    out, upper, queries = rest[8:]
    tokens = base.shape[0]
    rows = ups[0].shape[0]
    z = lax.axis_index("ctx")
    live = z * tokens < lengths[0]
    factor = LOG2E / math.sqrt(HD)
    block = GROUP * tokens

    @pl.when(live)
    def _():
        for flip, piece in enumerate(ups):
            upper[pl.ds(pl.multiple_of((z ^ flip) * rows, rows), rows), :] = piece[...]

        for j in range(HEADS):
            columns = slice(j * HD, (j + 1) * HD)
            delta = jnp.dot(low[...], upper[:, columns], preferred_element_type=jnp.float32)
            queries[j * tokens : (j + 1) * tokens, :] = (
                base[:, columns].astype(jnp.float32) + delta
            ).astype(jnp.bfloat16)

    @pl.when(jnp.logical_not(live))
    def _():
        out[...] = jnp.zeros_like(out)

    query_pos = lax.broadcasted_iota(jnp.int32, (tokens, tokens), 0)
    key_pos = lax.broadcasted_iota(jnp.int32, (tokens, tokens), 1)
    causal = key_pos <= query_pos
    for mine, needed in enumerate(((0,), (0, 1), (0, 2, 3), (0, 1, 2, 3))):

        @pl.when(live & (z == mine))
        def _():
            for h in range(KVH):
                keys = [kvs[i][:, h * HD : (h + 1) * HD] for i in needed]
                values = [kvs[i][:, (KVH + h) * HD : (KVH + h + 1) * HD] for i in needed]
                keys = jnp.concatenate(keys, axis=0)
                values = jnp.concatenate(values, axis=0)
                scores = lax.dot_general(
                    queries[h * block : (h + 1) * block, :],
                    keys,
                    (((1,), (1,)), ((), ())),
                    preferred_element_type=jnp.float32,
                )
                weights, totals = [], []
                for g in range(GROUP):
                    score = scores[g * tokens : (g + 1) * tokens, :]
                    own = jnp.where(causal, score[:, :tokens], -1e30)
                    if mine:
                        own = jnp.concatenate([own, score[:, tokens:]], axis=1)
                    largest = jnp.max(own, axis=1, keepdims=True)
                    weight = jnp.exp2((own - largest) * factor)
                    totals.append(jnp.sum(weight, axis=1, keepdims=True))
                    weights.append(weight.astype(jnp.bfloat16))
                product = jnp.dot(
                    jnp.concatenate(weights, axis=0), values, preferred_element_type=jnp.float32
                )
                for g in range(GROUP):
                    j = h * GROUP + g
                    out[:, j * HD : (j + 1) * HD] = (
                        product[g * tokens : (g + 1) * tokens, :] / totals[g]
                    ).astype(jnp.bfloat16)


def attend(lengths, base, low, kvs, ups):
    tokens, width = base.shape
    return pl.pallas_call(
        attend_kernel,
        out_shape=jax.ShapeDtypeStruct(base.shape, jnp.bfloat16),
        in_specs=[spec(SMEM)] + [spec(VMEM)] * (2 + len(kvs) + len(ups)),
        out_specs=spec(VMEM),
        scratch_shapes=[
            VMEM((low.shape[1], width), jnp.bfloat16),
            VMEM((HEADS * tokens, HD), jnp.bfloat16),
        ],
        compiler_params=PARAMS,
        cost_estimate=pl.CostEstimate(
            flops=1 << 30, bytes_accessed=1 << 22, transcendentals=1 << 21
        ),
    )(lengths, base, low, *kvs, *ups)


def body(
    hidden_states,
    queries_base,
    kv_base,
    adapter_down,
    adapter_up,
    adapter_ids,
    adapter_slots,
    rank_buckets,
    lengths,
):
    keep_down, give_down, keep_up, give_up = select(
        adapter_ids, adapter_slots, adapter_down, adapter_up
    )
    kv = kv_base[0]
    kv_one, kv_two = spread(kv)
    near_down = lax.ppermute(give_down, "req", SIBLING)
    near_up = lax.ppermute(give_up, "req", SIBLING)
    pass_down, kv = lax.optimization_barrier((keep_down[1] + near_down[1], kv))
    far_down = lax.ppermute(pass_down, "req", ACROSS)
    kv_three = lax.ppermute(kv, "ctx", THREE)
    far_up = lax.ppermute(keep_up[1] + near_up[1], "req", ACROSS)
    down = keep_down[0] + near_down[0] + far_down
    down, kv_one, kv_two = lax.optimization_barrier((down, kv_one, kv_two))
    down_one, down_two = spread(down)
    up = keep_up[0] + near_up[0] + far_up
    up_one, up_two = spread(up)
    down_two, up_one, kv_three = lax.optimization_barrier((down_two, up_one, kv_three))
    down_three = lax.ppermute(down_two, "ctx", ONE)
    up_three = lax.ppermute(up_two, "ctx", ONE)
    kvs = [kv, kv_one, kv_two, kv_three]
    downs = [down, down_one, down_two, down_three]
    ups = [up, up_one, up_two, up_three]
    low = low_rank(adapter_ids, rank_buckets, hidden_states[0], downs)
    return attend(lengths, queries_base[0], low, kvs, ups)[None]


def plain_body(
    hidden_states,
    queries_base,
    kv_base,
    adapter_down,
    adapter_up,
    adapter_ids,
    adapter_slots,
    rank_buckets,
    lengths,
):
    req_index = lax.axis_index("req")
    ctx_index = lax.axis_index("ctx")
    per_shard = adapter_down.shape[0]
    requests = adapter_ids.shape[0]
    store = adapter_slots.shape[0]
    rank_width = adapter_down.shape[2]
    tokens = hidden_states.shape[1]
    query_width = queries_base.shape[2]
    store_range = jnp.arange(store, dtype=jnp.int32)
    chosen = adapter_ids[:, None] == store_range[None, :]
    slot_of = jnp.sum(jnp.where(chosen, adapter_slots[None, :], 0), axis=1)
    rank_of = jnp.sum(jnp.where(chosen, rank_buckets[None, :], 0), axis=1)
    mine = jnp.arange(requests, dtype=jnp.int32) == req_index
    my_slot = jnp.sum(jnp.where(mine, slot_of, 0))
    my_rank = jnp.sum(jnp.where(mine, rank_of, 0))
    held = (
        slot_of[:, None] == req_index * per_shard + jnp.arange(per_shard, dtype=jnp.int32)[None, :]
    )
    select = held.astype(jnp.bfloat16)
    send_down = jnp.einsum(
        "qa,ard->qrd", select, adapter_down, preferred_element_type=jnp.float32
    ).astype(jnp.bfloat16)
    send_up = jnp.einsum(
        "qa,ard->qrd", select, adapter_up, preferred_element_type=jnp.float32
    ).astype(jnp.bfloat16)
    got_down, got_up = (
        lax.all_to_all(send_down, "req", split_axis=0, concat_axis=0, tiled=True),
        lax.all_to_all(send_up, "req", split_axis=0, concat_axis=0, tiled=True),
    )
    owner = my_slot // per_shard
    down_mine = lax.dynamic_index_in_dim(got_down, owner, 0, keepdims=False)
    up_mine = lax.dynamic_index_in_dim(got_up, owner, 0, keepdims=False)
    features = hidden_states[0]
    columns = features
    low_rank = jnp.dot(
        columns,
        lax.all_gather(down_mine, "ctx", axis=0, tiled=True),
        preferred_element_type=jnp.float32,
    )
    low_rank = jnp.where(
        jnp.arange(rank_width, dtype=jnp.int32)[None, :] < my_rank, low_rank, 0.0
    ).astype(jnp.bfloat16)
    columns = low_rank
    delta = jnp.dot(
        columns,
        lax.all_gather(up_mine, "ctx", axis=0, tiled=True),
        preferred_element_type=jnp.float32,
    )
    queries = (
        (queries_base[0].astype(jnp.float32) + delta)
        .astype(jnp.bfloat16)
        .reshape(tokens, KVH, GROUP, HD)
    )
    length = lengths[0]
    first_query = ctx_index * tokens
    query_pos = first_query + jnp.arange(tokens, dtype=jnp.int32)
    last_needed = jnp.minimum(first_query + tokens - 1, length - 1)
    scale = 1.0 / math.sqrt(HD)
    key_width = KVH * HD
    initial = (
        jnp.full((KVH, GROUP, tokens), -1e30, jnp.float32),
        jnp.zeros((KVH, GROUP, tokens), jnp.float32),
        jnp.zeros((KVH, GROUP, tokens, HD), jnp.float32),
    )
    piece = lax.all_gather(kv_base[0], "ctx", axis=0, tiled=True)
    count = piece.shape[0]
    width = math.gcd(count, 512)

    def key_block(index, state):
        largest, total, accum = state
        offset = index * width
        rows = lax.dynamic_slice_in_dim(piece, offset, width, 0)
        keys = rows[:, :key_width].reshape(width, KVH, HD)
        values = rows[:, key_width:].reshape(width, KVH, HD)
        key_pos = offset + jnp.arange(width, dtype=jnp.int32)
        score = (
            jnp.einsum("tkgd,skd->kgts", queries, keys, preferred_element_type=jnp.float32) * scale
        )
        allowed = (key_pos[None, :] <= query_pos[:, None]) & (key_pos[None, :] < length)
        masked = jnp.where(allowed, score, -1e30)
        newest = jnp.maximum(largest, jnp.max(masked, axis=-1))
        weight = jnp.where(allowed, jnp.exp(score - newest[..., None]), 0.0)
        factor = jnp.exp(largest - newest)
        total = total * factor + jnp.sum(weight, axis=-1)
        product = jnp.einsum(
            "kgts,skd->kgtd",
            weight.astype(jnp.bfloat16),
            values,
            preferred_element_type=jnp.float32,
        )
        accum = accum * factor[..., None] + product
        return (newest, total, accum)

    def compute(state):
        return lax.fori_loop(0, count // width, key_block, state)

    needed = (jnp.int32(0) <= last_needed) & (first_query < length)
    largest, total, accum = lax.cond(needed, compute, lambda state: state, initial)
    safe_total = jnp.where(total > 0.0, total, 1.0)
    output = accum / safe_total[..., None]
    output = jnp.transpose(output, (2, 0, 1, 3)).reshape(tokens, query_width)
    output = jnp.where(query_pos[:, None] < length, output, 0.0).astype(jnp.bfloat16)
    return output[None]


def solution(mesh):
    paired = mesh.shape["ctx"] == 4 and mesh.shape["req"] == 4
    return jax.shard_map(
        body if paired else plain_body,
        mesh=mesh,
        in_specs=(
            P(("group", "req"), "ctx", None),
            P(("group", "req"), "ctx", None),
            P(("group", "req"), "ctx", None),
            P(("group", "req"), "ctx", None),
            P(("group", "req"), "ctx", None),
            P("group"),
            P("group"),
            P("group"),
            P(("group", "req")),
        ),
        out_specs=P(("group", "req"), "ctx", None),
        check_vma=False,
    )
```

```python
import functools
import math

import jax
import jax.numpy as jnp
from jax import lax
from jax.experimental import pallas as pl
from jax.experimental.pallas import tpu as pltpu
from jax.sharding import PartitionSpec as P

HD = 128
KVH = 3
GROUP = 7
HEADS = KVH * GROUP
SMEM = pltpu.SMEM
VMEM = pltpu.VMEM
HBM = pltpu.HBM
LOG2E = 1.0 / math.log(2.0)
PARAMS = pltpu.CompilerParams(vmem_limit_bytes=48 * 1024 * 1024)
WHOLE = pltpu.CompilerParams(vmem_limit_bytes=52 * 1024 * 1024)


def spec(space):
    return pl.BlockSpec(memory_space=space)


def select_kernel(table, *rest, requests):
    stores, outs, sems = rest[:2], rest[2:6], rest[6]
    per_shard = stores[0].shape[0]
    me = lax.axis_index("req")
    first = me * per_shard
    copies = []
    for i, flip in enumerate((0, 2, 1, 3)):
        local = table[requests + table[me ^ flip]] - first
        held = (local >= 0) & (local < per_shard)
        for f, store in enumerate(stores):
            out = outs[2 * f + i // 2]
            copies.append((held, local, store, out, i % 2, sems.at[4 * f + i]))
    for held, local, store, out, k, sem in copies:

        @pl.when(held)
        def _():
            pltpu.make_async_copy(store.at[local], out.at[k], sem).start()

        @pl.when(jnp.logical_not(held))
        def _():
            out[k] = jnp.zeros(out.shape[1:], out.dtype)

    for held, local, store, out, k, sem in copies:

        @pl.when(held)
        def _():
            pltpu.make_async_copy(store.at[local], out.at[k], sem).wait()


def select(ids, slots, down, up):
    shapes = [jax.ShapeDtypeStruct((2, *x.shape[1:]), x.dtype) for x in (down, down, up, up)]
    return pl.pallas_call(
        functools.partial(select_kernel, requests=ids.shape[0]),
        out_shape=shapes,
        in_specs=[spec(SMEM), spec(HBM), spec(HBM)],
        out_specs=[spec(VMEM)] * 4,
        scratch_shapes=[pltpu.SemaphoreType.DMA((8,))],
        compiler_params=WHOLE,
    )(jnp.concatenate([ids, slots]), down, up)


SIBLING = [(0, 1), (1, 0), (2, 3), (3, 2)]
ACROSS = [(0, 2), (1, 3), (2, 0), (3, 1)]
ONE = [(i, i ^ 1) for i in range(4)]
TWO = [(i, i ^ 2) for i in range(4)]
LAST = [(0, 0), (1, 1), (2, 3), (3, 2)]


def spread(shard):
    return lax.ppermute(shard, "ctx", ONE), lax.ppermute(shard, "ctx", TWO)


def low_rank_kernel(ids, ranks, hidden, *rest):
    pieces, out, accum = rest[:-2], rest[-2], rest[-1]
    rows = pieces[0].shape[0]
    rank = ranks[ids[lax.axis_index("req")]]
    accum[...] = jnp.zeros_like(accum)
    for flip, piece in enumerate(pieces):
        place = lax.axis_index("ctx") ^ flip
        columns = pl.ds(pl.multiple_of(place * rows, HD), rows)
        accum[...] += jnp.dot(hidden[:, columns], piece[...], preferred_element_type=jnp.float32)

    column = lax.broadcasted_iota(jnp.int32, accum.shape, 1)
    out[...] = jnp.where(column < rank, accum[...], 0.0).astype(jnp.bfloat16)


def low_rank(ids, ranks, hidden, pieces):
    shape = (hidden.shape[0], pieces[0].shape[1])
    return pl.pallas_call(
        low_rank_kernel,
        out_shape=jax.ShapeDtypeStruct(shape, jnp.bfloat16),
        in_specs=[spec(SMEM)] * 2 + [spec(VMEM)] * (1 + len(pieces)),
        out_specs=spec(VMEM),
        scratch_shapes=[VMEM(shape, jnp.float32)],
        compiler_params=PARAMS,
        cost_estimate=pl.CostEstimate(flops=1 << 27, bytes_accessed=1 << 22, transcendentals=0),
    )(ids, ranks, hidden, *pieces)


def attend_kernel(lengths, base, low, *rest):
    kvs, ups = rest[:4], rest[4:8]
    out, upper, queries = rest[8:]
    tokens = base.shape[0]
    rows = ups[0].shape[0]
    z = lax.axis_index("ctx")
    live = z * tokens < lengths[0]
    factor = LOG2E / math.sqrt(HD)
    block = GROUP * tokens

    @pl.when(live)
    def _():
        for flip, piece in enumerate(ups):
            upper[pl.ds(pl.multiple_of((z ^ flip) * rows, rows), rows), :] = piece[...]

        for j in range(HEADS):
            columns = slice(j * HD, (j + 1) * HD)
            delta = jnp.dot(low[...], upper[:, columns], preferred_element_type=jnp.float32)
            queries[j * tokens : (j + 1) * tokens, :] = (
                base[:, columns].astype(jnp.float32) + delta
            ).astype(jnp.bfloat16)

    @pl.when(jnp.logical_not(live))
    def _():
        out[...] = jnp.zeros_like(out)

    query_pos = lax.broadcasted_iota(jnp.int32, (tokens, tokens), 0)
    key_pos = lax.broadcasted_iota(jnp.int32, (tokens, tokens), 1)
    causal = key_pos <= query_pos
    for mine, needed in enumerate(((0,), (0, 1), (0, 2, 3), (0, 1, 2, 3))):

        @pl.when(live & (z == mine))
        def _():
            for h in range(KVH):
                keys = [kvs[i][:, h * HD : (h + 1) * HD] for i in needed]
                values = [kvs[i][:, (KVH + h) * HD : (KVH + h + 1) * HD] for i in needed]
                keys = jnp.concatenate(keys, axis=0)
                values = jnp.concatenate(values, axis=0)
                scores = lax.dot_general(
                    queries[h * block : (h + 1) * block, :],
                    keys,
                    (((1,), (1,)), ((), ())),
                    preferred_element_type=jnp.float32,
                )
                weights, totals = [], []
                for g in range(GROUP):
                    score = scores[g * tokens : (g + 1) * tokens, :]
                    own = jnp.where(causal, score[:, :tokens], -1e30)
                    if mine:
                        own = jnp.concatenate([own, score[:, tokens:]], axis=1)
                    largest = jnp.max(own, axis=1, keepdims=True)
                    weight = jnp.exp2((own - largest) * factor)
                    totals.append(jnp.sum(weight, axis=1, keepdims=True))
                    weights.append(weight.astype(jnp.bfloat16))
                product = jnp.dot(
                    jnp.concatenate(weights, axis=0), values, preferred_element_type=jnp.float32
                )
                for g in range(GROUP):
                    j = h * GROUP + g
                    out[:, j * HD : (j + 1) * HD] = (
                        product[g * tokens : (g + 1) * tokens, :] / totals[g]
                    ).astype(jnp.bfloat16)


def attend(lengths, base, low, kvs, ups):
    tokens, width = base.shape
    return pl.pallas_call(
        attend_kernel,
        out_shape=jax.ShapeDtypeStruct(base.shape, jnp.bfloat16),
        in_specs=[spec(SMEM)] + [spec(VMEM)] * (2 + len(kvs) + len(ups)),
        out_specs=spec(VMEM),
        scratch_shapes=[
            VMEM((low.shape[1], width), jnp.bfloat16),
            VMEM((HEADS * tokens, HD), jnp.bfloat16),
        ],
        compiler_params=PARAMS,
        cost_estimate=pl.CostEstimate(
            flops=1 << 30, bytes_accessed=1 << 22, transcendentals=1 << 21
        ),
    )(lengths, base, low, *kvs, *ups)


def body(
    hidden_states,
    queries_base,
    kv_base,
    adapter_down,
    adapter_up,
    adapter_ids,
    adapter_slots,
    rank_buckets,
    lengths,
):
    keep_down, give_down, keep_up, give_up = select(
        adapter_ids, adapter_slots, adapter_down, adapter_up
    )
    kv = kv_base[0]
    kv_one, kv_two = spread(kv)
    kv_three = lax.ppermute(kv_two, "ctx", LAST)
    near_down = lax.ppermute(give_down, "req", SIBLING)
    near_up = lax.ppermute(give_up, "req", SIBLING)
    far_down = lax.ppermute(keep_down[1] + near_down[1], "req", ACROSS)
    far_up = lax.ppermute(keep_up[1] + near_up[1], "req", ACROSS)
    down = keep_down[0] + near_down[0] + far_down
    down, kv_one = lax.optimization_barrier((down, kv_one))
    down_one, down_two = spread(down)
    up = keep_up[0] + near_up[0] + far_up
    up_one, up_two = spread(up)
    down_two, up_one = lax.optimization_barrier((down_two, up_one))
    down_three = lax.ppermute(down_two, "ctx", ONE)
    up_two, kv_three = lax.optimization_barrier((up_two, kv_three))
    up_three = lax.ppermute(up_two, "ctx", ONE)
    kvs = [kv, kv_one, kv_two, kv_three]
    downs = [down, down_one, down_two, down_three]
    ups = [up, up_one, up_two, up_three]
    low = low_rank(adapter_ids, rank_buckets, hidden_states[0], downs)
    return attend(lengths, queries_base[0], low, kvs, ups)[None]


def plain_body(
    hidden_states,
    queries_base,
    kv_base,
    adapter_down,
    adapter_up,
    adapter_ids,
    adapter_slots,
    rank_buckets,
    lengths,
):
    req_index = lax.axis_index("req")
    ctx_index = lax.axis_index("ctx")
    per_shard = adapter_down.shape[0]
    requests = adapter_ids.shape[0]
    store = adapter_slots.shape[0]
    rank_width = adapter_down.shape[2]
    tokens = hidden_states.shape[1]
    query_width = queries_base.shape[2]
    store_range = jnp.arange(store, dtype=jnp.int32)
    chosen = adapter_ids[:, None] == store_range[None, :]
    slot_of = jnp.sum(jnp.where(chosen, adapter_slots[None, :], 0), axis=1)
    rank_of = jnp.sum(jnp.where(chosen, rank_buckets[None, :], 0), axis=1)
    mine = jnp.arange(requests, dtype=jnp.int32) == req_index
    my_slot = jnp.sum(jnp.where(mine, slot_of, 0))
    my_rank = jnp.sum(jnp.where(mine, rank_of, 0))
    held = (
        slot_of[:, None] == req_index * per_shard + jnp.arange(per_shard, dtype=jnp.int32)[None, :]
    )
    select = held.astype(jnp.bfloat16)
    send_down = jnp.einsum(
        "qa,ard->qrd", select, adapter_down, preferred_element_type=jnp.float32
    ).astype(jnp.bfloat16)
    send_up = jnp.einsum(
        "qa,ard->qrd", select, adapter_up, preferred_element_type=jnp.float32
    ).astype(jnp.bfloat16)
    got_down, got_up = (
        lax.all_to_all(send_down, "req", split_axis=0, concat_axis=0, tiled=True),
        lax.all_to_all(send_up, "req", split_axis=0, concat_axis=0, tiled=True),
    )
    owner = my_slot // per_shard
    down_mine = lax.dynamic_index_in_dim(got_down, owner, 0, keepdims=False)
    up_mine = lax.dynamic_index_in_dim(got_up, owner, 0, keepdims=False)
    features = hidden_states[0]
    columns = features
    low_rank = jnp.dot(
        columns,
        lax.all_gather(down_mine, "ctx", axis=0, tiled=True),
        preferred_element_type=jnp.float32,
    )
    low_rank = jnp.where(
        jnp.arange(rank_width, dtype=jnp.int32)[None, :] < my_rank, low_rank, 0.0
    ).astype(jnp.bfloat16)
    columns = low_rank
    delta = jnp.dot(
        columns,
        lax.all_gather(up_mine, "ctx", axis=0, tiled=True),
        preferred_element_type=jnp.float32,
    )
    queries = (
        (queries_base[0].astype(jnp.float32) + delta)
        .astype(jnp.bfloat16)
        .reshape(tokens, KVH, GROUP, HD)
    )
    length = lengths[0]
    first_query = ctx_index * tokens
    query_pos = first_query + jnp.arange(tokens, dtype=jnp.int32)
    last_needed = jnp.minimum(first_query + tokens - 1, length - 1)
    scale = 1.0 / math.sqrt(HD)
    key_width = KVH * HD
    initial = (
        jnp.full((KVH, GROUP, tokens), -1e30, jnp.float32),
        jnp.zeros((KVH, GROUP, tokens), jnp.float32),
        jnp.zeros((KVH, GROUP, tokens, HD), jnp.float32),
    )
    piece = lax.all_gather(kv_base[0], "ctx", axis=0, tiled=True)
    count = piece.shape[0]
    width = math.gcd(count, 512)

    def key_block(index, state):
        largest, total, accum = state
        offset = index * width
        rows = lax.dynamic_slice_in_dim(piece, offset, width, 0)
        keys = rows[:, :key_width].reshape(width, KVH, HD)
        values = rows[:, key_width:].reshape(width, KVH, HD)
        key_pos = offset + jnp.arange(width, dtype=jnp.int32)
        score = (
            jnp.einsum("tkgd,skd->kgts", queries, keys, preferred_element_type=jnp.float32) * scale
        )
        allowed = (key_pos[None, :] <= query_pos[:, None]) & (key_pos[None, :] < length)
        masked = jnp.where(allowed, score, -1e30)
        newest = jnp.maximum(largest, jnp.max(masked, axis=-1))
        weight = jnp.where(allowed, jnp.exp(score - newest[..., None]), 0.0)
        factor = jnp.exp(largest - newest)
        total = total * factor + jnp.sum(weight, axis=-1)
        product = jnp.einsum(
            "kgts,skd->kgtd",
            weight.astype(jnp.bfloat16),
            values,
            preferred_element_type=jnp.float32,
        )
        accum = accum * factor[..., None] + product
        return (newest, total, accum)

    def compute(state):
        return lax.fori_loop(0, count // width, key_block, state)

    needed = (jnp.int32(0) <= last_needed) & (first_query < length)
    largest, total, accum = lax.cond(needed, compute, lambda state: state, initial)
    safe_total = jnp.where(total > 0.0, total, 1.0)
    output = accum / safe_total[..., None]
    output = jnp.transpose(output, (2, 0, 1, 3)).reshape(tokens, query_width)
    output = jnp.where(query_pos[:, None] < length, output, 0.0).astype(jnp.bfloat16)
    return output[None]


def solution(mesh):
    paired = mesh.shape["ctx"] == 4 and mesh.shape["req"] == 4
    return jax.shard_map(
        body if paired else plain_body,
        mesh=mesh,
        in_specs=(
            P(("group", "req"), "ctx", None),
            P(("group", "req"), "ctx", None),
            P(("group", "req"), "ctx", None),
            P(("group", "req"), "ctx", None),
            P(("group", "req"), "ctx", None),
            P("group"),
            P("group"),
            P("group"),
            P(("group", "req")),
        ),
        out_specs=P(("group", "req"), "ctx", None),
        check_vma=False,
    )
```

```python
import functools
import math

import jax
import jax.numpy as jnp
from jax import lax
from jax.experimental import pallas as pl
from jax.experimental.pallas import tpu as pltpu
from jax.sharding import PartitionSpec as P

HD = 128
KVH = 3
GROUP = 7
HEADS = KVH * GROUP
SMEM = pltpu.SMEM
VMEM = pltpu.VMEM
HBM = pltpu.HBM
LOG2E = 1.0 / math.log(2.0)
PARAMS = pltpu.CompilerParams(vmem_limit_bytes=48 * 1024 * 1024)
WHOLE = pltpu.CompilerParams(vmem_limit_bytes=52 * 1024 * 1024)


def spec(space):
    return pl.BlockSpec(memory_space=space)


def select_kernel(table, *rest, requests):
    stores, outs, sems = rest[:2], rest[2:6], rest[6]
    per_shard = stores[0].shape[0]
    me = lax.axis_index("req")
    first = me * per_shard
    copies = []
    for i, flip in enumerate((0, 2, 1, 3)):
        local = table[requests + table[me ^ flip]] - first
        held = (local >= 0) & (local < per_shard)
        for f, store in enumerate(stores):
            out = outs[2 * f + i // 2]
            copies.append((held, local, store, out, i % 2, sems.at[4 * f + i]))
    for held, local, store, out, k, sem in copies:

        @pl.when(held)
        def _():
            pltpu.make_async_copy(store.at[local], out.at[k], sem).start()

        @pl.when(jnp.logical_not(held))
        def _():
            out[k] = jnp.zeros(out.shape[1:], out.dtype)

    for held, local, store, out, k, sem in copies:

        @pl.when(held)
        def _():
            pltpu.make_async_copy(store.at[local], out.at[k], sem).wait()


def select(ids, slots, down, up):
    shapes = [jax.ShapeDtypeStruct((2, *x.shape[1:]), x.dtype) for x in (down, down, up, up)]
    return pl.pallas_call(
        functools.partial(select_kernel, requests=ids.shape[0]),
        out_shape=shapes,
        in_specs=[spec(SMEM), spec(HBM), spec(HBM)],
        out_specs=[spec(VMEM)] * 4,
        scratch_shapes=[pltpu.SemaphoreType.DMA((8,))],
        compiler_params=WHOLE,
    )(jnp.concatenate([ids, slots]), down, up)


SIBLING = [(0, 1), (1, 0), (2, 3), (3, 2)]
ACROSS = [(0, 2), (1, 3), (2, 0), (3, 1)]
ONE = [(i, i ^ 1) for i in range(4)]
TWO = [(i, i ^ 2) for i in range(4)]
LAST = [(0, 0), (1, 1), (2, 3), (3, 2)]


def spread(shard):
    return lax.ppermute(shard, "ctx", ONE), lax.ppermute(shard, "ctx", TWO)


def low_rank_kernel(ids, ranks, hidden, *rest):
    pieces, out, accum = rest[:-2], rest[-2], rest[-1]
    rows = pieces[0].shape[0]
    rank = ranks[ids[lax.axis_index("req")]]
    accum[...] = jnp.zeros_like(accum)
    for flip, piece in enumerate(pieces):
        place = lax.axis_index("ctx") ^ flip
        columns = pl.ds(pl.multiple_of(place * rows, HD), rows)
        accum[...] += jnp.dot(hidden[:, columns], piece[...], preferred_element_type=jnp.float32)

    column = lax.broadcasted_iota(jnp.int32, accum.shape, 1)
    out[...] = jnp.where(column < rank, accum[...], 0.0).astype(jnp.bfloat16)


def low_rank(ids, ranks, hidden, pieces):
    shape = (hidden.shape[0], pieces[0].shape[1])
    return pl.pallas_call(
        low_rank_kernel,
        out_shape=jax.ShapeDtypeStruct(shape, jnp.bfloat16),
        in_specs=[spec(SMEM)] * 2 + [spec(VMEM)] * (1 + len(pieces)),
        out_specs=spec(VMEM),
        scratch_shapes=[VMEM(shape, jnp.float32)],
        compiler_params=PARAMS,
        cost_estimate=pl.CostEstimate(flops=1 << 27, bytes_accessed=1 << 22, transcendentals=0),
    )(ids, ranks, hidden, *pieces)


def attend_kernel(lengths, base, low, *rest):
    kvs, ups = rest[:4], rest[4:8]
    out, upper, queries = rest[8:]
    tokens = base.shape[0]
    rows = ups[0].shape[0]
    z = lax.axis_index("ctx")
    live = z * tokens < lengths[0]
    factor = LOG2E / math.sqrt(HD)
    block = GROUP * tokens

    @pl.when(live)
    def _():
        for flip, piece in enumerate(ups):
            upper[pl.ds(pl.multiple_of((z ^ flip) * rows, rows), rows), :] = piece[...]

        for j in range(HEADS):
            columns = slice(j * HD, (j + 1) * HD)
            delta = jnp.dot(low[...], upper[:, columns], preferred_element_type=jnp.float32)
            queries[j * tokens : (j + 1) * tokens, :] = (
                base[:, columns].astype(jnp.float32) + delta
            ).astype(jnp.bfloat16)

    @pl.when(jnp.logical_not(live))
    def _():
        out[...] = jnp.zeros_like(out)

    query_pos = lax.broadcasted_iota(jnp.int32, (tokens, tokens), 0)
    key_pos = lax.broadcasted_iota(jnp.int32, (tokens, tokens), 1)
    causal = key_pos <= query_pos
    for mine, needed in enumerate(((0,), (0, 1), (0, 2, 3), (0, 1, 2, 3))):

        @pl.when(live & (z == mine))
        def _():
            for h in range(KVH):
                keys = [kvs[i][:, h * HD : (h + 1) * HD] for i in needed]
                values = [kvs[i][:, (KVH + h) * HD : (KVH + h + 1) * HD] for i in needed]
                keys = jnp.concatenate(keys, axis=0)
                values = jnp.concatenate(values, axis=0)
                scores = lax.dot_general(
                    queries[h * block : (h + 1) * block, :],
                    keys,
                    (((1,), (1,)), ((), ())),
                    preferred_element_type=jnp.float32,
                )
                weights, totals = [], []
                for g in range(GROUP):
                    score = scores[g * tokens : (g + 1) * tokens, :]
                    own = jnp.where(causal, score[:, :tokens], -1e30)
                    if mine:
                        own = jnp.concatenate([own, score[:, tokens:]], axis=1)
                    largest = jnp.max(own, axis=1, keepdims=True)
                    weight = jnp.exp2((own - largest) * factor)
                    totals.append(jnp.sum(weight, axis=1, keepdims=True))
                    weights.append(weight.astype(jnp.bfloat16))
                product = jnp.dot(
                    jnp.concatenate(weights, axis=0), values, preferred_element_type=jnp.float32
                )
                for g in range(GROUP):
                    j = h * GROUP + g
                    out[:, j * HD : (j + 1) * HD] = (
                        product[g * tokens : (g + 1) * tokens, :] / totals[g]
                    ).astype(jnp.bfloat16)


def attend(lengths, base, low, kvs, ups):
    tokens, width = base.shape
    return pl.pallas_call(
        attend_kernel,
        out_shape=jax.ShapeDtypeStruct(base.shape, jnp.bfloat16),
        in_specs=[spec(SMEM)] + [spec(VMEM)] * (2 + len(kvs) + len(ups)),
        out_specs=spec(VMEM),
        scratch_shapes=[
            VMEM((low.shape[1], width), jnp.bfloat16),
            VMEM((HEADS * tokens, HD), jnp.bfloat16),
        ],
        compiler_params=PARAMS,
        cost_estimate=pl.CostEstimate(
            flops=1 << 30, bytes_accessed=1 << 22, transcendentals=1 << 21
        ),
    )(lengths, base, low, *kvs, *ups)


def body(
    hidden_states,
    queries_base,
    kv_base,
    adapter_down,
    adapter_up,
    adapter_ids,
    adapter_slots,
    rank_buckets,
    lengths,
):
    keep_down, give_down, keep_up, give_up = select(
        adapter_ids, adapter_slots, adapter_down, adapter_up
    )
    kv = kv_base[0]
    kv_one, kv_two = spread(kv)
    kv_three = lax.ppermute(kv_two, "ctx", LAST)
    near_down = lax.ppermute(give_down, "req", SIBLING)
    near_up = lax.ppermute(give_up, "req", SIBLING)
    far_down = lax.ppermute(keep_down[1] + near_down[1], "req", ACROSS)
    far_up = lax.ppermute(keep_up[1] + near_up[1], "req", ACROSS)
    down = keep_down[0] + near_down[0] + far_down
    down, kv_one = lax.optimization_barrier((down, kv_one))
    down_one, down_two = spread(down)
    up = keep_up[0] + near_up[0] + far_up
    up_one, up_two = spread(up)
    down_two, down_one = lax.optimization_barrier((down_two, down_one))
    down_three = lax.ppermute(down_two, "ctx", ONE)
    up_two, up_one = lax.optimization_barrier((up_two, up_one))
    up_three = lax.ppermute(up_two, "ctx", ONE)
    kvs = [kv, kv_one, kv_two, kv_three]
    downs = [down, down_one, down_two, down_three]
    ups = [up, up_one, up_two, up_three]
    low = low_rank(adapter_ids, rank_buckets, hidden_states[0], downs)
    return attend(lengths, queries_base[0], low, kvs, ups)[None]


def plain_body(
    hidden_states,
    queries_base,
    kv_base,
    adapter_down,
    adapter_up,
    adapter_ids,
    adapter_slots,
    rank_buckets,
    lengths,
):
    req_index = lax.axis_index("req")
    ctx_index = lax.axis_index("ctx")
    per_shard = adapter_down.shape[0]
    requests = adapter_ids.shape[0]
    store = adapter_slots.shape[0]
    rank_width = adapter_down.shape[2]
    tokens = hidden_states.shape[1]
    query_width = queries_base.shape[2]
    store_range = jnp.arange(store, dtype=jnp.int32)
    chosen = adapter_ids[:, None] == store_range[None, :]
    slot_of = jnp.sum(jnp.where(chosen, adapter_slots[None, :], 0), axis=1)
    rank_of = jnp.sum(jnp.where(chosen, rank_buckets[None, :], 0), axis=1)
    mine = jnp.arange(requests, dtype=jnp.int32) == req_index
    my_slot = jnp.sum(jnp.where(mine, slot_of, 0))
    my_rank = jnp.sum(jnp.where(mine, rank_of, 0))
    held = (
        slot_of[:, None] == req_index * per_shard + jnp.arange(per_shard, dtype=jnp.int32)[None, :]
    )
    select = held.astype(jnp.bfloat16)
    send_down = jnp.einsum(
        "qa,ard->qrd", select, adapter_down, preferred_element_type=jnp.float32
    ).astype(jnp.bfloat16)
    send_up = jnp.einsum(
        "qa,ard->qrd", select, adapter_up, preferred_element_type=jnp.float32
    ).astype(jnp.bfloat16)
    got_down, got_up = (
        lax.all_to_all(send_down, "req", split_axis=0, concat_axis=0, tiled=True),
        lax.all_to_all(send_up, "req", split_axis=0, concat_axis=0, tiled=True),
    )
    owner = my_slot // per_shard
    down_mine = lax.dynamic_index_in_dim(got_down, owner, 0, keepdims=False)
    up_mine = lax.dynamic_index_in_dim(got_up, owner, 0, keepdims=False)
    features = hidden_states[0]
    columns = features
    low_rank = jnp.dot(
        columns,
        lax.all_gather(down_mine, "ctx", axis=0, tiled=True),
        preferred_element_type=jnp.float32,
    )
    low_rank = jnp.where(
        jnp.arange(rank_width, dtype=jnp.int32)[None, :] < my_rank, low_rank, 0.0
    ).astype(jnp.bfloat16)
    columns = low_rank
    delta = jnp.dot(
        columns,
        lax.all_gather(up_mine, "ctx", axis=0, tiled=True),
        preferred_element_type=jnp.float32,
    )
    queries = (
        (queries_base[0].astype(jnp.float32) + delta)
        .astype(jnp.bfloat16)
        .reshape(tokens, KVH, GROUP, HD)
    )
    length = lengths[0]
    first_query = ctx_index * tokens
    query_pos = first_query + jnp.arange(tokens, dtype=jnp.int32)
    last_needed = jnp.minimum(first_query + tokens - 1, length - 1)
    scale = 1.0 / math.sqrt(HD)
    key_width = KVH * HD
    initial = (
        jnp.full((KVH, GROUP, tokens), -1e30, jnp.float32),
        jnp.zeros((KVH, GROUP, tokens), jnp.float32),
        jnp.zeros((KVH, GROUP, tokens, HD), jnp.float32),
    )
    piece = lax.all_gather(kv_base[0], "ctx", axis=0, tiled=True)
    count = piece.shape[0]
    width = math.gcd(count, 512)

    def key_block(index, state):
        largest, total, accum = state
        offset = index * width
        rows = lax.dynamic_slice_in_dim(piece, offset, width, 0)
        keys = rows[:, :key_width].reshape(width, KVH, HD)
        values = rows[:, key_width:].reshape(width, KVH, HD)
        key_pos = offset + jnp.arange(width, dtype=jnp.int32)
        score = (
            jnp.einsum("tkgd,skd->kgts", queries, keys, preferred_element_type=jnp.float32) * scale
        )
        allowed = (key_pos[None, :] <= query_pos[:, None]) & (key_pos[None, :] < length)
        masked = jnp.where(allowed, score, -1e30)
        newest = jnp.maximum(largest, jnp.max(masked, axis=-1))
        weight = jnp.where(allowed, jnp.exp(score - newest[..., None]), 0.0)
        factor = jnp.exp(largest - newest)
        total = total * factor + jnp.sum(weight, axis=-1)
        product = jnp.einsum(
            "kgts,skd->kgtd",
            weight.astype(jnp.bfloat16),
            values,
            preferred_element_type=jnp.float32,
        )
        accum = accum * factor[..., None] + product
        return (newest, total, accum)

    def compute(state):
        return lax.fori_loop(0, count // width, key_block, state)

    needed = (jnp.int32(0) <= last_needed) & (first_query < length)
    largest, total, accum = lax.cond(needed, compute, lambda state: state, initial)
    safe_total = jnp.where(total > 0.0, total, 1.0)
    output = accum / safe_total[..., None]
    output = jnp.transpose(output, (2, 0, 1, 3)).reshape(tokens, query_width)
    output = jnp.where(query_pos[:, None] < length, output, 0.0).astype(jnp.bfloat16)
    return output[None]


def solution(mesh):
    paired = mesh.shape["ctx"] == 4 and mesh.shape["req"] == 4
    return jax.shard_map(
        body if paired else plain_body,
        mesh=mesh,
        in_specs=(
            P(("group", "req"), "ctx", None),
            P(("group", "req"), "ctx", None),
            P(("group", "req"), "ctx", None),
            P(("group", "req"), "ctx", None),
            P(("group", "req"), "ctx", None),
            P("group"),
            P("group"),
            P("group"),
            P(("group", "req")),
        ),
        out_specs=P(("group", "req"), "ctx", None),
        check_vma=False,
    )
```

```python
import functools
import math

import jax
import jax.numpy as jnp
from jax import lax
from jax.experimental import pallas as pl
from jax.experimental.pallas import tpu as pltpu
from jax.sharding import PartitionSpec as P

HD = 128
KVH = 3
GROUP = 7
HEADS = KVH * GROUP
SMEM = pltpu.SMEM
VMEM = pltpu.VMEM
HBM = pltpu.HBM
LOG2E = 1.0 / math.log(2.0)
PARAMS = pltpu.CompilerParams(vmem_limit_bytes=48 * 1024 * 1024)
WHOLE = pltpu.CompilerParams(vmem_limit_bytes=52 * 1024 * 1024)


def spec(space):
    return pl.BlockSpec(memory_space=space)


def select_kernel(table, *rest, requests):
    stores, outs, sems = rest[:2], rest[2:6], rest[6]
    per_shard = stores[0].shape[0]
    me = lax.axis_index("req")
    first = me * per_shard
    copies = []
    for i, flip in enumerate((0, 2, 1, 3)):
        local = table[requests + table[me ^ flip]] - first
        held = (local >= 0) & (local < per_shard)
        for f, store in enumerate(stores):
            out = outs[2 * f + i // 2]
            copies.append((held, local, store, out, i % 2, sems.at[4 * f + i]))
    for held, local, store, out, k, sem in copies:

        @pl.when(held)
        def _():
            pltpu.make_async_copy(store.at[local], out.at[k], sem).start()

        @pl.when(jnp.logical_not(held))
        def _():
            out[k] = jnp.zeros(out.shape[1:], out.dtype)

    for held, local, store, out, k, sem in copies:

        @pl.when(held)
        def _():
            pltpu.make_async_copy(store.at[local], out.at[k], sem).wait()


def select(ids, slots, down, up):
    shapes = [jax.ShapeDtypeStruct((2, *x.shape[1:]), x.dtype) for x in (down, down, up, up)]
    return pl.pallas_call(
        functools.partial(select_kernel, requests=ids.shape[0]),
        out_shape=shapes,
        in_specs=[spec(SMEM), spec(HBM), spec(HBM)],
        out_specs=[spec(VMEM)] * 4,
        scratch_shapes=[pltpu.SemaphoreType.DMA((8,))],
        compiler_params=WHOLE,
    )(jnp.concatenate([ids, slots]), down, up)


SIBLING = [(0, 1), (1, 0), (2, 3), (3, 2)]
ACROSS = [(0, 2), (1, 3), (2, 0), (3, 1)]
ONE = [(i, i ^ 1) for i in range(4)]
TWO = [(i, i ^ 2) for i in range(4)]
LAST = [(0, 0), (1, 1), (2, 3), (3, 2)]
INWARD = [(0, 1), (3, 2)]
OUTWARD = [(1, 0), (2, 3)]


def spread(shard):
    return lax.ppermute(shard, "ctx", ONE), lax.ppermute(shard, "ctx", TWO)


def product_kernel(features, piece, out):
    out[...] = jnp.dot(features[...], piece[...], preferred_element_type=jnp.float32)


def product(features, piece):
    return pl.pallas_call(
        product_kernel,
        out_shape=jax.ShapeDtypeStruct((features.shape[0], piece.shape[1]), jnp.float32),
        in_specs=[spec(VMEM)] * 2,
        out_specs=spec(VMEM),
        compiler_params=PARAMS,
        cost_estimate=pl.CostEstimate(flops=1 << 25, bytes_accessed=1 << 19, transcendentals=0),
    )(features, piece)


def low_rank_kernel(ids, ranks, hidden, partial, *rest):
    pieces, out = rest[:-1], rest[-1]
    rows = pieces[0].shape[0]
    rank = ranks[ids[lax.axis_index("req")]]
    total = partial[...]
    for flip, piece in enumerate(pieces):
        place = lax.axis_index("ctx") ^ flip
        columns = pl.ds(pl.multiple_of(place * rows, HD), rows)
        total += jnp.dot(hidden[:, columns], piece[...], preferred_element_type=jnp.float32)
    column = lax.broadcasted_iota(jnp.int32, total.shape, 1)
    out[...] = jnp.where(column < rank, total, 0.0).astype(jnp.bfloat16)


def low_rank(ids, ranks, hidden, partial, pieces):
    return pl.pallas_call(
        low_rank_kernel,
        out_shape=jax.ShapeDtypeStruct(partial.shape, jnp.bfloat16),
        in_specs=[spec(SMEM)] * 2 + [spec(VMEM)] * (2 + len(pieces)),
        out_specs=spec(VMEM),
        compiler_params=PARAMS,
        cost_estimate=pl.CostEstimate(flops=1 << 27, bytes_accessed=1 << 22, transcendentals=0),
    )(ids, ranks, hidden, partial, *pieces)


def attend_kernel(lengths, base, low, *rest):
    kvs, ups = rest[:4], rest[4:8]
    out, upper, queries = rest[8:]
    tokens = base.shape[0]
    rows = ups[0].shape[0]
    z = lax.axis_index("ctx")
    live = z * tokens < lengths[0]
    factor = LOG2E / math.sqrt(HD)
    block = GROUP * tokens

    @pl.when(live)
    def _():
        for flip, piece in enumerate(ups):
            upper[pl.ds(pl.multiple_of((z ^ flip) * rows, rows), rows), :] = piece[...]

        for j in range(HEADS):
            columns = slice(j * HD, (j + 1) * HD)
            delta = jnp.dot(low[...], upper[:, columns], preferred_element_type=jnp.float32)
            queries[j * tokens : (j + 1) * tokens, :] = (
                base[:, columns].astype(jnp.float32) + delta
            ).astype(jnp.bfloat16)

    @pl.when(jnp.logical_not(live))
    def _():
        out[...] = jnp.zeros_like(out)

    query_pos = lax.broadcasted_iota(jnp.int32, (tokens, tokens), 0)
    key_pos = lax.broadcasted_iota(jnp.int32, (tokens, tokens), 1)
    causal = key_pos <= query_pos
    for mine, needed in enumerate(((0,), (0, 1), (0, 2, 3), (0, 1, 2, 3))):

        @pl.when(live & (z == mine))
        def _():
            for h in range(KVH):
                keys = [kvs[i][:, h * HD : (h + 1) * HD] for i in needed]
                values = [kvs[i][:, (KVH + h) * HD : (KVH + h + 1) * HD] for i in needed]
                keys = jnp.concatenate(keys, axis=0)
                values = jnp.concatenate(values, axis=0)
                scores = lax.dot_general(
                    queries[h * block : (h + 1) * block, :],
                    keys,
                    (((1,), (1,)), ((), ())),
                    preferred_element_type=jnp.float32,
                )
                weights, totals = [], []
                for g in range(GROUP):
                    score = scores[g * tokens : (g + 1) * tokens, :]
                    own = jnp.where(causal, score[:, :tokens], -1e30)
                    if mine:
                        own = jnp.concatenate([own, score[:, tokens:]], axis=1)
                    largest = jnp.max(own, axis=1, keepdims=True)
                    weight = jnp.exp2((own - largest) * factor)
                    totals.append(jnp.sum(weight, axis=1, keepdims=True))
                    weights.append(weight.astype(jnp.bfloat16))
                product = jnp.dot(
                    jnp.concatenate(weights, axis=0), values, preferred_element_type=jnp.float32
                )
                for g in range(GROUP):
                    j = h * GROUP + g
                    out[:, j * HD : (j + 1) * HD] = (
                        product[g * tokens : (g + 1) * tokens, :] / totals[g]
                    ).astype(jnp.bfloat16)


def attend(lengths, base, low, kvs, ups):
    tokens, width = base.shape
    return pl.pallas_call(
        attend_kernel,
        out_shape=jax.ShapeDtypeStruct(base.shape, jnp.bfloat16),
        in_specs=[spec(SMEM)] + [spec(VMEM)] * (2 + len(kvs) + len(ups)),
        out_specs=spec(VMEM),
        scratch_shapes=[
            VMEM((low.shape[1], width), jnp.bfloat16),
            VMEM((HEADS * tokens, HD), jnp.bfloat16),
        ],
        compiler_params=PARAMS,
        cost_estimate=pl.CostEstimate(
            flops=1 << 30, bytes_accessed=1 << 22, transcendentals=1 << 21
        ),
    )(lengths, base, low, *kvs, *ups)


def body(
    hidden_states,
    queries_base,
    kv_base,
    adapter_down,
    adapter_up,
    adapter_ids,
    adapter_slots,
    rank_buckets,
    lengths,
):
    keep_down, give_down, keep_up, give_up = select(
        adapter_ids, adapter_slots, adapter_down, adapter_up
    )
    kv = kv_base[0]
    kv_one, kv_two = spread(kv)
    kv_three = lax.ppermute(kv_two, "ctx", LAST)
    hidden = hidden_states[0]
    rows = adapter_down.shape[1]
    start = (lax.axis_index("ctx") ^ 1) * rows
    near_down = lax.ppermute(give_down, "req", SIBLING)
    near_up = lax.ppermute(give_up, "req", SIBLING)
    far_down = lax.ppermute(keep_down[1] + near_down[1], "req", ACROSS)
    pass_up, early = lax.optimization_barrier((keep_up[1] + near_up[1], hidden))
    far_up = lax.ppermute(pass_up, "req", ACROSS)
    features = lax.ppermute(lax.dynamic_slice_in_dim(early, start, rows, 1), "ctx", INWARD)
    down = keep_down[0] + near_down[0] + far_down
    down, kv_one = lax.optimization_barrier((down, kv_one))
    down_one = lax.ppermute(down, "ctx", INWARD)
    down_two = lax.ppermute(down, "ctx", TWO)
    up = keep_up[0] + near_up[0] + far_up
    up, features = lax.optimization_barrier((up, features))
    up_one, up_two = spread(up)
    partial = lax.ppermute(product(features, down), "ctx", OUTWARD)
    down_two, down_one = lax.optimization_barrier((down_two, down_one))
    down_three = lax.ppermute(down_two, "ctx", ONE)
    up_two, up_one, partial = lax.optimization_barrier((up_two, up_one, partial))
    up_three = lax.ppermute(up_two, "ctx", ONE)
    kvs = [kv, kv_one, kv_two, kv_three]
    downs = [down, down_one, down_two, down_three]
    ups = [up, up_one, up_two, up_three]
    low = low_rank(adapter_ids, rank_buckets, hidden, partial, downs)
    return attend(lengths, queries_base[0], low, kvs, ups)[None]


def plain_body(
    hidden_states,
    queries_base,
    kv_base,
    adapter_down,
    adapter_up,
    adapter_ids,
    adapter_slots,
    rank_buckets,
    lengths,
):
    req_index = lax.axis_index("req")
    ctx_index = lax.axis_index("ctx")
    per_shard = adapter_down.shape[0]
    requests = adapter_ids.shape[0]
    store = adapter_slots.shape[0]
    rank_width = adapter_down.shape[2]
    tokens = hidden_states.shape[1]
    query_width = queries_base.shape[2]
    store_range = jnp.arange(store, dtype=jnp.int32)
    chosen = adapter_ids[:, None] == store_range[None, :]
    slot_of = jnp.sum(jnp.where(chosen, adapter_slots[None, :], 0), axis=1)
    rank_of = jnp.sum(jnp.where(chosen, rank_buckets[None, :], 0), axis=1)
    mine = jnp.arange(requests, dtype=jnp.int32) == req_index
    my_slot = jnp.sum(jnp.where(mine, slot_of, 0))
    my_rank = jnp.sum(jnp.where(mine, rank_of, 0))
    held = (
        slot_of[:, None] == req_index * per_shard + jnp.arange(per_shard, dtype=jnp.int32)[None, :]
    )
    select = held.astype(jnp.bfloat16)
    send_down = jnp.einsum(
        "qa,ard->qrd", select, adapter_down, preferred_element_type=jnp.float32
    ).astype(jnp.bfloat16)
    send_up = jnp.einsum(
        "qa,ard->qrd", select, adapter_up, preferred_element_type=jnp.float32
    ).astype(jnp.bfloat16)
    got_down, got_up = (
        lax.all_to_all(send_down, "req", split_axis=0, concat_axis=0, tiled=True),
        lax.all_to_all(send_up, "req", split_axis=0, concat_axis=0, tiled=True),
    )
    owner = my_slot // per_shard
    down_mine = lax.dynamic_index_in_dim(got_down, owner, 0, keepdims=False)
    up_mine = lax.dynamic_index_in_dim(got_up, owner, 0, keepdims=False)
    features = hidden_states[0]
    columns = features
    low_rank = jnp.dot(
        columns,
        lax.all_gather(down_mine, "ctx", axis=0, tiled=True),
        preferred_element_type=jnp.float32,
    )
    low_rank = jnp.where(
        jnp.arange(rank_width, dtype=jnp.int32)[None, :] < my_rank, low_rank, 0.0
    ).astype(jnp.bfloat16)
    columns = low_rank
    delta = jnp.dot(
        columns,
        lax.all_gather(up_mine, "ctx", axis=0, tiled=True),
        preferred_element_type=jnp.float32,
    )
    queries = (
        (queries_base[0].astype(jnp.float32) + delta)
        .astype(jnp.bfloat16)
        .reshape(tokens, KVH, GROUP, HD)
    )
    length = lengths[0]
    first_query = ctx_index * tokens
    query_pos = first_query + jnp.arange(tokens, dtype=jnp.int32)
    last_needed = jnp.minimum(first_query + tokens - 1, length - 1)
    scale = 1.0 / math.sqrt(HD)
    key_width = KVH * HD
    initial = (
        jnp.full((KVH, GROUP, tokens), -1e30, jnp.float32),
        jnp.zeros((KVH, GROUP, tokens), jnp.float32),
        jnp.zeros((KVH, GROUP, tokens, HD), jnp.float32),
    )
    piece = lax.all_gather(kv_base[0], "ctx", axis=0, tiled=True)
    count = piece.shape[0]
    width = math.gcd(count, 512)

    def key_block(index, state):
        largest, total, accum = state
        offset = index * width
        rows = lax.dynamic_slice_in_dim(piece, offset, width, 0)
        keys = rows[:, :key_width].reshape(width, KVH, HD)
        values = rows[:, key_width:].reshape(width, KVH, HD)
        key_pos = offset + jnp.arange(width, dtype=jnp.int32)
        score = (
            jnp.einsum("tkgd,skd->kgts", queries, keys, preferred_element_type=jnp.float32) * scale
        )
        allowed = (key_pos[None, :] <= query_pos[:, None]) & (key_pos[None, :] < length)
        masked = jnp.where(allowed, score, -1e30)
        newest = jnp.maximum(largest, jnp.max(masked, axis=-1))
        weight = jnp.where(allowed, jnp.exp(score - newest[..., None]), 0.0)
        factor = jnp.exp(largest - newest)
        total = total * factor + jnp.sum(weight, axis=-1)
        product = jnp.einsum(
            "kgts,skd->kgtd",
            weight.astype(jnp.bfloat16),
            values,
            preferred_element_type=jnp.float32,
        )
        accum = accum * factor[..., None] + product
        return (newest, total, accum)

    def compute(state):
        return lax.fori_loop(0, count // width, key_block, state)

    needed = (jnp.int32(0) <= last_needed) & (first_query < length)
    largest, total, accum = lax.cond(needed, compute, lambda state: state, initial)
    safe_total = jnp.where(total > 0.0, total, 1.0)
    output = accum / safe_total[..., None]
    output = jnp.transpose(output, (2, 0, 1, 3)).reshape(tokens, query_width)
    output = jnp.where(query_pos[:, None] < length, output, 0.0).astype(jnp.bfloat16)
    return output[None]


def solution(mesh):
    paired = mesh.shape["ctx"] == 4 and mesh.shape["req"] == 4
    return jax.shard_map(
        body if paired else plain_body,
        mesh=mesh,
        in_specs=(
            P(("group", "req"), "ctx", None),
            P(("group", "req"), "ctx", None),
            P(("group", "req"), "ctx", None),
            P(("group", "req"), "ctx", None),
            P(("group", "req"), "ctx", None),
            P("group"),
            P("group"),
            P("group"),
            P(("group", "req")),
        ),
        out_specs=P(("group", "req"), "ctx", None),
        check_vma=False,
    )
```

```python
import functools
import math

import jax
import jax.numpy as jnp
from jax import lax
from jax.experimental import pallas as pl
from jax.experimental.pallas import tpu as pltpu
from jax.sharding import PartitionSpec as P

HD = 128
KVH = 3
GROUP = 7
HEADS = KVH * GROUP
SMEM = pltpu.SMEM
VMEM = pltpu.VMEM
HBM = pltpu.HBM
LOG2E = 1.0 / math.log(2.0)
PARAMS = pltpu.CompilerParams(vmem_limit_bytes=48 * 1024 * 1024)
WHOLE = pltpu.CompilerParams(vmem_limit_bytes=52 * 1024 * 1024)


def spec(space):
    return pl.BlockSpec(memory_space=space)


def select_kernel(table, *rest, requests):
    stores, outs, sems = rest[:2], rest[2:6], rest[6]
    per_shard = stores[0].shape[0]
    me = lax.axis_index("req")
    first = me * per_shard
    copies = []
    for i, flip in enumerate((0, 2, 1, 3)):
        local = table[requests + table[me ^ flip]] - first
        held = (local >= 0) & (local < per_shard)
        for f, store in enumerate(stores):
            out = outs[2 * f + i // 2]
            copies.append((held, local, store, out, i % 2, sems.at[4 * f + i]))
    for held, local, store, out, k, sem in copies:

        @pl.when(held)
        def _():
            pltpu.make_async_copy(store.at[local], out.at[k], sem).start()

    for held, local, store, out, k, sem in copies:

        @pl.when(jnp.logical_not(held))
        def _():
            out[k] = jnp.zeros(out.shape[1:], out.dtype)

    for held, local, store, out, k, sem in copies:

        @pl.when(held)
        def _():
            pltpu.make_async_copy(store.at[local], out.at[k], sem).wait()


def select(ids, slots, down, up):
    shapes = [jax.ShapeDtypeStruct((2, *x.shape[1:]), x.dtype) for x in (down, down, up, up)]
    return pl.pallas_call(
        functools.partial(select_kernel, requests=ids.shape[0]),
        out_shape=shapes,
        in_specs=[spec(SMEM), spec(HBM), spec(HBM)],
        out_specs=[spec(VMEM)] * 4,
        scratch_shapes=[pltpu.SemaphoreType.DMA((8,))],
        compiler_params=WHOLE,
    )(jnp.concatenate([ids, slots]), down, up)


SIBLING = [(0, 1), (1, 0), (2, 3), (3, 2)]
ACROSS = [(0, 2), (1, 3), (2, 0), (3, 1)]
ONE = [(i, i ^ 1) for i in range(4)]
TWO = [(i, i ^ 2) for i in range(4)]
LAST = [(0, 0), (1, 1), (2, 3), (3, 2)]


def spread(shard):
    return lax.ppermute(shard, "ctx", ONE), lax.ppermute(shard, "ctx", TWO)


def low_rank_kernel(ids, ranks, hidden, *rest):
    pieces, out, accum = rest[:-2], rest[-2], rest[-1]
    rows = pieces[0].shape[0]
    rank = ranks[ids[lax.axis_index("req")]]
    accum[...] = jnp.zeros_like(accum)
    for flip, piece in enumerate(pieces):
        place = lax.axis_index("ctx") ^ flip
        columns = pl.ds(pl.multiple_of(place * rows, HD), rows)
        accum[...] += jnp.dot(hidden[:, columns], piece[...], preferred_element_type=jnp.float32)

    column = lax.broadcasted_iota(jnp.int32, accum.shape, 1)
    out[...] = jnp.where(column < rank, accum[...], 0.0).astype(jnp.bfloat16)


def low_rank(ids, ranks, hidden, pieces):
    shape = (hidden.shape[0], pieces[0].shape[1])
    return pl.pallas_call(
        low_rank_kernel,
        out_shape=jax.ShapeDtypeStruct(shape, jnp.bfloat16),
        in_specs=[spec(SMEM)] * 2 + [spec(VMEM)] * (1 + len(pieces)),
        out_specs=spec(VMEM),
        scratch_shapes=[VMEM(shape, jnp.float32)],
        compiler_params=PARAMS,
        cost_estimate=pl.CostEstimate(flops=1 << 27, bytes_accessed=1 << 22, transcendentals=0),
    )(ids, ranks, hidden, *pieces)


FACTOR = LOG2E / math.sqrt(HD)


def head_columns(kvs, h):
    keys = [kv[:, h * HD : (h + 1) * HD] for kv in kvs]
    values = [kv[:, (KVH + h) * HD : (KVH + h + 1) * HD] for kv in kvs]
    return jnp.concatenate(keys, axis=0), jnp.concatenate(values, axis=0)


def dot_keys(queries, keys):
    return lax.dot_general(
        queries, keys, (((1,), (1,)), ((), ())), preferred_element_type=jnp.float32
    )


def out_copies(result, out, sems):
    width = GROUP * HD
    return [
        pltpu.make_async_copy(result.at[h], out.at[:, pl.ds(h * width, width)], sems.at[h])
        for h in range(KVH)
    ]


def attend_kernel(lengths, base, low, *rest):
    kvs, ups = rest[:3], rest[3:7]
    out, queries, sums, states, upper, result, sems = rest[7:]
    tokens = base.shape[0]
    rows = ups[0].shape[0]
    z = lax.axis_index("ctx")
    live = z * tokens < lengths[0]
    block = GROUP * tokens
    copies = out_copies(result, out, sems)

    @pl.when(jnp.logical_not(live))
    def _():
        result[...] = jnp.zeros_like(result)
        for copy in copies:
            copy.start()

    @pl.when(live)
    def _():
        for flip, piece in enumerate(ups):
            upper[pl.ds(pl.multiple_of((z ^ flip) * rows, rows), rows), :] = piece[...]
        for j in range(HEADS):
            columns = slice(j * HD, (j + 1) * HD)
            delta = jnp.dot(low[...], upper[:, columns], preferred_element_type=jnp.float32)
            queries[j * tokens : (j + 1) * tokens, :] = (
                base[:, columns].astype(jnp.float32) + delta
            ).astype(jnp.bfloat16)

    query_pos = lax.broadcasted_iota(jnp.int32, (tokens, tokens), 0)
    key_pos = lax.broadcasted_iota(jnp.int32, (tokens, tokens), 1)
    causal = key_pos <= query_pos
    lane = lax.broadcasted_iota(jnp.int32, (tokens, HD), 1)
    for mine, needed in enumerate(((0,), (0, 1), (0, 2), (0, 1, 2))):

        @pl.when(live & (z == mine))
        def _():
            for h in range(KVH):
                keys, values = head_columns([kvs[i] for i in needed], h)
                scores = dot_keys(queries[h * block : (h + 1) * block, :], keys)
                weights, tops, totals = [], [], []
                for g in range(GROUP):
                    score = scores[g * tokens : (g + 1) * tokens, :]
                    own = jnp.where(causal, score[:, :tokens], -1e30)
                    if mine:
                        own = jnp.concatenate([own, score[:, tokens:]], axis=1)
                    tops.append(jnp.max(own, axis=1, keepdims=True))
                    weight = jnp.exp2((own - tops[g]) * FACTOR)
                    totals.append(jnp.sum(weight, axis=1, keepdims=True))
                    weights.append(weight.astype(jnp.bfloat16))
                product = jnp.dot(
                    jnp.concatenate(weights, axis=0), values, preferred_element_type=jnp.float32
                )
                if mine < 2:
                    for g in range(GROUP):
                        result[h, :, g * HD : (g + 1) * HD] = (
                            product[g * tokens : (g + 1) * tokens, :] / totals[g]
                        ).astype(jnp.bfloat16)
                    copies[h].start()
                else:
                    sums[h * block : (h + 1) * block, :] = product
                    for g in range(GROUP):
                        start = h * block + g * tokens
                        states[start : start + tokens, :] = jnp.where(
                            lane < HD // 2, tops[g], totals[g]
                        )

    @pl.when(jnp.logical_not(live) | (z < 2))
    def _():
        for copy in copies:
            copy.wait()


def attend(lengths, base, low, kvs, ups):
    tokens, width = base.shape
    rows = HEADS * tokens
    shapes = [
        jax.ShapeDtypeStruct(base.shape, jnp.bfloat16),
        jax.ShapeDtypeStruct((rows, HD), jnp.bfloat16),
        jax.ShapeDtypeStruct((rows, HD), jnp.float32),
        jax.ShapeDtypeStruct((rows, HD), jnp.float32),
    ]
    return pl.pallas_call(
        attend_kernel,
        out_shape=shapes,
        in_specs=[spec(SMEM)] + [spec(VMEM)] * (2 + len(kvs) + len(ups)),
        out_specs=[spec(HBM)] + [spec(VMEM)] * 3,
        scratch_shapes=[
            VMEM((low.shape[1], width), jnp.bfloat16),
            VMEM((KVH, tokens, GROUP * HD), jnp.bfloat16),
            pltpu.SemaphoreType.DMA((KVH,)),
        ],
        compiler_params=PARAMS,
        cost_estimate=pl.CostEstimate(
            flops=1 << 30, bytes_accessed=1 << 22, transcendentals=1 << 21
        ),
    )(lengths, base, low, *kvs, *ups)


def finish_kernel(lengths, so_far, queries, sums, states, kv, out, result, sems):
    del so_far
    tokens = result.shape[1]
    z = lax.axis_index("ctx")
    block = GROUP * tokens
    copies = out_copies(result, out, sems)

    @pl.when((z * tokens < lengths[0]) & (z >= 2))
    def _():
        for h in range(KVH):
            keys, values = head_columns([kv], h)
            scores = dot_keys(queries[h * block : (h + 1) * block, :], keys)
            weights, factors, totals = [], [], []
            for g in range(GROUP):
                start = h * block + g * tokens
                state = states[start : start + tokens, :]
                top, total = state[:, :1], state[:, HD // 2 : HD // 2 + 1]
                score = scores[g * tokens : (g + 1) * tokens, :]
                newest = jnp.maximum(top, jnp.max(score, axis=1, keepdims=True))
                weight = jnp.exp2((score - newest) * FACTOR)
                factors.append(jnp.exp2((top - newest) * FACTOR))
                totals.append(total * factors[g] + jnp.sum(weight, axis=1, keepdims=True))
                weights.append(weight.astype(jnp.bfloat16))
            product = jnp.dot(
                jnp.concatenate(weights, axis=0), values, preferred_element_type=jnp.float32
            )
            for g in range(GROUP):
                start = h * block + g * tokens
                whole = sums[start : start + tokens, :] * factors[g]
                whole += product[g * tokens : (g + 1) * tokens, :]
                result[h, :, g * HD : (g + 1) * HD] = (whole / totals[g]).astype(jnp.bfloat16)
            copies[h].start()
        for copy in copies:
            copy.wait()


def finish(lengths, so_far, queries, sums, states, kv):
    tokens = so_far.shape[0]
    return pl.pallas_call(
        finish_kernel,
        out_shape=jax.ShapeDtypeStruct(so_far.shape, so_far.dtype),
        in_specs=[spec(SMEM), spec(HBM)] + [spec(VMEM)] * 4,
        out_specs=spec(HBM),
        input_output_aliases={1: 0},
        scratch_shapes=[
            VMEM((KVH, tokens, GROUP * HD), jnp.bfloat16),
            pltpu.SemaphoreType.DMA((KVH,)),
        ],
        compiler_params=PARAMS,
        cost_estimate=pl.CostEstimate(
            flops=1 << 28, bytes_accessed=1 << 21, transcendentals=1 << 19
        ),
    )(lengths, so_far, queries, sums, states, kv)


def body(
    hidden_states,
    queries_base,
    kv_base,
    adapter_down,
    adapter_up,
    adapter_ids,
    adapter_slots,
    rank_buckets,
    lengths,
):
    keep_down, give_down, keep_up, give_up = select(
        adapter_ids, adapter_slots, adapter_down, adapter_up
    )
    kv = kv_base[0]
    kv_one, kv_two = spread(kv)
    near_down = lax.ppermute(give_down, "req", SIBLING)
    near_up = lax.ppermute(give_up, "req", SIBLING)
    far_down = lax.ppermute(keep_down[1] + near_down[1], "req", ACROSS)
    far_up = lax.ppermute(keep_up[1] + near_up[1], "req", ACROSS)
    down = keep_down[0] + near_down[0] + far_down
    down, kv_one = lax.optimization_barrier((down, kv_one))
    down_one, down_two = spread(down)
    up = keep_up[0] + near_up[0] + far_up
    up_one, up_two = spread(up)
    down_two = lax.optimization_barrier((down_two, down_one, kv_two))[0]
    down_three = lax.ppermute(down_two, "ctx", ONE)
    up_two = lax.optimization_barrier((up_two, up_one))[0]
    up_three = lax.ppermute(up_two, "ctx", ONE)
    kv_last = lax.optimization_barrier((kv_two, up_two))[0]
    kv_three = lax.ppermute(kv_last, "ctx", LAST)
    downs = [down, down_one, down_two, down_three]
    ups = [up, up_one, up_two, up_three]
    low = low_rank(adapter_ids, rank_buckets, hidden_states[0], downs)
    parts = attend(lengths, queries_base[0], low, [kv, kv_one, kv_two], ups)
    return finish(lengths, *parts, kv_three)[None]


def plain_body(
    hidden_states,
    queries_base,
    kv_base,
    adapter_down,
    adapter_up,
    adapter_ids,
    adapter_slots,
    rank_buckets,
    lengths,
):
    req_index = lax.axis_index("req")
    ctx_index = lax.axis_index("ctx")
    per_shard = adapter_down.shape[0]
    requests = adapter_ids.shape[0]
    store = adapter_slots.shape[0]
    rank_width = adapter_down.shape[2]
    tokens = hidden_states.shape[1]
    query_width = queries_base.shape[2]
    store_range = jnp.arange(store, dtype=jnp.int32)
    chosen = adapter_ids[:, None] == store_range[None, :]
    slot_of = jnp.sum(jnp.where(chosen, adapter_slots[None, :], 0), axis=1)
    rank_of = jnp.sum(jnp.where(chosen, rank_buckets[None, :], 0), axis=1)
    mine = jnp.arange(requests, dtype=jnp.int32) == req_index
    my_slot = jnp.sum(jnp.where(mine, slot_of, 0))
    my_rank = jnp.sum(jnp.where(mine, rank_of, 0))
    held = (
        slot_of[:, None] == req_index * per_shard + jnp.arange(per_shard, dtype=jnp.int32)[None, :]
    )
    select = held.astype(jnp.bfloat16)
    send_down = jnp.einsum(
        "qa,ard->qrd", select, adapter_down, preferred_element_type=jnp.float32
    ).astype(jnp.bfloat16)
    send_up = jnp.einsum(
        "qa,ard->qrd", select, adapter_up, preferred_element_type=jnp.float32
    ).astype(jnp.bfloat16)
    got_down, got_up = (
        lax.all_to_all(send_down, "req", split_axis=0, concat_axis=0, tiled=True),
        lax.all_to_all(send_up, "req", split_axis=0, concat_axis=0, tiled=True),
    )
    owner = my_slot // per_shard
    down_mine = lax.dynamic_index_in_dim(got_down, owner, 0, keepdims=False)
    up_mine = lax.dynamic_index_in_dim(got_up, owner, 0, keepdims=False)
    features = hidden_states[0]
    columns = features
    low_rank = jnp.dot(
        columns,
        lax.all_gather(down_mine, "ctx", axis=0, tiled=True),
        preferred_element_type=jnp.float32,
    )
    low_rank = jnp.where(
        jnp.arange(rank_width, dtype=jnp.int32)[None, :] < my_rank, low_rank, 0.0
    ).astype(jnp.bfloat16)
    columns = low_rank
    delta = jnp.dot(
        columns,
        lax.all_gather(up_mine, "ctx", axis=0, tiled=True),
        preferred_element_type=jnp.float32,
    )
    queries = (
        (queries_base[0].astype(jnp.float32) + delta)
        .astype(jnp.bfloat16)
        .reshape(tokens, KVH, GROUP, HD)
    )
    length = lengths[0]
    first_query = ctx_index * tokens
    query_pos = first_query + jnp.arange(tokens, dtype=jnp.int32)
    last_needed = jnp.minimum(first_query + tokens - 1, length - 1)
    scale = 1.0 / math.sqrt(HD)
    key_width = KVH * HD
    initial = (
        jnp.full((KVH, GROUP, tokens), -1e30, jnp.float32),
        jnp.zeros((KVH, GROUP, tokens), jnp.float32),
        jnp.zeros((KVH, GROUP, tokens, HD), jnp.float32),
    )
    piece = lax.all_gather(kv_base[0], "ctx", axis=0, tiled=True)
    count = piece.shape[0]
    width = math.gcd(count, 512)

    def key_block(index, state):
        largest, total, accum = state
        offset = index * width
        rows = lax.dynamic_slice_in_dim(piece, offset, width, 0)
        keys = rows[:, :key_width].reshape(width, KVH, HD)
        values = rows[:, key_width:].reshape(width, KVH, HD)
        key_pos = offset + jnp.arange(width, dtype=jnp.int32)
        score = (
            jnp.einsum("tkgd,skd->kgts", queries, keys, preferred_element_type=jnp.float32) * scale
        )
        allowed = (key_pos[None, :] <= query_pos[:, None]) & (key_pos[None, :] < length)
        masked = jnp.where(allowed, score, -1e30)
        newest = jnp.maximum(largest, jnp.max(masked, axis=-1))
        weight = jnp.where(allowed, jnp.exp(score - newest[..., None]), 0.0)
        factor = jnp.exp(largest - newest)
        total = total * factor + jnp.sum(weight, axis=-1)
        product = jnp.einsum(
            "kgts,skd->kgtd",
            weight.astype(jnp.bfloat16),
            values,
            preferred_element_type=jnp.float32,
        )
        accum = accum * factor[..., None] + product
        return (newest, total, accum)

    def compute(state):
        return lax.fori_loop(0, count // width, key_block, state)

    needed = (jnp.int32(0) <= last_needed) & (first_query < length)
    largest, total, accum = lax.cond(needed, compute, lambda state: state, initial)
    safe_total = jnp.where(total > 0.0, total, 1.0)
    output = accum / safe_total[..., None]
    output = jnp.transpose(output, (2, 0, 1, 3)).reshape(tokens, query_width)
    output = jnp.where(query_pos[:, None] < length, output, 0.0).astype(jnp.bfloat16)
    return output[None]


def solution(mesh):
    paired = mesh.shape["ctx"] == 4 and mesh.shape["req"] == 4
    return jax.shard_map(
        body if paired else plain_body,
        mesh=mesh,
        in_specs=(
            P(("group", "req"), "ctx", None),
            P(("group", "req"), "ctx", None),
            P(("group", "req"), "ctx", None),
            P(("group", "req"), "ctx", None),
            P(("group", "req"), "ctx", None),
            P("group"),
            P("group"),
            P("group"),
            P(("group", "req")),
        ),
        out_specs=P(("group", "req"), "ctx", None),
        check_vma=False,
    )
```

```python
import functools
import math

import jax
import jax.numpy as jnp
from jax import lax
from jax.experimental import pallas as pl
from jax.experimental.pallas import tpu as pltpu
from jax.sharding import PartitionSpec as P

HD = 128
KVH = 3
GROUP = 7
HEADS = KVH * GROUP
SMEM = pltpu.SMEM
VMEM = pltpu.VMEM
HBM = pltpu.HBM
LOG2E = 1.0 / math.log(2.0)
PARAMS = pltpu.CompilerParams(vmem_limit_bytes=48 * 1024 * 1024)
WHOLE = pltpu.CompilerParams(vmem_limit_bytes=52 * 1024 * 1024)


def spec(space):
    return pl.BlockSpec(memory_space=space)


def select_kernel(table, *rest, requests):
    stores, outs, sems = rest[:2], rest[2:6], rest[6]
    per_shard = stores[0].shape[0]
    me = lax.axis_index("req")
    first = me * per_shard
    copies = []
    for i, flip in enumerate((0, 2, 1, 3)):
        local = table[requests + table[me ^ flip]] - first
        held = (local >= 0) & (local < per_shard)
        for f, store in enumerate(stores):
            out = outs[2 * f + i // 2]
            copies.append((held, local, store, out, i % 2, sems.at[4 * f + i]))
    for held, local, store, out, k, sem in copies:

        @pl.when(held)
        def _():
            pltpu.make_async_copy(store.at[local], out.at[k], sem).start()

    for held, local, store, out, k, sem in copies:

        @pl.when(jnp.logical_not(held))
        def _():
            out[k] = jnp.zeros(out.shape[1:], out.dtype)

    for held, local, store, out, k, sem in copies:

        @pl.when(held)
        def _():
            pltpu.make_async_copy(store.at[local], out.at[k], sem).wait()


def select(ids, slots, down, up):
    shapes = [jax.ShapeDtypeStruct((2, *x.shape[1:]), x.dtype) for x in (down, down, up, up)]
    return pl.pallas_call(
        functools.partial(select_kernel, requests=ids.shape[0]),
        out_shape=shapes,
        in_specs=[spec(SMEM), spec(HBM), spec(HBM)],
        out_specs=[spec(VMEM)] * 4,
        scratch_shapes=[pltpu.SemaphoreType.DMA((8,))],
        compiler_params=WHOLE,
    )(jnp.concatenate([ids, slots]), down, up)


SIBLING = [(0, 1), (1, 0), (2, 3), (3, 2)]
ACROSS = [(0, 2), (1, 3), (2, 0), (3, 1)]
ONE = [(i, i ^ 1) for i in range(4)]
TWO = [(i, i ^ 2) for i in range(4)]
LAST = [(0, 0), (1, 1), (2, 3), (3, 2)]


def spread(shard):
    return lax.ppermute(shard, "ctx", ONE), lax.ppermute(shard, "ctx", TWO)


def low_rank_kernel(ids, ranks, hidden, *rest):
    pieces, out, accum = rest[:-2], rest[-2], rest[-1]
    rows = pieces[0].shape[0]
    rank = ranks[ids[lax.axis_index("req")]]
    accum[...] = jnp.zeros_like(accum)
    for flip, piece in enumerate(pieces):
        place = lax.axis_index("ctx") ^ flip
        columns = pl.ds(pl.multiple_of(place * rows, HD), rows)
        accum[...] += jnp.dot(hidden[:, columns], piece[...], preferred_element_type=jnp.float32)

    column = lax.broadcasted_iota(jnp.int32, accum.shape, 1)
    out[...] = jnp.where(column < rank, accum[...], 0.0).astype(jnp.bfloat16)


def low_rank(ids, ranks, hidden, pieces):
    shape = (hidden.shape[0], pieces[0].shape[1])
    return pl.pallas_call(
        low_rank_kernel,
        out_shape=jax.ShapeDtypeStruct(shape, jnp.bfloat16),
        in_specs=[spec(SMEM)] * 2 + [spec(VMEM)] * (1 + len(pieces)),
        out_specs=spec(VMEM),
        scratch_shapes=[VMEM(shape, jnp.float32)],
        compiler_params=PARAMS,
        cost_estimate=pl.CostEstimate(flops=1 << 27, bytes_accessed=1 << 22, transcendentals=0),
    )(ids, ranks, hidden, *pieces)


FACTOR = LOG2E / math.sqrt(HD)


def head_columns(kvs, h):
    keys = [kv[:, h * HD : (h + 1) * HD] for kv in kvs]
    values = [kv[:, (KVH + h) * HD : (KVH + h + 1) * HD] for kv in kvs]
    return jnp.concatenate(keys, axis=0), jnp.concatenate(values, axis=0)


def dot_keys(queries, keys):
    return lax.dot_general(
        queries, keys, (((1,), (1,)), ((), ())), preferred_element_type=jnp.float32
    )


def out_copies(result, out, sems):
    width = GROUP * HD
    return [
        pltpu.make_async_copy(result.at[h], out.at[:, pl.ds(h * width, width)], sems.at[h])
        for h in range(KVH)
    ]


def attend_kernel(lengths, base, low, *rest):
    kvs, ups = rest[:3], rest[3:7]
    out, queries, sums, highs, counts, upper, result, sems = rest[7:]
    tokens = base.shape[0]
    rows = ups[0].shape[0]
    z = lax.axis_index("ctx")
    live = z * tokens < lengths[0]
    block = GROUP * tokens
    copies = out_copies(result, out, sems)

    @pl.when(jnp.logical_not(live))
    def _():
        result[...] = jnp.zeros_like(result)
        for copy in copies:
            copy.start()

    @pl.when(live)
    def _():
        for flip, piece in enumerate(ups):
            upper[pl.ds(pl.multiple_of((z ^ flip) * rows, rows), rows), :] = piece[...]
        for j in range(HEADS):
            columns = slice(j * HD, (j + 1) * HD)
            delta = jnp.dot(low[...], upper[:, columns], preferred_element_type=jnp.float32)
            queries[j * tokens : (j + 1) * tokens, :] = (
                base[:, columns].astype(jnp.float32) + delta
            ).astype(jnp.bfloat16)

    query_pos = lax.broadcasted_iota(jnp.int32, (tokens, tokens), 0)
    key_pos = lax.broadcasted_iota(jnp.int32, (tokens, tokens), 1)
    causal = key_pos <= query_pos
    for mine, needed in enumerate(((0,), (0, 1), (0, 2), (0, 1, 2))):

        @pl.when(live & (z == mine))
        def _():
            for h in range(KVH):
                keys, values = head_columns([kvs[i] for i in needed], h)
                scores = dot_keys(queries[h * block : (h + 1) * block, :], keys)
                weights, tops, totals = [], [], []
                for g in range(GROUP):
                    score = scores[g * tokens : (g + 1) * tokens, :]
                    own = jnp.where(causal, score[:, :tokens], -1e30)
                    if mine:
                        own = jnp.concatenate([own, score[:, tokens:]], axis=1)
                    tops.append(jnp.max(own, axis=1, keepdims=True))
                    weight = jnp.exp2((own - tops[g]) * FACTOR)
                    totals.append(jnp.sum(weight, axis=1, keepdims=True))
                    weights.append(weight.astype(jnp.bfloat16))
                product = jnp.dot(
                    jnp.concatenate(weights, axis=0), values, preferred_element_type=jnp.float32
                )
                if mine < 2:
                    for g in range(GROUP):
                        result[h, :, g * HD : (g + 1) * HD] = (
                            product[g * tokens : (g + 1) * tokens, :] / totals[g]
                        ).astype(jnp.bfloat16)
                    copies[h].start()
                else:
                    sums[h * block : (h + 1) * block, :] = product
                    for g in range(GROUP):
                        at = slice(h * block + g * tokens, h * block + (g + 1) * tokens)
                        highs[at, :] = jnp.broadcast_to(tops[g], (tokens, HD))
                        counts[at, :] = jnp.broadcast_to(totals[g], (tokens, HD))

    @pl.when(jnp.logical_not(live) | (z < 2))
    def _():
        for copy in copies:
            copy.wait()


def attend(lengths, base, low, kvs, ups):
    tokens, width = base.shape
    rows = HEADS * tokens
    shapes = [
        jax.ShapeDtypeStruct(base.shape, jnp.bfloat16),
        jax.ShapeDtypeStruct((rows, HD), jnp.bfloat16),
    ] + [jax.ShapeDtypeStruct((rows, HD), jnp.float32)] * 3
    return pl.pallas_call(
        attend_kernel,
        out_shape=shapes,
        in_specs=[spec(SMEM)] + [spec(VMEM)] * (2 + len(kvs) + len(ups)),
        out_specs=[spec(HBM)] + [spec(VMEM)] * 4,
        scratch_shapes=[
            VMEM((low.shape[1], width), jnp.bfloat16),
            VMEM((KVH, tokens, GROUP * HD), jnp.bfloat16),
            pltpu.SemaphoreType.DMA((KVH,)),
        ],
        compiler_params=PARAMS,
        cost_estimate=pl.CostEstimate(
            flops=1 << 30, bytes_accessed=1 << 22, transcendentals=1 << 21
        ),
    )(lengths, base, low, *kvs, *ups)


def finish_kernel(lengths, so_far, queries, sums, highs, counts, kv, out, result, sems):
    del so_far
    tokens = result.shape[1]
    z = lax.axis_index("ctx")
    block = GROUP * tokens
    copies = out_copies(result, out, sems)

    @pl.when((z * tokens < lengths[0]) & (z >= 2))
    def _():
        for h in range(KVH):
            keys, values = head_columns([kv], h)
            scores = dot_keys(queries[h * block : (h + 1) * block, :], keys)
            weights, factors, totals = [], [], []
            for g in range(GROUP):
                at = slice(h * block + g * tokens, h * block + (g + 1) * tokens)
                score = scores[g * tokens : (g + 1) * tokens, :]
                newest = jnp.maximum(highs[at, :], jnp.max(score, axis=1, keepdims=True))
                weight = jnp.exp2((score - newest) * FACTOR)
                factors.append(jnp.exp2((highs[at, :] - newest) * FACTOR))
                added = jnp.sum(weight, axis=1, keepdims=True)
                totals.append(counts[at, :] * factors[g] + added)
                weights.append(weight.astype(jnp.bfloat16))
            product = jnp.dot(
                jnp.concatenate(weights, axis=0), values, preferred_element_type=jnp.float32
            )
            for g in range(GROUP):
                at = slice(h * block + g * tokens, h * block + (g + 1) * tokens)
                whole = sums[at, :] * factors[g] + product[g * tokens : (g + 1) * tokens, :]
                result[h, :, g * HD : (g + 1) * HD] = (whole / totals[g]).astype(jnp.bfloat16)
            copies[h].start()
        for copy in copies:
            copy.wait()


def finish(lengths, so_far, queries, sums, highs, counts, kv):
    tokens = so_far.shape[0]
    return pl.pallas_call(
        finish_kernel,
        out_shape=jax.ShapeDtypeStruct(so_far.shape, so_far.dtype),
        in_specs=[spec(SMEM), spec(HBM)] + [spec(VMEM)] * 5,
        out_specs=spec(HBM),
        input_output_aliases={1: 0},
        scratch_shapes=[
            VMEM((KVH, tokens, GROUP * HD), jnp.bfloat16),
            pltpu.SemaphoreType.DMA((KVH,)),
        ],
        compiler_params=PARAMS,
        cost_estimate=pl.CostEstimate(
            flops=1 << 28, bytes_accessed=1 << 21, transcendentals=1 << 19
        ),
    )(lengths, so_far, queries, sums, highs, counts, kv)


def body(
    hidden_states,
    queries_base,
    kv_base,
    adapter_down,
    adapter_up,
    adapter_ids,
    adapter_slots,
    rank_buckets,
    lengths,
):
    keep_down, give_down, keep_up, give_up = select(
        adapter_ids, adapter_slots, adapter_down, adapter_up
    )
    kv = kv_base[0]
    kv_one, kv_two = spread(kv)
    near_down = lax.ppermute(give_down, "req", SIBLING)
    near_up = lax.ppermute(give_up, "req", SIBLING)
    far_down = lax.ppermute(keep_down[1] + near_down[1], "req", ACROSS)
    far_up = lax.ppermute(keep_up[1] + near_up[1], "req", ACROSS)
    down = keep_down[0] + near_down[0] + far_down
    down, kv_one = lax.optimization_barrier((down, kv_one))
    down_one, down_two = spread(down)
    up = keep_up[0] + near_up[0] + far_up
    up_one, up_two = spread(up)
    down_two = lax.optimization_barrier((down_two, down_one, kv_two))[0]
    down_three = lax.ppermute(down_two, "ctx", ONE)
    up_two = lax.optimization_barrier((up_two, up_one))[0]
    up_three = lax.ppermute(up_two, "ctx", ONE)
    kv_last = lax.optimization_barrier((kv_two, up_two))[0]
    kv_three = lax.ppermute(kv_last, "ctx", LAST)
    downs = [down, down_one, down_two, down_three]
    ups = [up, up_one, up_two, up_three]
    low = low_rank(adapter_ids, rank_buckets, hidden_states[0], downs)
    parts = attend(lengths, queries_base[0], low, [kv, kv_one, kv_two], ups)
    return finish(lengths, *parts, kv_three)[None]


def plain_body(
    hidden_states,
    queries_base,
    kv_base,
    adapter_down,
    adapter_up,
    adapter_ids,
    adapter_slots,
    rank_buckets,
    lengths,
):
    req_index = lax.axis_index("req")
    ctx_index = lax.axis_index("ctx")
    per_shard = adapter_down.shape[0]
    requests = adapter_ids.shape[0]
    store = adapter_slots.shape[0]
    rank_width = adapter_down.shape[2]
    tokens = hidden_states.shape[1]
    query_width = queries_base.shape[2]
    store_range = jnp.arange(store, dtype=jnp.int32)
    chosen = adapter_ids[:, None] == store_range[None, :]
    slot_of = jnp.sum(jnp.where(chosen, adapter_slots[None, :], 0), axis=1)
    rank_of = jnp.sum(jnp.where(chosen, rank_buckets[None, :], 0), axis=1)
    mine = jnp.arange(requests, dtype=jnp.int32) == req_index
    my_slot = jnp.sum(jnp.where(mine, slot_of, 0))
    my_rank = jnp.sum(jnp.where(mine, rank_of, 0))
    held = (
        slot_of[:, None] == req_index * per_shard + jnp.arange(per_shard, dtype=jnp.int32)[None, :]
    )
    select = held.astype(jnp.bfloat16)
    send_down = jnp.einsum(
        "qa,ard->qrd", select, adapter_down, preferred_element_type=jnp.float32
    ).astype(jnp.bfloat16)
    send_up = jnp.einsum(
        "qa,ard->qrd", select, adapter_up, preferred_element_type=jnp.float32
    ).astype(jnp.bfloat16)
    got_down, got_up = (
        lax.all_to_all(send_down, "req", split_axis=0, concat_axis=0, tiled=True),
        lax.all_to_all(send_up, "req", split_axis=0, concat_axis=0, tiled=True),
    )
    owner = my_slot // per_shard
    down_mine = lax.dynamic_index_in_dim(got_down, owner, 0, keepdims=False)
    up_mine = lax.dynamic_index_in_dim(got_up, owner, 0, keepdims=False)
    features = hidden_states[0]
    columns = features
    low_rank = jnp.dot(
        columns,
        lax.all_gather(down_mine, "ctx", axis=0, tiled=True),
        preferred_element_type=jnp.float32,
    )
    low_rank = jnp.where(
        jnp.arange(rank_width, dtype=jnp.int32)[None, :] < my_rank, low_rank, 0.0
    ).astype(jnp.bfloat16)
    columns = low_rank
    delta = jnp.dot(
        columns,
        lax.all_gather(up_mine, "ctx", axis=0, tiled=True),
        preferred_element_type=jnp.float32,
    )
    queries = (
        (queries_base[0].astype(jnp.float32) + delta)
        .astype(jnp.bfloat16)
        .reshape(tokens, KVH, GROUP, HD)
    )
    length = lengths[0]
    first_query = ctx_index * tokens
    query_pos = first_query + jnp.arange(tokens, dtype=jnp.int32)
    last_needed = jnp.minimum(first_query + tokens - 1, length - 1)
    scale = 1.0 / math.sqrt(HD)
    key_width = KVH * HD
    initial = (
        jnp.full((KVH, GROUP, tokens), -1e30, jnp.float32),
        jnp.zeros((KVH, GROUP, tokens), jnp.float32),
        jnp.zeros((KVH, GROUP, tokens, HD), jnp.float32),
    )
    piece = lax.all_gather(kv_base[0], "ctx", axis=0, tiled=True)
    count = piece.shape[0]
    width = math.gcd(count, 512)

    def key_block(index, state):
        largest, total, accum = state
        offset = index * width
        rows = lax.dynamic_slice_in_dim(piece, offset, width, 0)
        keys = rows[:, :key_width].reshape(width, KVH, HD)
        values = rows[:, key_width:].reshape(width, KVH, HD)
        key_pos = offset + jnp.arange(width, dtype=jnp.int32)
        score = (
            jnp.einsum("tkgd,skd->kgts", queries, keys, preferred_element_type=jnp.float32) * scale
        )
        allowed = (key_pos[None, :] <= query_pos[:, None]) & (key_pos[None, :] < length)
        masked = jnp.where(allowed, score, -1e30)
        newest = jnp.maximum(largest, jnp.max(masked, axis=-1))
        weight = jnp.where(allowed, jnp.exp(score - newest[..., None]), 0.0)
        factor = jnp.exp(largest - newest)
        total = total * factor + jnp.sum(weight, axis=-1)
        product = jnp.einsum(
            "kgts,skd->kgtd",
            weight.astype(jnp.bfloat16),
            values,
            preferred_element_type=jnp.float32,
        )
        accum = accum * factor[..., None] + product
        return (newest, total, accum)

    def compute(state):
        return lax.fori_loop(0, count // width, key_block, state)

    needed = (jnp.int32(0) <= last_needed) & (first_query < length)
    largest, total, accum = lax.cond(needed, compute, lambda state: state, initial)
    safe_total = jnp.where(total > 0.0, total, 1.0)
    output = accum / safe_total[..., None]
    output = jnp.transpose(output, (2, 0, 1, 3)).reshape(tokens, query_width)
    output = jnp.where(query_pos[:, None] < length, output, 0.0).astype(jnp.bfloat16)
    return output[None]


def solution(mesh):
    paired = mesh.shape["ctx"] == 4 and mesh.shape["req"] == 4
    return jax.shard_map(
        body if paired else plain_body,
        mesh=mesh,
        in_specs=(
            P(("group", "req"), "ctx", None),
            P(("group", "req"), "ctx", None),
            P(("group", "req"), "ctx", None),
            P(("group", "req"), "ctx", None),
            P(("group", "req"), "ctx", None),
            P("group"),
            P("group"),
            P("group"),
            P(("group", "req")),
        ),
        out_specs=P(("group", "req"), "ctx", None),
        check_vma=False,
    )
```

```python
import functools
import math

import jax
import jax.numpy as jnp
from jax import lax
from jax.experimental import pallas as pl
from jax.experimental.pallas import tpu as pltpu
from jax.sharding import PartitionSpec as P

HD = 128
KVH = 3
GROUP = 7
HEADS = KVH * GROUP
SMEM = pltpu.SMEM
VMEM = pltpu.VMEM
HBM = pltpu.HBM
LOG2E = 1.0 / math.log(2.0)
PARAMS = pltpu.CompilerParams(vmem_limit_bytes=32 * 1024 * 1024)
WHOLE = pltpu.CompilerParams(vmem_limit_bytes=52 * 1024 * 1024)


def spec(space):
    return pl.BlockSpec(memory_space=space)


def select_kernel(table, *rest, requests):
    stores, outs, sems = rest[:2], rest[2:6], rest[6]
    per_shard = stores[0].shape[0]
    me = lax.axis_index("req")
    first = me * per_shard
    copies = []
    for i, flip in enumerate((0, 2, 1, 3)):
        local = table[requests + table[me ^ flip]] - first
        held = (local >= 0) & (local < per_shard)
        for f, store in enumerate(stores):
            out = outs[2 * f + i // 2]
            copies.append((held, local, store, out, i % 2, sems.at[4 * f + i]))
    for held, local, store, out, k, sem in copies:

        @pl.when(held)
        def _():
            pltpu.make_async_copy(store.at[local], out.at[k], sem).start()

    for held, local, store, out, k, sem in copies:

        @pl.when(jnp.logical_not(held))
        def _():
            out[k] = jnp.zeros(out.shape[1:], out.dtype)

    for held, local, store, out, k, sem in copies:

        @pl.when(held)
        def _():
            pltpu.make_async_copy(store.at[local], out.at[k], sem).wait()


def select(ids, slots, down, up):
    shapes = [jax.ShapeDtypeStruct((2, *x.shape[1:]), x.dtype) for x in (down, down, up, up)]
    return pl.pallas_call(
        functools.partial(select_kernel, requests=ids.shape[0]),
        out_shape=shapes,
        in_specs=[spec(SMEM), spec(HBM), spec(HBM)],
        out_specs=[spec(VMEM)] * 4,
        scratch_shapes=[pltpu.SemaphoreType.DMA((8,))],
        compiler_params=WHOLE,
    )(jnp.concatenate([ids, slots]), down, up)


SIBLING = [(0, 1), (1, 0), (2, 3), (3, 2)]
ACROSS = [(0, 2), (1, 3), (2, 0), (3, 1)]
ONE = [(i, i ^ 1) for i in range(4)]
TWO = [(i, i ^ 2) for i in range(4)]
LAST = [(0, 0), (1, 1), (2, 3), (3, 2)]


def spread(shard):
    return lax.ppermute(shard, "ctx", ONE), lax.ppermute(shard, "ctx", TWO)


def low_rank_kernel(ids, ranks, hidden, *rest):
    pieces, out, accum = rest[:-2], rest[-2], rest[-1]
    rows = pieces[0].shape[0]
    rank = ranks[ids[lax.axis_index("req")]]
    accum[...] = jnp.zeros_like(accum)
    for flip, piece in enumerate(pieces):
        place = lax.axis_index("ctx") ^ flip
        columns = pl.ds(pl.multiple_of(place * rows, HD), rows)
        accum[...] += jnp.dot(hidden[:, columns], piece[...], preferred_element_type=jnp.float32)

    column = lax.broadcasted_iota(jnp.int32, accum.shape, 1)
    out[...] = jnp.where(column < rank, accum[...], 0.0).astype(jnp.bfloat16)


def low_rank(ids, ranks, hidden, pieces):
    shape = (hidden.shape[0], pieces[0].shape[1])
    return pl.pallas_call(
        low_rank_kernel,
        out_shape=jax.ShapeDtypeStruct(shape, jnp.bfloat16),
        in_specs=[spec(SMEM)] * 2 + [spec(VMEM)] * (1 + len(pieces)),
        out_specs=spec(VMEM),
        scratch_shapes=[VMEM(shape, jnp.float32)],
        compiler_params=PARAMS,
        cost_estimate=pl.CostEstimate(flops=1 << 27, bytes_accessed=1 << 22, transcendentals=0),
    )(ids, ranks, hidden, *pieces)


FACTOR = LOG2E / math.sqrt(HD)


def head_columns(kvs, h):
    keys = [kv[:, h * HD : (h + 1) * HD] for kv in kvs]
    values = [kv[:, (KVH + h) * HD : (KVH + h + 1) * HD] for kv in kvs]
    return jnp.concatenate(keys, axis=0), jnp.concatenate(values, axis=0)


def dot_keys(queries, keys):
    return lax.dot_general(
        queries, keys, (((1,), (1,)), ((), ())), preferred_element_type=jnp.float32
    )


def out_copies(result, out, sems):
    width = GROUP * HD
    return [
        pltpu.make_async_copy(result.at[h], out.at[:, pl.ds(h * width, width)], sems.at[h])
        for h in range(KVH)
    ]


def attend_kernel(lengths, base, low, *rest):
    kvs, ups = rest[:3], rest[3:7]
    out, queries, sums, highs, counts, upper, result, sems = rest[7:]
    tokens = base.shape[0]
    rows = ups[0].shape[0]
    z = lax.axis_index("ctx")
    live = z * tokens < lengths[0]
    block = GROUP * tokens
    copies = out_copies(result, out, sems)

    @pl.when(jnp.logical_not(live))
    def _():
        result[...] = jnp.zeros_like(result)
        for copy in copies:
            copy.start()

    @pl.when(live)
    def _():
        for flip, piece in enumerate(ups):
            upper[pl.ds(pl.multiple_of((z ^ flip) * rows, rows), rows), :] = piece[...]
        for j in range(HEADS):
            columns = slice(j * HD, (j + 1) * HD)
            delta = jnp.dot(low[...], upper[:, columns], preferred_element_type=jnp.float32)
            queries[j * tokens : (j + 1) * tokens, :] = (
                base[:, columns].astype(jnp.float32) + delta
            ).astype(jnp.bfloat16)

    query_pos = lax.broadcasted_iota(jnp.int32, (tokens, tokens), 0)
    key_pos = lax.broadcasted_iota(jnp.int32, (tokens, tokens), 1)
    causal = key_pos <= query_pos
    for mine, needed in enumerate(((0,), (0, 1), (0, 2), (0, 1, 2))):

        @pl.when(live & (z == mine))
        def _():
            for h in range(KVH):
                keys, values = head_columns([kvs[i] for i in needed], h)
                scores = dot_keys(queries[h * block : (h + 1) * block, :], keys)
                weights, tops, totals = [], [], []
                for g in range(GROUP):
                    score = scores[g * tokens : (g + 1) * tokens, :]
                    own = jnp.where(causal, score[:, :tokens], -1e30)
                    if mine:
                        own = jnp.concatenate([own, score[:, tokens:]], axis=1)
                    tops.append(jnp.max(own, axis=1, keepdims=True))
                    weight = jnp.exp2((own - tops[g]) * FACTOR)
                    totals.append(jnp.sum(weight, axis=1, keepdims=True))
                    weights.append(weight.astype(jnp.bfloat16))
                product = jnp.dot(
                    jnp.concatenate(weights, axis=0), values, preferred_element_type=jnp.float32
                )
                if mine < 2:
                    for g in range(GROUP):
                        result[h, :, g * HD : (g + 1) * HD] = (
                            product[g * tokens : (g + 1) * tokens, :] / totals[g]
                        ).astype(jnp.bfloat16)
                    copies[h].start()
                else:
                    sums[h * block : (h + 1) * block, :] = product
                    for g in range(GROUP):
                        at = slice(h * block + g * tokens, h * block + (g + 1) * tokens)
                        highs[at, :] = jnp.broadcast_to(tops[g], (tokens, HD))
                        counts[at, :] = jnp.broadcast_to(totals[g], (tokens, HD))

    @pl.when(jnp.logical_not(live) | (z < 2))
    def _():
        for copy in copies:
            copy.wait()


def attend(lengths, base, low, kvs, ups):
    tokens, width = base.shape
    rows = HEADS * tokens
    shapes = [
        jax.ShapeDtypeStruct(base.shape, jnp.bfloat16),
        jax.ShapeDtypeStruct((rows, HD), jnp.bfloat16),
    ] + [jax.ShapeDtypeStruct((rows, HD), jnp.float32)] * 3
    return pl.pallas_call(
        attend_kernel,
        out_shape=shapes,
        in_specs=[spec(SMEM)] + [spec(VMEM)] * (2 + len(kvs) + len(ups)),
        out_specs=[spec(HBM)] + [spec(VMEM)] * 4,
        scratch_shapes=[
            VMEM((low.shape[1], width), jnp.bfloat16),
            VMEM((KVH, tokens, GROUP * HD), jnp.bfloat16),
            pltpu.SemaphoreType.DMA((KVH,)),
        ],
        compiler_params=PARAMS,
        cost_estimate=pl.CostEstimate(
            flops=1 << 30, bytes_accessed=1 << 22, transcendentals=1 << 21
        ),
    )(lengths, base, low, *kvs, *ups)


def finish_kernel(lengths, so_far, queries, sums, highs, counts, kv, out, result, sems):
    del so_far
    tokens = result.shape[1]
    z = lax.axis_index("ctx")
    block = GROUP * tokens
    copies = out_copies(result, out, sems)

    @pl.when((z * tokens < lengths[0]) & (z >= 2))
    def _():
        for h in range(KVH):
            keys, values = head_columns([kv], h)
            scores = dot_keys(queries[h * block : (h + 1) * block, :], keys)
            weights, factors, totals = [], [], []
            for g in range(GROUP):
                at = slice(h * block + g * tokens, h * block + (g + 1) * tokens)
                score = scores[g * tokens : (g + 1) * tokens, :]
                newest = jnp.maximum(highs[at, :], jnp.max(score, axis=1, keepdims=True))
                weight = jnp.exp2((score - newest) * FACTOR)
                factors.append(jnp.exp2((highs[at, :] - newest) * FACTOR))
                added = jnp.sum(weight, axis=1, keepdims=True)
                totals.append(counts[at, :] * factors[g] + added)
                weights.append(weight.astype(jnp.bfloat16))
            product = jnp.dot(
                jnp.concatenate(weights, axis=0), values, preferred_element_type=jnp.float32
            )
            for g in range(GROUP):
                at = slice(h * block + g * tokens, h * block + (g + 1) * tokens)
                whole = sums[at, :] * factors[g] + product[g * tokens : (g + 1) * tokens, :]
                result[h, :, g * HD : (g + 1) * HD] = (whole / totals[g]).astype(jnp.bfloat16)
            copies[h].start()
        for copy in copies:
            copy.wait()


def finish(lengths, so_far, queries, sums, highs, counts, kv):
    tokens = so_far.shape[0]
    return pl.pallas_call(
        finish_kernel,
        out_shape=jax.ShapeDtypeStruct(so_far.shape, so_far.dtype),
        in_specs=[spec(SMEM), spec(HBM)] + [spec(VMEM)] * 5,
        out_specs=spec(HBM),
        input_output_aliases={1: 0},
        scratch_shapes=[
            VMEM((KVH, tokens, GROUP * HD), jnp.bfloat16),
            pltpu.SemaphoreType.DMA((KVH,)),
        ],
        compiler_params=PARAMS,
        cost_estimate=pl.CostEstimate(
            flops=1 << 28, bytes_accessed=1 << 21, transcendentals=1 << 19
        ),
    )(lengths, so_far, queries, sums, highs, counts, kv)


def body(
    hidden_states,
    queries_base,
    kv_base,
    adapter_down,
    adapter_up,
    adapter_ids,
    adapter_slots,
    rank_buckets,
    lengths,
):
    keep_down, give_down, keep_up, give_up = select(
        adapter_ids, adapter_slots, adapter_down, adapter_up
    )
    kv = kv_base[0]
    kv_one, kv_two = spread(kv)
    near_down = lax.ppermute(give_down, "req", SIBLING)
    near_up = lax.ppermute(give_up, "req", SIBLING)
    far_down = lax.ppermute(keep_down[1] + near_down[1], "req", ACROSS)
    far_up = lax.ppermute(keep_up[1] + near_up[1], "req", ACROSS)
    down = keep_down[0] + near_down[0] + far_down
    down, kv_one = lax.optimization_barrier((down, kv_one))
    down_one, down_two = spread(down)
    up = keep_up[0] + near_up[0] + far_up
    up_one, up_two = spread(up)
    down_two = lax.optimization_barrier((down_two, down_one, kv_two))[0]
    down_three = lax.ppermute(down_two, "ctx", ONE)
    up_two = lax.optimization_barrier((up_two, up_one))[0]
    up_three = lax.ppermute(up_two, "ctx", ONE)
    kv_last = lax.optimization_barrier((kv_two, up_two))[0]
    kv_three = lax.ppermute(kv_last, "ctx", LAST)
    downs = [down, down_one, down_two, down_three]
    ups = [up, up_one, up_two, up_three]
    low = low_rank(adapter_ids, rank_buckets, hidden_states[0], downs)
    parts = attend(lengths, queries_base[0], low, [kv, kv_one, kv_two], ups)
    return finish(lengths, *parts, kv_three)[None]


def plain_body(
    hidden_states,
    queries_base,
    kv_base,
    adapter_down,
    adapter_up,
    adapter_ids,
    adapter_slots,
    rank_buckets,
    lengths,
):
    req_index = lax.axis_index("req")
    ctx_index = lax.axis_index("ctx")
    per_shard = adapter_down.shape[0]
    requests = adapter_ids.shape[0]
    store = adapter_slots.shape[0]
    rank_width = adapter_down.shape[2]
    tokens = hidden_states.shape[1]
    query_width = queries_base.shape[2]
    store_range = jnp.arange(store, dtype=jnp.int32)
    chosen = adapter_ids[:, None] == store_range[None, :]
    slot_of = jnp.sum(jnp.where(chosen, adapter_slots[None, :], 0), axis=1)
    rank_of = jnp.sum(jnp.where(chosen, rank_buckets[None, :], 0), axis=1)
    mine = jnp.arange(requests, dtype=jnp.int32) == req_index
    my_slot = jnp.sum(jnp.where(mine, slot_of, 0))
    my_rank = jnp.sum(jnp.where(mine, rank_of, 0))
    held = (
        slot_of[:, None] == req_index * per_shard + jnp.arange(per_shard, dtype=jnp.int32)[None, :]
    )
    select = held.astype(jnp.bfloat16)
    send_down = jnp.einsum(
        "qa,ard->qrd", select, adapter_down, preferred_element_type=jnp.float32
    ).astype(jnp.bfloat16)
    send_up = jnp.einsum(
        "qa,ard->qrd", select, adapter_up, preferred_element_type=jnp.float32
    ).astype(jnp.bfloat16)
    got_down, got_up = (
        lax.all_to_all(send_down, "req", split_axis=0, concat_axis=0, tiled=True),
        lax.all_to_all(send_up, "req", split_axis=0, concat_axis=0, tiled=True),
    )
    owner = my_slot // per_shard
    down_mine = lax.dynamic_index_in_dim(got_down, owner, 0, keepdims=False)
    up_mine = lax.dynamic_index_in_dim(got_up, owner, 0, keepdims=False)
    features = hidden_states[0]
    columns = features
    low_rank = jnp.dot(
        columns,
        lax.all_gather(down_mine, "ctx", axis=0, tiled=True),
        preferred_element_type=jnp.float32,
    )
    low_rank = jnp.where(
        jnp.arange(rank_width, dtype=jnp.int32)[None, :] < my_rank, low_rank, 0.0
    ).astype(jnp.bfloat16)
    columns = low_rank
    delta = jnp.dot(
        columns,
        lax.all_gather(up_mine, "ctx", axis=0, tiled=True),
        preferred_element_type=jnp.float32,
    )
    queries = (
        (queries_base[0].astype(jnp.float32) + delta)
        .astype(jnp.bfloat16)
        .reshape(tokens, KVH, GROUP, HD)
    )
    length = lengths[0]
    first_query = ctx_index * tokens
    query_pos = first_query + jnp.arange(tokens, dtype=jnp.int32)
    last_needed = jnp.minimum(first_query + tokens - 1, length - 1)
    scale = 1.0 / math.sqrt(HD)
    key_width = KVH * HD
    initial = (
        jnp.full((KVH, GROUP, tokens), -1e30, jnp.float32),
        jnp.zeros((KVH, GROUP, tokens), jnp.float32),
        jnp.zeros((KVH, GROUP, tokens, HD), jnp.float32),
    )
    piece = lax.all_gather(kv_base[0], "ctx", axis=0, tiled=True)
    count = piece.shape[0]
    width = math.gcd(count, 512)

    def key_block(index, state):
        largest, total, accum = state
        offset = index * width
        rows = lax.dynamic_slice_in_dim(piece, offset, width, 0)
        keys = rows[:, :key_width].reshape(width, KVH, HD)
        values = rows[:, key_width:].reshape(width, KVH, HD)
        key_pos = offset + jnp.arange(width, dtype=jnp.int32)
        score = (
            jnp.einsum("tkgd,skd->kgts", queries, keys, preferred_element_type=jnp.float32) * scale
        )
        allowed = (key_pos[None, :] <= query_pos[:, None]) & (key_pos[None, :] < length)
        masked = jnp.where(allowed, score, -1e30)
        newest = jnp.maximum(largest, jnp.max(masked, axis=-1))
        weight = jnp.where(allowed, jnp.exp(score - newest[..., None]), 0.0)
        factor = jnp.exp(largest - newest)
        total = total * factor + jnp.sum(weight, axis=-1)
        product = jnp.einsum(
            "kgts,skd->kgtd",
            weight.astype(jnp.bfloat16),
            values,
            preferred_element_type=jnp.float32,
        )
        accum = accum * factor[..., None] + product
        return (newest, total, accum)

    def compute(state):
        return lax.fori_loop(0, count // width, key_block, state)

    needed = (jnp.int32(0) <= last_needed) & (first_query < length)
    largest, total, accum = lax.cond(needed, compute, lambda state: state, initial)
    safe_total = jnp.where(total > 0.0, total, 1.0)
    output = accum / safe_total[..., None]
    output = jnp.transpose(output, (2, 0, 1, 3)).reshape(tokens, query_width)
    output = jnp.where(query_pos[:, None] < length, output, 0.0).astype(jnp.bfloat16)
    return output[None]


def solution(mesh):
    paired = mesh.shape["ctx"] == 4 and mesh.shape["req"] == 4
    return jax.shard_map(
        body if paired else plain_body,
        mesh=mesh,
        in_specs=(
            P(("group", "req"), "ctx", None),
            P(("group", "req"), "ctx", None),
            P(("group", "req"), "ctx", None),
            P(("group", "req"), "ctx", None),
            P(("group", "req"), "ctx", None),
            P("group"),
            P("group"),
            P("group"),
            P(("group", "req")),
        ),
        out_specs=P(("group", "req"), "ctx", None),
        check_vma=False,
    )
```

```python
import functools
import math

import jax
import jax.numpy as jnp
from jax import lax
from jax.experimental import pallas as pl
from jax.experimental.pallas import tpu as pltpu
from jax.sharding import PartitionSpec as P

HD = 128
KVH = 3
GROUP = 7
HEADS = KVH * GROUP
SMEM = pltpu.SMEM
VMEM = pltpu.VMEM
HBM = pltpu.HBM
LOG2E = 1.0 / math.log(2.0)
PARAMS = pltpu.CompilerParams(vmem_limit_bytes=32 * 1024 * 1024)
WHOLE = pltpu.CompilerParams(vmem_limit_bytes=52 * 1024 * 1024)


def spec(space):
    return pl.BlockSpec(memory_space=space)


def select_kernel(table, *rest, requests):
    stores, outs, sems = rest[:2], rest[2:6], rest[6]
    per_shard = stores[0].shape[0]
    me = lax.axis_index("req")
    first = me * per_shard
    copies = []
    for i, flip in enumerate((0, 2, 1, 3)):
        local = table[requests + table[me ^ flip]] - first
        held = (local >= 0) & (local < per_shard)
        for f, store in enumerate(stores):
            out = outs[2 * f + i // 2]
            copies.append((held, local, store, out, i % 2, sems.at[4 * f + i]))
    for held, local, store, out, k, sem in copies:

        @pl.when(held)
        def _():
            pltpu.make_async_copy(store.at[local], out.at[k], sem).start()

    for held, local, store, out, k, sem in copies:

        @pl.when(jnp.logical_not(held))
        def _():
            out[k] = jnp.zeros(out.shape[1:], out.dtype)

    for held, local, store, out, k, sem in copies:

        @pl.when(held)
        def _():
            pltpu.make_async_copy(store.at[local], out.at[k], sem).wait()


def select(ids, slots, down, up):
    shapes = [jax.ShapeDtypeStruct((2, *x.shape[1:]), x.dtype) for x in (down, down, up, up)]
    return pl.pallas_call(
        functools.partial(select_kernel, requests=ids.shape[0]),
        out_shape=shapes,
        in_specs=[spec(SMEM), spec(HBM), spec(HBM)],
        out_specs=[spec(VMEM)] * 4,
        scratch_shapes=[pltpu.SemaphoreType.DMA((8,))],
        compiler_params=WHOLE,
    )(jnp.concatenate([ids, slots]), down, up)


SIBLING = [(0, 1), (1, 0), (2, 3), (3, 2)]
ACROSS = [(0, 2), (1, 3), (2, 0), (3, 1)]
ONE = [(i, i ^ 1) for i in range(4)]
TWO = [(i, i ^ 2) for i in range(4)]
LAST = [(0, 0), (1, 1), (2, 3), (3, 2)]


def spread(shard):
    return lax.ppermute(shard, "ctx", ONE), lax.ppermute(shard, "ctx", TWO)


def low_rank_kernel(ids, ranks, hidden, *rest):
    pieces, out, accum = rest[:-2], rest[-2], rest[-1]
    rows = pieces[0].shape[0]
    rank = ranks[ids[lax.axis_index("req")]]
    accum[...] = jnp.zeros_like(accum)
    for flip, piece in enumerate(pieces):
        place = lax.axis_index("ctx") ^ flip
        columns = pl.ds(pl.multiple_of(place * rows, HD), rows)
        accum[...] += jnp.dot(hidden[:, columns], piece[...], preferred_element_type=jnp.float32)

    column = lax.broadcasted_iota(jnp.int32, accum.shape, 1)
    out[...] = jnp.where(column < rank, accum[...], 0.0).astype(jnp.bfloat16)


def low_rank(ids, ranks, hidden, pieces):
    shape = (hidden.shape[0], pieces[0].shape[1])
    return pl.pallas_call(
        low_rank_kernel,
        out_shape=jax.ShapeDtypeStruct(shape, jnp.bfloat16),
        in_specs=[spec(SMEM)] * 2 + [spec(VMEM)] * (1 + len(pieces)),
        out_specs=spec(VMEM),
        scratch_shapes=[VMEM(shape, jnp.float32)],
        compiler_params=PARAMS,
        cost_estimate=pl.CostEstimate(flops=1 << 27, bytes_accessed=1 << 22, transcendentals=0),
    )(ids, ranks, hidden, *pieces)


FACTOR = LOG2E / math.sqrt(HD)


def head_columns(kvs, h):
    keys = [kv[:, h * HD : (h + 1) * HD] for kv in kvs]
    values = [kv[:, (KVH + h) * HD : (KVH + h + 1) * HD] for kv in kvs]
    return jnp.concatenate(keys, axis=0), jnp.concatenate(values, axis=0)


def dot_keys(queries, keys):
    return lax.dot_general(
        queries, keys, (((1,), (1,)), ((), ())), preferred_element_type=jnp.float32
    )


def out_copies(result, out, sems):
    width = GROUP * HD
    return [
        pltpu.make_async_copy(result.at[h], out.at[:, pl.ds(h * width, width)], sems.at[h])
        for h in range(KVH)
    ]


def attend_kernel(lengths, base, low, *rest):
    kvs, ups = rest[:3], rest[3:7]
    out, queries, sums, highs, counts, upper, result, sems = rest[7:]
    tokens = base.shape[0]
    rows = ups[0].shape[0]
    z = lax.axis_index("ctx")
    live = z * tokens < lengths[0]
    block = GROUP * tokens
    copies = out_copies(result, out, sems)

    @pl.when(jnp.logical_not(live))
    def _():
        result[...] = jnp.zeros_like(result)
        for copy in copies:
            copy.start()

    @pl.when(live)
    def _():
        for flip, piece in enumerate(ups):
            upper[pl.ds(pl.multiple_of((z ^ flip) * rows, rows), rows), :] = piece[...]
        for j in range(HEADS):
            columns = slice(j * HD, (j + 1) * HD)
            delta = jnp.dot(low[...], upper[:, columns], preferred_element_type=jnp.float32)
            queries[j * tokens : (j + 1) * tokens, :] = (
                base[:, columns].astype(jnp.float32) + delta
            ).astype(jnp.bfloat16)

    query_pos = lax.broadcasted_iota(jnp.int32, (tokens, tokens), 0)
    key_pos = lax.broadcasted_iota(jnp.int32, (tokens, tokens), 1)
    causal = key_pos <= query_pos
    for mine, needed in enumerate(((0,), (0, 1), (0, 2), (0, 1, 2))):

        @pl.when(live & (z == mine))
        def _():
            for h in range(KVH):
                keys, values = head_columns([kvs[i] for i in needed], h)
                scores = dot_keys(queries[h * block : (h + 1) * block, :], keys)
                weights, tops, totals = [], [], []
                for g in range(GROUP):
                    score = scores[g * tokens : (g + 1) * tokens, :]
                    own = jnp.where(causal, score[:, :tokens], -1e30)
                    if mine:
                        own = jnp.concatenate([own, score[:, tokens:]], axis=1)
                    tops.append(jnp.max(own, axis=1, keepdims=True))
                    weight = jnp.exp2((own - tops[g]) * FACTOR)
                    totals.append(jnp.sum(weight, axis=1, keepdims=True))
                    weights.append(weight.astype(jnp.bfloat16))
                product = jnp.dot(
                    jnp.concatenate(weights, axis=0), values, preferred_element_type=jnp.float32
                )
                if mine < 2:
                    for g in range(GROUP):
                        result[h, :, g * HD : (g + 1) * HD] = (
                            product[g * tokens : (g + 1) * tokens, :] / totals[g]
                        ).astype(jnp.bfloat16)
                    copies[h].start()
                else:
                    sums[h * block : (h + 1) * block, :] = product
                    for g in range(GROUP):
                        at = slice(h * block + g * tokens, h * block + (g + 1) * tokens)
                        highs[at, :] = jnp.broadcast_to(tops[g], (tokens, HD))
                        counts[at, :] = jnp.broadcast_to(totals[g], (tokens, HD))

    @pl.when(jnp.logical_not(live) | (z < 2))
    def _():
        for copy in copies:
            copy.wait()


def attend(lengths, base, low, kvs, ups):
    tokens, width = base.shape
    rows = HEADS * tokens
    shapes = [
        jax.ShapeDtypeStruct(base.shape, jnp.bfloat16),
        jax.ShapeDtypeStruct((rows, HD), jnp.bfloat16),
    ] + [jax.ShapeDtypeStruct((rows, HD), jnp.float32)] * 3
    return pl.pallas_call(
        attend_kernel,
        out_shape=shapes,
        in_specs=[spec(SMEM)] + [spec(VMEM)] * (2 + len(kvs) + len(ups)),
        out_specs=[spec(HBM)] + [spec(VMEM)] * 4,
        scratch_shapes=[
            VMEM((low.shape[1], width), jnp.bfloat16),
            VMEM((KVH, tokens, GROUP * HD), jnp.bfloat16),
            pltpu.SemaphoreType.DMA((KVH,)),
        ],
        compiler_params=PARAMS,
        cost_estimate=pl.CostEstimate(
            flops=1 << 30, bytes_accessed=1 << 22, transcendentals=1 << 21
        ),
    )(lengths, base, low, *kvs, *ups)


def finish_kernel(lengths, so_far, queries, sums, highs, counts, kv, out, result, sems):
    del so_far
    tokens = result.shape[1]
    z = lax.axis_index("ctx")
    block = GROUP * tokens
    copies = out_copies(result, out, sems)

    @pl.when((z * tokens < lengths[0]) & (z >= 2))
    def _():
        for h in range(KVH):
            keys, values = head_columns([kv], h)
            scores = dot_keys(queries[h * block : (h + 1) * block, :], keys)
            weights, factors, totals = [], [], []
            for g in range(GROUP):
                at = slice(h * block + g * tokens, h * block + (g + 1) * tokens)
                score = scores[g * tokens : (g + 1) * tokens, :]
                newest = jnp.maximum(highs[at, :], jnp.max(score, axis=1, keepdims=True))
                weight = jnp.exp2((score - newest) * FACTOR)
                factors.append(jnp.exp2((highs[at, :] - newest) * FACTOR))
                added = jnp.sum(weight, axis=1, keepdims=True)
                totals.append(counts[at, :] * factors[g] + added)
                weights.append(weight.astype(jnp.bfloat16))
            product = jnp.dot(
                jnp.concatenate(weights, axis=0), values, preferred_element_type=jnp.float32
            )
            for g in range(GROUP):
                at = slice(h * block + g * tokens, h * block + (g + 1) * tokens)
                whole = sums[at, :] * factors[g] + product[g * tokens : (g + 1) * tokens, :]
                result[h, :, g * HD : (g + 1) * HD] = (whole / totals[g]).astype(jnp.bfloat16)
            copies[h].start()
        for copy in copies:
            copy.wait()


def finish(lengths, so_far, queries, sums, highs, counts, kv):
    tokens = so_far.shape[0]
    return pl.pallas_call(
        finish_kernel,
        out_shape=jax.ShapeDtypeStruct(so_far.shape, so_far.dtype),
        in_specs=[spec(SMEM), spec(HBM)] + [spec(VMEM)] * 5,
        out_specs=spec(HBM),
        input_output_aliases={1: 0},
        scratch_shapes=[
            VMEM((KVH, tokens, GROUP * HD), jnp.bfloat16),
            pltpu.SemaphoreType.DMA((KVH,)),
        ],
        compiler_params=PARAMS,
        cost_estimate=pl.CostEstimate(
            flops=1 << 28, bytes_accessed=1 << 21, transcendentals=1 << 19
        ),
    )(lengths, so_far, queries, sums, highs, counts, kv)


def body(
    hidden_states,
    queries_base,
    kv_base,
    adapter_down,
    adapter_up,
    adapter_ids,
    adapter_slots,
    rank_buckets,
    lengths,
):
    keep_down, give_down, keep_up, give_up = select(
        adapter_ids, adapter_slots, adapter_down, adapter_up
    )
    kv = kv_base[0]
    kv_one, kv_two = spread(kv)
    near_down = lax.ppermute(give_down, "req", SIBLING)
    near_up = lax.ppermute(give_up, "req", SIBLING)
    far_down = lax.ppermute(keep_down[1] + near_down[1], "req", ACROSS)
    far_up = lax.ppermute(keep_up[1] + near_up[1], "req", ACROSS)
    down = keep_down[0] + near_down[0] + far_down
    down, kv_one = lax.optimization_barrier((down, kv_one))
    down_one, down_two = spread(down)
    up = keep_up[0] + near_up[0] + far_up
    up_one, up_two = spread(up)
    down_two = lax.optimization_barrier((down_two, kv_two))[0]
    down_three = lax.ppermute(down_two, "ctx", ONE)
    up_two = lax.optimization_barrier((up_two, down_one))[0]
    up_three = lax.ppermute(up_two, "ctx", ONE)
    kv_last = lax.optimization_barrier((kv_two, up_two, up_one))[0]
    kv_three = lax.ppermute(kv_last, "ctx", LAST)
    downs = [down, down_one, down_two, down_three]
    ups = [up, up_one, up_two, up_three]
    low = low_rank(adapter_ids, rank_buckets, hidden_states[0], downs)
    parts = attend(lengths, queries_base[0], low, [kv, kv_one, kv_two], ups)
    return finish(lengths, *parts, kv_three)[None]


def plain_body(
    hidden_states,
    queries_base,
    kv_base,
    adapter_down,
    adapter_up,
    adapter_ids,
    adapter_slots,
    rank_buckets,
    lengths,
):
    req_index = lax.axis_index("req")
    ctx_index = lax.axis_index("ctx")
    per_shard = adapter_down.shape[0]
    requests = adapter_ids.shape[0]
    store = adapter_slots.shape[0]
    rank_width = adapter_down.shape[2]
    tokens = hidden_states.shape[1]
    query_width = queries_base.shape[2]
    store_range = jnp.arange(store, dtype=jnp.int32)
    chosen = adapter_ids[:, None] == store_range[None, :]
    slot_of = jnp.sum(jnp.where(chosen, adapter_slots[None, :], 0), axis=1)
    rank_of = jnp.sum(jnp.where(chosen, rank_buckets[None, :], 0), axis=1)
    mine = jnp.arange(requests, dtype=jnp.int32) == req_index
    my_slot = jnp.sum(jnp.where(mine, slot_of, 0))
    my_rank = jnp.sum(jnp.where(mine, rank_of, 0))
    held = (
        slot_of[:, None] == req_index * per_shard + jnp.arange(per_shard, dtype=jnp.int32)[None, :]
    )
    select = held.astype(jnp.bfloat16)
    send_down = jnp.einsum(
        "qa,ard->qrd", select, adapter_down, preferred_element_type=jnp.float32
    ).astype(jnp.bfloat16)
    send_up = jnp.einsum(
        "qa,ard->qrd", select, adapter_up, preferred_element_type=jnp.float32
    ).astype(jnp.bfloat16)
    got_down, got_up = (
        lax.all_to_all(send_down, "req", split_axis=0, concat_axis=0, tiled=True),
        lax.all_to_all(send_up, "req", split_axis=0, concat_axis=0, tiled=True),
    )
    owner = my_slot // per_shard
    down_mine = lax.dynamic_index_in_dim(got_down, owner, 0, keepdims=False)
    up_mine = lax.dynamic_index_in_dim(got_up, owner, 0, keepdims=False)
    features = hidden_states[0]
    columns = features
    low_rank = jnp.dot(
        columns,
        lax.all_gather(down_mine, "ctx", axis=0, tiled=True),
        preferred_element_type=jnp.float32,
    )
    low_rank = jnp.where(
        jnp.arange(rank_width, dtype=jnp.int32)[None, :] < my_rank, low_rank, 0.0
    ).astype(jnp.bfloat16)
    columns = low_rank
    delta = jnp.dot(
        columns,
        lax.all_gather(up_mine, "ctx", axis=0, tiled=True),
        preferred_element_type=jnp.float32,
    )
    queries = (
        (queries_base[0].astype(jnp.float32) + delta)
        .astype(jnp.bfloat16)
        .reshape(tokens, KVH, GROUP, HD)
    )
    length = lengths[0]
    first_query = ctx_index * tokens
    query_pos = first_query + jnp.arange(tokens, dtype=jnp.int32)
    last_needed = jnp.minimum(first_query + tokens - 1, length - 1)
    scale = 1.0 / math.sqrt(HD)
    key_width = KVH * HD
    initial = (
        jnp.full((KVH, GROUP, tokens), -1e30, jnp.float32),
        jnp.zeros((KVH, GROUP, tokens), jnp.float32),
        jnp.zeros((KVH, GROUP, tokens, HD), jnp.float32),
    )
    piece = lax.all_gather(kv_base[0], "ctx", axis=0, tiled=True)
    count = piece.shape[0]
    width = math.gcd(count, 512)

    def key_block(index, state):
        largest, total, accum = state
        offset = index * width
        rows = lax.dynamic_slice_in_dim(piece, offset, width, 0)
        keys = rows[:, :key_width].reshape(width, KVH, HD)
        values = rows[:, key_width:].reshape(width, KVH, HD)
        key_pos = offset + jnp.arange(width, dtype=jnp.int32)
        score = (
            jnp.einsum("tkgd,skd->kgts", queries, keys, preferred_element_type=jnp.float32) * scale
        )
        allowed = (key_pos[None, :] <= query_pos[:, None]) & (key_pos[None, :] < length)
        masked = jnp.where(allowed, score, -1e30)
        newest = jnp.maximum(largest, jnp.max(masked, axis=-1))
        weight = jnp.where(allowed, jnp.exp(score - newest[..., None]), 0.0)
        factor = jnp.exp(largest - newest)
        total = total * factor + jnp.sum(weight, axis=-1)
        product = jnp.einsum(
            "kgts,skd->kgtd",
            weight.astype(jnp.bfloat16),
            values,
            preferred_element_type=jnp.float32,
        )
        accum = accum * factor[..., None] + product
        return (newest, total, accum)

    def compute(state):
        return lax.fori_loop(0, count // width, key_block, state)

    needed = (jnp.int32(0) <= last_needed) & (first_query < length)
    largest, total, accum = lax.cond(needed, compute, lambda state: state, initial)
    safe_total = jnp.where(total > 0.0, total, 1.0)
    output = accum / safe_total[..., None]
    output = jnp.transpose(output, (2, 0, 1, 3)).reshape(tokens, query_width)
    output = jnp.where(query_pos[:, None] < length, output, 0.0).astype(jnp.bfloat16)
    return output[None]


def solution(mesh):
    paired = mesh.shape["ctx"] == 4 and mesh.shape["req"] == 4
    return jax.shard_map(
        body if paired else plain_body,
        mesh=mesh,
        in_specs=(
            P(("group", "req"), "ctx", None),
            P(("group", "req"), "ctx", None),
            P(("group", "req"), "ctx", None),
            P(("group", "req"), "ctx", None),
            P(("group", "req"), "ctx", None),
            P("group"),
            P("group"),
            P("group"),
            P(("group", "req")),
        ),
        out_specs=P(("group", "req"), "ctx", None),
        check_vma=False,
    )
```

```python
import functools
import math

import jax
import jax.numpy as jnp
from jax import lax
from jax.experimental import pallas as pl
from jax.experimental.pallas import tpu as pltpu
from jax.sharding import PartitionSpec as P

HD = 128
KVH = 3
GROUP = 7
HEADS = KVH * GROUP
SMEM = pltpu.SMEM
VMEM = pltpu.VMEM
HBM = pltpu.HBM
LOG2E = 1.0 / math.log(2.0)
PARAMS = pltpu.CompilerParams(vmem_limit_bytes=32 * 1024 * 1024)
WHOLE = pltpu.CompilerParams(vmem_limit_bytes=52 * 1024 * 1024)


def spec(space):
    return pl.BlockSpec(memory_space=space)


def select_kernel(table, *rest, requests):
    stores, outs, sems = rest[:2], rest[2:6], rest[6]
    per_shard = stores[0].shape[0]
    me = lax.axis_index("req")
    first = me * per_shard
    copies = []
    for i, flip in enumerate((0, 2, 1, 3)):
        local = table[requests + table[me ^ flip]] - first
        held = (local >= 0) & (local < per_shard)
        for f, store in enumerate(stores):
            out = outs[2 * f + i // 2]
            copies.append((held, local, store, out, i % 2, sems.at[4 * f + i]))
    for held, local, store, out, k, sem in copies:

        @pl.when(held)
        def _():
            pltpu.make_async_copy(store.at[local], out.at[k], sem).start()

    for held, local, store, out, k, sem in copies:

        @pl.when(jnp.logical_not(held))
        def _():
            out[k] = jnp.zeros(out.shape[1:], out.dtype)

    for held, local, store, out, k, sem in copies:

        @pl.when(held)
        def _():
            pltpu.make_async_copy(store.at[local], out.at[k], sem).wait()


def select(ids, slots, down, up):
    shapes = [jax.ShapeDtypeStruct((2, *x.shape[1:]), x.dtype) for x in (down, down, up, up)]
    return pl.pallas_call(
        functools.partial(select_kernel, requests=ids.shape[0]),
        out_shape=shapes,
        in_specs=[spec(SMEM), spec(HBM), spec(HBM)],
        out_specs=[spec(VMEM)] * 4,
        scratch_shapes=[pltpu.SemaphoreType.DMA((8,))],
        compiler_params=WHOLE,
    )(jnp.concatenate([ids, slots]), down, up)


SIBLING = [(0, 1), (1, 0), (2, 3), (3, 2)]
ACROSS = [(0, 2), (1, 3), (2, 0), (3, 1)]
ONE = [(i, i ^ 1) for i in range(4)]
TWO = [(i, i ^ 2) for i in range(4)]
LAST = [(0, 0), (1, 1), (2, 3), (3, 2)]


def spread(shard):
    return lax.ppermute(shard, "ctx", ONE), lax.ppermute(shard, "ctx", TWO)


def low_rank_kernel(ids, ranks, hidden, *rest):
    pieces, out, accum = rest[:-2], rest[-2], rest[-1]
    rows = pieces[0].shape[0]
    rank = ranks[ids[lax.axis_index("req")]]
    accum[...] = jnp.zeros_like(accum)
    for flip, piece in enumerate(pieces):
        place = lax.axis_index("ctx") ^ flip
        columns = pl.ds(pl.multiple_of(place * rows, HD), rows)
        accum[...] += jnp.dot(hidden[:, columns], piece[...], preferred_element_type=jnp.float32)

    column = lax.broadcasted_iota(jnp.int32, accum.shape, 1)
    out[...] = jnp.where(column < rank, accum[...], 0.0).astype(jnp.bfloat16)


def low_rank(ids, ranks, hidden, pieces):
    shape = (hidden.shape[0], pieces[0].shape[1])
    return pl.pallas_call(
        low_rank_kernel,
        out_shape=jax.ShapeDtypeStruct(shape, jnp.bfloat16),
        in_specs=[spec(SMEM)] * 2 + [spec(VMEM)] * (1 + len(pieces)),
        out_specs=spec(VMEM),
        scratch_shapes=[VMEM(shape, jnp.float32)],
        compiler_params=PARAMS,
        cost_estimate=pl.CostEstimate(flops=1 << 27, bytes_accessed=1 << 22, transcendentals=0),
    )(ids, ranks, hidden, *pieces)


FACTOR = LOG2E / math.sqrt(HD)


def head_columns(kvs, h):
    keys = [kv[:, h * HD : (h + 1) * HD] for kv in kvs]
    values = [kv[:, (KVH + h) * HD : (KVH + h + 1) * HD] for kv in kvs]
    return jnp.concatenate(keys, axis=0), jnp.concatenate(values, axis=0)


def dot_keys(queries, keys):
    return lax.dot_general(
        queries, keys, (((1,), (1,)), ((), ())), preferred_element_type=jnp.float32
    )


def out_copies(result, out, sems):
    width = GROUP * HD
    return [
        pltpu.make_async_copy(result.at[h], out.at[:, pl.ds(h * width, width)], sems.at[h])
        for h in range(KVH)
    ]


def attend_kernel(lengths, base, low, *rest):
    kvs, ups = rest[:3], rest[3:7]
    out, queries, sums, highs, counts, upper, result, sems = rest[7:]
    tokens = base.shape[0]
    rows = ups[0].shape[0]
    z = lax.axis_index("ctx")
    live = z * tokens < lengths[0]
    block = GROUP * tokens
    copies = out_copies(result, out, sems)

    @pl.when(jnp.logical_not(live))
    def _():
        result[...] = jnp.zeros_like(result)
        for copy in copies:
            copy.start()

    @pl.when(live)
    def _():
        for flip, piece in enumerate(ups):
            upper[pl.ds(pl.multiple_of((z ^ flip) * rows, rows), rows), :] = piece[...]
        for j in range(HEADS):
            columns = slice(j * HD, (j + 1) * HD)
            delta = jnp.dot(low[...], upper[:, columns], preferred_element_type=jnp.float32)
            queries[j * tokens : (j + 1) * tokens, :] = (
                base[:, columns].astype(jnp.float32) + delta
            ).astype(jnp.bfloat16)

    query_pos = lax.broadcasted_iota(jnp.int32, (tokens, tokens), 0)
    key_pos = lax.broadcasted_iota(jnp.int32, (tokens, tokens), 1)
    causal = key_pos <= query_pos
    for mine, needed in enumerate(((0,), (0, 1), (0, 2), (0, 1, 2))):

        @pl.when(live & (z == mine))
        def _():
            for h in range(KVH):
                keys, values = head_columns([kvs[i] for i in needed], h)
                scores = dot_keys(queries[h * block : (h + 1) * block, :], keys)
                weights, tops, totals = [], [], []
                for g in range(GROUP):
                    score = scores[g * tokens : (g + 1) * tokens, :]
                    own = jnp.where(causal, score[:, :tokens], -1e30)
                    if mine:
                        own = jnp.concatenate([own, score[:, tokens:]], axis=1)
                    tops.append(jnp.max(own, axis=1, keepdims=True))
                    weight = jnp.exp2((own - tops[g]) * FACTOR)
                    totals.append(jnp.sum(weight, axis=1, keepdims=True))
                    weights.append(weight.astype(jnp.bfloat16))
                product = jnp.dot(
                    jnp.concatenate(weights, axis=0), values, preferred_element_type=jnp.float32
                )
                if mine < 2:
                    for g in range(GROUP):
                        result[h, :, g * HD : (g + 1) * HD] = (
                            product[g * tokens : (g + 1) * tokens, :] / totals[g]
                        ).astype(jnp.bfloat16)
                    copies[h].start()
                else:
                    sums[h * block : (h + 1) * block, :] = product
                    for g in range(GROUP):
                        at = slice(h * block + g * tokens, h * block + (g + 1) * tokens)
                        highs[at, :] = jnp.broadcast_to(tops[g], (tokens, HD))
                        counts[at, :] = jnp.broadcast_to(totals[g], (tokens, HD))

    @pl.when(jnp.logical_not(live) | (z < 2))
    def _():
        for copy in copies:
            copy.wait()


def attend(lengths, base, low, kvs, ups):
    tokens, width = base.shape
    rows = HEADS * tokens
    shapes = [
        jax.ShapeDtypeStruct(base.shape, jnp.bfloat16),
        jax.ShapeDtypeStruct((rows, HD), jnp.bfloat16),
    ] + [jax.ShapeDtypeStruct((rows, HD), jnp.float32)] * 3
    return pl.pallas_call(
        attend_kernel,
        out_shape=shapes,
        in_specs=[spec(SMEM)] + [spec(VMEM)] * (2 + len(kvs) + len(ups)),
        out_specs=[spec(HBM)] + [spec(VMEM)] * 4,
        scratch_shapes=[
            VMEM((low.shape[1], width), jnp.bfloat16),
            VMEM((KVH, tokens, GROUP * HD), jnp.bfloat16),
            pltpu.SemaphoreType.DMA((KVH,)),
        ],
        compiler_params=PARAMS,
        cost_estimate=pl.CostEstimate(
            flops=1 << 30, bytes_accessed=1 << 22, transcendentals=1 << 21
        ),
    )(lengths, base, low, *kvs, *ups)


def finish_kernel(lengths, so_far, queries, sums, highs, counts, kv, out, result, sems):
    del so_far
    tokens = result.shape[1]
    z = lax.axis_index("ctx")
    block = GROUP * tokens
    copies = out_copies(result, out, sems)

    @pl.when((z * tokens < lengths[0]) & (z >= 2))
    def _():
        for h in range(KVH):
            keys, values = head_columns([kv], h)
            scores = dot_keys(queries[h * block : (h + 1) * block, :], keys)
            weights, factors, totals = [], [], []
            for g in range(GROUP):
                at = slice(h * block + g * tokens, h * block + (g + 1) * tokens)
                score = scores[g * tokens : (g + 1) * tokens, :]
                newest = jnp.maximum(highs[at, :], jnp.max(score, axis=1, keepdims=True))
                weight = jnp.exp2((score - newest) * FACTOR)
                factors.append(jnp.exp2((highs[at, :] - newest) * FACTOR))
                added = jnp.sum(weight, axis=1, keepdims=True)
                totals.append(counts[at, :] * factors[g] + added)
                weights.append(weight.astype(jnp.bfloat16))
            product = jnp.dot(
                jnp.concatenate(weights, axis=0), values, preferred_element_type=jnp.float32
            )
            for g in range(GROUP):
                at = slice(h * block + g * tokens, h * block + (g + 1) * tokens)
                whole = sums[at, :] * factors[g] + product[g * tokens : (g + 1) * tokens, :]
                result[h, :, g * HD : (g + 1) * HD] = (whole / totals[g]).astype(jnp.bfloat16)
            copies[h].start()
        for copy in copies:
            copy.wait()


def finish(lengths, so_far, queries, sums, highs, counts, kv):
    tokens = so_far.shape[0]
    return pl.pallas_call(
        finish_kernel,
        out_shape=jax.ShapeDtypeStruct(so_far.shape, so_far.dtype),
        in_specs=[spec(SMEM), spec(HBM)] + [spec(VMEM)] * 5,
        out_specs=spec(HBM),
        input_output_aliases={1: 0},
        scratch_shapes=[
            VMEM((KVH, tokens, GROUP * HD), jnp.bfloat16),
            pltpu.SemaphoreType.DMA((KVH,)),
        ],
        compiler_params=PARAMS,
        cost_estimate=pl.CostEstimate(
            flops=1 << 28, bytes_accessed=1 << 21, transcendentals=1 << 19
        ),
    )(lengths, so_far, queries, sums, highs, counts, kv)


def body(
    hidden_states,
    queries_base,
    kv_base,
    adapter_down,
    adapter_up,
    adapter_ids,
    adapter_slots,
    rank_buckets,
    lengths,
):
    keep_down, give_down, keep_up, give_up = select(
        adapter_ids, adapter_slots, adapter_down, adapter_up
    )
    kv = kv_base[0]
    kv_two = lax.ppermute(kv, "ctx", TWO)
    near_down = lax.ppermute(give_down, "req", SIBLING)
    near_up = lax.ppermute(give_up, "req", SIBLING)
    pass_down = keep_down[1] + near_down[1]
    later = lax.optimization_barrier((kv, pass_down))[0]
    kv_one = lax.ppermute(later, "ctx", ONE)
    far_down = lax.ppermute(pass_down, "req", ACROSS)
    far_up = lax.ppermute(keep_up[1] + near_up[1], "req", ACROSS)
    down = keep_down[0] + near_down[0] + far_down
    down_one, down_two = spread(down)
    up = keep_up[0] + near_up[0] + far_up
    up = lax.optimization_barrier((up, kv_one))[0]
    up_one, up_two = spread(up)
    ready = lax.optimization_barrier((down_two, kv_two))[0]
    down_three = lax.ppermute(ready, "ctx", ONE)
    ready = lax.optimization_barrier((up_two, down_one))[0]
    up_three = lax.ppermute(ready, "ctx", ONE)
    kv_last = lax.optimization_barrier((kv_two, up_two, up_one))[0]
    kv_three = lax.ppermute(kv_last, "ctx", LAST)
    downs = [down, down_one, down_two, down_three]
    ups = [up, up_one, up_two, up_three]
    low = low_rank(adapter_ids, rank_buckets, hidden_states[0], downs)
    parts = attend(lengths, queries_base[0], low, [kv, kv_one, kv_two], ups)
    return finish(lengths, *parts, kv_three)[None]


def plain_body(
    hidden_states,
    queries_base,
    kv_base,
    adapter_down,
    adapter_up,
    adapter_ids,
    adapter_slots,
    rank_buckets,
    lengths,
):
    req_index = lax.axis_index("req")
    ctx_index = lax.axis_index("ctx")
    per_shard = adapter_down.shape[0]
    requests = adapter_ids.shape[0]
    store = adapter_slots.shape[0]
    rank_width = adapter_down.shape[2]
    tokens = hidden_states.shape[1]
    query_width = queries_base.shape[2]
    store_range = jnp.arange(store, dtype=jnp.int32)
    chosen = adapter_ids[:, None] == store_range[None, :]
    slot_of = jnp.sum(jnp.where(chosen, adapter_slots[None, :], 0), axis=1)
    rank_of = jnp.sum(jnp.where(chosen, rank_buckets[None, :], 0), axis=1)
    mine = jnp.arange(requests, dtype=jnp.int32) == req_index
    my_slot = jnp.sum(jnp.where(mine, slot_of, 0))
    my_rank = jnp.sum(jnp.where(mine, rank_of, 0))
    held = (
        slot_of[:, None] == req_index * per_shard + jnp.arange(per_shard, dtype=jnp.int32)[None, :]
    )
    select = held.astype(jnp.bfloat16)
    send_down = jnp.einsum(
        "qa,ard->qrd", select, adapter_down, preferred_element_type=jnp.float32
    ).astype(jnp.bfloat16)
    send_up = jnp.einsum(
        "qa,ard->qrd", select, adapter_up, preferred_element_type=jnp.float32
    ).astype(jnp.bfloat16)
    got_down, got_up = (
        lax.all_to_all(send_down, "req", split_axis=0, concat_axis=0, tiled=True),
        lax.all_to_all(send_up, "req", split_axis=0, concat_axis=0, tiled=True),
    )
    owner = my_slot // per_shard
    down_mine = lax.dynamic_index_in_dim(got_down, owner, 0, keepdims=False)
    up_mine = lax.dynamic_index_in_dim(got_up, owner, 0, keepdims=False)
    features = hidden_states[0]
    columns = features
    low_rank = jnp.dot(
        columns,
        lax.all_gather(down_mine, "ctx", axis=0, tiled=True),
        preferred_element_type=jnp.float32,
    )
    low_rank = jnp.where(
        jnp.arange(rank_width, dtype=jnp.int32)[None, :] < my_rank, low_rank, 0.0
    ).astype(jnp.bfloat16)
    columns = low_rank
    delta = jnp.dot(
        columns,
        lax.all_gather(up_mine, "ctx", axis=0, tiled=True),
        preferred_element_type=jnp.float32,
    )
    queries = (
        (queries_base[0].astype(jnp.float32) + delta)
        .astype(jnp.bfloat16)
        .reshape(tokens, KVH, GROUP, HD)
    )
    length = lengths[0]
    first_query = ctx_index * tokens
    query_pos = first_query + jnp.arange(tokens, dtype=jnp.int32)
    last_needed = jnp.minimum(first_query + tokens - 1, length - 1)
    scale = 1.0 / math.sqrt(HD)
    key_width = KVH * HD
    initial = (
        jnp.full((KVH, GROUP, tokens), -1e30, jnp.float32),
        jnp.zeros((KVH, GROUP, tokens), jnp.float32),
        jnp.zeros((KVH, GROUP, tokens, HD), jnp.float32),
    )
    piece = lax.all_gather(kv_base[0], "ctx", axis=0, tiled=True)
    count = piece.shape[0]
    width = math.gcd(count, 512)

    def key_block(index, state):
        largest, total, accum = state
        offset = index * width
        rows = lax.dynamic_slice_in_dim(piece, offset, width, 0)
        keys = rows[:, :key_width].reshape(width, KVH, HD)
        values = rows[:, key_width:].reshape(width, KVH, HD)
        key_pos = offset + jnp.arange(width, dtype=jnp.int32)
        score = (
            jnp.einsum("tkgd,skd->kgts", queries, keys, preferred_element_type=jnp.float32) * scale
        )
        allowed = (key_pos[None, :] <= query_pos[:, None]) & (key_pos[None, :] < length)
        masked = jnp.where(allowed, score, -1e30)
        newest = jnp.maximum(largest, jnp.max(masked, axis=-1))
        weight = jnp.where(allowed, jnp.exp(score - newest[..., None]), 0.0)
        factor = jnp.exp(largest - newest)
        total = total * factor + jnp.sum(weight, axis=-1)
        product = jnp.einsum(
            "kgts,skd->kgtd",
            weight.astype(jnp.bfloat16),
            values,
            preferred_element_type=jnp.float32,
        )
        accum = accum * factor[..., None] + product
        return (newest, total, accum)

    def compute(state):
        return lax.fori_loop(0, count // width, key_block, state)

    needed = (jnp.int32(0) <= last_needed) & (first_query < length)
    largest, total, accum = lax.cond(needed, compute, lambda state: state, initial)
    safe_total = jnp.where(total > 0.0, total, 1.0)
    output = accum / safe_total[..., None]
    output = jnp.transpose(output, (2, 0, 1, 3)).reshape(tokens, query_width)
    output = jnp.where(query_pos[:, None] < length, output, 0.0).astype(jnp.bfloat16)
    return output[None]


def solution(mesh):
    paired = mesh.shape["ctx"] == 4 and mesh.shape["req"] == 4
    return jax.shard_map(
        body if paired else plain_body,
        mesh=mesh,
        in_specs=(
            P(("group", "req"), "ctx", None),
            P(("group", "req"), "ctx", None),
            P(("group", "req"), "ctx", None),
            P(("group", "req"), "ctx", None),
            P(("group", "req"), "ctx", None),
            P("group"),
            P("group"),
            P("group"),
            P(("group", "req")),
        ),
        out_specs=P(("group", "req"), "ctx", None),
        check_vma=False,
    )
```

```python
import functools
import math

import jax
import jax.numpy as jnp
from jax import lax
from jax.experimental import pallas as pl
from jax.experimental.pallas import tpu as pltpu
from jax.sharding import PartitionSpec as P

HD = 128
KVH = 3
GROUP = 7
HEADS = KVH * GROUP
SMEM = pltpu.SMEM
VMEM = pltpu.VMEM
HBM = pltpu.HBM
LOG2E = 1.0 / math.log(2.0)
PARAMS = pltpu.CompilerParams(vmem_limit_bytes=32 * 1024 * 1024)
WHOLE = pltpu.CompilerParams(vmem_limit_bytes=52 * 1024 * 1024)


def spec(space):
    return pl.BlockSpec(memory_space=space)


def select_kernel(table, *rest, requests):
    stores, outs, sems = rest[:2], rest[2:6], rest[6]
    per_shard = stores[0].shape[0]
    me = lax.axis_index("req")
    first = me * per_shard
    copies = []
    for i, flip in enumerate((0, 2, 1, 3)):
        local = table[requests + table[me ^ flip]] - first
        held = (local >= 0) & (local < per_shard)
        for f, store in enumerate(stores):
            out = outs[2 * f + i // 2]
            copies.append((held, local, store, out, i % 2, sems.at[4 * f + i]))
    for held, local, store, out, k, sem in copies:

        @pl.when(held)
        def _():
            pltpu.make_async_copy(store.at[local], out.at[k], sem).start()

    for held, local, store, out, k, sem in copies:

        @pl.when(jnp.logical_not(held))
        def _():
            out[k] = jnp.zeros(out.shape[1:], out.dtype)

    for held, local, store, out, k, sem in copies:

        @pl.when(held)
        def _():
            pltpu.make_async_copy(store.at[local], out.at[k], sem).wait()


def select(ids, slots, down, up):
    shapes = [jax.ShapeDtypeStruct((2, *x.shape[1:]), x.dtype) for x in (down, down, up, up)]
    return pl.pallas_call(
        functools.partial(select_kernel, requests=ids.shape[0]),
        out_shape=shapes,
        in_specs=[spec(SMEM), spec(HBM), spec(HBM)],
        out_specs=[spec(VMEM)] * 4,
        scratch_shapes=[pltpu.SemaphoreType.DMA((8,))],
        compiler_params=WHOLE,
    )(jnp.concatenate([ids, slots]), down, up)


SIBLING = [(0, 1), (1, 0), (2, 3), (3, 2)]
ACROSS = [(0, 2), (1, 3), (2, 0), (3, 1)]
ONE = [(i, i ^ 1) for i in range(4)]
TWO = [(i, i ^ 2) for i in range(4)]
LAST = [(0, 0), (1, 1), (2, 3), (3, 2)]


def spread(shard):
    return lax.ppermute(shard, "ctx", ONE), lax.ppermute(shard, "ctx", TWO)


def low_rank_kernel(ids, ranks, hidden, *rest):
    pieces, out, accum = rest[:-2], rest[-2], rest[-1]
    rows = pieces[0].shape[0]
    rank = ranks[ids[lax.axis_index("req")]]
    accum[...] = jnp.zeros_like(accum)
    for flip, piece in enumerate(pieces):
        place = lax.axis_index("ctx") ^ flip
        columns = pl.ds(pl.multiple_of(place * rows, HD), rows)
        accum[...] += jnp.dot(hidden[:, columns], piece[...], preferred_element_type=jnp.float32)

    column = lax.broadcasted_iota(jnp.int32, accum.shape, 1)
    out[...] = jnp.where(column < rank, accum[...], 0.0).astype(jnp.bfloat16)


def low_rank(ids, ranks, hidden, pieces):
    shape = (hidden.shape[0], pieces[0].shape[1])
    return pl.pallas_call(
        low_rank_kernel,
        out_shape=jax.ShapeDtypeStruct(shape, jnp.bfloat16),
        in_specs=[spec(SMEM)] * 2 + [spec(VMEM)] * (1 + len(pieces)),
        out_specs=spec(VMEM),
        scratch_shapes=[VMEM(shape, jnp.float32)],
        compiler_params=PARAMS,
        cost_estimate=pl.CostEstimate(flops=1 << 27, bytes_accessed=1 << 22, transcendentals=0),
    )(ids, ranks, hidden, *pieces)


FACTOR = LOG2E / math.sqrt(HD)


def head_columns(kvs, h):
    keys = [kv[:, h * HD : (h + 1) * HD] for kv in kvs]
    values = [kv[:, (KVH + h) * HD : (KVH + h + 1) * HD] for kv in kvs]
    return jnp.concatenate(keys, axis=0), jnp.concatenate(values, axis=0)


def dot_keys(queries, keys):
    return lax.dot_general(
        queries, keys, (((1,), (1,)), ((), ())), preferred_element_type=jnp.float32
    )


def out_copies(result, out, sems):
    width = GROUP * HD
    return [
        pltpu.make_async_copy(result.at[h], out.at[:, pl.ds(h * width, width)], sems.at[h])
        for h in range(KVH)
    ]


def attend_kernel(lengths, base, low, *rest):
    kvs, ups = rest[:3], rest[3:7]
    out, queries, sums, highs, counts, upper, result, sems = rest[7:]
    tokens = base.shape[0]
    rows = ups[0].shape[0]
    z = lax.axis_index("ctx")
    live = z * tokens < lengths[0]
    block = GROUP * tokens
    copies = out_copies(result, out, sems)

    @pl.when(jnp.logical_not(live))
    def _():
        result[...] = jnp.zeros_like(result)
        for copy in copies:
            copy.start()

    @pl.when(live)
    def _():
        for flip, piece in enumerate(ups):
            upper[pl.ds(pl.multiple_of((z ^ flip) * rows, rows), rows), :] = piece[...]

    query_pos = lax.broadcasted_iota(jnp.int32, (tokens, tokens), 0)
    key_pos = lax.broadcasted_iota(jnp.int32, (tokens, tokens), 1)
    causal = key_pos <= query_pos

    def scores_of(h, blocks):
        columns = slice(h * GROUP * HD, (h + 1) * GROUP * HD)
        delta = jnp.dot(low[...], upper[:, columns], preferred_element_type=jnp.float32)
        query = (base[:, columns].astype(jnp.float32) + delta).astype(jnp.bfloat16)
        query = [query[:, g * HD : (g + 1) * HD] for g in range(GROUP)]
        query = jnp.concatenate(query, axis=0)
        keys, values = head_columns(blocks, h)
        return query, dot_keys(query, keys), values

    for mine, needed in enumerate(((0,), (0, 1), (0, 2), (0, 1, 2))):

        @pl.when(live & (z == mine))
        def _():
            blocks = [kvs[i] for i in needed]
            ahead = scores_of(0, blocks)
            for h in range(KVH):
                query, scores, values = ahead
                if h + 1 < KVH:
                    ahead = scores_of(h + 1, blocks)
                weights, tops, totals = [], [], []
                for g in range(GROUP):
                    score = scores[g * tokens : (g + 1) * tokens, :]
                    own = jnp.where(causal, score[:, :tokens], -1e30)
                    if mine:
                        own = jnp.concatenate([own, score[:, tokens:]], axis=1)
                    tops.append(jnp.max(own, axis=1, keepdims=True))
                    weight = jnp.exp2((own - tops[g]) * FACTOR)
                    totals.append(jnp.sum(weight, axis=1, keepdims=True))
                    weights.append(weight.astype(jnp.bfloat16))
                product = jnp.dot(
                    jnp.concatenate(weights, axis=0), values, preferred_element_type=jnp.float32
                )
                if mine < 2:
                    for g in range(GROUP):
                        result[h, :, g * HD : (g + 1) * HD] = (
                            product[g * tokens : (g + 1) * tokens, :] / totals[g]
                        ).astype(jnp.bfloat16)
                    copies[h].start()
                else:
                    queries[h * block : (h + 1) * block, :] = query
                    sums[h * block : (h + 1) * block, :] = product
                    for g in range(GROUP):
                        at = slice(h * block + g * tokens, h * block + (g + 1) * tokens)
                        highs[at, :] = jnp.broadcast_to(tops[g], (tokens, HD))
                        counts[at, :] = jnp.broadcast_to(totals[g], (tokens, HD))

    @pl.when(jnp.logical_not(live) | (z < 2))
    def _():
        for copy in copies:
            copy.wait()


def attend(lengths, base, low, kvs, ups):
    tokens, width = base.shape
    rows = HEADS * tokens
    shapes = [
        jax.ShapeDtypeStruct(base.shape, jnp.bfloat16),
        jax.ShapeDtypeStruct((rows, HD), jnp.bfloat16),
    ] + [jax.ShapeDtypeStruct((rows, HD), jnp.float32)] * 3
    return pl.pallas_call(
        attend_kernel,
        out_shape=shapes,
        in_specs=[spec(SMEM)] + [spec(VMEM)] * (2 + len(kvs) + len(ups)),
        out_specs=[spec(HBM)] + [spec(VMEM)] * 4,
        scratch_shapes=[
            VMEM((low.shape[1], width), jnp.bfloat16),
            VMEM((KVH, tokens, GROUP * HD), jnp.bfloat16),
            pltpu.SemaphoreType.DMA((KVH,)),
        ],
        compiler_params=PARAMS,
        cost_estimate=pl.CostEstimate(
            flops=1 << 30, bytes_accessed=1 << 22, transcendentals=1 << 21
        ),
    )(lengths, base, low, *kvs, *ups)


def finish_kernel(lengths, so_far, queries, sums, highs, counts, kv, out, result, sems):
    del so_far
    tokens = result.shape[1]
    z = lax.axis_index("ctx")
    block = GROUP * tokens
    copies = out_copies(result, out, sems)

    @pl.when((z * tokens < lengths[0]) & (z >= 2))
    def _():
        heads = [head_columns([kv], h) for h in range(KVH)]
        all_scores = [
            dot_keys(queries[h * block : (h + 1) * block, :], heads[h][0]) for h in range(KVH)
        ]
        for h in range(KVH):
            scores, values = all_scores[h], heads[h][1]
            weights, factors, totals = [], [], []
            for g in range(GROUP):
                at = slice(h * block + g * tokens, h * block + (g + 1) * tokens)
                score = scores[g * tokens : (g + 1) * tokens, :]
                newest = jnp.maximum(highs[at, :], jnp.max(score, axis=1, keepdims=True))
                weight = jnp.exp2((score - newest) * FACTOR)
                factors.append(jnp.exp2((highs[at, :] - newest) * FACTOR))
                added = jnp.sum(weight, axis=1, keepdims=True)
                totals.append(counts[at, :] * factors[g] + added)
                weights.append(weight.astype(jnp.bfloat16))
            product = jnp.dot(
                jnp.concatenate(weights, axis=0), values, preferred_element_type=jnp.float32
            )
            for g in range(GROUP):
                at = slice(h * block + g * tokens, h * block + (g + 1) * tokens)
                whole = sums[at, :] * factors[g] + product[g * tokens : (g + 1) * tokens, :]
                result[h, :, g * HD : (g + 1) * HD] = (whole / totals[g]).astype(jnp.bfloat16)
            copies[h].start()
        for copy in copies:
            copy.wait()


def finish(lengths, so_far, queries, sums, highs, counts, kv):
    tokens = so_far.shape[0]
    return pl.pallas_call(
        finish_kernel,
        out_shape=jax.ShapeDtypeStruct(so_far.shape, so_far.dtype),
        in_specs=[spec(SMEM), spec(HBM)] + [spec(VMEM)] * 5,
        out_specs=spec(HBM),
        input_output_aliases={1: 0},
        scratch_shapes=[
            VMEM((KVH, tokens, GROUP * HD), jnp.bfloat16),
            pltpu.SemaphoreType.DMA((KVH,)),
        ],
        compiler_params=PARAMS,
        cost_estimate=pl.CostEstimate(
            flops=1 << 28, bytes_accessed=1 << 21, transcendentals=1 << 19
        ),
    )(lengths, so_far, queries, sums, highs, counts, kv)


def body(
    hidden_states,
    queries_base,
    kv_base,
    adapter_down,
    adapter_up,
    adapter_ids,
    adapter_slots,
    rank_buckets,
    lengths,
):
    keep_down, give_down, keep_up, give_up = select(
        adapter_ids, adapter_slots, adapter_down, adapter_up
    )
    kv = kv_base[0]
    kv_one, kv_two = spread(kv)
    near_down = lax.ppermute(give_down, "req", SIBLING)
    near_up = lax.ppermute(give_up, "req", SIBLING)
    far_down = lax.ppermute(keep_down[1] + near_down[1], "req", ACROSS)
    far_up = lax.ppermute(keep_up[1] + near_up[1], "req", ACROSS)
    down = keep_down[0] + near_down[0] + far_down
    down, kv_one = lax.optimization_barrier((down, kv_one))
    down_one, down_two = spread(down)
    up = keep_up[0] + near_up[0] + far_up
    up_one, up_two = spread(up)
    down_two = lax.optimization_barrier((down_two, kv_two))[0]
    down_three = lax.ppermute(down_two, "ctx", ONE)
    up_two = lax.optimization_barrier((up_two, down_one))[0]
    up_three = lax.ppermute(up_two, "ctx", ONE)
    kv_last = lax.optimization_barrier((kv_two, up_two, up_one))[0]
    kv_three = lax.ppermute(kv_last, "ctx", LAST)
    downs = [down, down_one, down_two, down_three]
    ups = [up, up_one, up_two, up_three]
    low = low_rank(adapter_ids, rank_buckets, hidden_states[0], downs)
    parts = attend(lengths, queries_base[0], low, [kv, kv_one, kv_two], ups)
    return finish(lengths, *parts, kv_three)[None]


def plain_body(
    hidden_states,
    queries_base,
    kv_base,
    adapter_down,
    adapter_up,
    adapter_ids,
    adapter_slots,
    rank_buckets,
    lengths,
):
    req_index = lax.axis_index("req")
    ctx_index = lax.axis_index("ctx")
    per_shard = adapter_down.shape[0]
    requests = adapter_ids.shape[0]
    store = adapter_slots.shape[0]
    rank_width = adapter_down.shape[2]
    tokens = hidden_states.shape[1]
    query_width = queries_base.shape[2]
    store_range = jnp.arange(store, dtype=jnp.int32)
    chosen = adapter_ids[:, None] == store_range[None, :]
    slot_of = jnp.sum(jnp.where(chosen, adapter_slots[None, :], 0), axis=1)
    rank_of = jnp.sum(jnp.where(chosen, rank_buckets[None, :], 0), axis=1)
    mine = jnp.arange(requests, dtype=jnp.int32) == req_index
    my_slot = jnp.sum(jnp.where(mine, slot_of, 0))
    my_rank = jnp.sum(jnp.where(mine, rank_of, 0))
    held = (
        slot_of[:, None] == req_index * per_shard + jnp.arange(per_shard, dtype=jnp.int32)[None, :]
    )
    select = held.astype(jnp.bfloat16)
    send_down = jnp.einsum(
        "qa,ard->qrd", select, adapter_down, preferred_element_type=jnp.float32
    ).astype(jnp.bfloat16)
    send_up = jnp.einsum(
        "qa,ard->qrd", select, adapter_up, preferred_element_type=jnp.float32
    ).astype(jnp.bfloat16)
    got_down, got_up = (
        lax.all_to_all(send_down, "req", split_axis=0, concat_axis=0, tiled=True),
        lax.all_to_all(send_up, "req", split_axis=0, concat_axis=0, tiled=True),
    )
    owner = my_slot // per_shard
    down_mine = lax.dynamic_index_in_dim(got_down, owner, 0, keepdims=False)
    up_mine = lax.dynamic_index_in_dim(got_up, owner, 0, keepdims=False)
    features = hidden_states[0]
    columns = features
    low_rank = jnp.dot(
        columns,
        lax.all_gather(down_mine, "ctx", axis=0, tiled=True),
        preferred_element_type=jnp.float32,
    )
    low_rank = jnp.where(
        jnp.arange(rank_width, dtype=jnp.int32)[None, :] < my_rank, low_rank, 0.0
    ).astype(jnp.bfloat16)
    columns = low_rank
    delta = jnp.dot(
        columns,
        lax.all_gather(up_mine, "ctx", axis=0, tiled=True),
        preferred_element_type=jnp.float32,
    )
    queries = (
        (queries_base[0].astype(jnp.float32) + delta)
        .astype(jnp.bfloat16)
        .reshape(tokens, KVH, GROUP, HD)
    )
    length = lengths[0]
    first_query = ctx_index * tokens
    query_pos = first_query + jnp.arange(tokens, dtype=jnp.int32)
    last_needed = jnp.minimum(first_query + tokens - 1, length - 1)
    scale = 1.0 / math.sqrt(HD)
    key_width = KVH * HD
    initial = (
        jnp.full((KVH, GROUP, tokens), -1e30, jnp.float32),
        jnp.zeros((KVH, GROUP, tokens), jnp.float32),
        jnp.zeros((KVH, GROUP, tokens, HD), jnp.float32),
    )
    piece = lax.all_gather(kv_base[0], "ctx", axis=0, tiled=True)
    count = piece.shape[0]
    width = math.gcd(count, 512)

    def key_block(index, state):
        largest, total, accum = state
        offset = index * width
        rows = lax.dynamic_slice_in_dim(piece, offset, width, 0)
        keys = rows[:, :key_width].reshape(width, KVH, HD)
        values = rows[:, key_width:].reshape(width, KVH, HD)
        key_pos = offset + jnp.arange(width, dtype=jnp.int32)
        score = (
            jnp.einsum("tkgd,skd->kgts", queries, keys, preferred_element_type=jnp.float32) * scale
        )
        allowed = (key_pos[None, :] <= query_pos[:, None]) & (key_pos[None, :] < length)
        masked = jnp.where(allowed, score, -1e30)
        newest = jnp.maximum(largest, jnp.max(masked, axis=-1))
        weight = jnp.where(allowed, jnp.exp(score - newest[..., None]), 0.0)
        factor = jnp.exp(largest - newest)
        total = total * factor + jnp.sum(weight, axis=-1)
        product = jnp.einsum(
            "kgts,skd->kgtd",
            weight.astype(jnp.bfloat16),
            values,
            preferred_element_type=jnp.float32,
        )
        accum = accum * factor[..., None] + product
        return (newest, total, accum)

    def compute(state):
        return lax.fori_loop(0, count // width, key_block, state)

    needed = (jnp.int32(0) <= last_needed) & (first_query < length)
    largest, total, accum = lax.cond(needed, compute, lambda state: state, initial)
    safe_total = jnp.where(total > 0.0, total, 1.0)
    output = accum / safe_total[..., None]
    output = jnp.transpose(output, (2, 0, 1, 3)).reshape(tokens, query_width)
    output = jnp.where(query_pos[:, None] < length, output, 0.0).astype(jnp.bfloat16)
    return output[None]


def solution(mesh):
    paired = mesh.shape["ctx"] == 4 and mesh.shape["req"] == 4
    return jax.shard_map(
        body if paired else plain_body,
        mesh=mesh,
        in_specs=(
            P(("group", "req"), "ctx", None),
            P(("group", "req"), "ctx", None),
            P(("group", "req"), "ctx", None),
            P(("group", "req"), "ctx", None),
            P(("group", "req"), "ctx", None),
            P("group"),
            P("group"),
            P("group"),
            P(("group", "req")),
        ),
        out_specs=P(("group", "req"), "ctx", None),
        check_vma=False,
    )
```

```python
import functools
import math

import jax
import jax.numpy as jnp
from jax import lax
from jax.experimental import pallas as pl
from jax.experimental.pallas import tpu as pltpu
from jax.sharding import PartitionSpec as P

HD = 128
KVH = 3
GROUP = 7
HEADS = KVH * GROUP
SMEM = pltpu.SMEM
VMEM = pltpu.VMEM
HBM = pltpu.HBM
LOG2E = 1.0 / math.log(2.0)
PARAMS = pltpu.CompilerParams(vmem_limit_bytes=32 * 1024 * 1024)
WHOLE = pltpu.CompilerParams(vmem_limit_bytes=52 * 1024 * 1024)


def spec(space):
    return pl.BlockSpec(memory_space=space)


def select_kernel(table, *rest, requests):
    stores, outs, sems = rest[:2], rest[2:6], rest[6]
    per_shard = stores[0].shape[0]
    me = lax.axis_index("req")
    first = me * per_shard
    copies = []
    for i, flip in enumerate((0, 2, 1, 3)):
        local = table[requests + table[me ^ flip]] - first
        held = (local >= 0) & (local < per_shard)
        for f, store in enumerate(stores):
            out = outs[2 * f + i // 2]
            copies.append((held, local, store, out, i % 2, sems.at[4 * f + i]))
    for held, local, store, out, k, sem in copies:

        @pl.when(held)
        def _():
            pltpu.make_async_copy(store.at[local], out.at[k], sem).start()

    for held, local, store, out, k, sem in copies:

        @pl.when(jnp.logical_not(held))
        def _():
            out[k] = jnp.zeros(out.shape[1:], out.dtype)

    for held, local, store, out, k, sem in copies:

        @pl.when(held)
        def _():
            pltpu.make_async_copy(store.at[local], out.at[k], sem).wait()


def select(ids, slots, down, up):
    shapes = [jax.ShapeDtypeStruct((2, *x.shape[1:]), x.dtype) for x in (down, down, up, up)]
    return pl.pallas_call(
        functools.partial(select_kernel, requests=ids.shape[0]),
        out_shape=shapes,
        in_specs=[spec(SMEM), spec(HBM), spec(HBM)],
        out_specs=[spec(VMEM)] * 4,
        scratch_shapes=[pltpu.SemaphoreType.DMA((8,))],
        compiler_params=WHOLE,
    )(jnp.concatenate([ids, slots]), down, up)


SIBLING = [(0, 1), (1, 0), (2, 3), (3, 2)]
ACROSS = [(0, 2), (1, 3), (2, 0), (3, 1)]
ONE = [(i, i ^ 1) for i in range(4)]
TWO = [(i, i ^ 2) for i in range(4)]
LAST = [(0, 0), (1, 1), (2, 3), (3, 2)]


def spread(shard):
    return lax.ppermute(shard, "ctx", ONE), lax.ppermute(shard, "ctx", TWO)


def low_rank_kernel(ids, ranks, hidden, *rest):
    pieces, out, accum = rest[:-2], rest[-2], rest[-1]
    rows = pieces[0].shape[0]
    rank = ranks[ids[lax.axis_index("req")]]
    accum[...] = jnp.zeros_like(accum)
    for flip, piece in enumerate(pieces):
        place = lax.axis_index("ctx") ^ flip
        columns = pl.ds(pl.multiple_of(place * rows, HD), rows)
        accum[...] += jnp.dot(hidden[:, columns], piece[...], preferred_element_type=jnp.float32)

    column = lax.broadcasted_iota(jnp.int32, accum.shape, 1)
    out[...] = jnp.where(column < rank, accum[...], 0.0).astype(jnp.bfloat16)


def low_rank(ids, ranks, hidden, pieces):
    shape = (hidden.shape[0], pieces[0].shape[1])
    return pl.pallas_call(
        low_rank_kernel,
        out_shape=jax.ShapeDtypeStruct(shape, jnp.bfloat16),
        in_specs=[spec(SMEM)] * 2 + [spec(VMEM)] * (1 + len(pieces)),
        out_specs=spec(VMEM),
        scratch_shapes=[VMEM(shape, jnp.float32)],
        compiler_params=PARAMS,
        cost_estimate=pl.CostEstimate(flops=1 << 27, bytes_accessed=1 << 22, transcendentals=0),
    )(ids, ranks, hidden, *pieces)


FACTOR = LOG2E / math.sqrt(HD)


def head_columns(kvs, h):
    keys = [kv[:, h * HD : (h + 1) * HD] for kv in kvs]
    values = [kv[:, (KVH + h) * HD : (KVH + h + 1) * HD] for kv in kvs]
    return jnp.concatenate(keys, axis=0), jnp.concatenate(values, axis=0)


def dot_keys(queries, keys):
    return lax.dot_general(
        queries, keys, (((1,), (1,)), ((), ())), preferred_element_type=jnp.float32
    )


def out_copies(result, out, sems):
    width = GROUP * HD
    return [
        pltpu.make_async_copy(result.at[h], out.at[:, pl.ds(h * width, width)], sems.at[h])
        for h in range(KVH)
    ]


def attend_kernel(lengths, base, low, *rest):
    kvs, ups = rest[:3], rest[3:7]
    out, queries, sums, highs, counts, upper, result, sems = rest[7:]
    tokens = base.shape[0]
    rows = ups[0].shape[0]
    z = lax.axis_index("ctx")
    live = z * tokens < lengths[0]
    block = GROUP * tokens
    copies = out_copies(result, out, sems)

    @pl.when(jnp.logical_not(live))
    def _():
        result[...] = jnp.zeros_like(result)
        for copy in copies:
            copy.start()

    @pl.when(live)
    def _():
        for flip, piece in enumerate(ups):
            upper[pl.ds(pl.multiple_of((z ^ flip) * rows, rows), rows), :] = piece[...]

    query_pos = lax.broadcasted_iota(jnp.int32, (tokens, tokens), 0)
    key_pos = lax.broadcasted_iota(jnp.int32, (tokens, tokens), 1)
    causal = key_pos <= query_pos

    def scores_of(h, blocks):
        columns = slice(h * GROUP * HD, (h + 1) * GROUP * HD)
        delta = jnp.dot(low[...], upper[:, columns], preferred_element_type=jnp.float32)
        query = (base[:, columns].astype(jnp.float32) + delta).astype(jnp.bfloat16)
        query = [query[:, g * HD : (g + 1) * HD] for g in range(GROUP)]
        query = jnp.concatenate(query, axis=0)
        keys, values = head_columns(blocks, h)
        return query, dot_keys(query, keys), values

    for mine, needed in enumerate(((0,), (0, 1), (0, 2), (0, 1, 2))):

        @pl.when(live & (z == mine))
        def _():
            blocks = [kvs[i] for i in needed]
            ahead = scores_of(0, blocks)
            for h in range(KVH):
                query, scores, values = ahead
                if h + 1 < KVH:
                    ahead = scores_of(h + 1, blocks)
                weights, tops, totals = [], [], []
                for g in range(GROUP):
                    score = scores[g * tokens : (g + 1) * tokens, :]
                    own = jnp.where(causal, score[:, :tokens], -1e30)
                    if mine:
                        own = jnp.concatenate([own, score[:, tokens:]], axis=1)
                    tops.append(jnp.max(own, axis=1, keepdims=True))
                    weight = jnp.exp2((own - tops[g]) * FACTOR)
                    totals.append(jnp.sum(weight, axis=1, keepdims=True))
                    weights.append(weight.astype(jnp.bfloat16))
                product = jnp.dot(
                    jnp.concatenate(weights, axis=0), values, preferred_element_type=jnp.float32
                )
                if mine < 2:
                    for g in range(GROUP):
                        result[h, :, g * HD : (g + 1) * HD] = (
                            product[g * tokens : (g + 1) * tokens, :] / totals[g]
                        ).astype(jnp.bfloat16)
                    copies[h].start()
                else:
                    queries[h * block : (h + 1) * block, :] = query
                    sums[h * block : (h + 1) * block, :] = product
                    for g in range(GROUP):
                        at = slice(h * block + g * tokens, h * block + (g + 1) * tokens)
                        highs[at, :] = jnp.broadcast_to(tops[g], (tokens, HD))
                        counts[at, :] = jnp.broadcast_to(totals[g], (tokens, HD))

    @pl.when(jnp.logical_not(live) | (z < 2))
    def _():
        for copy in copies:
            copy.wait()


def attend(lengths, base, low, kvs, ups):
    tokens, width = base.shape
    rows = HEADS * tokens
    shapes = [
        jax.ShapeDtypeStruct(base.shape, jnp.bfloat16),
        jax.ShapeDtypeStruct((rows, HD), jnp.bfloat16),
    ] + [jax.ShapeDtypeStruct((rows, HD), jnp.float32)] * 3
    return pl.pallas_call(
        attend_kernel,
        out_shape=shapes,
        in_specs=[spec(SMEM)] + [spec(VMEM)] * (2 + len(kvs) + len(ups)),
        out_specs=[spec(HBM)] + [spec(VMEM)] * 4,
        scratch_shapes=[
            VMEM((low.shape[1], width), jnp.bfloat16),
            VMEM((KVH, tokens, GROUP * HD), jnp.bfloat16),
            pltpu.SemaphoreType.DMA((KVH,)),
        ],
        compiler_params=PARAMS,
        cost_estimate=pl.CostEstimate(
            flops=1 << 30, bytes_accessed=1 << 22, transcendentals=1 << 21
        ),
    )(lengths, base, low, *kvs, *ups)


def finish_kernel(lengths, so_far, queries, sums, highs, counts, kv, out, result, sems):
    del so_far
    tokens = result.shape[1]
    z = lax.axis_index("ctx")
    block = GROUP * tokens
    copies = out_copies(result, out, sems)

    @pl.when((z * tokens < lengths[0]) & (z >= 2))
    def _():
        for h in range(KVH):
            keys, values = head_columns([kv], h)
            scores = dot_keys(queries[h * block : (h + 1) * block, :], keys)
            weights, factors, totals = [], [], []
            for g in range(GROUP):
                at = slice(h * block + g * tokens, h * block + (g + 1) * tokens)
                score = scores[g * tokens : (g + 1) * tokens, :]
                newest = jnp.maximum(highs[at, :], jnp.max(score, axis=1, keepdims=True))
                weight = jnp.exp2((score - newest) * FACTOR)
                factors.append(jnp.exp2((highs[at, :] - newest) * FACTOR))
                added = jnp.sum(weight, axis=1, keepdims=True)
                totals.append(counts[at, :] * factors[g] + added)
                weights.append(weight.astype(jnp.bfloat16))
            product = jnp.dot(
                jnp.concatenate(weights, axis=0), values, preferred_element_type=jnp.float32
            )
            for g in range(GROUP):
                at = slice(h * block + g * tokens, h * block + (g + 1) * tokens)
                whole = sums[at, :] * factors[g] + product[g * tokens : (g + 1) * tokens, :]
                result[h, :, g * HD : (g + 1) * HD] = (whole / totals[g]).astype(jnp.bfloat16)
            copies[h].start()
        for copy in copies:
            copy.wait()


def finish(lengths, so_far, queries, sums, highs, counts, kv):
    tokens = so_far.shape[0]
    return pl.pallas_call(
        finish_kernel,
        out_shape=jax.ShapeDtypeStruct(so_far.shape, so_far.dtype),
        in_specs=[spec(SMEM), spec(HBM)] + [spec(VMEM)] * 5,
        out_specs=spec(HBM),
        input_output_aliases={1: 0},
        scratch_shapes=[
            VMEM((KVH, tokens, GROUP * HD), jnp.bfloat16),
            pltpu.SemaphoreType.DMA((KVH,)),
        ],
        compiler_params=PARAMS,
        cost_estimate=pl.CostEstimate(
            flops=1 << 28, bytes_accessed=1 << 21, transcendentals=1 << 19
        ),
    )(lengths, so_far, queries, sums, highs, counts, kv)


def body(
    hidden_states,
    queries_base,
    kv_base,
    adapter_down,
    adapter_up,
    adapter_ids,
    adapter_slots,
    rank_buckets,
    lengths,
):
    keep_down, give_down, keep_up, give_up = select(
        adapter_ids, adapter_slots, adapter_down, adapter_up
    )
    kv = kv_base[0]
    kv_two = lax.ppermute(kv, "ctx", TWO)
    near_down = lax.ppermute(give_down, "req", SIBLING)
    near_up = lax.ppermute(give_up, "req", SIBLING)
    pass_down = keep_down[1] + near_down[1]
    later = lax.optimization_barrier((kv, pass_down))[0]
    kv_one = lax.ppermute(later, "ctx", ONE)
    far_down = lax.ppermute(pass_down, "req", ACROSS)
    far_up = lax.ppermute(keep_up[1] + near_up[1], "req", ACROSS)
    down = keep_down[0] + near_down[0] + far_down
    down_one, down_two = spread(down)
    up = keep_up[0] + near_up[0] + far_up
    up_one, up_two = spread(up)
    ready = lax.optimization_barrier((down_two, kv_two))[0]
    down_three = lax.ppermute(ready, "ctx", ONE)
    ready = lax.optimization_barrier((up_two, down_one, kv_one))[0]
    up_three = lax.ppermute(ready, "ctx", ONE)
    kv_last = lax.optimization_barrier((kv_two, up_two, up_one))[0]
    kv_three = lax.ppermute(kv_last, "ctx", LAST)
    downs = [down, down_one, down_two, down_three]
    ups = [up, up_one, up_two, up_three]
    low = low_rank(adapter_ids, rank_buckets, hidden_states[0], downs)
    parts = attend(lengths, queries_base[0], low, [kv, kv_one, kv_two], ups)
    return finish(lengths, *parts, kv_three)[None]


def plain_body(
    hidden_states,
    queries_base,
    kv_base,
    adapter_down,
    adapter_up,
    adapter_ids,
    adapter_slots,
    rank_buckets,
    lengths,
):
    req_index = lax.axis_index("req")
    ctx_index = lax.axis_index("ctx")
    per_shard = adapter_down.shape[0]
    requests = adapter_ids.shape[0]
    store = adapter_slots.shape[0]
    rank_width = adapter_down.shape[2]
    tokens = hidden_states.shape[1]
    query_width = queries_base.shape[2]
    store_range = jnp.arange(store, dtype=jnp.int32)
    chosen = adapter_ids[:, None] == store_range[None, :]
    slot_of = jnp.sum(jnp.where(chosen, adapter_slots[None, :], 0), axis=1)
    rank_of = jnp.sum(jnp.where(chosen, rank_buckets[None, :], 0), axis=1)
    mine = jnp.arange(requests, dtype=jnp.int32) == req_index
    my_slot = jnp.sum(jnp.where(mine, slot_of, 0))
    my_rank = jnp.sum(jnp.where(mine, rank_of, 0))
    held = (
        slot_of[:, None] == req_index * per_shard + jnp.arange(per_shard, dtype=jnp.int32)[None, :]
    )
    select = held.astype(jnp.bfloat16)
    send_down = jnp.einsum(
        "qa,ard->qrd", select, adapter_down, preferred_element_type=jnp.float32
    ).astype(jnp.bfloat16)
    send_up = jnp.einsum(
        "qa,ard->qrd", select, adapter_up, preferred_element_type=jnp.float32
    ).astype(jnp.bfloat16)
    got_down, got_up = (
        lax.all_to_all(send_down, "req", split_axis=0, concat_axis=0, tiled=True),
        lax.all_to_all(send_up, "req", split_axis=0, concat_axis=0, tiled=True),
    )
    owner = my_slot // per_shard
    down_mine = lax.dynamic_index_in_dim(got_down, owner, 0, keepdims=False)
    up_mine = lax.dynamic_index_in_dim(got_up, owner, 0, keepdims=False)
    features = hidden_states[0]
    columns = features
    low_rank = jnp.dot(
        columns,
        lax.all_gather(down_mine, "ctx", axis=0, tiled=True),
        preferred_element_type=jnp.float32,
    )
    low_rank = jnp.where(
        jnp.arange(rank_width, dtype=jnp.int32)[None, :] < my_rank, low_rank, 0.0
    ).astype(jnp.bfloat16)
    columns = low_rank
    delta = jnp.dot(
        columns,
        lax.all_gather(up_mine, "ctx", axis=0, tiled=True),
        preferred_element_type=jnp.float32,
    )
    queries = (
        (queries_base[0].astype(jnp.float32) + delta)
        .astype(jnp.bfloat16)
        .reshape(tokens, KVH, GROUP, HD)
    )
    length = lengths[0]
    first_query = ctx_index * tokens
    query_pos = first_query + jnp.arange(tokens, dtype=jnp.int32)
    last_needed = jnp.minimum(first_query + tokens - 1, length - 1)
    scale = 1.0 / math.sqrt(HD)
    key_width = KVH * HD
    initial = (
        jnp.full((KVH, GROUP, tokens), -1e30, jnp.float32),
        jnp.zeros((KVH, GROUP, tokens), jnp.float32),
        jnp.zeros((KVH, GROUP, tokens, HD), jnp.float32),
    )
    piece = lax.all_gather(kv_base[0], "ctx", axis=0, tiled=True)
    count = piece.shape[0]
    width = math.gcd(count, 512)

    def key_block(index, state):
        largest, total, accum = state
        offset = index * width
        rows = lax.dynamic_slice_in_dim(piece, offset, width, 0)
        keys = rows[:, :key_width].reshape(width, KVH, HD)
        values = rows[:, key_width:].reshape(width, KVH, HD)
        key_pos = offset + jnp.arange(width, dtype=jnp.int32)
        score = (
            jnp.einsum("tkgd,skd->kgts", queries, keys, preferred_element_type=jnp.float32) * scale
        )
        allowed = (key_pos[None, :] <= query_pos[:, None]) & (key_pos[None, :] < length)
        masked = jnp.where(allowed, score, -1e30)
        newest = jnp.maximum(largest, jnp.max(masked, axis=-1))
        weight = jnp.where(allowed, jnp.exp(score - newest[..., None]), 0.0)
        factor = jnp.exp(largest - newest)
        total = total * factor + jnp.sum(weight, axis=-1)
        product = jnp.einsum(
            "kgts,skd->kgtd",
            weight.astype(jnp.bfloat16),
            values,
            preferred_element_type=jnp.float32,
        )
        accum = accum * factor[..., None] + product
        return (newest, total, accum)

    def compute(state):
        return lax.fori_loop(0, count // width, key_block, state)

    needed = (jnp.int32(0) <= last_needed) & (first_query < length)
    largest, total, accum = lax.cond(needed, compute, lambda state: state, initial)
    safe_total = jnp.where(total > 0.0, total, 1.0)
    output = accum / safe_total[..., None]
    output = jnp.transpose(output, (2, 0, 1, 3)).reshape(tokens, query_width)
    output = jnp.where(query_pos[:, None] < length, output, 0.0).astype(jnp.bfloat16)
    return output[None]


def solution(mesh):
    paired = mesh.shape["ctx"] == 4 and mesh.shape["req"] == 4
    return jax.shard_map(
        body if paired else plain_body,
        mesh=mesh,
        in_specs=(
            P(("group", "req"), "ctx", None),
            P(("group", "req"), "ctx", None),
            P(("group", "req"), "ctx", None),
            P(("group", "req"), "ctx", None),
            P(("group", "req"), "ctx", None),
            P("group"),
            P("group"),
            P("group"),
            P(("group", "req")),
        ),
        out_specs=P(("group", "req"), "ctx", None),
        check_vma=False,
    )
```

```python
import functools
import math

import jax
import jax.numpy as jnp
from jax import lax
from jax.experimental import pallas as pl
from jax.experimental.pallas import tpu as pltpu
from jax.sharding import PartitionSpec as P

HD = 128
KVH = 3
GROUP = 7
HEADS = KVH * GROUP
SMEM = pltpu.SMEM
VMEM = pltpu.VMEM
HBM = pltpu.HBM
LOG2E = 1.0 / math.log(2.0)
PARAMS = pltpu.CompilerParams(vmem_limit_bytes=32 * 1024 * 1024)
WHOLE = pltpu.CompilerParams(vmem_limit_bytes=52 * 1024 * 1024)


def spec(space):
    return pl.BlockSpec(memory_space=space)


def select_kernel(table, *rest, requests):
    stores, outs, sems = rest[:2], rest[2:6], rest[6]
    per_shard = stores[0].shape[0]
    me = lax.axis_index("req")
    first = me * per_shard
    copies = []
    for i, flip in enumerate((0, 2, 1, 3)):
        local = table[requests + table[me ^ flip]] - first
        held = (local >= 0) & (local < per_shard)
        for f, store in enumerate(stores):
            out = outs[2 * f + i // 2]
            copies.append((held, local, store, out, i % 2, sems.at[4 * f + i]))
    for held, local, store, out, k, sem in copies:

        @pl.when(held)
        def _():
            pltpu.make_async_copy(store.at[local], out.at[k], sem).start()

    for held, local, store, out, k, sem in copies:

        @pl.when(jnp.logical_not(held))
        def _():
            out[k] = jnp.zeros(out.shape[1:], out.dtype)

    for held, local, store, out, k, sem in copies:

        @pl.when(held)
        def _():
            pltpu.make_async_copy(store.at[local], out.at[k], sem).wait()


def select(ids, slots, down, up):
    shapes = [jax.ShapeDtypeStruct((2, *x.shape[1:]), x.dtype) for x in (down, down, up, up)]
    return pl.pallas_call(
        functools.partial(select_kernel, requests=ids.shape[0]),
        out_shape=shapes,
        in_specs=[spec(SMEM), spec(HBM), spec(HBM)],
        out_specs=[spec(VMEM)] * 4,
        scratch_shapes=[pltpu.SemaphoreType.DMA((8,))],
        compiler_params=WHOLE,
    )(jnp.concatenate([ids, slots]), down, up)


SIBLING = [(0, 1), (1, 0), (2, 3), (3, 2)]
ACROSS = [(0, 2), (1, 3), (2, 0), (3, 1)]
ONE = [(i, i ^ 1) for i in range(4)]
TWO = [(i, i ^ 2) for i in range(4)]
LAST = [(0, 0), (1, 1), (2, 3), (3, 2)]


def spread(shard):
    return lax.ppermute(shard, "ctx", ONE), lax.ppermute(shard, "ctx", TWO)


def product_kernel(features, piece, out):
    rows = piece.shape[0]
    out[...] = jnp.dot(features[:, -rows:], piece[...], preferred_element_type=jnp.float32)


def product(features, piece):
    return pl.pallas_call(
        product_kernel,
        out_shape=jax.ShapeDtypeStruct((features.shape[0], piece.shape[1]), jnp.float32),
        in_specs=[spec(VMEM)] * 2,
        out_specs=spec(VMEM),
        compiler_params=PARAMS,
        cost_estimate=pl.CostEstimate(flops=1 << 25, bytes_accessed=1 << 19, transcendentals=0),
    )(features, piece)


def low_rank_kernel(ids, ranks, hidden, partial, *rest):
    pieces, out = rest[:-1], rest[-1]
    rows = pieces[0].shape[0]
    rank = ranks[ids[lax.axis_index("req")]]
    total = partial[...]
    for flip, piece in zip((0, 2, 3), pieces):
        place = lax.axis_index("ctx") ^ flip
        columns = pl.ds(pl.multiple_of(place * rows, HD), rows)
        total += jnp.dot(hidden[:, columns], piece[...], preferred_element_type=jnp.float32)
    column = lax.broadcasted_iota(jnp.int32, total.shape, 1)
    out[...] = jnp.where(column < rank, total, 0.0).astype(jnp.bfloat16)


def low_rank(ids, ranks, hidden, partial, pieces):
    return pl.pallas_call(
        low_rank_kernel,
        out_shape=jax.ShapeDtypeStruct(partial.shape, jnp.bfloat16),
        in_specs=[spec(SMEM)] * 2 + [spec(VMEM)] * (2 + len(pieces)),
        out_specs=spec(VMEM),
        compiler_params=PARAMS,
        cost_estimate=pl.CostEstimate(flops=1 << 27, bytes_accessed=1 << 22, transcendentals=0),
    )(ids, ranks, hidden, partial, *pieces)


FACTOR = LOG2E / math.sqrt(HD)


def head_columns(kvs, h):
    keys = [kv[:, h * HD : (h + 1) * HD] for kv in kvs]
    values = [kv[:, (KVH + h) * HD : (KVH + h + 1) * HD] for kv in kvs]
    return jnp.concatenate(keys, axis=0), jnp.concatenate(values, axis=0)


def dot_keys(queries, keys):
    return lax.dot_general(
        queries, keys, (((1,), (1,)), ((), ())), preferred_element_type=jnp.float32
    )


def out_copies(result, out, sems):
    width = GROUP * HD
    return [
        pltpu.make_async_copy(result.at[h], out.at[:, pl.ds(h * width, width)], sems.at[h])
        for h in range(KVH)
    ]


def attend_kernel(lengths, base, low, *rest):
    kvs, ups = rest[:3], rest[3:7]
    out, queries, sums, highs, counts, upper, result, sems = rest[7:]
    tokens = base.shape[0]
    rows = ups[0].shape[0]
    z = lax.axis_index("ctx")
    live = z * tokens < lengths[0]
    block = GROUP * tokens
    copies = out_copies(result, out, sems)

    @pl.when(jnp.logical_not(live))
    def _():
        result[...] = jnp.zeros_like(result)
        for copy in copies:
            copy.start()

    @pl.when(live)
    def _():
        for flip, piece in enumerate(ups):
            upper[pl.ds(pl.multiple_of((z ^ flip) * rows, rows), rows), :] = piece[...]

    query_pos = lax.broadcasted_iota(jnp.int32, (tokens, tokens), 0)
    key_pos = lax.broadcasted_iota(jnp.int32, (tokens, tokens), 1)
    causal = key_pos <= query_pos

    def scores_of(h, blocks):
        columns = slice(h * GROUP * HD, (h + 1) * GROUP * HD)
        delta = jnp.dot(low[...], upper[:, columns], preferred_element_type=jnp.float32)
        query = (base[:, columns].astype(jnp.float32) + delta).astype(jnp.bfloat16)
        query = [query[:, g * HD : (g + 1) * HD] for g in range(GROUP)]
        query = jnp.concatenate(query, axis=0)
        keys, values = head_columns(blocks, h)
        return query, dot_keys(query, keys), values

    for mine, needed in enumerate(((0,), (0, 1), (0, 2), (0, 1, 2))):

        @pl.when(live & (z == mine))
        def _():
            blocks = [kvs[i] for i in needed]
            ahead = scores_of(0, blocks)
            for h in range(KVH):
                query, scores, values = ahead
                if h + 1 < KVH:
                    ahead = scores_of(h + 1, blocks)
                weights, tops, totals = [], [], []
                for g in range(GROUP):
                    score = scores[g * tokens : (g + 1) * tokens, :]
                    own = jnp.where(causal, score[:, :tokens], -1e30)
                    if mine:
                        own = jnp.concatenate([own, score[:, tokens:]], axis=1)
                    tops.append(jnp.max(own, axis=1, keepdims=True))
                    weight = jnp.exp2((own - tops[g]) * FACTOR)
                    totals.append(jnp.sum(weight, axis=1, keepdims=True))
                    weights.append(weight.astype(jnp.bfloat16))
                product = jnp.dot(
                    jnp.concatenate(weights, axis=0), values, preferred_element_type=jnp.float32
                )
                if mine < 2:
                    for g in range(GROUP):
                        result[h, :, g * HD : (g + 1) * HD] = (
                            product[g * tokens : (g + 1) * tokens, :] / totals[g]
                        ).astype(jnp.bfloat16)
                    copies[h].start()
                else:
                    queries[h * block : (h + 1) * block, :] = query
                    sums[h * block : (h + 1) * block, :] = product
                    for g in range(GROUP):
                        at = slice(h * block + g * tokens, h * block + (g + 1) * tokens)
                        highs[at, :] = jnp.broadcast_to(tops[g], (tokens, HD))
                        counts[at, :] = jnp.broadcast_to(totals[g], (tokens, HD))

    @pl.when(jnp.logical_not(live) | (z < 2))
    def _():
        for copy in copies:
            copy.wait()


def attend(lengths, base, low, kvs, ups):
    tokens, width = base.shape
    rows = HEADS * tokens
    shapes = [
        jax.ShapeDtypeStruct(base.shape, jnp.bfloat16),
        jax.ShapeDtypeStruct((rows, HD), jnp.bfloat16),
    ] + [jax.ShapeDtypeStruct((rows, HD), jnp.float32)] * 3
    return pl.pallas_call(
        attend_kernel,
        out_shape=shapes,
        in_specs=[spec(SMEM)] + [spec(VMEM)] * (2 + len(kvs) + len(ups)),
        out_specs=[spec(HBM)] + [spec(VMEM)] * 4,
        scratch_shapes=[
            VMEM((low.shape[1], width), jnp.bfloat16),
            VMEM((KVH, tokens, GROUP * HD), jnp.bfloat16),
            pltpu.SemaphoreType.DMA((KVH,)),
        ],
        compiler_params=PARAMS,
        cost_estimate=pl.CostEstimate(
            flops=1 << 30, bytes_accessed=1 << 22, transcendentals=1 << 21
        ),
    )(lengths, base, low, *kvs, *ups)


def finish_kernel(lengths, so_far, queries, sums, highs, counts, kv, out, result, sems):
    del so_far
    tokens = result.shape[1]
    z = lax.axis_index("ctx")
    block = GROUP * tokens
    copies = out_copies(result, out, sems)

    @pl.when((z * tokens < lengths[0]) & (z >= 2))
    def _():
        for h in range(KVH):
            keys, values = head_columns([kv], h)
            scores = dot_keys(queries[h * block : (h + 1) * block, :], keys)
            weights, factors, totals = [], [], []
            for g in range(GROUP):
                at = slice(h * block + g * tokens, h * block + (g + 1) * tokens)
                score = scores[g * tokens : (g + 1) * tokens, :]
                newest = jnp.maximum(highs[at, :], jnp.max(score, axis=1, keepdims=True))
                weight = jnp.exp2((score - newest) * FACTOR)
                factors.append(jnp.exp2((highs[at, :] - newest) * FACTOR))
                added = jnp.sum(weight, axis=1, keepdims=True)
                totals.append(counts[at, :] * factors[g] + added)
                weights.append(weight.astype(jnp.bfloat16))
            product = jnp.dot(
                jnp.concatenate(weights, axis=0), values, preferred_element_type=jnp.float32
            )
            for g in range(GROUP):
                at = slice(h * block + g * tokens, h * block + (g + 1) * tokens)
                whole = sums[at, :] * factors[g] + product[g * tokens : (g + 1) * tokens, :]
                result[h, :, g * HD : (g + 1) * HD] = (whole / totals[g]).astype(jnp.bfloat16)
            copies[h].start()
        for copy in copies:
            copy.wait()


def finish(lengths, so_far, queries, sums, highs, counts, kv):
    tokens = so_far.shape[0]
    return pl.pallas_call(
        finish_kernel,
        out_shape=jax.ShapeDtypeStruct(so_far.shape, so_far.dtype),
        in_specs=[spec(SMEM), spec(HBM)] + [spec(VMEM)] * 5,
        out_specs=spec(HBM),
        input_output_aliases={1: 0},
        scratch_shapes=[
            VMEM((KVH, tokens, GROUP * HD), jnp.bfloat16),
            pltpu.SemaphoreType.DMA((KVH,)),
        ],
        compiler_params=PARAMS,
        cost_estimate=pl.CostEstimate(
            flops=1 << 28, bytes_accessed=1 << 21, transcendentals=1 << 19
        ),
    )(lengths, so_far, queries, sums, highs, counts, kv)


def body(
    hidden_states,
    queries_base,
    kv_base,
    adapter_down,
    adapter_up,
    adapter_ids,
    adapter_slots,
    rank_buckets,
    lengths,
):
    keep_down, give_down, keep_up, give_up = select(
        adapter_ids, adapter_slots, adapter_down, adapter_up
    )
    kv, hidden = kv_base[0], hidden_states[0]
    rows = adapter_down.shape[1]
    start = (lax.axis_index("ctx") ^ 1) * rows
    columns = lax.dynamic_slice_in_dim(hidden, start, rows, 1)
    kv_one = lax.ppermute(jnp.concatenate([kv, columns], axis=1), "ctx", ONE)
    kv_two = lax.ppermute(kv, "ctx", TWO)
    near_down = lax.ppermute(give_down, "req", SIBLING)
    near_up = lax.ppermute(give_up, "req", SIBLING)
    far_down = lax.ppermute(keep_down[1] + near_down[1], "req", ACROSS)
    far_up = lax.ppermute(keep_up[1] + near_up[1], "req", ACROSS)
    down = keep_down[0] + near_down[0] + far_down
    down_two = lax.ppermute(down, "ctx", TWO)
    partial = lax.ppermute(product(kv_one, down), "ctx", ONE)
    up = keep_up[0] + near_up[0] + far_up
    up_one, up_two = spread(up)
    ready = lax.optimization_barrier((down_two, kv_two, partial))[0]
    down_three = lax.ppermute(ready, "ctx", ONE)
    ready = up_two
    up_three = lax.ppermute(ready, "ctx", ONE)
    kv_last = lax.optimization_barrier((kv_two, up_two, up_one))[0]
    kv_three = lax.ppermute(kv_last, "ctx", LAST)
    downs = [down, down_two, down_three]
    ups = [up, up_one, up_two, up_three]
    low = low_rank(adapter_ids, rank_buckets, hidden, partial, downs)
    parts = attend(lengths, queries_base[0], low, [kv, kv_one, kv_two], ups)
    return finish(lengths, *parts, kv_three)[None]


def plain_body(
    hidden_states,
    queries_base,
    kv_base,
    adapter_down,
    adapter_up,
    adapter_ids,
    adapter_slots,
    rank_buckets,
    lengths,
):
    req_index = lax.axis_index("req")
    ctx_index = lax.axis_index("ctx")
    per_shard = adapter_down.shape[0]
    requests = adapter_ids.shape[0]
    store = adapter_slots.shape[0]
    rank_width = adapter_down.shape[2]
    tokens = hidden_states.shape[1]
    query_width = queries_base.shape[2]
    store_range = jnp.arange(store, dtype=jnp.int32)
    chosen = adapter_ids[:, None] == store_range[None, :]
    slot_of = jnp.sum(jnp.where(chosen, adapter_slots[None, :], 0), axis=1)
    rank_of = jnp.sum(jnp.where(chosen, rank_buckets[None, :], 0), axis=1)
    mine = jnp.arange(requests, dtype=jnp.int32) == req_index
    my_slot = jnp.sum(jnp.where(mine, slot_of, 0))
    my_rank = jnp.sum(jnp.where(mine, rank_of, 0))
    held = (
        slot_of[:, None] == req_index * per_shard + jnp.arange(per_shard, dtype=jnp.int32)[None, :]
    )
    select = held.astype(jnp.bfloat16)
    send_down = jnp.einsum(
        "qa,ard->qrd", select, adapter_down, preferred_element_type=jnp.float32
    ).astype(jnp.bfloat16)
    send_up = jnp.einsum(
        "qa,ard->qrd", select, adapter_up, preferred_element_type=jnp.float32
    ).astype(jnp.bfloat16)
    got_down, got_up = (
        lax.all_to_all(send_down, "req", split_axis=0, concat_axis=0, tiled=True),
        lax.all_to_all(send_up, "req", split_axis=0, concat_axis=0, tiled=True),
    )
    owner = my_slot // per_shard
    down_mine = lax.dynamic_index_in_dim(got_down, owner, 0, keepdims=False)
    up_mine = lax.dynamic_index_in_dim(got_up, owner, 0, keepdims=False)
    features = hidden_states[0]
    columns = features
    low_rank = jnp.dot(
        columns,
        lax.all_gather(down_mine, "ctx", axis=0, tiled=True),
        preferred_element_type=jnp.float32,
    )
    low_rank = jnp.where(
        jnp.arange(rank_width, dtype=jnp.int32)[None, :] < my_rank, low_rank, 0.0
    ).astype(jnp.bfloat16)
    columns = low_rank
    delta = jnp.dot(
        columns,
        lax.all_gather(up_mine, "ctx", axis=0, tiled=True),
        preferred_element_type=jnp.float32,
    )
    queries = (
        (queries_base[0].astype(jnp.float32) + delta)
        .astype(jnp.bfloat16)
        .reshape(tokens, KVH, GROUP, HD)
    )
    length = lengths[0]
    first_query = ctx_index * tokens
    query_pos = first_query + jnp.arange(tokens, dtype=jnp.int32)
    last_needed = jnp.minimum(first_query + tokens - 1, length - 1)
    scale = 1.0 / math.sqrt(HD)
    key_width = KVH * HD
    initial = (
        jnp.full((KVH, GROUP, tokens), -1e30, jnp.float32),
        jnp.zeros((KVH, GROUP, tokens), jnp.float32),
        jnp.zeros((KVH, GROUP, tokens, HD), jnp.float32),
    )
    piece = lax.all_gather(kv_base[0], "ctx", axis=0, tiled=True)
    count = piece.shape[0]
    width = math.gcd(count, 512)

    def key_block(index, state):
        largest, total, accum = state
        offset = index * width
        rows = lax.dynamic_slice_in_dim(piece, offset, width, 0)
        keys = rows[:, :key_width].reshape(width, KVH, HD)
        values = rows[:, key_width:].reshape(width, KVH, HD)
        key_pos = offset + jnp.arange(width, dtype=jnp.int32)
        score = (
            jnp.einsum("tkgd,skd->kgts", queries, keys, preferred_element_type=jnp.float32) * scale
        )
        allowed = (key_pos[None, :] <= query_pos[:, None]) & (key_pos[None, :] < length)
        masked = jnp.where(allowed, score, -1e30)
        newest = jnp.maximum(largest, jnp.max(masked, axis=-1))
        weight = jnp.where(allowed, jnp.exp(score - newest[..., None]), 0.0)
        factor = jnp.exp(largest - newest)
        total = total * factor + jnp.sum(weight, axis=-1)
        product = jnp.einsum(
            "kgts,skd->kgtd",
            weight.astype(jnp.bfloat16),
            values,
            preferred_element_type=jnp.float32,
        )
        accum = accum * factor[..., None] + product
        return (newest, total, accum)

    def compute(state):
        return lax.fori_loop(0, count // width, key_block, state)

    needed = (jnp.int32(0) <= last_needed) & (first_query < length)
    largest, total, accum = lax.cond(needed, compute, lambda state: state, initial)
    safe_total = jnp.where(total > 0.0, total, 1.0)
    output = accum / safe_total[..., None]
    output = jnp.transpose(output, (2, 0, 1, 3)).reshape(tokens, query_width)
    output = jnp.where(query_pos[:, None] < length, output, 0.0).astype(jnp.bfloat16)
    return output[None]


def solution(mesh):
    paired = mesh.shape["ctx"] == 4 and mesh.shape["req"] == 4
    return jax.shard_map(
        body if paired else plain_body,
        mesh=mesh,
        in_specs=(
            P(("group", "req"), "ctx", None),
            P(("group", "req"), "ctx", None),
            P(("group", "req"), "ctx", None),
            P(("group", "req"), "ctx", None),
            P(("group", "req"), "ctx", None),
            P("group"),
            P("group"),
            P("group"),
            P(("group", "req")),
        ),
        out_specs=P(("group", "req"), "ctx", None),
        check_vma=False,
    )
```

```python
import functools
import math

import jax
import jax.numpy as jnp
from jax import lax
from jax.experimental import pallas as pl
from jax.experimental.pallas import tpu as pltpu
from jax.sharding import PartitionSpec as P

HD = 128
KVH = 3
GROUP = 7
HEADS = KVH * GROUP
SMEM = pltpu.SMEM
VMEM = pltpu.VMEM
HBM = pltpu.HBM
LOG2E = 1.0 / math.log(2.0)
PARAMS = pltpu.CompilerParams(vmem_limit_bytes=32 * 1024 * 1024)
WHOLE = pltpu.CompilerParams(vmem_limit_bytes=50 * 1024 * 1024)


def spec(space):
    return pl.BlockSpec(memory_space=space)


def select_kernel(table, *rest, requests):
    stores, outs, sems = rest[:2], rest[2:6], rest[6]
    per_shard = stores[0].shape[0]
    me = lax.axis_index("req")
    first = me * per_shard
    copies = []
    for i, flip in enumerate((0, 2, 1, 3)):
        local = table[requests + table[me ^ flip]] - first
        held = (local >= 0) & (local < per_shard)
        for f, store in enumerate(stores):
            out = outs[2 * f + i // 2]
            copies.append((held, local, store, out, i % 2, sems.at[4 * f + i]))
    for held, local, store, out, k, sem in copies:

        @pl.when(held)
        def _():
            pltpu.make_async_copy(store.at[local], out.at[k], sem).start()

    for held, local, store, out, k, sem in copies:

        @pl.when(jnp.logical_not(held))
        def _():
            out[k] = jnp.zeros(out.shape[1:], out.dtype)

    for held, local, store, out, k, sem in copies:

        @pl.when(held)
        def _():
            pltpu.make_async_copy(store.at[local], out.at[k], sem).wait()


def select(ids, slots, down, up):
    shapes = [jax.ShapeDtypeStruct((2, *x.shape[1:]), x.dtype) for x in (down, down, up, up)]
    return pl.pallas_call(
        functools.partial(select_kernel, requests=ids.shape[0]),
        out_shape=shapes,
        in_specs=[spec(SMEM), spec(HBM), spec(HBM)],
        out_specs=[spec(VMEM)] * 4,
        scratch_shapes=[pltpu.SemaphoreType.DMA((8,))],
        compiler_params=WHOLE,
    )(jnp.concatenate([ids, slots]), down, up)


SIBLING = [(0, 1), (1, 0), (2, 3), (3, 2)]
ACROSS = [(0, 2), (1, 3), (2, 0), (3, 1)]
ONE = [(i, i ^ 1) for i in range(4)]
TWO = [(i, i ^ 2) for i in range(4)]
LAST = [(0, 0), (1, 1), (2, 3), (3, 2)]


def spread(shard):
    return lax.ppermute(shard, "ctx", ONE), lax.ppermute(shard, "ctx", TWO)


def product_kernel(features, piece, out):
    rows = piece.shape[0]
    out[...] = jnp.dot(features[:, -rows:], piece[...], preferred_element_type=jnp.float32)


def product(features, piece):
    return pl.pallas_call(
        product_kernel,
        out_shape=jax.ShapeDtypeStruct((features.shape[0], piece.shape[1]), jnp.float32),
        in_specs=[spec(VMEM)] * 2,
        out_specs=spec(VMEM),
        compiler_params=PARAMS,
        cost_estimate=pl.CostEstimate(flops=1 << 25, bytes_accessed=1 << 19, transcendentals=0),
    )(features, piece)


def low_rank_kernel(ids, ranks, hidden, partial, *rest):
    pieces, out = rest[:-1], rest[-1]
    rows = pieces[0].shape[0]
    rank = ranks[ids[lax.axis_index("req")]]
    total = partial[...]
    for flip, piece in zip((0, 2, 3), pieces):
        place = lax.axis_index("ctx") ^ flip
        columns = pl.ds(pl.multiple_of(place * rows, HD), rows)
        total += jnp.dot(hidden[:, columns], piece[...], preferred_element_type=jnp.float32)
    column = lax.broadcasted_iota(jnp.int32, total.shape, 1)
    out[...] = jnp.where(column < rank, total, 0.0).astype(jnp.bfloat16)


def low_rank(ids, ranks, hidden, partial, pieces):
    return pl.pallas_call(
        low_rank_kernel,
        out_shape=jax.ShapeDtypeStruct(partial.shape, jnp.bfloat16),
        in_specs=[spec(SMEM)] * 2 + [spec(VMEM)] * (2 + len(pieces)),
        out_specs=spec(VMEM),
        compiler_params=PARAMS,
        cost_estimate=pl.CostEstimate(flops=1 << 27, bytes_accessed=1 << 22, transcendentals=0),
    )(ids, ranks, hidden, partial, *pieces)


FACTOR = LOG2E / math.sqrt(HD)


def head_columns(kvs, h):
    keys = [kv[:, h * HD : (h + 1) * HD] for kv in kvs]
    values = [kv[:, (KVH + h) * HD : (KVH + h + 1) * HD] for kv in kvs]
    return jnp.concatenate(keys, axis=0), jnp.concatenate(values, axis=0)


def dot_keys(queries, keys):
    return lax.dot_general(
        queries, keys, (((1,), (1,)), ((), ())), preferred_element_type=jnp.float32
    )


def out_copies(result, out, sems):
    width = GROUP * HD
    return [
        pltpu.make_async_copy(result.at[h], out.at[:, pl.ds(h * width, width)], sems.at[h])
        for h in range(KVH)
    ]


def attend_kernel(lengths, base, low, *rest):
    kvs, ups = rest[:3], rest[3:7]
    out, queries, sums, highs, counts, upper, result, sems = rest[7:]
    tokens = base.shape[0]
    rows = ups[0].shape[0]
    z = lax.axis_index("ctx")
    live = z * tokens < lengths[0]
    block = GROUP * tokens
    copies = out_copies(result, out, sems)

    @pl.when(jnp.logical_not(live))
    def _():
        result[...] = jnp.zeros_like(result)
        for copy in copies:
            copy.start()

    @pl.when(live)
    def _():
        for flip, piece in enumerate(ups):
            upper[pl.ds(pl.multiple_of((z ^ flip) * rows, rows), rows), :] = piece[...]

    query_pos = lax.broadcasted_iota(jnp.int32, (tokens, tokens), 0)
    key_pos = lax.broadcasted_iota(jnp.int32, (tokens, tokens), 1)
    causal = key_pos <= query_pos

    def scores_of(h, blocks):
        columns = slice(h * GROUP * HD, (h + 1) * GROUP * HD)
        delta = jnp.dot(low[...], upper[:, columns], preferred_element_type=jnp.float32)
        query = (base[:, columns].astype(jnp.float32) + delta).astype(jnp.bfloat16)
        query = [query[:, g * HD : (g + 1) * HD] for g in range(GROUP)]
        query = jnp.concatenate(query, axis=0)
        keys, values = head_columns(blocks, h)
        return query, dot_keys(query, keys), values

    for mine, needed in enumerate(((0,), (0, 1), (0, 2), (0, 1, 2))):

        @pl.when(live & (z == mine))
        def _():
            blocks = [kvs[i] for i in needed]
            ahead = scores_of(0, blocks)
            for h in range(KVH):
                query, scores, values = ahead
                if h + 1 < KVH:
                    ahead = scores_of(h + 1, blocks)
                weights, tops, totals = [], [], []
                for g in range(GROUP):
                    score = scores[g * tokens : (g + 1) * tokens, :]
                    own = jnp.where(causal, score[:, :tokens], -1e30)
                    if mine:
                        own = jnp.concatenate([own, score[:, tokens:]], axis=1)
                    tops.append(jnp.max(own, axis=1, keepdims=True))
                    weight = jnp.exp2((own - tops[g]) * FACTOR)
                    totals.append(jnp.sum(weight, axis=1, keepdims=True))
                    weights.append(weight.astype(jnp.bfloat16))
                product = jnp.dot(
                    jnp.concatenate(weights, axis=0), values, preferred_element_type=jnp.float32
                )
                if mine < 2:
                    for g in range(GROUP):
                        result[h, :, g * HD : (g + 1) * HD] = (
                            product[g * tokens : (g + 1) * tokens, :] / totals[g]
                        ).astype(jnp.bfloat16)
                    copies[h].start()
                else:
                    queries[h * block : (h + 1) * block, :] = query
                    sums[h * block : (h + 1) * block, :] = product
                    for g in range(GROUP):
                        at = slice(h * block + g * tokens, h * block + (g + 1) * tokens)
                        highs[at, :] = jnp.broadcast_to(tops[g], (tokens, HD))
                        counts[at, :] = jnp.broadcast_to(totals[g], (tokens, HD))

    @pl.when(jnp.logical_not(live) | (z < 2))
    def _():
        for copy in copies:
            copy.wait()


def attend(lengths, base, low, kvs, ups):
    tokens, width = base.shape
    rows = HEADS * tokens
    shapes = [
        jax.ShapeDtypeStruct(base.shape, jnp.bfloat16),
        jax.ShapeDtypeStruct((rows, HD), jnp.bfloat16),
    ] + [jax.ShapeDtypeStruct((rows, HD), jnp.float32)] * 3
    return pl.pallas_call(
        attend_kernel,
        out_shape=shapes,
        in_specs=[spec(SMEM)] + [spec(VMEM)] * (2 + len(kvs) + len(ups)),
        out_specs=[spec(HBM)] + [spec(VMEM)] * 4,
        scratch_shapes=[
            VMEM((low.shape[1], width), jnp.bfloat16),
            VMEM((KVH, tokens, GROUP * HD), jnp.bfloat16),
            pltpu.SemaphoreType.DMA((KVH,)),
        ],
        compiler_params=PARAMS,
        cost_estimate=pl.CostEstimate(
            flops=1 << 30, bytes_accessed=1 << 22, transcendentals=1 << 21
        ),
    )(lengths, base, low, *kvs, *ups)


def finish_kernel(lengths, so_far, queries, sums, highs, counts, kv, out, result, sems):
    del so_far
    tokens = result.shape[1]
    z = lax.axis_index("ctx")
    block = GROUP * tokens
    copies = out_copies(result, out, sems)

    @pl.when((z * tokens < lengths[0]) & (z >= 2))
    def _():
        for h in range(KVH):
            keys, values = head_columns([kv], h)
            scores = dot_keys(queries[h * block : (h + 1) * block, :], keys)
            weights, factors, totals = [], [], []
            for g in range(GROUP):
                at = slice(h * block + g * tokens, h * block + (g + 1) * tokens)
                score = scores[g * tokens : (g + 1) * tokens, :]
                newest = jnp.maximum(highs[at, :], jnp.max(score, axis=1, keepdims=True))
                weight = jnp.exp2((score - newest) * FACTOR)
                factors.append(jnp.exp2((highs[at, :] - newest) * FACTOR))
                added = jnp.sum(weight, axis=1, keepdims=True)
                totals.append(counts[at, :] * factors[g] + added)
                weights.append(weight.astype(jnp.bfloat16))
            product = jnp.dot(
                jnp.concatenate(weights, axis=0), values, preferred_element_type=jnp.float32
            )
            for g in range(GROUP):
                at = slice(h * block + g * tokens, h * block + (g + 1) * tokens)
                whole = sums[at, :] * factors[g] + product[g * tokens : (g + 1) * tokens, :]
                result[h, :, g * HD : (g + 1) * HD] = (whole / totals[g]).astype(jnp.bfloat16)
            copies[h].start()
        for copy in copies:
            copy.wait()


def finish(lengths, so_far, queries, sums, highs, counts, kv):
    tokens = so_far.shape[0]
    return pl.pallas_call(
        finish_kernel,
        out_shape=jax.ShapeDtypeStruct(so_far.shape, so_far.dtype),
        in_specs=[spec(SMEM), spec(HBM)] + [spec(VMEM)] * 5,
        out_specs=spec(HBM),
        input_output_aliases={1: 0},
        scratch_shapes=[
            VMEM((KVH, tokens, GROUP * HD), jnp.bfloat16),
            pltpu.SemaphoreType.DMA((KVH,)),
        ],
        compiler_params=PARAMS,
        cost_estimate=pl.CostEstimate(
            flops=1 << 28, bytes_accessed=1 << 21, transcendentals=1 << 19
        ),
    )(lengths, so_far, queries, sums, highs, counts, kv)


def body(
    hidden_states,
    queries_base,
    kv_base,
    adapter_down,
    adapter_up,
    adapter_ids,
    adapter_slots,
    rank_buckets,
    lengths,
):
    keep_down, give_down, keep_up, give_up = select(
        adapter_ids, adapter_slots, adapter_down, adapter_up
    )
    kv, hidden = kv_base[0], hidden_states[0]
    rows = adapter_down.shape[1]
    start = (lax.axis_index("ctx") ^ 1) * rows
    columns = lax.dynamic_slice_in_dim(hidden, start, rows, 1)
    kv_one = lax.ppermute(jnp.concatenate([kv, columns], axis=1), "ctx", ONE)
    kv_two = lax.ppermute(kv, "ctx", TWO)
    near_down = lax.ppermute(give_down, "req", SIBLING)
    near_up = lax.ppermute(give_up, "req", SIBLING)
    far_down = lax.ppermute(keep_down[1] + near_down[1], "req", ACROSS)
    far_up = lax.ppermute(keep_up[1] + near_up[1], "req", ACROSS)
    down = keep_down[0] + near_down[0] + far_down
    down_two = lax.ppermute(down, "ctx", TWO)
    mine = product(kv_one, down)
    partial = lax.ppermute(mine, "ctx", ONE)
    up = keep_up[0] + near_up[0] + far_up
    up_one, up_two = spread(up)
    ready = lax.optimization_barrier((down_two, kv_two))[0]
    down_three = lax.ppermute(ready, "ctx", ONE)
    ready = lax.optimization_barrier((up_two, mine))[0]
    up_three = lax.ppermute(ready, "ctx", ONE)
    kv_last = lax.optimization_barrier((kv_two, up_two, up_one))[0]
    kv_three = lax.ppermute(kv_last, "ctx", LAST)
    downs = [down, down_two, down_three]
    ups = [up, up_one, up_two, up_three]
    low = low_rank(adapter_ids, rank_buckets, hidden, partial, downs)
    parts = attend(lengths, queries_base[0], low, [kv, kv_one, kv_two], ups)
    return finish(lengths, *parts, kv_three)[None]


def plain_body(
    hidden_states,
    queries_base,
    kv_base,
    adapter_down,
    adapter_up,
    adapter_ids,
    adapter_slots,
    rank_buckets,
    lengths,
):
    req_index = lax.axis_index("req")
    ctx_index = lax.axis_index("ctx")
    per_shard = adapter_down.shape[0]
    requests = adapter_ids.shape[0]
    store = adapter_slots.shape[0]
    rank_width = adapter_down.shape[2]
    tokens = hidden_states.shape[1]
    query_width = queries_base.shape[2]
    store_range = jnp.arange(store, dtype=jnp.int32)
    chosen = adapter_ids[:, None] == store_range[None, :]
    slot_of = jnp.sum(jnp.where(chosen, adapter_slots[None, :], 0), axis=1)
    rank_of = jnp.sum(jnp.where(chosen, rank_buckets[None, :], 0), axis=1)
    mine = jnp.arange(requests, dtype=jnp.int32) == req_index
    my_slot = jnp.sum(jnp.where(mine, slot_of, 0))
    my_rank = jnp.sum(jnp.where(mine, rank_of, 0))
    held = (
        slot_of[:, None] == req_index * per_shard + jnp.arange(per_shard, dtype=jnp.int32)[None, :]
    )
    select = held.astype(jnp.bfloat16)
    send_down = jnp.einsum(
        "qa,ard->qrd", select, adapter_down, preferred_element_type=jnp.float32
    ).astype(jnp.bfloat16)
    send_up = jnp.einsum(
        "qa,ard->qrd", select, adapter_up, preferred_element_type=jnp.float32
    ).astype(jnp.bfloat16)
    got_down, got_up = (
        lax.all_to_all(send_down, "req", split_axis=0, concat_axis=0, tiled=True),
        lax.all_to_all(send_up, "req", split_axis=0, concat_axis=0, tiled=True),
    )
    owner = my_slot // per_shard
    down_mine = lax.dynamic_index_in_dim(got_down, owner, 0, keepdims=False)
    up_mine = lax.dynamic_index_in_dim(got_up, owner, 0, keepdims=False)
    features = hidden_states[0]
    columns = features
    low_rank = jnp.dot(
        columns,
        lax.all_gather(down_mine, "ctx", axis=0, tiled=True),
        preferred_element_type=jnp.float32,
    )
    low_rank = jnp.where(
        jnp.arange(rank_width, dtype=jnp.int32)[None, :] < my_rank, low_rank, 0.0
    ).astype(jnp.bfloat16)
    columns = low_rank
    delta = jnp.dot(
        columns,
        lax.all_gather(up_mine, "ctx", axis=0, tiled=True),
        preferred_element_type=jnp.float32,
    )
    queries = (
        (queries_base[0].astype(jnp.float32) + delta)
        .astype(jnp.bfloat16)
        .reshape(tokens, KVH, GROUP, HD)
    )
    length = lengths[0]
    first_query = ctx_index * tokens
    query_pos = first_query + jnp.arange(tokens, dtype=jnp.int32)
    last_needed = jnp.minimum(first_query + tokens - 1, length - 1)
    scale = 1.0 / math.sqrt(HD)
    key_width = KVH * HD
    initial = (
        jnp.full((KVH, GROUP, tokens), -1e30, jnp.float32),
        jnp.zeros((KVH, GROUP, tokens), jnp.float32),
        jnp.zeros((KVH, GROUP, tokens, HD), jnp.float32),
    )
    piece = lax.all_gather(kv_base[0], "ctx", axis=0, tiled=True)
    count = piece.shape[0]
    width = math.gcd(count, 512)

    def key_block(index, state):
        largest, total, accum = state
        offset = index * width
        rows = lax.dynamic_slice_in_dim(piece, offset, width, 0)
        keys = rows[:, :key_width].reshape(width, KVH, HD)
        values = rows[:, key_width:].reshape(width, KVH, HD)
        key_pos = offset + jnp.arange(width, dtype=jnp.int32)
        score = (
            jnp.einsum("tkgd,skd->kgts", queries, keys, preferred_element_type=jnp.float32) * scale
        )
        allowed = (key_pos[None, :] <= query_pos[:, None]) & (key_pos[None, :] < length)
        masked = jnp.where(allowed, score, -1e30)
        newest = jnp.maximum(largest, jnp.max(masked, axis=-1))
        weight = jnp.where(allowed, jnp.exp(score - newest[..., None]), 0.0)
        factor = jnp.exp(largest - newest)
        total = total * factor + jnp.sum(weight, axis=-1)
        product = jnp.einsum(
            "kgts,skd->kgtd",
            weight.astype(jnp.bfloat16),
            values,
            preferred_element_type=jnp.float32,
        )
        accum = accum * factor[..., None] + product
        return (newest, total, accum)

    def compute(state):
        return lax.fori_loop(0, count // width, key_block, state)

    needed = (jnp.int32(0) <= last_needed) & (first_query < length)
    largest, total, accum = lax.cond(needed, compute, lambda state: state, initial)
    safe_total = jnp.where(total > 0.0, total, 1.0)
    output = accum / safe_total[..., None]
    output = jnp.transpose(output, (2, 0, 1, 3)).reshape(tokens, query_width)
    output = jnp.where(query_pos[:, None] < length, output, 0.0).astype(jnp.bfloat16)
    return output[None]


def solution(mesh):
    paired = mesh.shape["ctx"] == 4 and mesh.shape["req"] == 4
    return jax.shard_map(
        body if paired else plain_body,
        mesh=mesh,
        in_specs=(
            P(("group", "req"), "ctx", None),
            P(("group", "req"), "ctx", None),
            P(("group", "req"), "ctx", None),
            P(("group", "req"), "ctx", None),
            P(("group", "req"), "ctx", None),
            P("group"),
            P("group"),
            P("group"),
            P(("group", "req")),
        ),
        out_specs=P(("group", "req"), "ctx", None),
        check_vma=False,
    )
```

```python
import functools
import math

import jax
import jax.numpy as jnp
from jax import lax
from jax.experimental import pallas as pl
from jax.experimental.pallas import tpu as pltpu
from jax.sharding import PartitionSpec as P

HD = 128
KVH = 3
GROUP = 7
HEADS = KVH * GROUP
SMEM = pltpu.SMEM
VMEM = pltpu.VMEM
HBM = pltpu.HBM
LOG2E = 1.0 / math.log(2.0)
PARAMS = pltpu.CompilerParams(vmem_limit_bytes=32 * 1024 * 1024)
WHOLE = pltpu.CompilerParams(vmem_limit_bytes=52 * 1024 * 1024)


def spec(space):
    return pl.BlockSpec(memory_space=space)


def select_kernel(table, *rest, requests):
    stores, outs, sems = rest[:2], rest[2:6], rest[6]
    per_shard = stores[0].shape[0]
    me = lax.axis_index("req")
    first = me * per_shard
    copies = []
    for i, flip in enumerate((0, 2, 1, 3)):
        local = table[requests + table[me ^ flip]] - first
        held = (local >= 0) & (local < per_shard)
        for f, store in enumerate(stores):
            out = outs[2 * f + i // 2]
            copies.append((held, local, store, out, i % 2, sems.at[4 * f + i]))
    for held, local, store, out, k, sem in copies:

        @pl.when(held)
        def _():
            pltpu.make_async_copy(store.at[local], out.at[k], sem).start()

    for held, local, store, out, k, sem in copies:

        @pl.when(jnp.logical_not(held))
        def _():
            out[k] = jnp.zeros(out.shape[1:], out.dtype)

    for held, local, store, out, k, sem in copies:

        @pl.when(held)
        def _():
            pltpu.make_async_copy(store.at[local], out.at[k], sem).wait()


def select(ids, slots, down, up):
    shapes = [jax.ShapeDtypeStruct((2, *x.shape[1:]), x.dtype) for x in (down, down, up, up)]
    return pl.pallas_call(
        functools.partial(select_kernel, requests=ids.shape[0]),
        out_shape=shapes,
        in_specs=[spec(SMEM), spec(HBM), spec(HBM)],
        out_specs=[spec(VMEM)] * 4,
        scratch_shapes=[pltpu.SemaphoreType.DMA((8,))],
        compiler_params=WHOLE,
    )(jnp.concatenate([ids, slots]), down, up)


SIBLING = [(0, 1), (1, 0), (2, 3), (3, 2)]
ACROSS = [(0, 2), (1, 3), (2, 0), (3, 1)]
ONE = [(i, i ^ 1) for i in range(4)]
TWO = [(i, i ^ 2) for i in range(4)]
LAST = [(0, 0), (1, 1), (2, 3), (3, 2)]


def spread(shard):
    return lax.ppermute(shard, "ctx", ONE), lax.ppermute(shard, "ctx", TWO)


def low_rank_kernel(ids, ranks, hidden, *rest):
    pieces, out, accum = rest[:-2], rest[-2], rest[-1]
    rows = pieces[0].shape[0]
    rank = ranks[ids[lax.axis_index("req")]]
    accum[...] = jnp.zeros_like(accum)
    for flip, piece in enumerate(pieces):
        place = lax.axis_index("ctx") ^ flip
        columns = pl.ds(pl.multiple_of(place * rows, HD), rows)
        accum[...] += jnp.dot(hidden[:, columns], piece[...], preferred_element_type=jnp.float32)

    column = lax.broadcasted_iota(jnp.int32, accum.shape, 1)
    out[...] = jnp.where(column < rank, accum[...], 0.0).astype(jnp.bfloat16)


def low_rank(ids, ranks, hidden, pieces):
    shape = (hidden.shape[0], pieces[0].shape[1])
    return pl.pallas_call(
        low_rank_kernel,
        out_shape=jax.ShapeDtypeStruct(shape, jnp.bfloat16),
        in_specs=[spec(SMEM)] * 2 + [spec(VMEM)] * (1 + len(pieces)),
        out_specs=spec(VMEM),
        scratch_shapes=[VMEM(shape, jnp.float32)],
        compiler_params=PARAMS,
        cost_estimate=pl.CostEstimate(flops=1 << 27, bytes_accessed=1 << 22, transcendentals=0),
    )(ids, ranks, hidden, *pieces)


FACTOR = LOG2E / math.sqrt(HD)


def head_columns(kvs, h):
    keys = [kv[:, h * HD : (h + 1) * HD] for kv in kvs]
    values = [kv[:, (KVH + h) * HD : (KVH + h + 1) * HD] for kv in kvs]
    return jnp.concatenate(keys, axis=0), jnp.concatenate(values, axis=0)


def dot_keys(queries, keys):
    return lax.dot_general(
        queries, keys, (((1,), (1,)), ((), ())), preferred_element_type=jnp.float32
    )


def out_copies(result, out, sems):
    width = GROUP * HD
    return [
        pltpu.make_async_copy(result.at[h], out.at[:, pl.ds(h * width, width)], sems.at[h])
        for h in range(KVH)
    ]


def attend_kernel(lengths, base, low, *rest):
    kvs, ups = rest[:3], rest[3:7]
    out, queries, sums, highs, counts, upper, result, sems = rest[7:]
    tokens = base.shape[0]
    rows = ups[0].shape[0]
    z = lax.axis_index("ctx")
    live = z * tokens < lengths[0]
    block = GROUP * tokens
    copies = out_copies(result, out, sems)

    @pl.when(jnp.logical_not(live))
    def _():
        result[...] = jnp.zeros_like(result)
        for copy in copies:
            copy.start()

    @pl.when(live)
    def _():
        for flip, piece in enumerate(ups):
            upper[pl.ds(pl.multiple_of((z ^ flip) * rows, rows), rows), :] = piece[...]

    query_pos = lax.broadcasted_iota(jnp.int32, (tokens, tokens), 0)
    key_pos = lax.broadcasted_iota(jnp.int32, (tokens, tokens), 1)
    causal = key_pos <= query_pos

    def scores_of(h, blocks):
        columns = slice(h * GROUP * HD, (h + 1) * GROUP * HD)
        delta = jnp.dot(low[...], upper[:, columns], preferred_element_type=jnp.float32)
        query = (base[:, columns].astype(jnp.float32) + delta).astype(jnp.bfloat16)
        query = [query[:, g * HD : (g + 1) * HD] for g in range(GROUP)]
        query = jnp.concatenate(query, axis=0)
        keys, values = head_columns(blocks, h)
        return query, dot_keys(query, keys), values

    for mine, needed in enumerate(((0,), (0, 1), (0, 2), (0, 1, 2))):

        @pl.when(live & (z == mine))
        def _():
            blocks = [kvs[i] for i in needed]
            ahead = scores_of(0, blocks)
            for h in range(KVH):
                query, scores, values = ahead
                if h + 1 < KVH:
                    ahead = scores_of(h + 1, blocks)
                weights, tops, totals = [], [], []
                for g in range(GROUP):
                    score = scores[g * tokens : (g + 1) * tokens, :]
                    own = jnp.where(causal, score[:, :tokens], -1e30)
                    if mine:
                        own = jnp.concatenate([own, score[:, tokens:]], axis=1)
                    tops.append(jnp.max(own, axis=1, keepdims=True))
                    weight = jnp.exp2((own - tops[g]) * FACTOR)
                    totals.append(jnp.sum(weight, axis=1, keepdims=True))
                    weights.append(weight.astype(jnp.bfloat16))
                product = jnp.dot(
                    jnp.concatenate(weights, axis=0), values, preferred_element_type=jnp.float32
                )
                if mine < 2:
                    for g in range(GROUP):
                        result[h, :, g * HD : (g + 1) * HD] = (
                            product[g * tokens : (g + 1) * tokens, :] / totals[g]
                        ).astype(jnp.bfloat16)
                    copies[h].start()
                else:
                    queries[h * block : (h + 1) * block, :] = query
                    sums[h * block : (h + 1) * block, :] = product
                    for g in range(GROUP):
                        at = slice(h * block + g * tokens, h * block + (g + 1) * tokens)
                        highs[at, :] = jnp.broadcast_to(tops[g], (tokens, HD))
                        counts[at, :] = jnp.broadcast_to(totals[g], (tokens, HD))

    @pl.when(jnp.logical_not(live) | (z < 2))
    def _():
        for copy in copies:
            copy.wait()


def attend(lengths, base, low, kvs, ups):
    tokens, width = base.shape
    rows = HEADS * tokens
    shapes = [
        jax.ShapeDtypeStruct(base.shape, jnp.bfloat16),
        jax.ShapeDtypeStruct((rows, HD), jnp.bfloat16),
    ] + [jax.ShapeDtypeStruct((rows, HD), jnp.float32)] * 3
    return pl.pallas_call(
        attend_kernel,
        out_shape=shapes,
        in_specs=[spec(SMEM)] + [spec(VMEM)] * (2 + len(kvs) + len(ups)),
        out_specs=[spec(HBM)] + [spec(VMEM)] * 4,
        scratch_shapes=[
            VMEM((low.shape[1], width), jnp.bfloat16),
            VMEM((KVH, tokens, GROUP * HD), jnp.bfloat16),
            pltpu.SemaphoreType.DMA((KVH,)),
        ],
        compiler_params=PARAMS,
        cost_estimate=pl.CostEstimate(
            flops=1 << 30, bytes_accessed=1 << 22, transcendentals=1 << 21
        ),
    )(lengths, base, low, *kvs, *ups)


def finish_kernel(lengths, so_far, queries, sums, highs, counts, kv, out, result, sems, *, heads):
    del so_far
    tokens = result.shape[1]
    z = lax.axis_index("ctx")
    block = GROUP * tokens
    copies = out_copies(result, out, sems)

    @pl.when((z * tokens < lengths[0]) & (z >= 2))
    def _():
        for i, h in enumerate(heads):
            keys = kv[:, i * HD : (i + 1) * HD]
            values = kv[:, (len(heads) + i) * HD : (len(heads) + i + 1) * HD]
            scores = dot_keys(queries[h * block : (h + 1) * block, :], keys)
            weights, factors, totals = [], [], []
            for g in range(GROUP):
                at = slice(h * block + g * tokens, h * block + (g + 1) * tokens)
                score = scores[g * tokens : (g + 1) * tokens, :]
                newest = jnp.maximum(highs[at, :], jnp.max(score, axis=1, keepdims=True))
                weight = jnp.exp2((score - newest) * FACTOR)
                factors.append(jnp.exp2((highs[at, :] - newest) * FACTOR))
                added = jnp.sum(weight, axis=1, keepdims=True)
                totals.append(counts[at, :] * factors[g] + added)
                weights.append(weight.astype(jnp.bfloat16))
            product = jnp.dot(
                jnp.concatenate(weights, axis=0), values, preferred_element_type=jnp.float32
            )
            for g in range(GROUP):
                at = slice(h * block + g * tokens, h * block + (g + 1) * tokens)
                whole = sums[at, :] * factors[g] + product[g * tokens : (g + 1) * tokens, :]
                result[h, :, g * HD : (g + 1) * HD] = (whole / totals[g]).astype(jnp.bfloat16)
            copies[h].start()
        for h in heads:
            copies[h].wait()


def finish(lengths, so_far, queries, sums, highs, counts, kv, heads):
    tokens = so_far.shape[0]
    return pl.pallas_call(
        functools.partial(finish_kernel, heads=heads),
        out_shape=jax.ShapeDtypeStruct(so_far.shape, so_far.dtype),
        in_specs=[spec(SMEM), spec(HBM)] + [spec(VMEM)] * 5,
        out_specs=spec(HBM),
        input_output_aliases={1: 0},
        scratch_shapes=[
            VMEM((KVH, tokens, GROUP * HD), jnp.bfloat16),
            pltpu.SemaphoreType.DMA((KVH,)),
        ],
        compiler_params=PARAMS,
        cost_estimate=pl.CostEstimate(
            flops=1 << 28, bytes_accessed=1 << 21, transcendentals=1 << 19
        ),
    )(lengths, so_far, queries, sums, highs, counts, kv)


def pick_heads(kv, heads):
    columns = [h for h in heads] + [KVH + h for h in heads]
    return jnp.concatenate([kv[:, c * HD : (c + 1) * HD] for c in columns], axis=1)


def body(
    hidden_states,
    queries_base,
    kv_base,
    adapter_down,
    adapter_up,
    adapter_ids,
    adapter_slots,
    rank_buckets,
    lengths,
):
    keep_down, give_down, keep_up, give_up = select(
        adapter_ids, adapter_slots, adapter_down, adapter_up
    )
    kv = kv_base[0]
    kv_one, kv_two = spread(kv)
    near_down = lax.ppermute(give_down, "req", SIBLING)
    near_up = lax.ppermute(give_up, "req", SIBLING)
    far_down = lax.ppermute(keep_down[1] + near_down[1], "req", ACROSS)
    far_up = lax.ppermute(keep_up[1] + near_up[1], "req", ACROSS)
    down = keep_down[0] + near_down[0] + far_down
    down, kv_one = lax.optimization_barrier((down, kv_one))
    down_one, down_two = spread(down)
    up = keep_up[0] + near_up[0] + far_up
    up_one, up_two = spread(up)
    down_two = lax.optimization_barrier((down_two, kv_two))[0]
    down_three = lax.ppermute(down_two, "ctx", ONE)
    up_two = lax.optimization_barrier((up_two, down_one))[0]
    up_three = lax.ppermute(up_two, "ctx", ONE)
    kv_last = lax.optimization_barrier((kv_two, down_one))[0]
    kv_last = [pick_heads(kv_last, heads) for heads in ((0, 1), (2,))]
    kv_last = lax.optimization_barrier((*kv_last, up_two, up_one))[:2]
    kv_three = [lax.ppermute(part, "ctx", LAST) for part in kv_last]
    downs = [down, down_one, down_two, down_three]
    ups = [up, up_one, up_two, up_three]
    low = low_rank(adapter_ids, rank_buckets, hidden_states[0], downs)
    parts = attend(lengths, queries_base[0], low, [kv, kv_one, kv_two], ups)
    output, *state = parts
    for part, heads in zip(kv_three, ((0, 1), (2,))):
        output = finish(lengths, output, *state, part, heads)
    return output[None]


def plain_body(
    hidden_states,
    queries_base,
    kv_base,
    adapter_down,
    adapter_up,
    adapter_ids,
    adapter_slots,
    rank_buckets,
    lengths,
):
    req_index = lax.axis_index("req")
    ctx_index = lax.axis_index("ctx")
    per_shard = adapter_down.shape[0]
    requests = adapter_ids.shape[0]
    store = adapter_slots.shape[0]
    rank_width = adapter_down.shape[2]
    tokens = hidden_states.shape[1]
    query_width = queries_base.shape[2]
    store_range = jnp.arange(store, dtype=jnp.int32)
    chosen = adapter_ids[:, None] == store_range[None, :]
    slot_of = jnp.sum(jnp.where(chosen, adapter_slots[None, :], 0), axis=1)
    rank_of = jnp.sum(jnp.where(chosen, rank_buckets[None, :], 0), axis=1)
    mine = jnp.arange(requests, dtype=jnp.int32) == req_index
    my_slot = jnp.sum(jnp.where(mine, slot_of, 0))
    my_rank = jnp.sum(jnp.where(mine, rank_of, 0))
    held = (
        slot_of[:, None] == req_index * per_shard + jnp.arange(per_shard, dtype=jnp.int32)[None, :]
    )
    select = held.astype(jnp.bfloat16)
    send_down = jnp.einsum(
        "qa,ard->qrd", select, adapter_down, preferred_element_type=jnp.float32
    ).astype(jnp.bfloat16)
    send_up = jnp.einsum(
        "qa,ard->qrd", select, adapter_up, preferred_element_type=jnp.float32
    ).astype(jnp.bfloat16)
    got_down, got_up = (
        lax.all_to_all(send_down, "req", split_axis=0, concat_axis=0, tiled=True),
        lax.all_to_all(send_up, "req", split_axis=0, concat_axis=0, tiled=True),
    )
    owner = my_slot // per_shard
    down_mine = lax.dynamic_index_in_dim(got_down, owner, 0, keepdims=False)
    up_mine = lax.dynamic_index_in_dim(got_up, owner, 0, keepdims=False)
    features = hidden_states[0]
    columns = features
    low_rank = jnp.dot(
        columns,
        lax.all_gather(down_mine, "ctx", axis=0, tiled=True),
        preferred_element_type=jnp.float32,
    )
    low_rank = jnp.where(
        jnp.arange(rank_width, dtype=jnp.int32)[None, :] < my_rank, low_rank, 0.0
    ).astype(jnp.bfloat16)
    columns = low_rank
    delta = jnp.dot(
        columns,
        lax.all_gather(up_mine, "ctx", axis=0, tiled=True),
        preferred_element_type=jnp.float32,
    )
    queries = (
        (queries_base[0].astype(jnp.float32) + delta)
        .astype(jnp.bfloat16)
        .reshape(tokens, KVH, GROUP, HD)
    )
    length = lengths[0]
    first_query = ctx_index * tokens
    query_pos = first_query + jnp.arange(tokens, dtype=jnp.int32)
    last_needed = jnp.minimum(first_query + tokens - 1, length - 1)
    scale = 1.0 / math.sqrt(HD)
    key_width = KVH * HD
    initial = (
        jnp.full((KVH, GROUP, tokens), -1e30, jnp.float32),
        jnp.zeros((KVH, GROUP, tokens), jnp.float32),
        jnp.zeros((KVH, GROUP, tokens, HD), jnp.float32),
    )
    piece = lax.all_gather(kv_base[0], "ctx", axis=0, tiled=True)
    count = piece.shape[0]
    width = math.gcd(count, 512)

    def key_block(index, state):
        largest, total, accum = state
        offset = index * width
        rows = lax.dynamic_slice_in_dim(piece, offset, width, 0)
        keys = rows[:, :key_width].reshape(width, KVH, HD)
        values = rows[:, key_width:].reshape(width, KVH, HD)
        key_pos = offset + jnp.arange(width, dtype=jnp.int32)
        score = (
            jnp.einsum("tkgd,skd->kgts", queries, keys, preferred_element_type=jnp.float32) * scale
        )
        allowed = (key_pos[None, :] <= query_pos[:, None]) & (key_pos[None, :] < length)
        masked = jnp.where(allowed, score, -1e30)
        newest = jnp.maximum(largest, jnp.max(masked, axis=-1))
        weight = jnp.where(allowed, jnp.exp(score - newest[..., None]), 0.0)
        factor = jnp.exp(largest - newest)
        total = total * factor + jnp.sum(weight, axis=-1)
        product = jnp.einsum(
            "kgts,skd->kgtd",
            weight.astype(jnp.bfloat16),
            values,
            preferred_element_type=jnp.float32,
        )
        accum = accum * factor[..., None] + product
        return (newest, total, accum)

    def compute(state):
        return lax.fori_loop(0, count // width, key_block, state)

    needed = (jnp.int32(0) <= last_needed) & (first_query < length)
    largest, total, accum = lax.cond(needed, compute, lambda state: state, initial)
    safe_total = jnp.where(total > 0.0, total, 1.0)
    output = accum / safe_total[..., None]
    output = jnp.transpose(output, (2, 0, 1, 3)).reshape(tokens, query_width)
    output = jnp.where(query_pos[:, None] < length, output, 0.0).astype(jnp.bfloat16)
    return output[None]


def solution(mesh):
    paired = mesh.shape["ctx"] == 4 and mesh.shape["req"] == 4
    return jax.shard_map(
        body if paired else plain_body,
        mesh=mesh,
        in_specs=(
            P(("group", "req"), "ctx", None),
            P(("group", "req"), "ctx", None),
            P(("group", "req"), "ctx", None),
            P(("group", "req"), "ctx", None),
            P(("group", "req"), "ctx", None),
            P("group"),
            P("group"),
            P("group"),
            P(("group", "req")),
        ),
        out_specs=P(("group", "req"), "ctx", None),
        check_vma=False,
    )
```

```python
import functools
import math

import jax
import jax.numpy as jnp
from jax import lax
from jax.experimental import pallas as pl
from jax.experimental.pallas import tpu as pltpu
from jax.sharding import PartitionSpec as P

HD = 128
KVH = 3
GROUP = 7
HEADS = KVH * GROUP
SMEM = pltpu.SMEM
VMEM = pltpu.VMEM
HBM = pltpu.HBM
LOG2E = 1.0 / math.log(2.0)
PARAMS = pltpu.CompilerParams(vmem_limit_bytes=32 * 1024 * 1024)
WHOLE = pltpu.CompilerParams(vmem_limit_bytes=52 * 1024 * 1024)


def spec(space):
    return pl.BlockSpec(memory_space=space)


def select_kernel(table, *rest, requests):
    stores, outs, sems = rest[:2], rest[2:6], rest[6]
    per_shard = stores[0].shape[0]
    me = lax.axis_index("req")
    first = me * per_shard
    copies = []
    for i, flip in enumerate((0, 2, 1, 3)):
        local = table[requests + table[me ^ flip]] - first
        held = (local >= 0) & (local < per_shard)
        for f, store in enumerate(stores):
            out = outs[2 * f + i // 2]
            copies.append((held, local, store, out, i % 2, sems.at[4 * f + i]))
    for held, local, store, out, k, sem in copies:

        @pl.when(held)
        def _():
            pltpu.make_async_copy(store.at[local], out.at[k], sem).start()

    for held, local, store, out, k, sem in copies:

        @pl.when(jnp.logical_not(held))
        def _():
            out[k] = jnp.zeros(out.shape[1:], out.dtype)

    for held, local, store, out, k, sem in copies:

        @pl.when(held)
        def _():
            pltpu.make_async_copy(store.at[local], out.at[k], sem).wait()


def select(ids, slots, down, up):
    shapes = [jax.ShapeDtypeStruct((2, *x.shape[1:]), x.dtype) for x in (down, down, up, up)]
    return pl.pallas_call(
        functools.partial(select_kernel, requests=ids.shape[0]),
        out_shape=shapes,
        in_specs=[spec(SMEM), spec(HBM), spec(HBM)],
        out_specs=[spec(VMEM)] * 4,
        scratch_shapes=[pltpu.SemaphoreType.DMA((8,))],
        compiler_params=WHOLE,
    )(jnp.concatenate([ids, slots]), down, up)


SIBLING = [(0, 1), (1, 0), (2, 3), (3, 2)]
ACROSS = [(0, 2), (1, 3), (2, 0), (3, 1)]
ONE = [(i, i ^ 1) for i in range(4)]
TWO = [(i, i ^ 2) for i in range(4)]
LAST = [(0, 0), (1, 1), (2, 3), (3, 2)]
INWARD = [(0, 1), (3, 2)]
OUTWARD = [(1, 0), (2, 3)]


def spread(shard):
    return lax.ppermute(shard, "ctx", ONE), lax.ppermute(shard, "ctx", TWO)


def product_kernel(features, piece, out):
    out[...] = jnp.dot(features[...], piece[...], preferred_element_type=jnp.float32)


def product(features, piece):
    return pl.pallas_call(
        product_kernel,
        out_shape=jax.ShapeDtypeStruct((features.shape[0], piece.shape[1]), jnp.float32),
        in_specs=[spec(VMEM)] * 2,
        out_specs=spec(VMEM),
        compiler_params=PARAMS,
        cost_estimate=pl.CostEstimate(flops=1 << 25, bytes_accessed=1 << 19, transcendentals=0),
    )(features, piece)


def low_rank_kernel(ids, ranks, hidden, partial, *rest):
    pieces, out = rest[:-1], rest[-1]
    rows = pieces[0].shape[0]
    rank = ranks[ids[lax.axis_index("req")]]
    total = partial[...]
    for flip, piece in enumerate(pieces):
        place = lax.axis_index("ctx") ^ flip
        columns = pl.ds(pl.multiple_of(place * rows, HD), rows)
        total += jnp.dot(hidden[:, columns], piece[...], preferred_element_type=jnp.float32)
    column = lax.broadcasted_iota(jnp.int32, total.shape, 1)
    out[...] = jnp.where(column < rank, total, 0.0).astype(jnp.bfloat16)


def low_rank(ids, ranks, hidden, partial, pieces):
    return pl.pallas_call(
        low_rank_kernel,
        out_shape=jax.ShapeDtypeStruct(partial.shape, jnp.bfloat16),
        in_specs=[spec(SMEM)] * 2 + [spec(VMEM)] * (2 + len(pieces)),
        out_specs=spec(VMEM),
        compiler_params=PARAMS,
        cost_estimate=pl.CostEstimate(flops=1 << 27, bytes_accessed=1 << 22, transcendentals=0),
    )(ids, ranks, hidden, partial, *pieces)


FACTOR = LOG2E / math.sqrt(HD)


def head_columns(kvs, h):
    keys = [kv[:, h * HD : (h + 1) * HD] for kv in kvs]
    values = [kv[:, (KVH + h) * HD : (KVH + h + 1) * HD] for kv in kvs]
    return jnp.concatenate(keys, axis=0), jnp.concatenate(values, axis=0)


def dot_keys(queries, keys):
    return lax.dot_general(
        queries, keys, (((1,), (1,)), ((), ())), preferred_element_type=jnp.float32
    )


def out_copies(result, out, sems):
    width = GROUP * HD
    return [
        pltpu.make_async_copy(result.at[h], out.at[:, pl.ds(h * width, width)], sems.at[h])
        for h in range(KVH)
    ]


def attend_kernel(lengths, base, low, *rest):
    kvs, ups = rest[:3], rest[3:7]
    out, queries, sums, highs, counts, upper, result, sems = rest[7:]
    tokens = base.shape[0]
    rows = ups[0].shape[0]
    z = lax.axis_index("ctx")
    live = z * tokens < lengths[0]
    block = GROUP * tokens
    copies = out_copies(result, out, sems)

    @pl.when(jnp.logical_not(live))
    def _():
        result[...] = jnp.zeros_like(result)
        for copy in copies:
            copy.start()

    @pl.when(live)
    def _():
        for flip, piece in enumerate(ups):
            upper[pl.ds(pl.multiple_of((z ^ flip) * rows, rows), rows), :] = piece[...]

    query_pos = lax.broadcasted_iota(jnp.int32, (tokens, tokens), 0)
    key_pos = lax.broadcasted_iota(jnp.int32, (tokens, tokens), 1)
    causal = key_pos <= query_pos

    def scores_of(h, blocks):
        columns = slice(h * GROUP * HD, (h + 1) * GROUP * HD)
        delta = jnp.dot(low[...], upper[:, columns], preferred_element_type=jnp.float32)
        query = (base[:, columns].astype(jnp.float32) + delta).astype(jnp.bfloat16)
        query = [query[:, g * HD : (g + 1) * HD] for g in range(GROUP)]
        query = jnp.concatenate(query, axis=0)
        keys, values = head_columns(blocks, h)
        return query, dot_keys(query, keys), values

    for mine, needed in enumerate(((0,), (0, 1), (0, 2), (0, 1, 2))):

        @pl.when(live & (z == mine))
        def _():
            blocks = [kvs[i] for i in needed]
            ahead = scores_of(0, blocks)
            for h in range(KVH):
                query, scores, values = ahead
                if h + 1 < KVH:
                    ahead = scores_of(h + 1, blocks)
                weights, tops, totals = [], [], []
                for g in range(GROUP):
                    score = scores[g * tokens : (g + 1) * tokens, :]
                    own = jnp.where(causal, score[:, :tokens], -1e30)
                    if mine:
                        own = jnp.concatenate([own, score[:, tokens:]], axis=1)
                    tops.append(jnp.max(own, axis=1, keepdims=True))
                    weight = jnp.exp2((own - tops[g]) * FACTOR)
                    totals.append(jnp.sum(weight, axis=1, keepdims=True))
                    weights.append(weight.astype(jnp.bfloat16))
                product = jnp.dot(
                    jnp.concatenate(weights, axis=0), values, preferred_element_type=jnp.float32
                )
                if mine < 2:
                    for g in range(GROUP):
                        result[h, :, g * HD : (g + 1) * HD] = (
                            product[g * tokens : (g + 1) * tokens, :] / totals[g]
                        ).astype(jnp.bfloat16)
                    copies[h].start()
                else:
                    queries[h * block : (h + 1) * block, :] = query
                    sums[h * block : (h + 1) * block, :] = product
                    for g in range(GROUP):
                        at = slice(h * block + g * tokens, h * block + (g + 1) * tokens)
                        highs[at, :] = jnp.broadcast_to(tops[g], (tokens, HD))
                        counts[at, :] = jnp.broadcast_to(totals[g], (tokens, HD))

    @pl.when(jnp.logical_not(live) | (z < 2))
    def _():
        for copy in copies:
            copy.wait()


def attend(lengths, base, low, kvs, ups):
    tokens, width = base.shape
    rows = HEADS * tokens
    shapes = [
        jax.ShapeDtypeStruct(base.shape, jnp.bfloat16),
        jax.ShapeDtypeStruct((rows, HD), jnp.bfloat16),
    ] + [jax.ShapeDtypeStruct((rows, HD), jnp.float32)] * 3
    return pl.pallas_call(
        attend_kernel,
        out_shape=shapes,
        in_specs=[spec(SMEM)] + [spec(VMEM)] * (2 + len(kvs) + len(ups)),
        out_specs=[spec(HBM)] + [spec(VMEM)] * 4,
        scratch_shapes=[
            VMEM((low.shape[1], width), jnp.bfloat16),
            VMEM((KVH, tokens, GROUP * HD), jnp.bfloat16),
            pltpu.SemaphoreType.DMA((KVH,)),
        ],
        compiler_params=PARAMS,
        cost_estimate=pl.CostEstimate(
            flops=1 << 30, bytes_accessed=1 << 22, transcendentals=1 << 21
        ),
    )(lengths, base, low, *kvs, *ups)


def finish_kernel(lengths, so_far, queries, sums, highs, counts, kv, out, result, sems):
    del so_far
    tokens = result.shape[1]
    z = lax.axis_index("ctx")
    block = GROUP * tokens
    copies = out_copies(result, out, sems)

    @pl.when((z * tokens < lengths[0]) & (z >= 2))
    def _():
        for h in range(KVH):
            keys, values = head_columns([kv], h)
            scores = dot_keys(queries[h * block : (h + 1) * block, :], keys)
            weights, factors, totals = [], [], []
            for g in range(GROUP):
                at = slice(h * block + g * tokens, h * block + (g + 1) * tokens)
                score = scores[g * tokens : (g + 1) * tokens, :]
                newest = jnp.maximum(highs[at, :], jnp.max(score, axis=1, keepdims=True))
                weight = jnp.exp2((score - newest) * FACTOR)
                factors.append(jnp.exp2((highs[at, :] - newest) * FACTOR))
                added = jnp.sum(weight, axis=1, keepdims=True)
                totals.append(counts[at, :] * factors[g] + added)
                weights.append(weight.astype(jnp.bfloat16))
            product = jnp.dot(
                jnp.concatenate(weights, axis=0), values, preferred_element_type=jnp.float32
            )
            for g in range(GROUP):
                at = slice(h * block + g * tokens, h * block + (g + 1) * tokens)
                whole = sums[at, :] * factors[g] + product[g * tokens : (g + 1) * tokens, :]
                result[h, :, g * HD : (g + 1) * HD] = (whole / totals[g]).astype(jnp.bfloat16)
            copies[h].start()
        for copy in copies:
            copy.wait()


def finish(lengths, so_far, queries, sums, highs, counts, kv):
    tokens = so_far.shape[0]
    return pl.pallas_call(
        finish_kernel,
        out_shape=jax.ShapeDtypeStruct(so_far.shape, so_far.dtype),
        in_specs=[spec(SMEM), spec(HBM)] + [spec(VMEM)] * 5,
        out_specs=spec(HBM),
        input_output_aliases={1: 0},
        scratch_shapes=[
            VMEM((KVH, tokens, GROUP * HD), jnp.bfloat16),
            pltpu.SemaphoreType.DMA((KVH,)),
        ],
        compiler_params=PARAMS,
        cost_estimate=pl.CostEstimate(
            flops=1 << 28, bytes_accessed=1 << 21, transcendentals=1 << 19
        ),
    )(lengths, so_far, queries, sums, highs, counts, kv)


def body(
    hidden_states,
    queries_base,
    kv_base,
    adapter_down,
    adapter_up,
    adapter_ids,
    adapter_slots,
    rank_buckets,
    lengths,
):
    keep_down, give_down, keep_up, give_up = select(
        adapter_ids, adapter_slots, adapter_down, adapter_up
    )
    kv, hidden = kv_base[0], hidden_states[0]
    kv_one, kv_two = spread(kv)
    near_down = lax.ppermute(give_down, "req", SIBLING)
    near_up = lax.ppermute(give_up, "req", SIBLING)
    far_down = lax.ppermute(keep_down[1] + near_down[1], "req", ACROSS)
    pass_up, early = lax.optimization_barrier((keep_up[1] + near_up[1], hidden))
    far_up = lax.ppermute(pass_up, "req", ACROSS)
    rows = adapter_down.shape[1]
    start = (lax.axis_index("ctx") ^ 1) * rows
    features = lax.ppermute(lax.dynamic_slice_in_dim(early, start, rows, 1), "ctx", INWARD)
    down = keep_down[0] + near_down[0] + far_down
    down, kv_one = lax.optimization_barrier((down, kv_one))
    down_one = lax.ppermute(down, "ctx", INWARD)
    down_two = lax.ppermute(down, "ctx", TWO)
    mine = product(features, down)
    partial = lax.ppermute(mine, "ctx", OUTWARD)
    up = keep_up[0] + near_up[0] + far_up
    up_one, up_two = spread(up)
    ready = lax.optimization_barrier((down_two, kv_two))[0]
    down_three = lax.ppermute(ready, "ctx", ONE)
    ready = lax.optimization_barrier((up_two, down_one, partial))[0]
    up_three = lax.ppermute(ready, "ctx", ONE)
    kv_last = lax.optimization_barrier((kv_two, up_two, up_one))[0]
    kv_three = lax.ppermute(kv_last, "ctx", LAST)
    downs = [down, down_one, down_two, down_three]
    ups = [up, up_one, up_two, up_three]
    low = low_rank(adapter_ids, rank_buckets, hidden, partial, downs)
    parts = attend(lengths, queries_base[0], low, [kv, kv_one, kv_two], ups)
    return finish(lengths, *parts, kv_three)[None]


def plain_body(
    hidden_states,
    queries_base,
    kv_base,
    adapter_down,
    adapter_up,
    adapter_ids,
    adapter_slots,
    rank_buckets,
    lengths,
):
    req_index = lax.axis_index("req")
    ctx_index = lax.axis_index("ctx")
    per_shard = adapter_down.shape[0]
    requests = adapter_ids.shape[0]
    store = adapter_slots.shape[0]
    rank_width = adapter_down.shape[2]
    tokens = hidden_states.shape[1]
    query_width = queries_base.shape[2]
    store_range = jnp.arange(store, dtype=jnp.int32)
    chosen = adapter_ids[:, None] == store_range[None, :]
    slot_of = jnp.sum(jnp.where(chosen, adapter_slots[None, :], 0), axis=1)
    rank_of = jnp.sum(jnp.where(chosen, rank_buckets[None, :], 0), axis=1)
    mine = jnp.arange(requests, dtype=jnp.int32) == req_index
    my_slot = jnp.sum(jnp.where(mine, slot_of, 0))
    my_rank = jnp.sum(jnp.where(mine, rank_of, 0))
    held = (
        slot_of[:, None] == req_index * per_shard + jnp.arange(per_shard, dtype=jnp.int32)[None, :]
    )
    select = held.astype(jnp.bfloat16)
    send_down = jnp.einsum(
        "qa,ard->qrd", select, adapter_down, preferred_element_type=jnp.float32
    ).astype(jnp.bfloat16)
    send_up = jnp.einsum(
        "qa,ard->qrd", select, adapter_up, preferred_element_type=jnp.float32
    ).astype(jnp.bfloat16)
    got_down, got_up = (
        lax.all_to_all(send_down, "req", split_axis=0, concat_axis=0, tiled=True),
        lax.all_to_all(send_up, "req", split_axis=0, concat_axis=0, tiled=True),
    )
    owner = my_slot // per_shard
    down_mine = lax.dynamic_index_in_dim(got_down, owner, 0, keepdims=False)
    up_mine = lax.dynamic_index_in_dim(got_up, owner, 0, keepdims=False)
    features = hidden_states[0]
    columns = features
    low_rank = jnp.dot(
        columns,
        lax.all_gather(down_mine, "ctx", axis=0, tiled=True),
        preferred_element_type=jnp.float32,
    )
    low_rank = jnp.where(
        jnp.arange(rank_width, dtype=jnp.int32)[None, :] < my_rank, low_rank, 0.0
    ).astype(jnp.bfloat16)
    columns = low_rank
    delta = jnp.dot(
        columns,
        lax.all_gather(up_mine, "ctx", axis=0, tiled=True),
        preferred_element_type=jnp.float32,
    )
    queries = (
        (queries_base[0].astype(jnp.float32) + delta)
        .astype(jnp.bfloat16)
        .reshape(tokens, KVH, GROUP, HD)
    )
    length = lengths[0]
    first_query = ctx_index * tokens
    query_pos = first_query + jnp.arange(tokens, dtype=jnp.int32)
    last_needed = jnp.minimum(first_query + tokens - 1, length - 1)
    scale = 1.0 / math.sqrt(HD)
    key_width = KVH * HD
    initial = (
        jnp.full((KVH, GROUP, tokens), -1e30, jnp.float32),
        jnp.zeros((KVH, GROUP, tokens), jnp.float32),
        jnp.zeros((KVH, GROUP, tokens, HD), jnp.float32),
    )
    piece = lax.all_gather(kv_base[0], "ctx", axis=0, tiled=True)
    count = piece.shape[0]
    width = math.gcd(count, 512)

    def key_block(index, state):
        largest, total, accum = state
        offset = index * width
        rows = lax.dynamic_slice_in_dim(piece, offset, width, 0)
        keys = rows[:, :key_width].reshape(width, KVH, HD)
        values = rows[:, key_width:].reshape(width, KVH, HD)
        key_pos = offset + jnp.arange(width, dtype=jnp.int32)
        score = (
            jnp.einsum("tkgd,skd->kgts", queries, keys, preferred_element_type=jnp.float32) * scale
        )
        allowed = (key_pos[None, :] <= query_pos[:, None]) & (key_pos[None, :] < length)
        masked = jnp.where(allowed, score, -1e30)
        newest = jnp.maximum(largest, jnp.max(masked, axis=-1))
        weight = jnp.where(allowed, jnp.exp(score - newest[..., None]), 0.0)
        factor = jnp.exp(largest - newest)
        total = total * factor + jnp.sum(weight, axis=-1)
        product = jnp.einsum(
            "kgts,skd->kgtd",
            weight.astype(jnp.bfloat16),
            values,
            preferred_element_type=jnp.float32,
        )
        accum = accum * factor[..., None] + product
        return (newest, total, accum)

    def compute(state):
        return lax.fori_loop(0, count // width, key_block, state)

    needed = (jnp.int32(0) <= last_needed) & (first_query < length)
    largest, total, accum = lax.cond(needed, compute, lambda state: state, initial)
    safe_total = jnp.where(total > 0.0, total, 1.0)
    output = accum / safe_total[..., None]
    output = jnp.transpose(output, (2, 0, 1, 3)).reshape(tokens, query_width)
    output = jnp.where(query_pos[:, None] < length, output, 0.0).astype(jnp.bfloat16)
    return output[None]


def solution(mesh):
    paired = mesh.shape["ctx"] == 4 and mesh.shape["req"] == 4
    return jax.shard_map(
        body if paired else plain_body,
        mesh=mesh,
        in_specs=(
            P(("group", "req"), "ctx", None),
            P(("group", "req"), "ctx", None),
            P(("group", "req"), "ctx", None),
            P(("group", "req"), "ctx", None),
            P(("group", "req"), "ctx", None),
            P("group"),
            P("group"),
            P("group"),
            P(("group", "req")),
        ),
        out_specs=P(("group", "req"), "ctx", None),
        check_vma=False,
    )
```

```python
import functools
import math

import jax
import jax.numpy as jnp
from jax import lax
from jax.experimental import pallas as pl
from jax.experimental.pallas import tpu as pltpu
from jax.sharding import PartitionSpec as P

HD = 128
KVH = 3
GROUP = 7
HEADS = KVH * GROUP
SMEM = pltpu.SMEM
VMEM = pltpu.VMEM
HBM = pltpu.HBM
LOG2E = 1.0 / math.log(2.0)
PARAMS = pltpu.CompilerParams(vmem_limit_bytes=32 * 1024 * 1024)
WHOLE = pltpu.CompilerParams(vmem_limit_bytes=52 * 1024 * 1024)


def spec(space):
    return pl.BlockSpec(memory_space=space)


def select_kernel(table, *rest, requests):
    stores, outs, sems = rest[:2], rest[2:6], rest[6]
    per_shard = stores[0].shape[0]
    me = lax.axis_index("req")
    first = me * per_shard
    copies = []
    for i, flip in enumerate((0, 2, 1, 3)):
        local = table[requests + table[me ^ flip]] - first
        held = (local >= 0) & (local < per_shard)
        for f, store in enumerate(stores):
            out = outs[2 * f + i // 2]
            copies.append((held, local, store, out, i % 2, sems.at[4 * f + i]))
    for held, local, store, out, k, sem in copies:

        @pl.when(held)
        def _():
            pltpu.make_async_copy(store.at[local], out.at[k], sem).start()

    for held, local, store, out, k, sem in copies:

        @pl.when(jnp.logical_not(held))
        def _():
            out[k] = jnp.zeros(out.shape[1:], out.dtype)

    for held, local, store, out, k, sem in copies:

        @pl.when(held)
        def _():
            pltpu.make_async_copy(store.at[local], out.at[k], sem).wait()


def select(ids, slots, down, up):
    shapes = [jax.ShapeDtypeStruct((2, *x.shape[1:]), x.dtype) for x in (down, down, up, up)]
    return pl.pallas_call(
        functools.partial(select_kernel, requests=ids.shape[0]),
        out_shape=shapes,
        in_specs=[spec(SMEM), spec(HBM), spec(HBM)],
        out_specs=[spec(VMEM)] * 4,
        scratch_shapes=[pltpu.SemaphoreType.DMA((8,))],
        compiler_params=WHOLE,
    )(jnp.concatenate([ids, slots]), down, up)


SIBLING = [(0, 1), (1, 0), (2, 3), (3, 2)]
ACROSS = [(0, 2), (1, 3), (2, 0), (3, 1)]
ONE = [(i, i ^ 1) for i in range(4)]
TWO = [(i, i ^ 2) for i in range(4)]
LAST = [(0, 0), (1, 1), (2, 3), (3, 2)]


def spread(shard):
    return lax.ppermute(shard, "ctx", ONE), lax.ppermute(shard, "ctx", TWO)


def low_rank_kernel(ids, ranks, hidden, *rest):
    pieces, out, accum = rest[:-2], rest[-2], rest[-1]
    rows = pieces[0].shape[0]
    rank = ranks[ids[lax.axis_index("req")]]
    accum[...] = jnp.zeros_like(accum)
    for flip, piece in enumerate(pieces):
        place = lax.axis_index("ctx") ^ flip
        columns = pl.ds(pl.multiple_of(place * rows, HD), rows)
        accum[...] += jnp.dot(hidden[:, columns], piece[...], preferred_element_type=jnp.float32)

    column = lax.broadcasted_iota(jnp.int32, accum.shape, 1)
    out[...] = jnp.where(column < rank, accum[...], 0.0).astype(jnp.bfloat16)


def low_rank(ids, ranks, hidden, pieces):
    shape = (hidden.shape[0], pieces[0].shape[1])
    return pl.pallas_call(
        low_rank_kernel,
        out_shape=jax.ShapeDtypeStruct(shape, jnp.bfloat16),
        in_specs=[spec(SMEM)] * 2 + [spec(VMEM)] * (1 + len(pieces)),
        out_specs=spec(VMEM),
        scratch_shapes=[VMEM(shape, jnp.float32)],
        compiler_params=PARAMS,
        cost_estimate=pl.CostEstimate(flops=1 << 27, bytes_accessed=1 << 22, transcendentals=0),
    )(ids, ranks, hidden, *pieces)


FACTOR = LOG2E / math.sqrt(HD)


def head_columns(kvs, h):
    keys = [kv[:, h * HD : (h + 1) * HD] for kv in kvs]
    values = [kv[:, (KVH + h) * HD : (KVH + h + 1) * HD] for kv in kvs]
    return jnp.concatenate(keys, axis=0), jnp.concatenate(values, axis=0)


def dot_keys(queries, keys):
    return lax.dot_general(
        queries, keys, (((1,), (1,)), ((), ())), preferred_element_type=jnp.float32
    )


def out_copies(result, out, sems):
    width = GROUP * HD
    return [
        pltpu.make_async_copy(result.at[h], out.at[:, pl.ds(h * width, width)], sems.at[h])
        for h in range(KVH)
    ]


def attend_kernel(lengths, base, low, *rest):
    kvs, ups = rest[:3], rest[3:7]
    out, queries, sums, highs, counts, upper, result, sems = rest[7:]
    tokens = base.shape[0]
    rows = ups[0].shape[0]
    z = lax.axis_index("ctx")
    live = z * tokens < lengths[0]
    block = GROUP * tokens
    copies = out_copies(result, out, sems)

    @pl.when(jnp.logical_not(live))
    def _():
        result[...] = jnp.zeros_like(result)
        for copy in copies:
            copy.start()

    @pl.when(live)
    def _():
        for flip, piece in enumerate(ups):
            upper[pl.ds(pl.multiple_of((z ^ flip) * rows, rows), rows), :] = piece[...]

    query_pos = lax.broadcasted_iota(jnp.int32, (tokens, tokens), 0)
    key_pos = lax.broadcasted_iota(jnp.int32, (tokens, tokens), 1)
    causal = key_pos <= query_pos

    def scores_of(h, blocks):
        columns = slice(h * GROUP * HD, (h + 1) * GROUP * HD)
        delta = jnp.dot(low[...], upper[:, columns], preferred_element_type=jnp.float32)
        query = (base[:, columns].astype(jnp.float32) + delta).astype(jnp.bfloat16)
        query = [query[:, g * HD : (g + 1) * HD] for g in range(GROUP)]
        query = jnp.concatenate(query, axis=0)
        keys, values = head_columns(blocks, h)
        return query, dot_keys(query, keys), values

    for mine, needed in enumerate(((0,), (0, 1), (0, 2), (0, 1, 2))):

        @pl.when(live & (z == mine))
        def _():
            blocks = [kvs[i] for i in needed]
            ahead = scores_of(0, blocks)
            for h in range(KVH):
                query, scores, values = ahead
                if h + 1 < KVH:
                    ahead = scores_of(h + 1, blocks)
                weights, tops, totals = [], [], []
                for g in range(GROUP):
                    score = scores[g * tokens : (g + 1) * tokens, :]
                    own = jnp.where(causal, score[:, :tokens], -1e30)
                    if mine:
                        own = jnp.concatenate([own, score[:, tokens:]], axis=1)
                    tops.append(jnp.max(own, axis=1, keepdims=True))
                    weight = jnp.exp2((own - tops[g]) * FACTOR)
                    totals.append(jnp.sum(weight, axis=1, keepdims=True))
                    weights.append(weight.astype(jnp.bfloat16))
                product = jnp.dot(
                    jnp.concatenate(weights, axis=0), values, preferred_element_type=jnp.float32
                )
                if mine < 2:
                    for g in range(GROUP):
                        result[h, :, g * HD : (g + 1) * HD] = (
                            product[g * tokens : (g + 1) * tokens, :] / totals[g]
                        ).astype(jnp.bfloat16)
                    if h:
                        copies[h - 1].start()
                else:
                    queries[h * block : (h + 1) * block, :] = query
                    sums[h * block : (h + 1) * block, :] = product
                    for g in range(GROUP):
                        at = slice(h * block + g * tokens, h * block + (g + 1) * tokens)
                        highs[at, :] = jnp.broadcast_to(tops[g], (tokens, HD))
                        counts[at, :] = jnp.broadcast_to(totals[g], (tokens, HD))
            if mine < 2:
                copies[KVH - 1].start()

    @pl.when(jnp.logical_not(live) | (z < 2))
    def _():
        for copy in copies:
            copy.wait()


def attend(lengths, base, low, kvs, ups):
    tokens, width = base.shape
    rows = HEADS * tokens
    shapes = [
        jax.ShapeDtypeStruct(base.shape, jnp.bfloat16),
        jax.ShapeDtypeStruct((rows, HD), jnp.bfloat16),
    ] + [jax.ShapeDtypeStruct((rows, HD), jnp.float32)] * 3
    return pl.pallas_call(
        attend_kernel,
        out_shape=shapes,
        in_specs=[spec(SMEM)] + [spec(VMEM)] * (2 + len(kvs) + len(ups)),
        out_specs=[spec(HBM)] + [spec(VMEM)] * 4,
        scratch_shapes=[
            VMEM((low.shape[1], width), jnp.bfloat16),
            VMEM((KVH, tokens, GROUP * HD), jnp.bfloat16),
            pltpu.SemaphoreType.DMA((KVH,)),
        ],
        compiler_params=PARAMS,
        cost_estimate=pl.CostEstimate(
            flops=1 << 30, bytes_accessed=1 << 22, transcendentals=1 << 21
        ),
    )(lengths, base, low, *kvs, *ups)


def finish_kernel(lengths, so_far, queries, sums, highs, counts, kv, out, result, sems):
    del so_far
    tokens = result.shape[1]
    z = lax.axis_index("ctx")
    block = GROUP * tokens
    copies = out_copies(result, out, sems)

    @pl.when((z * tokens < lengths[0]) & (z >= 2))
    def _():
        for h in range(KVH):
            keys, values = head_columns([kv], h)
            scores = dot_keys(queries[h * block : (h + 1) * block, :], keys)
            weights, factors, totals = [], [], []
            for g in range(GROUP):
                at = slice(h * block + g * tokens, h * block + (g + 1) * tokens)
                score = scores[g * tokens : (g + 1) * tokens, :]
                newest = jnp.maximum(highs[at, :], jnp.max(score, axis=1, keepdims=True))
                weight = jnp.exp2((score - newest) * FACTOR)
                factors.append(jnp.exp2((highs[at, :] - newest) * FACTOR))
                added = jnp.sum(weight, axis=1, keepdims=True)
                totals.append(counts[at, :] * factors[g] + added)
                weights.append(weight.astype(jnp.bfloat16))
            product = jnp.dot(
                jnp.concatenate(weights, axis=0), values, preferred_element_type=jnp.float32
            )
            for g in range(GROUP):
                at = slice(h * block + g * tokens, h * block + (g + 1) * tokens)
                whole = sums[at, :] * factors[g] + product[g * tokens : (g + 1) * tokens, :]
                result[h, :, g * HD : (g + 1) * HD] = (whole / totals[g]).astype(jnp.bfloat16)
            if h:
                copies[h - 1].start()
        copies[KVH - 1].start()
        for copy in copies:
            copy.wait()


def finish(lengths, so_far, queries, sums, highs, counts, kv):
    tokens = so_far.shape[0]
    return pl.pallas_call(
        finish_kernel,
        out_shape=jax.ShapeDtypeStruct(so_far.shape, so_far.dtype),
        in_specs=[spec(SMEM), spec(HBM)] + [spec(VMEM)] * 5,
        out_specs=spec(HBM),
        input_output_aliases={1: 0},
        scratch_shapes=[
            VMEM((KVH, tokens, GROUP * HD), jnp.bfloat16),
            pltpu.SemaphoreType.DMA((KVH,)),
        ],
        compiler_params=PARAMS,
        cost_estimate=pl.CostEstimate(
            flops=1 << 28, bytes_accessed=1 << 21, transcendentals=1 << 19
        ),
    )(lengths, so_far, queries, sums, highs, counts, kv)


def body(
    hidden_states,
    queries_base,
    kv_base,
    adapter_down,
    adapter_up,
    adapter_ids,
    adapter_slots,
    rank_buckets,
    lengths,
):
    keep_down, give_down, keep_up, give_up = select(
        adapter_ids, adapter_slots, adapter_down, adapter_up
    )
    kv = kv_base[0]
    kv_one, kv_two = spread(kv)
    near_down = lax.ppermute(give_down, "req", SIBLING)
    near_up = lax.ppermute(give_up, "req", SIBLING)
    far_down = lax.ppermute(keep_down[1] + near_down[1], "req", ACROSS)
    far_up = lax.ppermute(keep_up[1] + near_up[1], "req", ACROSS)
    down = keep_down[0] + near_down[0] + far_down
    down, kv_one = lax.optimization_barrier((down, kv_one))
    down_one, down_two = spread(down)
    up = keep_up[0] + near_up[0] + far_up
    up_one, up_two = spread(up)
    down_two = lax.optimization_barrier((down_two, kv_two))[0]
    down_three = lax.ppermute(down_two, "ctx", ONE)
    up_two = lax.optimization_barrier((up_two, down_one))[0]
    up_three = lax.ppermute(up_two, "ctx", ONE)
    kv_last = lax.optimization_barrier((kv_two, up_two, up_one))[0]
    kv_three = lax.ppermute(kv_last, "ctx", LAST)
    downs = [down, down_one, down_two, down_three]
    ups = [up, up_one, up_two, up_three]
    low = low_rank(adapter_ids, rank_buckets, hidden_states[0], downs)
    parts = attend(lengths, queries_base[0], low, [kv, kv_one, kv_two], ups)
    return finish(lengths, *parts, kv_three)[None]


def plain_body(
    hidden_states,
    queries_base,
    kv_base,
    adapter_down,
    adapter_up,
    adapter_ids,
    adapter_slots,
    rank_buckets,
    lengths,
):
    req_index = lax.axis_index("req")
    ctx_index = lax.axis_index("ctx")
    per_shard = adapter_down.shape[0]
    requests = adapter_ids.shape[0]
    store = adapter_slots.shape[0]
    rank_width = adapter_down.shape[2]
    tokens = hidden_states.shape[1]
    query_width = queries_base.shape[2]
    store_range = jnp.arange(store, dtype=jnp.int32)
    chosen = adapter_ids[:, None] == store_range[None, :]
    slot_of = jnp.sum(jnp.where(chosen, adapter_slots[None, :], 0), axis=1)
    rank_of = jnp.sum(jnp.where(chosen, rank_buckets[None, :], 0), axis=1)
    mine = jnp.arange(requests, dtype=jnp.int32) == req_index
    my_slot = jnp.sum(jnp.where(mine, slot_of, 0))
    my_rank = jnp.sum(jnp.where(mine, rank_of, 0))
    held = (
        slot_of[:, None] == req_index * per_shard + jnp.arange(per_shard, dtype=jnp.int32)[None, :]
    )
    select = held.astype(jnp.bfloat16)
    send_down = jnp.einsum(
        "qa,ard->qrd", select, adapter_down, preferred_element_type=jnp.float32
    ).astype(jnp.bfloat16)
    send_up = jnp.einsum(
        "qa,ard->qrd", select, adapter_up, preferred_element_type=jnp.float32
    ).astype(jnp.bfloat16)
    got_down, got_up = (
        lax.all_to_all(send_down, "req", split_axis=0, concat_axis=0, tiled=True),
        lax.all_to_all(send_up, "req", split_axis=0, concat_axis=0, tiled=True),
    )
    owner = my_slot // per_shard
    down_mine = lax.dynamic_index_in_dim(got_down, owner, 0, keepdims=False)
    up_mine = lax.dynamic_index_in_dim(got_up, owner, 0, keepdims=False)
    features = hidden_states[0]
    columns = features
    low_rank = jnp.dot(
        columns,
        lax.all_gather(down_mine, "ctx", axis=0, tiled=True),
        preferred_element_type=jnp.float32,
    )
    low_rank = jnp.where(
        jnp.arange(rank_width, dtype=jnp.int32)[None, :] < my_rank, low_rank, 0.0
    ).astype(jnp.bfloat16)
    columns = low_rank
    delta = jnp.dot(
        columns,
        lax.all_gather(up_mine, "ctx", axis=0, tiled=True),
        preferred_element_type=jnp.float32,
    )
    queries = (
        (queries_base[0].astype(jnp.float32) + delta)
        .astype(jnp.bfloat16)
        .reshape(tokens, KVH, GROUP, HD)
    )
    length = lengths[0]
    first_query = ctx_index * tokens
    query_pos = first_query + jnp.arange(tokens, dtype=jnp.int32)
    last_needed = jnp.minimum(first_query + tokens - 1, length - 1)
    scale = 1.0 / math.sqrt(HD)
    key_width = KVH * HD
    initial = (
        jnp.full((KVH, GROUP, tokens), -1e30, jnp.float32),
        jnp.zeros((KVH, GROUP, tokens), jnp.float32),
        jnp.zeros((KVH, GROUP, tokens, HD), jnp.float32),
    )
    piece = lax.all_gather(kv_base[0], "ctx", axis=0, tiled=True)
    count = piece.shape[0]
    width = math.gcd(count, 512)

    def key_block(index, state):
        largest, total, accum = state
        offset = index * width
        rows = lax.dynamic_slice_in_dim(piece, offset, width, 0)
        keys = rows[:, :key_width].reshape(width, KVH, HD)
        values = rows[:, key_width:].reshape(width, KVH, HD)
        key_pos = offset + jnp.arange(width, dtype=jnp.int32)
        score = (
            jnp.einsum("tkgd,skd->kgts", queries, keys, preferred_element_type=jnp.float32) * scale
        )
        allowed = (key_pos[None, :] <= query_pos[:, None]) & (key_pos[None, :] < length)
        masked = jnp.where(allowed, score, -1e30)
        newest = jnp.maximum(largest, jnp.max(masked, axis=-1))
        weight = jnp.where(allowed, jnp.exp(score - newest[..., None]), 0.0)
        factor = jnp.exp(largest - newest)
        total = total * factor + jnp.sum(weight, axis=-1)
        product = jnp.einsum(
            "kgts,skd->kgtd",
            weight.astype(jnp.bfloat16),
            values,
            preferred_element_type=jnp.float32,
        )
        accum = accum * factor[..., None] + product
        return (newest, total, accum)

    def compute(state):
        return lax.fori_loop(0, count // width, key_block, state)

    needed = (jnp.int32(0) <= last_needed) & (first_query < length)
    largest, total, accum = lax.cond(needed, compute, lambda state: state, initial)
    safe_total = jnp.where(total > 0.0, total, 1.0)
    output = accum / safe_total[..., None]
    output = jnp.transpose(output, (2, 0, 1, 3)).reshape(tokens, query_width)
    output = jnp.where(query_pos[:, None] < length, output, 0.0).astype(jnp.bfloat16)
    return output[None]


def solution(mesh):
    paired = mesh.shape["ctx"] == 4 and mesh.shape["req"] == 4
    return jax.shard_map(
        body if paired else plain_body,
        mesh=mesh,
        in_specs=(
            P(("group", "req"), "ctx", None),
            P(("group", "req"), "ctx", None),
            P(("group", "req"), "ctx", None),
            P(("group", "req"), "ctx", None),
            P(("group", "req"), "ctx", None),
            P("group"),
            P("group"),
            P("group"),
            P(("group", "req")),
        ),
        out_specs=P(("group", "req"), "ctx", None),
        check_vma=False,
    )
```

```python
import functools
import math

import jax
import jax.numpy as jnp
from jax import lax
from jax.experimental import pallas as pl
from jax.experimental.pallas import tpu as pltpu
from jax.sharding import PartitionSpec as P

HD = 128
KVH = 3
GROUP = 7
HEADS = KVH * GROUP
SMEM = pltpu.SMEM
VMEM = pltpu.VMEM
HBM = pltpu.HBM
LOG2E = 1.0 / math.log(2.0)
PARAMS = pltpu.CompilerParams(vmem_limit_bytes=32 * 1024 * 1024)
WHOLE = pltpu.CompilerParams(vmem_limit_bytes=52 * 1024 * 1024)


def spec(space):
    return pl.BlockSpec(memory_space=space)


def select_kernel(table, *rest, requests):
    stores, outs, sems = rest[:2], rest[2:6], rest[6]
    per_shard = stores[0].shape[0]
    me = lax.axis_index("req")
    first = me * per_shard
    copies = []
    for i, flip in enumerate((0, 2, 1, 3)):
        local = table[requests + table[me ^ flip]] - first
        held = (local >= 0) & (local < per_shard)
        for f, store in enumerate(stores):
            out = outs[2 * f + i // 2]
            copies.append((held, local, store, out, i % 2, sems.at[4 * f + i]))
    for held, local, store, out, k, sem in copies:

        @pl.when(held)
        def _():
            pltpu.make_async_copy(store.at[local], out.at[k], sem).start()

    for held, local, store, out, k, sem in copies:

        @pl.when(jnp.logical_not(held))
        def _():
            out[k] = jnp.zeros(out.shape[1:], out.dtype)

    for held, local, store, out, k, sem in copies:

        @pl.when(held)
        def _():
            pltpu.make_async_copy(store.at[local], out.at[k], sem).wait()


def select(ids, slots, down, up):
    shapes = [jax.ShapeDtypeStruct((2, *x.shape[1:]), x.dtype) for x in (down, down, up, up)]
    return pl.pallas_call(
        functools.partial(select_kernel, requests=ids.shape[0]),
        out_shape=shapes,
        in_specs=[spec(SMEM), spec(HBM), spec(HBM)],
        out_specs=[spec(VMEM)] * 4,
        scratch_shapes=[pltpu.SemaphoreType.DMA((8,))],
        compiler_params=WHOLE,
    )(jnp.concatenate([ids, slots]), down, up)


SIBLING = [(0, 1), (1, 0), (2, 3), (3, 2)]
ACROSS = [(0, 2), (1, 3), (2, 0), (3, 1)]
ONE = [(i, i ^ 1) for i in range(4)]
TWO = [(i, i ^ 2) for i in range(4)]
LAST = [(0, 0), (1, 1), (2, 3), (3, 2)]


def spread(shard):
    return lax.ppermute(shard, "ctx", ONE), lax.ppermute(shard, "ctx", TWO)


def low_rank_kernel(ids, ranks, hidden, *rest):
    pieces, out, accum = rest[:-2], rest[-2], rest[-1]
    rows = pieces[0].shape[0]
    rank = ranks[ids[lax.axis_index("req")]]
    accum[...] = jnp.zeros_like(accum)
    for flip, piece in enumerate(pieces):
        place = lax.axis_index("ctx") ^ flip
        columns = pl.ds(pl.multiple_of(place * rows, HD), rows)
        accum[...] += jnp.dot(hidden[:, columns], piece[...], preferred_element_type=jnp.float32)

    column = lax.broadcasted_iota(jnp.int32, accum.shape, 1)
    out[...] = jnp.where(column < rank, accum[...], 0.0).astype(jnp.bfloat16)


def low_rank(ids, ranks, hidden, pieces):
    shape = (hidden.shape[0], pieces[0].shape[1])
    return pl.pallas_call(
        low_rank_kernel,
        out_shape=jax.ShapeDtypeStruct(shape, jnp.bfloat16),
        in_specs=[spec(SMEM)] * 2 + [spec(VMEM)] * (1 + len(pieces)),
        out_specs=spec(VMEM),
        scratch_shapes=[VMEM(shape, jnp.float32)],
        compiler_params=PARAMS,
        cost_estimate=pl.CostEstimate(flops=1 << 27, bytes_accessed=1 << 22, transcendentals=0),
    )(ids, ranks, hidden, *pieces)


FACTOR = LOG2E / math.sqrt(HD)


def head_columns(kvs, h):
    keys = [kv[:, h * HD : (h + 1) * HD] for kv in kvs]
    values = [kv[:, (KVH + h) * HD : (KVH + h + 1) * HD] for kv in kvs]
    return jnp.concatenate(keys, axis=0), jnp.concatenate(values, axis=0)


def dot_keys(queries, keys):
    return lax.dot_general(
        queries, keys, (((1,), (1,)), ((), ())), preferred_element_type=jnp.float32
    )


def out_copies(result, out, sems):
    return [
        [
            pltpu.make_async_copy(
                result.at[h, :, pl.ds(g * HD, HD)],
                out.at[:, pl.ds((h * GROUP + g) * HD, HD)],
                sems.at[h * GROUP + g],
            )
            for g in range(GROUP)
        ]
        for h in range(KVH)
    ]


def attend_kernel(lengths, base, low, *rest):
    kvs, ups = rest[:3], rest[3:7]
    out, queries, sums, highs, counts, upper, result, sems = rest[7:]
    tokens = base.shape[0]
    rows = ups[0].shape[0]
    z = lax.axis_index("ctx")
    live = z * tokens < lengths[0]
    block = GROUP * tokens
    copies = out_copies(result, out, sems)

    @pl.when(jnp.logical_not(live))
    def _():
        result[...] = jnp.zeros_like(result)
        for copy in sum(copies, []):
            copy.start()

    @pl.when(live)
    def _():
        for flip, piece in enumerate(ups):
            upper[pl.ds(pl.multiple_of((z ^ flip) * rows, rows), rows), :] = piece[...]
        for j in range(HEADS):
            columns = slice(j * HD, (j + 1) * HD)
            delta = jnp.dot(low[...], upper[:, columns], preferred_element_type=jnp.float32)
            queries[j * tokens : (j + 1) * tokens, :] = (
                base[:, columns].astype(jnp.float32) + delta
            ).astype(jnp.bfloat16)

    query_pos = lax.broadcasted_iota(jnp.int32, (tokens, tokens), 0)
    key_pos = lax.broadcasted_iota(jnp.int32, (tokens, tokens), 1)
    causal = key_pos <= query_pos
    for mine, needed in enumerate(((0,), (0, 1), (0, 2), (0, 1, 2))):

        @pl.when(live & (z == mine))
        def _():
            for h in range(KVH):
                keys, values = head_columns([kvs[i] for i in needed], h)
                scores = dot_keys(queries[h * block : (h + 1) * block, :], keys)
                weights, tops, totals = [], [], []
                for g in range(GROUP):
                    score = scores[g * tokens : (g + 1) * tokens, :]
                    own = jnp.where(causal, score[:, :tokens], -1e30)
                    if mine:
                        own = jnp.concatenate([own, score[:, tokens:]], axis=1)
                    tops.append(jnp.max(own, axis=1, keepdims=True))
                    weight = jnp.exp2((own - tops[g]) * FACTOR)
                    totals.append(jnp.sum(weight, axis=1, keepdims=True))
                    weights.append(weight.astype(jnp.bfloat16))
                product = jnp.dot(
                    jnp.concatenate(weights, axis=0), values, preferred_element_type=jnp.float32
                )
                if mine < 2:
                    for g in range(GROUP):
                        result[h, :, g * HD : (g + 1) * HD] = (
                            product[g * tokens : (g + 1) * tokens, :] / totals[g]
                        ).astype(jnp.bfloat16)
                        copies[h][g].start()
                else:
                    sums[h * block : (h + 1) * block, :] = product
                    for g in range(GROUP):
                        at = slice(h * block + g * tokens, h * block + (g + 1) * tokens)
                        highs[at, :] = jnp.broadcast_to(tops[g], (tokens, HD))
                        counts[at, :] = jnp.broadcast_to(totals[g], (tokens, HD))

    @pl.when(jnp.logical_not(live) | (z < 2))
    def _():
        for copy in sum(copies, []):
            copy.wait()


def attend(lengths, base, low, kvs, ups):
    tokens, width = base.shape
    rows = HEADS * tokens
    shapes = [
        jax.ShapeDtypeStruct(base.shape, jnp.bfloat16),
        jax.ShapeDtypeStruct((rows, HD), jnp.bfloat16),
    ] + [jax.ShapeDtypeStruct((rows, HD), jnp.float32)] * 3
    return pl.pallas_call(
        attend_kernel,
        out_shape=shapes,
        in_specs=[spec(SMEM)] + [spec(VMEM)] * (2 + len(kvs) + len(ups)),
        out_specs=[spec(HBM)] + [spec(VMEM)] * 4,
        scratch_shapes=[
            VMEM((low.shape[1], width), jnp.bfloat16),
            VMEM((KVH, tokens, GROUP * HD), jnp.bfloat16),
            pltpu.SemaphoreType.DMA((HEADS,)),
        ],
        compiler_params=PARAMS,
        cost_estimate=pl.CostEstimate(
            flops=1 << 30, bytes_accessed=1 << 22, transcendentals=1 << 21
        ),
    )(lengths, base, low, *kvs, *ups)


def finish_kernel(lengths, so_far, queries, sums, highs, counts, kv, out, result, sems):
    del so_far
    tokens = result.shape[1]
    z = lax.axis_index("ctx")
    block = GROUP * tokens
    copies = out_copies(result, out, sems)

    @pl.when((z * tokens < lengths[0]) & (z >= 2))
    def _():
        for h in range(KVH):
            keys, values = head_columns([kv], h)
            scores = dot_keys(queries[h * block : (h + 1) * block, :], keys)
            weights, factors, totals = [], [], []
            for g in range(GROUP):
                at = slice(h * block + g * tokens, h * block + (g + 1) * tokens)
                score = scores[g * tokens : (g + 1) * tokens, :]
                newest = jnp.maximum(highs[at, :], jnp.max(score, axis=1, keepdims=True))
                weight = jnp.exp2((score - newest) * FACTOR)
                factors.append(jnp.exp2((highs[at, :] - newest) * FACTOR))
                added = jnp.sum(weight, axis=1, keepdims=True)
                totals.append(counts[at, :] * factors[g] + added)
                weights.append(weight.astype(jnp.bfloat16))
            product = jnp.dot(
                jnp.concatenate(weights, axis=0), values, preferred_element_type=jnp.float32
            )
            for g in range(GROUP):
                at = slice(h * block + g * tokens, h * block + (g + 1) * tokens)
                whole = sums[at, :] * factors[g] + product[g * tokens : (g + 1) * tokens, :]
                result[h, :, g * HD : (g + 1) * HD] = (whole / totals[g]).astype(jnp.bfloat16)
                copies[h][g].start()
        for copy in sum(copies, []):
            copy.wait()


def finish(lengths, so_far, queries, sums, highs, counts, kv):
    tokens = so_far.shape[0]
    return pl.pallas_call(
        finish_kernel,
        out_shape=jax.ShapeDtypeStruct(so_far.shape, so_far.dtype),
        in_specs=[spec(SMEM), spec(HBM)] + [spec(VMEM)] * 5,
        out_specs=spec(HBM),
        input_output_aliases={1: 0},
        scratch_shapes=[
            VMEM((KVH, tokens, GROUP * HD), jnp.bfloat16),
            pltpu.SemaphoreType.DMA((HEADS,)),
        ],
        compiler_params=PARAMS,
        cost_estimate=pl.CostEstimate(
            flops=1 << 28, bytes_accessed=1 << 21, transcendentals=1 << 19
        ),
    )(lengths, so_far, queries, sums, highs, counts, kv)


def body(
    hidden_states,
    queries_base,
    kv_base,
    adapter_down,
    adapter_up,
    adapter_ids,
    adapter_slots,
    rank_buckets,
    lengths,
):
    keep_down, give_down, keep_up, give_up = select(
        adapter_ids, adapter_slots, adapter_down, adapter_up
    )
    kv = kv_base[0]
    kv_one, kv_two = spread(kv)
    near_down = lax.ppermute(give_down, "req", SIBLING)
    near_up = lax.ppermute(give_up, "req", SIBLING)
    far_down = lax.ppermute(keep_down[1] + near_down[1], "req", ACROSS)
    far_up = lax.ppermute(keep_up[1] + near_up[1], "req", ACROSS)
    down = keep_down[0] + near_down[0] + far_down
    down, kv_one = lax.optimization_barrier((down, kv_one))
    down_one, down_two = spread(down)
    up = keep_up[0] + near_up[0] + far_up
    up_one, up_two = spread(up)
    down_two = lax.optimization_barrier((down_two, kv_two))[0]
    down_three = lax.ppermute(down_two, "ctx", ONE)
    up_two = lax.optimization_barrier((up_two, down_one))[0]
    up_three = lax.ppermute(up_two, "ctx", ONE)
    kv_last = lax.optimization_barrier((kv_two, up_two, up_one))[0]
    kv_three = lax.ppermute(kv_last, "ctx", LAST)
    downs = [down, down_one, down_two, down_three]
    ups = [up, up_one, up_two, up_three]
    low = low_rank(adapter_ids, rank_buckets, hidden_states[0], downs)
    parts = attend(lengths, queries_base[0], low, [kv, kv_one, kv_two], ups)
    return finish(lengths, *parts, kv_three)[None]


def plain_body(
    hidden_states,
    queries_base,
    kv_base,
    adapter_down,
    adapter_up,
    adapter_ids,
    adapter_slots,
    rank_buckets,
    lengths,
):
    req_index = lax.axis_index("req")
    ctx_index = lax.axis_index("ctx")
    per_shard = adapter_down.shape[0]
    requests = adapter_ids.shape[0]
    store = adapter_slots.shape[0]
    rank_width = adapter_down.shape[2]
    tokens = hidden_states.shape[1]
    query_width = queries_base.shape[2]
    store_range = jnp.arange(store, dtype=jnp.int32)
    chosen = adapter_ids[:, None] == store_range[None, :]
    slot_of = jnp.sum(jnp.where(chosen, adapter_slots[None, :], 0), axis=1)
    rank_of = jnp.sum(jnp.where(chosen, rank_buckets[None, :], 0), axis=1)
    mine = jnp.arange(requests, dtype=jnp.int32) == req_index
    my_slot = jnp.sum(jnp.where(mine, slot_of, 0))
    my_rank = jnp.sum(jnp.where(mine, rank_of, 0))
    held = (
        slot_of[:, None] == req_index * per_shard + jnp.arange(per_shard, dtype=jnp.int32)[None, :]
    )
    select = held.astype(jnp.bfloat16)
    send_down = jnp.einsum(
        "qa,ard->qrd", select, adapter_down, preferred_element_type=jnp.float32
    ).astype(jnp.bfloat16)
    send_up = jnp.einsum(
        "qa,ard->qrd", select, adapter_up, preferred_element_type=jnp.float32
    ).astype(jnp.bfloat16)
    got_down, got_up = (
        lax.all_to_all(send_down, "req", split_axis=0, concat_axis=0, tiled=True),
        lax.all_to_all(send_up, "req", split_axis=0, concat_axis=0, tiled=True),
    )
    owner = my_slot // per_shard
    down_mine = lax.dynamic_index_in_dim(got_down, owner, 0, keepdims=False)
    up_mine = lax.dynamic_index_in_dim(got_up, owner, 0, keepdims=False)
    features = hidden_states[0]
    columns = features
    low_rank = jnp.dot(
        columns,
        lax.all_gather(down_mine, "ctx", axis=0, tiled=True),
        preferred_element_type=jnp.float32,
    )
    low_rank = jnp.where(
        jnp.arange(rank_width, dtype=jnp.int32)[None, :] < my_rank, low_rank, 0.0
    ).astype(jnp.bfloat16)
    columns = low_rank
    delta = jnp.dot(
        columns,
        lax.all_gather(up_mine, "ctx", axis=0, tiled=True),
        preferred_element_type=jnp.float32,
    )
    queries = (
        (queries_base[0].astype(jnp.float32) + delta)
        .astype(jnp.bfloat16)
        .reshape(tokens, KVH, GROUP, HD)
    )
    length = lengths[0]
    first_query = ctx_index * tokens
    query_pos = first_query + jnp.arange(tokens, dtype=jnp.int32)
    last_needed = jnp.minimum(first_query + tokens - 1, length - 1)
    scale = 1.0 / math.sqrt(HD)
    key_width = KVH * HD
    initial = (
        jnp.full((KVH, GROUP, tokens), -1e30, jnp.float32),
        jnp.zeros((KVH, GROUP, tokens), jnp.float32),
        jnp.zeros((KVH, GROUP, tokens, HD), jnp.float32),
    )
    piece = lax.all_gather(kv_base[0], "ctx", axis=0, tiled=True)
    count = piece.shape[0]
    width = math.gcd(count, 512)

    def key_block(index, state):
        largest, total, accum = state
        offset = index * width
        rows = lax.dynamic_slice_in_dim(piece, offset, width, 0)
        keys = rows[:, :key_width].reshape(width, KVH, HD)
        values = rows[:, key_width:].reshape(width, KVH, HD)
        key_pos = offset + jnp.arange(width, dtype=jnp.int32)
        score = (
            jnp.einsum("tkgd,skd->kgts", queries, keys, preferred_element_type=jnp.float32) * scale
        )
        allowed = (key_pos[None, :] <= query_pos[:, None]) & (key_pos[None, :] < length)
        masked = jnp.where(allowed, score, -1e30)
        newest = jnp.maximum(largest, jnp.max(masked, axis=-1))
        weight = jnp.where(allowed, jnp.exp(score - newest[..., None]), 0.0)
        factor = jnp.exp(largest - newest)
        total = total * factor + jnp.sum(weight, axis=-1)
        product = jnp.einsum(
            "kgts,skd->kgtd",
            weight.astype(jnp.bfloat16),
            values,
            preferred_element_type=jnp.float32,
        )
        accum = accum * factor[..., None] + product
        return (newest, total, accum)

    def compute(state):
        return lax.fori_loop(0, count // width, key_block, state)

    needed = (jnp.int32(0) <= last_needed) & (first_query < length)
    largest, total, accum = lax.cond(needed, compute, lambda state: state, initial)
    safe_total = jnp.where(total > 0.0, total, 1.0)
    output = accum / safe_total[..., None]
    output = jnp.transpose(output, (2, 0, 1, 3)).reshape(tokens, query_width)
    output = jnp.where(query_pos[:, None] < length, output, 0.0).astype(jnp.bfloat16)
    return output[None]


def solution(mesh):
    paired = mesh.shape["ctx"] == 4 and mesh.shape["req"] == 4
    return jax.shard_map(
        body if paired else plain_body,
        mesh=mesh,
        in_specs=(
            P(("group", "req"), "ctx", None),
            P(("group", "req"), "ctx", None),
            P(("group", "req"), "ctx", None),
            P(("group", "req"), "ctx", None),
            P(("group", "req"), "ctx", None),
            P("group"),
            P("group"),
            P("group"),
            P(("group", "req")),
        ),
        out_specs=P(("group", "req"), "ctx", None),
        check_vma=False,
    )
```

```python
import functools
import math

import jax
import jax.numpy as jnp
from jax import lax
from jax.experimental import pallas as pl
from jax.experimental.pallas import tpu as pltpu
from jax.sharding import PartitionSpec as P

HD = 128
KVH = 3
GROUP = 7
HEADS = KVH * GROUP
SMEM = pltpu.SMEM
VMEM = pltpu.VMEM
HBM = pltpu.HBM
LOG2E = 1.0 / math.log(2.0)
PARAMS = pltpu.CompilerParams(vmem_limit_bytes=32 * 1024 * 1024)
WHOLE = pltpu.CompilerParams(vmem_limit_bytes=52 * 1024 * 1024)


def spec(space):
    return pl.BlockSpec(memory_space=space)


def select_kernel(table, *rest, requests):
    stores, outs, sems = rest[:2], rest[2:6], rest[6]
    per_shard = stores[0].shape[0]
    me = lax.axis_index("req")
    first = me * per_shard
    copies = []
    for i, flip in enumerate((0, 2, 1, 3)):
        local = table[requests + table[me ^ flip]] - first
        held = (local >= 0) & (local < per_shard)
        for f, store in enumerate(stores):
            out = outs[2 * f + i // 2]
            copies.append((held, local, store, out, i % 2, sems.at[4 * f + i]))
    for held, local, store, out, k, sem in copies:

        @pl.when(held)
        def _():
            pltpu.make_async_copy(store.at[local], out.at[k], sem).start()

    for held, local, store, out, k, sem in copies:

        @pl.when(jnp.logical_not(held))
        def _():
            out[k] = jnp.zeros(out.shape[1:], out.dtype)

    for held, local, store, out, k, sem in copies:

        @pl.when(held)
        def _():
            pltpu.make_async_copy(store.at[local], out.at[k], sem).wait()


def select(ids, slots, down, up):
    shapes = [jax.ShapeDtypeStruct((2, *x.shape[1:]), x.dtype) for x in (down, down, up, up)]
    return pl.pallas_call(
        functools.partial(select_kernel, requests=ids.shape[0]),
        out_shape=shapes,
        in_specs=[spec(SMEM), spec(HBM), spec(HBM)],
        out_specs=[spec(VMEM)] * 4,
        scratch_shapes=[pltpu.SemaphoreType.DMA((8,))],
        compiler_params=WHOLE,
    )(jnp.concatenate([ids, slots]), down, up)


SIBLING = [(0, 1), (1, 0), (2, 3), (3, 2)]
ACROSS = [(0, 2), (1, 3), (2, 0), (3, 1)]
ONE = [(i, i ^ 1) for i in range(4)]
TWO = [(i, i ^ 2) for i in range(4)]
LAST = [(0, 0), (1, 1), (2, 3), (3, 2)]


def spread(shard):
    return lax.ppermute(shard, "ctx", ONE), lax.ppermute(shard, "ctx", TWO)


def low_rank_kernel(ids, ranks, hidden, *rest):
    pieces, out, accum = rest[:-2], rest[-2], rest[-1]
    rows = pieces[0].shape[0]
    rank = ranks[ids[lax.axis_index("req")]]
    accum[...] = jnp.zeros_like(accum)
    for flip, piece in enumerate(pieces):
        place = lax.axis_index("ctx") ^ flip
        columns = pl.ds(pl.multiple_of(place * rows, HD), rows)
        accum[...] += jnp.dot(hidden[:, columns], piece[...], preferred_element_type=jnp.float32)

    column = lax.broadcasted_iota(jnp.int32, accum.shape, 1)
    out[...] = jnp.where(column < rank, accum[...], 0.0).astype(jnp.bfloat16)


def low_rank(ids, ranks, hidden, pieces):
    shape = (hidden.shape[0], pieces[0].shape[1])
    return pl.pallas_call(
        low_rank_kernel,
        out_shape=jax.ShapeDtypeStruct(shape, jnp.bfloat16),
        in_specs=[spec(SMEM)] * 2 + [spec(VMEM)] * (1 + len(pieces)),
        out_specs=spec(VMEM),
        scratch_shapes=[VMEM(shape, jnp.float32)],
        compiler_params=PARAMS,
        cost_estimate=pl.CostEstimate(flops=1 << 27, bytes_accessed=1 << 22, transcendentals=0),
    )(ids, ranks, hidden, *pieces)


FACTOR = LOG2E / math.sqrt(HD)


def head_columns(kvs, h):
    keys = [kv[:, h * HD : (h + 1) * HD] for kv in kvs]
    values = [kv[:, (KVH + h) * HD : (KVH + h + 1) * HD] for kv in kvs]
    return jnp.concatenate(keys, axis=0), jnp.concatenate(values, axis=0)


def dot_keys(queries, keys):
    return lax.dot_general(
        queries, keys, (((1,), (1,)), ((), ())), preferred_element_type=jnp.float32
    )


def out_copies(result, out, sems):
    width = GROUP * HD
    return [
        pltpu.make_async_copy(result.at[h], out.at[:, pl.ds(h * width, width)], sems.at[h])
        for h in range(KVH)
    ]


def attend_kernel(lengths, base, low, *rest):
    kvs, ups = rest[:3], rest[3:7]
    out, queries, sums, highs, counts, upper, result, sems = rest[7:]
    tokens = base.shape[0]
    rows = ups[0].shape[0]
    z = lax.axis_index("ctx")
    live = z * tokens < lengths[0]
    block = GROUP * tokens
    copies = out_copies(result, out, sems)

    @pl.when(jnp.logical_not(live))
    def _():
        result[...] = jnp.zeros_like(result)
        for copy in copies:
            copy.start()

    @pl.when(live)
    def _():
        for flip, piece in enumerate(ups):
            upper[pl.ds(pl.multiple_of((z ^ flip) * rows, rows), rows), :] = piece[...]
        for j in range(HEADS):
            columns = slice(j * HD, (j + 1) * HD)
            delta = jnp.dot(low[...], upper[:, columns], preferred_element_type=jnp.float32)
            queries[j * tokens : (j + 1) * tokens, :] = (
                base[:, columns].astype(jnp.float32) + delta
            ).astype(jnp.bfloat16)

    query_pos = lax.broadcasted_iota(jnp.int32, (tokens, tokens), 0)
    key_pos = lax.broadcasted_iota(jnp.int32, (tokens, tokens), 1)
    causal = key_pos <= query_pos
    for mine, needed in enumerate(((0,), (0, 1), (0, 2), (0, 1, 2))):

        @pl.when(live & (z == mine))
        def _():
            for h in range(KVH):
                keys, values = head_columns([kvs[i] for i in needed], h)
                scores = dot_keys(queries[h * block : (h + 1) * block, :], keys)
                weights, tops, totals = [], [], []
                for g in range(GROUP):
                    score = scores[g * tokens : (g + 1) * tokens, :]
                    own = jnp.where(causal, score[:, :tokens], -1e30)
                    if mine:
                        own = jnp.concatenate([own, score[:, tokens:]], axis=1)
                    tops.append(jnp.max(own, axis=1, keepdims=True))
                    weight = jnp.exp2((own - tops[g]) * FACTOR)
                    totals.append(jnp.sum(weight, axis=1, keepdims=True))
                    weights.append(weight.astype(jnp.bfloat16))
                product = jnp.dot(
                    jnp.concatenate(weights, axis=0), values, preferred_element_type=jnp.float32
                )
                if mine < 2:
                    for g in range(GROUP):
                        result[h, :, g * HD : (g + 1) * HD] = (
                            product[g * tokens : (g + 1) * tokens, :] / totals[g]
                        ).astype(jnp.bfloat16)
                    copies[h].start()
                else:
                    sums[h * block : (h + 1) * block, :] = product
                    for g in range(GROUP):
                        at = slice(h * block + g * tokens, h * block + (g + 1) * tokens)
                        highs[at, :] = jnp.broadcast_to(tops[g], (tokens, HD))
                        counts[at, :] = jnp.broadcast_to(totals[g], (tokens, HD))

    @pl.when(jnp.logical_not(live) | (z < 2))
    def _():
        for copy in copies:
            copy.wait()


def attend(lengths, base, low, kvs, ups):
    tokens, width = base.shape
    rows = HEADS * tokens
    shapes = [
        jax.ShapeDtypeStruct(base.shape, jnp.bfloat16),
        jax.ShapeDtypeStruct((rows, HD), jnp.bfloat16),
    ] + [jax.ShapeDtypeStruct((rows, HD), jnp.float32)] * 3
    return pl.pallas_call(
        attend_kernel,
        out_shape=shapes,
        in_specs=[spec(SMEM)] + [spec(VMEM)] * (2 + len(kvs) + len(ups)),
        out_specs=[spec(HBM)] + [spec(VMEM)] * 4,
        scratch_shapes=[
            VMEM((low.shape[1], width), jnp.bfloat16),
            VMEM((KVH, tokens, GROUP * HD), jnp.bfloat16),
            pltpu.SemaphoreType.DMA((KVH,)),
        ],
        compiler_params=PARAMS,
        cost_estimate=pl.CostEstimate(
            flops=1 << 30, bytes_accessed=1 << 22, transcendentals=1 << 21
        ),
    )(lengths, base, low, *kvs, *ups)


def finish_kernel(lengths, so_far, queries, sums, highs, counts, kv, out, result, sems):
    del so_far
    tokens = result.shape[1]
    z = lax.axis_index("ctx")
    block = GROUP * tokens
    copies = out_copies(result, out, sems)

    @pl.when((z * tokens < lengths[0]) & (z >= 2))
    def _():
        for h in range(KVH):
            keys, values = head_columns([kv], h)
            scores = dot_keys(queries[h * block : (h + 1) * block, :], keys)
            weights, factors, totals = [], [], []
            for g in range(GROUP):
                at = slice(h * block + g * tokens, h * block + (g + 1) * tokens)
                score = scores[g * tokens : (g + 1) * tokens, :]
                newest = jnp.maximum(highs[at, :], jnp.max(score, axis=1, keepdims=True))
                weight = jnp.exp2((score - newest) * FACTOR)
                factors.append(jnp.exp2((highs[at, :] - newest) * FACTOR))
                added = jnp.sum(weight, axis=1, keepdims=True)
                totals.append(counts[at, :] * factors[g] + added)
                weights.append(weight.astype(jnp.bfloat16))
            product = jnp.dot(
                jnp.concatenate(weights, axis=0), values, preferred_element_type=jnp.float32
            )
            for g in range(GROUP):
                at = slice(h * block + g * tokens, h * block + (g + 1) * tokens)
                whole = sums[at, :] * factors[g] + product[g * tokens : (g + 1) * tokens, :]
                result[h, :, g * HD : (g + 1) * HD] = (whole / totals[g]).astype(jnp.bfloat16)
            copies[h].start()
        for copy in copies:
            copy.wait()


def finish(lengths, so_far, queries, sums, highs, counts, kv):
    tokens = so_far.shape[0]
    return pl.pallas_call(
        finish_kernel,
        out_shape=jax.ShapeDtypeStruct(so_far.shape, so_far.dtype),
        in_specs=[spec(SMEM), spec(HBM)] + [spec(VMEM)] * 5,
        out_specs=spec(HBM),
        input_output_aliases={1: 0},
        scratch_shapes=[
            VMEM((KVH, tokens, GROUP * HD), jnp.bfloat16),
            pltpu.SemaphoreType.DMA((KVH,)),
        ],
        compiler_params=PARAMS,
        cost_estimate=pl.CostEstimate(
            flops=1 << 28, bytes_accessed=1 << 21, transcendentals=1 << 19
        ),
    )(lengths, so_far, queries, sums, highs, counts, kv)


def body(
    hidden_states,
    queries_base,
    kv_base,
    adapter_down,
    adapter_up,
    adapter_ids,
    adapter_slots,
    rank_buckets,
    lengths,
):
    keep_down, give_down, keep_up, give_up = select(
        adapter_ids, adapter_slots, adapter_down, adapter_up
    )
    kv = kv_base[0]
    kv_one, kv_two = spread(kv)
    near_down = lax.ppermute(give_down, "req", SIBLING)
    near_up = lax.ppermute(give_up, "req", SIBLING)
    far_down = lax.ppermute(keep_down[1] + near_down[1], "req", ACROSS)
    far_up = lax.ppermute(keep_up[1] + near_up[1], "req", ACROSS)
    down = keep_down[0] + near_down[0] + far_down
    down, kv_one = lax.optimization_barrier((down, kv_one))
    down_one, down_two = spread(down)
    up = keep_up[0] + near_up[0] + far_up
    up_one, up_two = spread(up)
    down_two = lax.optimization_barrier((down_two, kv_two))[0]
    down_three = lax.ppermute(down_two, "ctx", ONE)
    up_two = lax.optimization_barrier((up_two, down_one))[0]
    up_three = lax.ppermute(up_two, "ctx", ONE)
    kv_last = lax.optimization_barrier((kv_two, up_two))[0]
    kv_three = lax.ppermute(kv_last, "ctx", LAST)
    downs = [down, down_one, down_two, down_three]
    ups = [up, up_one, up_two, up_three]
    down_three, up_one = lax.optimization_barrier((down_three, up_one))
    downs[3], ups[1] = down_three, up_one
    low = low_rank(adapter_ids, rank_buckets, hidden_states[0], downs)
    parts = attend(lengths, queries_base[0], low, [kv, kv_one, kv_two], ups)
    return finish(lengths, *parts, kv_three)[None]


def plain_body(
    hidden_states,
    queries_base,
    kv_base,
    adapter_down,
    adapter_up,
    adapter_ids,
    adapter_slots,
    rank_buckets,
    lengths,
):
    req_index = lax.axis_index("req")
    ctx_index = lax.axis_index("ctx")
    per_shard = adapter_down.shape[0]
    requests = adapter_ids.shape[0]
    store = adapter_slots.shape[0]
    rank_width = adapter_down.shape[2]
    tokens = hidden_states.shape[1]
    query_width = queries_base.shape[2]
    store_range = jnp.arange(store, dtype=jnp.int32)
    chosen = adapter_ids[:, None] == store_range[None, :]
    slot_of = jnp.sum(jnp.where(chosen, adapter_slots[None, :], 0), axis=1)
    rank_of = jnp.sum(jnp.where(chosen, rank_buckets[None, :], 0), axis=1)
    mine = jnp.arange(requests, dtype=jnp.int32) == req_index
    my_slot = jnp.sum(jnp.where(mine, slot_of, 0))
    my_rank = jnp.sum(jnp.where(mine, rank_of, 0))
    held = (
        slot_of[:, None] == req_index * per_shard + jnp.arange(per_shard, dtype=jnp.int32)[None, :]
    )
    select = held.astype(jnp.bfloat16)
    send_down = jnp.einsum(
        "qa,ard->qrd", select, adapter_down, preferred_element_type=jnp.float32
    ).astype(jnp.bfloat16)
    send_up = jnp.einsum(
        "qa,ard->qrd", select, adapter_up, preferred_element_type=jnp.float32
    ).astype(jnp.bfloat16)
    got_down, got_up = (
        lax.all_to_all(send_down, "req", split_axis=0, concat_axis=0, tiled=True),
        lax.all_to_all(send_up, "req", split_axis=0, concat_axis=0, tiled=True),
    )
    owner = my_slot // per_shard
    down_mine = lax.dynamic_index_in_dim(got_down, owner, 0, keepdims=False)
    up_mine = lax.dynamic_index_in_dim(got_up, owner, 0, keepdims=False)
    features = hidden_states[0]
    columns = features
    low_rank = jnp.dot(
        columns,
        lax.all_gather(down_mine, "ctx", axis=0, tiled=True),
        preferred_element_type=jnp.float32,
    )
    low_rank = jnp.where(
        jnp.arange(rank_width, dtype=jnp.int32)[None, :] < my_rank, low_rank, 0.0
    ).astype(jnp.bfloat16)
    columns = low_rank
    delta = jnp.dot(
        columns,
        lax.all_gather(up_mine, "ctx", axis=0, tiled=True),
        preferred_element_type=jnp.float32,
    )
    queries = (
        (queries_base[0].astype(jnp.float32) + delta)
        .astype(jnp.bfloat16)
        .reshape(tokens, KVH, GROUP, HD)
    )
    length = lengths[0]
    first_query = ctx_index * tokens
    query_pos = first_query + jnp.arange(tokens, dtype=jnp.int32)
    last_needed = jnp.minimum(first_query + tokens - 1, length - 1)
    scale = 1.0 / math.sqrt(HD)
    key_width = KVH * HD
    initial = (
        jnp.full((KVH, GROUP, tokens), -1e30, jnp.float32),
        jnp.zeros((KVH, GROUP, tokens), jnp.float32),
        jnp.zeros((KVH, GROUP, tokens, HD), jnp.float32),
    )
    piece = lax.all_gather(kv_base[0], "ctx", axis=0, tiled=True)
    count = piece.shape[0]
    width = math.gcd(count, 512)

    def key_block(index, state):
        largest, total, accum = state
        offset = index * width
        rows = lax.dynamic_slice_in_dim(piece, offset, width, 0)
        keys = rows[:, :key_width].reshape(width, KVH, HD)
        values = rows[:, key_width:].reshape(width, KVH, HD)
        key_pos = offset + jnp.arange(width, dtype=jnp.int32)
        score = (
            jnp.einsum("tkgd,skd->kgts", queries, keys, preferred_element_type=jnp.float32) * scale
        )
        allowed = (key_pos[None, :] <= query_pos[:, None]) & (key_pos[None, :] < length)
        masked = jnp.where(allowed, score, -1e30)
        newest = jnp.maximum(largest, jnp.max(masked, axis=-1))
        weight = jnp.where(allowed, jnp.exp(score - newest[..., None]), 0.0)
        factor = jnp.exp(largest - newest)
        total = total * factor + jnp.sum(weight, axis=-1)
        product = jnp.einsum(
            "kgts,skd->kgtd",
            weight.astype(jnp.bfloat16),
            values,
            preferred_element_type=jnp.float32,
        )
        accum = accum * factor[..., None] + product
        return (newest, total, accum)

    def compute(state):
        return lax.fori_loop(0, count // width, key_block, state)

    needed = (jnp.int32(0) <= last_needed) & (first_query < length)
    largest, total, accum = lax.cond(needed, compute, lambda state: state, initial)
    safe_total = jnp.where(total > 0.0, total, 1.0)
    output = accum / safe_total[..., None]
    output = jnp.transpose(output, (2, 0, 1, 3)).reshape(tokens, query_width)
    output = jnp.where(query_pos[:, None] < length, output, 0.0).astype(jnp.bfloat16)
    return output[None]


def solution(mesh):
    paired = mesh.shape["ctx"] == 4 and mesh.shape["req"] == 4
    return jax.shard_map(
        body if paired else plain_body,
        mesh=mesh,
        in_specs=(
            P(("group", "req"), "ctx", None),
            P(("group", "req"), "ctx", None),
            P(("group", "req"), "ctx", None),
            P(("group", "req"), "ctx", None),
            P(("group", "req"), "ctx", None),
            P("group"),
            P("group"),
            P("group"),
            P(("group", "req")),
        ),
        out_specs=P(("group", "req"), "ctx", None),
        check_vma=False,
    )
```
